256 devices in a mesh: dp: 32 (over y, x, core), mp: 8 (over z).
Axes of the slice: x: 4, y: 4, z: 8, core: 2. Of those that a mesh axis runs over, the one named last changes fastest.
Arguments:
- tile_features: bfloat16 [6144, 1536], P('dp'), may hold values from -6 to 6
- tile_slide: int32 [6144, 1], P('dp'), may hold values from 0 to 31; in each aligned block of 192 rows (0 to 191, 192 to 383, ...) at most 12 rows name the same one
- slide_pair: int32 [32], replicated, may hold values from 0 to 31, each once
- reports: bfloat16 [32, 1536], P('dp'), may hold values from -6 to 6
- w_one: bfloat16 [1536, 6144], P(None, 'mp'), may hold values from -0.15625 to 0.15625
- w_two: bfloat16 [6144, 1536], P('mp'), may hold values from -0.078125 to 0.078125
- w_query: bfloat16 [1536, 1536], P(None, 'mp'), may hold values from -0.15625 to 0.15625
- w_key: bfloat16 [1536, 1536], P(None, 'mp'), may hold values from -0.15625 to 0.15625
- w_value: bfloat16 [1536, 1536], P(None, 'mp'), may hold values from -0.15625 to 0.15625
- w_out: bfloat16 [1536, 1536], P('mp'), may hold values from -0.15625 to 0.15625
Outputs:
- contrast_loss: float32 [], replicated
- grad_one: float32 [1536, 6144], P('dp', 'mp')
- grad_two: float32 [6144, 1536], P('mp', 'dp')
- grad_query: float32 [1536, 1536], P('dp', 'mp')
- grad_key: float32 [1536, 1536], P('dp', 'mp')
- grad_value: float32 [1536, 1536], P('dp', 'mp')
- grad_out: float32 [1536, 1536], P('mp', 'dp')
The draws below stay inside these ranges and needn't reach their ends.
Inputs may be any that keep to these rules, and one draw needn't show every extreme that they name: `tile_slide`: within the 192 tiles of one device (aligned blocks) no slide has more than 12 tiles, and some slide has exactly 12; every slide has at least one tile. `slide_pair`: each report is paired with exactly one slide.
All inputs are finite; a program needn't handle non-finite values.
Results may differ from the reference program's by a relative error of at most 0.039.
Values may be sent and summed in bfloat16 or wider, within the bound.
No kernel may reach another device: no remote copies, remote signals or barrier semaphores. Data moves between devices by JAX's collectives and lax.ppermute only.
A program may use at most 128 MiB of HBM per device.

```python
import math
import jax
import jax.numpy as jnp
import numpy as np
from jax import lax

D = 1536
FF = 6144
HEAD = 96
TOK_DEV = 192
CAP = 12
SLIDES = 32
TILES = 6144
N_DP = 32


def levels(stream_key, dims, split, smallest, high):
    factor_of, own = 1.0, jax.random.fold_in(stream_key, 6)
    for dim, blocks in split:
        steps = jnp.exp(jax.random.uniform(jax.random.fold_in(own, dim), (blocks,), jnp.float32, smallest / len(split), high / len(split)))
        factor_of = factor_of * jnp.repeat(steps, dims[dim] // blocks).reshape([-1 if axis == dim else 1 for axis in range(len(dims))])
    return factor_of


def deal_out(stream_key, own, number, rows, number_of, top, bound, slope):
    sequence = jax.random.permutation(stream_key, number_of)
    packed, common = load_shares(number_of, rows * top, bound, slope, True), load_shares(number_of, rows * top, bound, slope, False)
    places = jnp.arange(number_of)

    def named(tallies, turn):
        used = int((tallies > 0).sum())
        fixed = max(1, used // 4)
        moved = fixed + (places - fixed + turn * (used - fixed)) % max(1, number_of - fixed)
        return jnp.zeros((number_of,), jnp.int32).at[sequence[jnp.where(places < fixed, places, moved)]].set(jnp.asarray(tallies, jnp.int32))

    tallies = jnp.where(number % 4 == 0, named(packed, number // 4), named(common, number - number // 4 - 1))
    mixed = jax.random.permutation(jax.random.fold_in(own, 3), number_of)
    donor, sink = mixed[0:number_of // 2 * 2:2], mixed[1:number_of // 2 * 2:2]
    margin = jnp.minimum(tallies[donor] - 1, bound - tallies[sink]) // 2
    margin = jnp.where((donor == sequence[0]) | (sink == sequence[0]) | (tallies[sink] == 0), 0, jnp.maximum(margin, 0))
    moved = jax.random.randint(jax.random.fold_in(own, 4), (number_of // 2,), 0, 1 << 20) % (margin + 1)
    tallies = tallies.at[donor].add(-moved).at[sink].add(moved)
    labels = jnp.searchsorted(jnp.cumsum(tallies), jnp.arange(rows * top), side="right").astype(jnp.int32)
    table = labels.reshape(top, rows).T
    table = table[jax.random.permutation(jax.random.fold_in(own, 1), rows)]
    turn = jax.random.randint(jax.random.fold_in(own, 2), (rows, 1), 0, top)
    return jnp.take_along_axis(table, (jnp.arange(top)[None, :] + turn) % top, axis=1)


def load_shares(amount, total, reach, skew, full):
    portions = [(1 << 20) // math.isqrt(standing ** skew) + 1 for standing in range(1, amount + 1)]
    largest = reach if full else min(reach, max(-(-total // amount), total * portions[0] // sum(portions)))
    least = 1 if total - largest >= amount - 1 else 0
    given, spare = [largest] + [least] * (amount - 1), total - largest - least * (amount - 1)
    while spare > 0:
        candidates = [i for i in range(1, amount) if given[i] < largest] or [i for i in range(1, amount) if given[i] < reach]
        whole, left = sum([portions[i] for i in candidates]), spare
        for i in candidates:
            addition = min(reach - given[i], max(1, left * portions[i] // whole), spare)
            given[i] = given[i] + addition
            spare = spare - addition
    return np.array(given)


def gaussian(rng, dims, width, limit, shards=(), kind=jnp.bfloat16):
    factor_of = levels(rng, dims, shards, -0.22, 0.18) if shards else 1.0
    values = jax.random.normal(rng, dims, jnp.float32) * width * factor_of
    return jnp.minimum(jnp.maximum(values, -limit), limit).astype(kind)


def setup_inputs(seed: int = 0) -> dict:
    seeds = jax.random.split(jax.random.key(seed), 11)
    tile_features = gaussian(seeds[0], (TILES, D), 1.0, 6.0, ((0, 32),))
    tile_slide_keys = jax.random.split(jax.random.fold_in(seeds[1], 1), TILES // TOK_DEV)
    tile_slide_turns = jax.random.permutation(jax.random.fold_in(seeds[1], 3), TILES // TOK_DEV)
    tile_slide = jax.vmap(lambda own, number: deal_out(jax.random.fold_in(seeds[1], 2), own, number, TOK_DEV, SLIDES, 1, CAP, 2))(tile_slide_keys, tile_slide_turns).reshape((TILES, 1))
    slide_pair = jax.random.permutation(seeds[2], SLIDES).astype(jnp.int32)
    reports = gaussian(seeds[3], (SLIDES, D), 1.0, 6.0, ((0, 32),))
    w_one = gaussian(seeds[4], (D, FF), D ** -0.5, 0.15625, ((1, 8),))
    w_two = gaussian(seeds[5], (FF, D), FF ** -0.5, 0.078125, ((0, 8),))
    w_query = gaussian(seeds[6], (D, D), D ** -0.5, 0.15625, ((1, 8),))
    w_key = gaussian(seeds[7], (D, D), D ** -0.5, 0.15625, ((1, 8),))
    w_value = gaussian(seeds[8], (D, D), D ** -0.5, 0.15625, ((1, 8),))
    w_out = gaussian(seeds[9], (D, D), D ** -0.5, 0.15625, ((0, 8),))
    return {"tile_features": tile_features, "tile_slide": tile_slide, "slide_pair": slide_pair, "reports": reports, "w_one": w_one, "w_two": w_two, "w_query": w_query, "w_key": w_key, "w_value": w_value, "w_out": w_out}


eps = 1e-05
contrast_divisor_factor = 0.07
score_scale = 10.0
loss_scale = 4096.0
finest_arithmetic_mode = lax.Precision.HIGHEST

def norm_parts(values):
    centred = values - lax.optimization_barrier(jnp.mean(values, -1, keepdims=True))
    inverse = lax.rsqrt(lax.optimization_barrier(jnp.mean(centred * centred, -1, keepdims=True)) + eps)
    return (centred * inverse, inverse)

def gelu_value(values):
    return 0.5 * values * (1.0 + jax.scipy.special.erf(values * 0.7071067811865476))

def gelu_slope(values):
    return 0.5 * (1.0 + jax.scipy.special.erf(values * 0.7071067811865476)) + values * jnp.exp(-0.5 * values * values) * 0.3989422804014327

def unit_heads(values):
    return values * lax.rsqrt(lax.optimization_barrier(jnp.mean(values * values, -1, keepdims=True)) + eps)

def attend(query, keys, values, validity):
    length = query.shape[0]
    heads = query.shape[1] // HEAD
    query_unit = unit_heads(query.reshape(length, heads, HEAD))
    key_unit = unit_heads(keys.reshape(length, heads, HEAD))
    scores = jnp.einsum('qhd,khd->hqk', query_unit, key_unit, precision=finest_arithmetic_mode) * (score_scale / HEAD)
    weights = jnp.exp(scores) * validity[None, None, :]
    weights = weights / lax.optimization_barrier(jnp.sum(weights, -1, keepdims=True))
    mixed = jnp.einsum('hqk,khd->qhd', weights, values.reshape(length, heads, HEAD), precision=finest_arithmetic_mode)
    return mixed.reshape(length, heads * HEAD)

def slide_forward(slide_rows, validity, w_query, w_key, w_value, w_out):
    rows_float = slide_rows.astype(jnp.float32)
    normed, inverse = norm_parts(rows_float)
    slide_norm = normed.astype(jnp.bfloat16)
    query = jnp.dot(slide_norm, w_query, preferred_element_type=jnp.float32)
    keys = jnp.dot(slide_norm, w_key, preferred_element_type=jnp.float32)
    values = jnp.dot(slide_norm, w_value, preferred_element_type=jnp.float32)
    attended = attend(query, keys, values, validity).astype(jnp.bfloat16)
    output = rows_float + jnp.dot(attended, w_out, preferred_element_type=jnp.float32)
    pooled = lax.optimization_barrier(jnp.sum(output * validity[:, None], 0)) / jnp.sum(validity)
    return (normed, inverse, slide_norm, query, keys, values, attended, pooled)

def contrast(pooled, reports, slide_pair):
    inverse = lax.rsqrt(lax.optimization_barrier(jnp.sum(pooled * pooled, -1, keepdims=True)) + eps)
    unit_mean_image_vector = pooled * inverse
    report_float = reports.astype(jnp.float32)
    unit_caption_vector = report_float * lax.rsqrt(lax.optimization_barrier(jnp.sum(report_float * report_float, -1, keepdims=True)) + eps)
    affinity_matrix_entries = jnp.dot(unit_mean_image_vector, unit_caption_vector.T, precision=finest_arithmetic_mode) / contrast_divisor_factor
    expo = jnp.exp(affinity_matrix_entries)
    row_total = lax.optimization_barrier(jnp.sum(expo, 1))
    column_total = lax.optimization_barrier(jnp.sum(expo, 0))
    count_all = affinity_matrix_entries.shape[0]
    target = (slide_pair[:, None] == jnp.arange(count_all, dtype=jnp.int32)[None, :]).astype(jnp.float32)
    positive = lax.optimization_barrier(jnp.sum(affinity_matrix_entries * target, 1))
    loss_value = (jnp.sum(-positive + 0.5 * jnp.log(row_total)) + 0.5 * jnp.sum(jnp.log(column_total))) / count_all
    affinity_matrix_derivative = (0.5 * expo / row_total[:, None] + 0.5 * expo / column_total[None, :] - target) * (loss_scale / count_all)
    unit_mean_image_derivative = jnp.dot(affinity_matrix_derivative, unit_caption_vector, precision=finest_arithmetic_mode) / contrast_divisor_factor
    grad_pooled = (unit_mean_image_derivative - unit_mean_image_vector * lax.optimization_barrier(jnp.sum(unit_mean_image_vector * unit_mean_image_derivative, -1, keepdims=True))) * inverse
    return (loss_value, grad_pooled)

def slide_backward(slide_rows, validity, grad_pooled, w_query, w_key, w_value, w_out):
    normed, inverse, slide_norm, query, keys, values, attended, pooled = slide_forward(slide_rows, validity, w_query, w_key, w_value, w_out)
    grad_rows_out = validity[:, None] * grad_pooled[None, :] / jnp.sum(validity)
    grad_low = grad_rows_out.astype(jnp.bfloat16)
    grad_wo = jnp.dot(attended.T, grad_low, preferred_element_type=jnp.float32)
    grad_attended = jnp.dot(grad_low, w_out.T, preferred_element_type=jnp.float32)
    unused, pull = jax.vjp(lambda qa, ka, va: attend(qa, ka, va, validity), query, keys, values)
    grad_q, grad_k, grad_v = pull(grad_attended)
    grad_q = grad_q.astype(jnp.bfloat16)
    grad_k = grad_k.astype(jnp.bfloat16)
    grad_v = grad_v.astype(jnp.bfloat16)
    grad_wq = jnp.dot(slide_norm.T, grad_q, preferred_element_type=jnp.float32)
    grad_wk = jnp.dot(slide_norm.T, grad_k, preferred_element_type=jnp.float32)
    grad_wv = jnp.dot(slide_norm.T, grad_v, preferred_element_type=jnp.float32)
    grad_normed = jnp.dot(grad_q, w_query.T, preferred_element_type=jnp.float32)
    grad_normed = grad_normed + jnp.dot(grad_k, w_key.T, preferred_element_type=jnp.float32)
    grad_normed = grad_normed + jnp.dot(grad_v, w_value.T, preferred_element_type=jnp.float32)
    first = lax.optimization_barrier(jnp.mean(grad_normed, -1, keepdims=True))
    second = lax.optimization_barrier(jnp.mean(grad_normed * normed, -1, keepdims=True))
    grad_rows = grad_rows_out + (grad_normed - first - normed * second) * inverse
    return ((grad_wq, grad_wk, grad_wv, grad_wo), grad_rows)

def reference(tile_features, tile_slide, slide_pair, reports, w_one, w_two, w_query, w_key, w_value, w_out):
    tile_float = tile_features.astype(jnp.float32)
    tile_normed, unused = norm_parts(tile_float)
    tile_norm = tile_normed.astype(jnp.bfloat16)
    hidden_pre = jnp.dot(tile_norm, w_one, preferred_element_type=jnp.float32)
    hidden = gelu_value(hidden_pre).astype(jnp.bfloat16)
    embedding = (tile_float + jnp.dot(hidden, w_two, preferred_element_type=jnp.float32)).astype(jnp.bfloat16)
    blocks = tile_slide[:, 0].reshape(N_DP, TOK_DEV)
    matches = (blocks[:, :, None] == jnp.arange(SLIDES, dtype=jnp.int32)[None, None, :]).astype(jnp.int32)
    ordinal = lax.optimization_barrier(jnp.sum(matches * (jnp.cumsum(matches, 1) - 1), 2)).astype(jnp.int32)
    source = jnp.broadcast_to(jnp.arange(N_DP, dtype=jnp.int32)[:, None], blocks.shape)
    buffers = jnp.zeros((SLIDES, N_DP, CAP, D), jnp.bfloat16).at[blocks, source, ordinal].set(embedding.reshape(N_DP, TOK_DEV, D))
    buffers = buffers.reshape(SLIDES, N_DP * CAP, D)
    validity = jnp.zeros((SLIDES, N_DP, CAP), jnp.float32).at[blocks, source, ordinal].set(1.0)
    validity = validity.reshape(SLIDES, N_DP * CAP)
    pooled = lax.map(lambda item: slide_forward(item[0], item[1], w_query, w_key, w_value, w_out)[-1], (buffers, validity))
    contrast_loss, grad_pooled = contrast(pooled, reports, slide_pair)

    def accumulate(carry, item):
        grads, grad_rows = slide_backward(item[0], item[1], item[2], w_query, w_key, w_value, w_out)
        return (tuple((left + right for left, right in zip(carry, grads))), grad_rows)
    zeros_square = jnp.zeros((D, D), jnp.float32)
    totals, grad_rows_all = lax.scan(accumulate, (zeros_square, zeros_square, zeros_square, zeros_square), (buffers, validity, grad_pooled))
    grad_wq, grad_wk, grad_wv, grad_wo = totals
    grad_embedding = grad_rows_all.reshape(SLIDES, N_DP, CAP, D)[blocks, source, ordinal].reshape(TILES, D).astype(jnp.bfloat16)
    grad_two = jnp.dot(hidden.T, grad_embedding, preferred_element_type=jnp.float32)
    grad_hidden = (jnp.dot(grad_embedding, w_two.T, preferred_element_type=jnp.float32) * gelu_slope(hidden_pre)).astype(jnp.bfloat16)
    grad_one = jnp.dot(tile_norm.T, grad_hidden, preferred_element_type=jnp.float32)
    return (contrast_loss, grad_one, grad_two, grad_wq, grad_wk, grad_wv, grad_wo)
```

```python
import jax
import jax.numpy as jnp
from jax import lax
from jax.sharding import Mesh, PartitionSpec as P

HEAD = 96
CORES = 2
ROWS = 16

eps = 1e-05
contrast_divisor_factor = 0.07
score_scale = 10.0
loss_scale = 4096.0
exact = lax.Precision.HIGHEST
f32 = jnp.float32
bf16 = jnp.bfloat16
DP = ("chip", "core")


def contract(left, right, left_dim, right_dim, **kw):
    return lax.dot_general(
        left, right, (((left_dim,), (right_dim,)), ((), ())), preferred_element_type=f32, **kw
    )


def exchange(values, axis):
    return lax.all_to_all(values, axis, 0, 0, tiled=True)


def spread(values, axis, count):
    copies = jnp.broadcast_to(values[None], (count,) + values.shape)
    return exchange(lax.optimization_barrier(copies), axis)


def gelu_value(values):
    return 0.5 * values * (1.0 + jax.scipy.special.erf(values * 0.7071067811865476))


def gelu_slope(values):
    return (
        0.5 * (1.0 + jax.scipy.special.erf(values * 0.7071067811865476))
        + values * jnp.exp(-0.5 * values * values) * 0.3989422804014327
    )


def pick(values, index, axis):
    return lax.dynamic_index_in_dim(values, index, axis, keepdims=False)


def per_device(
    tile_features, tile_slide, slide_pair, reports, w_one, w_two, w_query, w_key, w_value, w_out
):
    chips = lax.axis_size("chip")
    owners = chips * CORES
    parts = lax.axis_size("mp")
    core = lax.axis_index("core")
    owner_index = lax.axis_index(DP)
    part_index = lax.axis_index("mp")
    tiles, width = tile_features.shape
    capacity = 2 * tiles // owners
    length = owners * capacity
    block = width // parts
    share = width // owners
    heads = w_query.shape[1] // HEAD

    all_reports = spread(reports, DP, owners).reshape(owners, width).astype(f32)
    report_unit = all_reports * lax.rsqrt(
        jnp.sum(all_reports * all_reports, -1, keepdims=True) + eps
    )

    tile_float = tile_features.astype(f32)
    centred = tile_float - jnp.mean(tile_float, -1, keepdims=True)
    tile_norm = (centred * lax.rsqrt(jnp.mean(centred * centred, -1, keepdims=True) + eps)).astype(
        bf16
    )
    hidden_pre = jnp.dot(tile_norm, w_one, preferred_element_type=f32)
    hidden = gelu_value(hidden_pre).astype(bf16)
    partial_out = jnp.dot(hidden, w_two, preferred_element_type=f32).astype(bf16)
    partial_out = partial_out.reshape(tiles, parts, block).transpose(1, 0, 2)
    summed = jnp.sum(exchange(partial_out, "mp").astype(f32), 0)
    own_columns = pick(tile_features.reshape(tiles, parts, block), part_index, 1)
    embedding = (own_columns.astype(f32) + summed).astype(bf16)

    slide_ids = tile_slide[:, 0]
    matches = (slide_ids[:, None] == jnp.arange(owners, dtype=jnp.int32)[None, :]).astype(jnp.int32)
    ordinal = jnp.sum(matches * (jnp.cumsum(matches, 0) - 1), 1)
    position = slide_ids * ROWS + ordinal
    dispatch = (
        jnp.arange(owners * ROWS, dtype=jnp.int32)[:, None] == position[None, :]
    ).astype(bf16)
    flagged = jnp.concatenate(
        [embedding, jnp.ones((tiles, 1), bf16), jnp.zeros((tiles, 255 - block), bf16)], 1
    )
    outgoing = jnp.dot(dispatch, flagged, preferred_element_type=f32).astype(bf16)
    arrived = exchange(outgoing.reshape(owners, ROWS, 256), DP).reshape(owners * ROWS, 256)
    slot = jnp.arange(owners * ROWS, dtype=jnp.int32)
    row_of_slot = jnp.where(slot % ROWS < capacity, slot // ROWS * capacity + slot % ROWS, -1)
    select = (row_of_slot[:, None] == jnp.arange(length, dtype=jnp.int32)[None, :]).astype(bf16)
    chunk = contract(arrived, select, 0, 0)
    validity = chunk[block]
    valid_low = validity.astype(bf16)[None, :]
    chunk = chunk[:block].astype(bf16)
    count = jnp.sum(validity)
    slide = spread(chunk, "mp", parts).reshape(width, length)

    slide_float = slide.astype(f32)
    mean = jnp.mean(slide_float, 0, keepdims=True)
    centred = slide_float - mean
    inverse = lax.rsqrt(jnp.mean(centred * centred, 0, keepdims=True) + eps)
    normed = centred * inverse
    slide_norm = normed.astype(bf16)
    weights_in = jnp.concatenate([w_query, w_key, w_value], 1)
    projected = contract(weights_in, slide_norm, 0, 0).reshape(3, heads, HEAD, length)
    query, keys, values = projected[0], projected[1], projected[2]
    query_scale = lax.rsqrt(jnp.mean(query * query, 1, keepdims=True) + eps)
    key_scale = lax.rsqrt(jnp.mean(keys * keys, 1, keepdims=True) + eps)
    query_unit = query * query_scale
    key_unit = keys * key_scale
    query_low = query_unit.astype(bf16)
    key_low = key_unit.astype(bf16)
    scores = jnp.einsum("hdk,hdq->hkq", key_low, query_low, preferred_element_type=f32) * (
        score_scale / HEAD
    )
    weights = jnp.exp(scores) * validity[None, :, None]
    weights = weights / jnp.sum(weights, 1, keepdims=True)
    attended = jnp.einsum(
        "hdk,hkq->hdq", values.astype(bf16), weights.astype(bf16), preferred_element_type=f32
    )
    attended = attended.reshape(heads * HEAD, length).astype(bf16)
    key_mass = jnp.sum(weights * validity[None, None, :], 2)
    attended_sum = contract(valid_low, attended, 1, 1)
    slide_sum = contract(valid_low, slide, 1, 1)
    pooled_part = jnp.dot(attended_sum, w_out.astype(f32), precision=exact)
    pooled = jnp.sum(spread(pooled_part, "mp", parts), 0)
    pooled = ((pooled + slide_sum) / count)[0]

    pooled_inverse = lax.rsqrt(jnp.sum(pooled * pooled) + eps)
    pooled_unit = pooled * pooled_inverse
    logits_row = jnp.sum(report_unit * pooled_unit[None, :], -1) / contrast_divisor_factor
    logits_row = jnp.pad(logits_row, (0, 128 - owners))[None, :]
    logits = spread(logits_row, DP, owners)[:, 0, :owners]
    expo = jnp.exp(logits)
    row_total = jnp.sum(expo, 1)
    column_total = jnp.sum(expo, 0)
    target = (slide_pair[:, None] == jnp.arange(owners, dtype=jnp.int32)[None, :]).astype(f32)
    positive = jnp.sum(logits * target, 1)
    contrast_loss = (
        jnp.sum(-positive + 0.5 * jnp.log(row_total)) + 0.5 * jnp.sum(jnp.log(column_total))
    ) / owners
    grad_logits = (
        0.5 * expo / row_total[:, None] + 0.5 * expo / column_total[None, :] - target
    ) * (loss_scale / owners)
    grad_row = pick(grad_logits, owner_index, 0)
    grad_unit = jnp.sum(grad_row[:, None] * report_unit, 0) / contrast_divisor_factor
    grad_pooled = (grad_unit - pooled_unit * jnp.sum(pooled_unit * grad_unit)) * pooled_inverse
    grad_row_out = grad_pooled / count
    grad_low = grad_row_out.astype(bf16)

    up = contract(w_out, grad_low[None, :], 1, 1)
    up_heads = up.reshape(heads, HEAD, 1)
    pull = jnp.sum(up_heads * values, 1)
    pull_mean = jnp.sum(weights * pull[:, :, None], 1)
    grad_scores = (
        weights
        * (pull[:, :, None] - pull_mean[:, None, :])
        * (validity * (score_scale / HEAD))[None, None, :]
    ).astype(bf16)
    grad_query_unit = jnp.einsum("hdk,hkq->hdq", key_low, grad_scores, preferred_element_type=f32)
    grad_key_unit = jnp.einsum("hdq,hkq->hdk", query_low, grad_scores, preferred_element_type=f32)
    grad_q = query_scale * (
        grad_query_unit - query_unit * jnp.mean(query_unit * grad_query_unit, 1, keepdims=True)
    )
    grad_k = key_scale * (
        grad_key_unit - key_unit * jnp.mean(key_unit * grad_key_unit, 1, keepdims=True)
    )
    grad_v = up_heads * key_mass[:, None, :]
    grads_in = jnp.stack([grad_q, grad_k, grad_v]).astype(bf16).reshape(3 * heads * HEAD, length)
    grad_normed = jnp.dot(weights_in, grads_in, preferred_element_type=f32)
    first = jnp.mean(grad_normed, 0, keepdims=True)
    second = jnp.mean(grad_normed * normed, 0, keepdims=True)
    stats = jnp.concatenate([first, second], 0)
    stats_high = stats.astype(bf16)
    stats_low = (stats - stats_high.astype(f32)).astype(bf16)
    stats = jnp.concatenate([stats_high, stats_low, jnp.zeros((12, length), bf16)], 0)
    sending = jnp.concatenate(
        [
            grad_normed.astype(bf16).reshape(parts, block, length),
            jnp.broadcast_to(stats[None], (parts, 16, length)),
        ],
        1,
    )
    total = jnp.sum(exchange(sending, "mp").astype(f32), 0)
    first = total[block : block + 1] + total[block + 2 : block + 3]
    second = total[block + 1 : block + 2] + total[block + 3 : block + 4]
    own_normed = (chunk.astype(f32) - mean) * inverse
    own_grad = pick(grad_row_out.reshape(parts, block), part_index, 0)
    grad_rows = (
        own_grad[:, None] * validity[None, :]
        + (total[:block] - first - own_normed * second) * inverse
    ).astype(bf16)

    going = contract(select, grad_rows, 1, 1).astype(bf16)
    back = exchange(going.reshape(owners, ROWS, block), DP).reshape(owners * ROWS, block)
    grad_block = contract(back, dispatch, 0, 0).astype(bf16)
    grad_embedding = spread(grad_block, "mp", parts).reshape(width, tiles)

    def halves(values, axis):
        split = values.shape[:axis] + (chips, CORES, share) + values.shape[axis + 1 :]
        values = values.reshape(split)
        merged = split[:axis] + (chips * share,) + split[axis + 3 :]
        own = pick(values, core, axis + 1).reshape(merged)
        other = pick(values, 1 - core, axis + 1).reshape(merged)
        return own, other

    def reduce_over_owners(own, other):
        got = lax.ppermute(other.astype(bf16), "core", [(0, 1), (1, 0)])
        both = (own + got.astype(f32)).astype(bf16)
        return jnp.sum(exchange(both, "chip").astype(f32), 0)

    norm_own, norm_other = halves(slide_norm, 0)
    grads_wide = grads_in[: 2 * heads * HEAD]
    wide = (chips, share, 2 * heads * HEAD)
    grad_wide = reduce_over_owners(
        contract(norm_own, grads_wide, 1, 1).reshape(wide),
        contract(norm_other, grads_wide, 1, 1).reshape(wide),
    )
    grad_query = grad_wide[:, : heads * HEAD]
    grad_key = grad_wide[:, heads * HEAD :]
    value_rows = contract(key_mass.astype(bf16), slide_norm, 1, 1)
    pieces = jnp.concatenate(
        [
            value_rows.reshape(heads, owners, share).transpose(1, 0, 2).reshape(owners, -1),
            grad_row_out.astype(bf16).astype(f32).reshape(owners, share),
            jnp.broadcast_to(up.reshape(1, -1), (owners, heads * HEAD)),
            jnp.broadcast_to(attended_sum, (owners, heads * HEAD)),
        ],
        1,
    )
    pieces = jnp.pad(pieces, ((0, 0), (0, -pieces.shape[1] % 128)))
    pieces = exchange(pieces[:, None, :], DP)[:, 0, :]
    edge = heads * share
    from_values = pieces[:, :edge].reshape(owners, heads, share)
    from_grads = pieces[:, edge : edge + share]
    edge = edge + share
    from_up = pieces[:, edge : edge + heads * HEAD].reshape(owners, heads, HEAD)
    edge = edge + heads * HEAD
    from_attended = pieces[:, edge : edge + heads * HEAD]
    grad_value = jnp.einsum("ohs,ohd->shd", from_values, from_up, precision=exact)
    grad_value = grad_value.reshape(share, heads * HEAD)
    grad_out = contract(from_attended, from_grads, 0, 0, precision=exact)

    grad_hidden = (contract(grad_embedding, w_two, 0, 1) * gelu_slope(hidden_pre)).astype(bf16)
    tile_own, tile_other = halves(tile_norm, 1)
    grad_own, grad_other = halves(grad_embedding, 0)
    size = (chips, share, w_one.shape[1])

    def both_layers(tile_part, grad_part):
        one = contract(tile_part, grad_hidden, 0, 0).reshape(size)
        two = jnp.dot(grad_part, hidden, preferred_element_type=f32).reshape(size)
        return jnp.concatenate([one, two], 1)

    grad_tile = reduce_over_owners(
        both_layers(tile_own, grad_own), both_layers(tile_other, grad_other)
    )
    grad_one = grad_tile[:share]
    grad_two = grad_tile[share:].T
    return (contrast_loss, grad_one, grad_two, grad_query, grad_key, grad_value, grad_out)


def solution(mesh):
    owners, parts = mesh.devices.shape
    split = Mesh(
        mesh.devices.reshape(owners // CORES, CORES, parts), ("chip", "core", "mp")
    )
    return jax.shard_map(
        per_device,
        mesh=split,
        in_specs=(
            P(DP, None),
            P(DP, None),
            P(),
            P(DP, None),
            P(None, "mp"),
            P("mp", None),
            P(None, "mp"),
            P(None, "mp"),
            P(None, "mp"),
            P("mp", None),
        ),
        out_specs=(
            P(),
            P(DP, "mp"),
            P("mp", DP),
            P(DP, "mp"),
            P(DP, "mp"),
            P(DP, "mp"),
            P("mp", DP),
        ),
        check_vma=False,
    )
```

```python
import jax
import jax.numpy as jnp
from jax import lax
from jax.experimental import pallas as pl
from jax.experimental.pallas import tpu as pltpu
from jax.sharding import Mesh, PartitionSpec as P

HEAD = 96
CORES = 2
ROWS = 16
EXTRA = 16

eps = 1e-05
contrast_divisor_factor = 0.07
score_scale = 10.0
loss_scale = 4096.0
exact = lax.Precision.HIGHEST
f32 = jnp.float32
bf16 = jnp.bfloat16
i32 = jnp.int32
DP = ("chip", "core")


def contract(left, right, left_dim, right_dim, **kw):
    return lax.dot_general(
        left, right, (((left_dim,), (right_dim,)), ((), ())), preferred_element_type=f32, **kw
    )


def exchange(values, axis):
    return lax.all_to_all(values, axis, 0, 0, tiled=True)


def spread(values, axis, count):
    copies = jnp.broadcast_to(values[None], (count,) + values.shape)
    return exchange(lax.optimization_barrier(copies), axis)


def pick(values, index, axis):
    return lax.dynamic_index_in_dim(values, index, axis, keepdims=False)


def call(body, outs, *args, scalars=(), scratch=()):
    count = len(scalars)
    return pl.pallas_call(
        body,
        out_shape=[jax.ShapeDtypeStruct(shape, kind) for shape, kind in outs],
        in_specs=[pl.BlockSpec(memory_space=pltpu.SMEM)] * count
        + [pl.BlockSpec(memory_space=pltpu.VMEM)] * len(args),
        out_specs=[pl.BlockSpec(memory_space=pltpu.VMEM)] * len(outs),
        scratch_shapes=[pltpu.VMEM(shape, kind) for shape, kind in scratch],
        compiler_params=pltpu.CompilerParams(vmem_limit_bytes=48 * 1024 * 1024),
    )(*[jnp.reshape(s, (1,)).astype(i32) for s in scalars], *args)


def turn(count, step):
    return [(index, (index + step) % count) for index in range(count)]


def scatter_ring(pieces, count):
    return [pieces[0]] + [
        lax.ppermute(pieces[k], "mp", turn(count, k)) for k in range(1, count)
    ]


def gather_ring(piece, count):
    found = [piece]
    back = ahead = piece
    for _ in range(count // 2 - 1):
        back = lax.ppermute(back, "mp", turn(count, 1))
        ahead = lax.ppermute(ahead, "mp", turn(count, count - 1))
        found += [back, ahead]
    half = piece.shape[0] // 2
    found.append(lax.ppermute(back[:half], "mp", turn(count, 1)))
    found.append(lax.ppermute(ahead[half:], "mp", turn(count, count - 1)))
    return found


def place(refs, target, here, count, rows, unpack):
    half = count // 2
    target[pl.ds(pl.multiple_of(here * rows, 16), rows), :] = unpack(refs[0][...])
    for step in range(1, half):
        for ref, sign in ((refs[2 * step - 1], -1), (refs[2 * step], 1)):
            start = pl.multiple_of(lax.rem(here + sign * step + count, count) * rows, 16)
            target[pl.ds(start, rows), :] = unpack(ref[...])
    start = pl.multiple_of(lax.rem(here + half, count) * rows, 16)
    both = jnp.concatenate([refs[-2][...], refs[-1][...]], 0)
    target[pl.ds(start, rows), :] = unpack(both)


def pack(square):
    half = square.shape[0] // 2
    side = square[:, 128:]
    return jnp.concatenate(
        [square[:, :128], jnp.concatenate([side[:half], side[half:]], 1)], 0
    )


def unpack(packed):
    rows = packed.shape[0] // 3 * 2
    side = packed[rows:]
    return jnp.concatenate(
        [packed[:rows], jnp.concatenate([side[:, :64], side[:, 64:]], 0)], 1
    )


def tile_forward(here, x_ref, one_ref, two_ref, norm_ref, hidden_ref, slope_ref, *rest):
    outs, chunks = rest[:-1], rest[-1]
    count = len(outs)
    x = x_ref[...].astype(f32)
    centred = x - jnp.mean(x, -1, keepdims=True)
    normed = centred * lax.rsqrt(jnp.mean(centred * centred, -1, keepdims=True) + eps)
    normed = normed.astype(bf16)
    norm_ref[...] = normed
    pre = jnp.dot(normed, one_ref[...], preferred_element_type=f32)
    bell = 0.5 * (1.0 + lax.erf(pre * 0.7071067811865476))
    hidden = (pre * bell).astype(bf16)
    hidden_ref[...] = hidden
    slope_ref[...] = bell + pre * jnp.exp(-0.5 * pre * pre) * 0.3989422804014327
    partial = jnp.dot(hidden, two_ref[...], preferred_element_type=f32).astype(bf16)
    block = partial.shape[1] // count
    for j in range(count):
        chunks[j] = pack(partial[:, j * block : (j + 1) * block])
    for k in range(count):
        outs[k][...] = chunks[lax.rem(here[0] + k, count)]


def tile_dispatch(own_ref, dispatch_ref, flags_ref, *rest):
    refs, out_ref = rest[:-1], rest[-1]
    total = refs[0][...].astype(f32)
    for ref in refs[1:]:
        total = total + ref[...].astype(f32)
    embedding = (own_ref[...].astype(f32) + unpack(total)).astype(bf16)
    rows = jnp.dot(dispatch_ref[...], embedding, preferred_element_type=f32)
    out_ref[...] = jnp.concatenate([rows.astype(bf16), flags_ref[...]], 1)


def slot_rows(arrived_ref, select_ref, chunk_ref, valid_ref):
    chunk = contract(arrived_ref[...], select_ref[...], 0, 0)
    block = chunk_ref.shape[0]
    chunk_ref[...] = chunk[:block].astype(bf16)
    valid_ref[...] = chunk[block : block + 1]


def slide_forward(
    here,
    valid_ref,
    weights_ref,
    out_weights_ref,
    *rest,
):
    pieces = rest[:9]
    (
        norm_ref,
        stat_ref,
        query_ref,
        key_ref,
        value_ref,
        scale_ref,
        attention_ref,
        mass_ref,
        attended_ref,
        pooled_ref,
        slide_ref,
    ) = rest[9:]
    count = slide_ref.shape[0] // pieces[0].shape[0]
    place(pieces, slide_ref, here[0], count, pieces[0].shape[0], lambda values: values)
    valid = valid_ref[...]
    valid_low = valid.astype(bf16)
    low = slide_ref[...]
    slide = low.astype(f32)
    mean = jnp.mean(slide, 0, keepdims=True)
    centred = slide - mean
    inverse = lax.rsqrt(jnp.mean(centred * centred, 0, keepdims=True) + eps)
    stat_ref[...] = jnp.concatenate([mean, inverse], 0)
    norm_ref[...] = (centred * inverse).astype(bf16)
    projected = jnp.dot(weights_ref[...], norm_ref[...], preferred_element_type=f32)
    inner = projected.shape[0] // 3
    heads = inner // HEAD
    attended = []
    for h in range(heads):
        low_rows, high_rows = h * HEAD, (h + 1) * HEAD
        query = projected[low_rows:high_rows]
        keys = projected[inner + low_rows : inner + high_rows]
        values = projected[2 * inner + low_rows : 2 * inner + high_rows]
        query_scale = lax.rsqrt(jnp.mean(query * query, 0, keepdims=True) + eps)
        key_scale = lax.rsqrt(jnp.mean(keys * keys, 0, keepdims=True) + eps)
        query_unit = query * query_scale
        key_unit = keys * key_scale
        query_ref[h] = query_unit
        key_ref[h] = key_unit
        value_ref[h] = values
        scale_ref[h] = jnp.concatenate([query_scale, key_scale], 0)
        scores = contract(query_unit.astype(bf16), key_unit.astype(bf16), 0, 0)
        weights = jnp.exp(scores * (score_scale / HEAD)) * valid
        weights = weights * (1.0 / jnp.sum(weights, 1, keepdims=True))
        attention_ref[h] = weights
        weights_low = weights.astype(bf16)
        mass_ref[h : h + 1, :] = jnp.dot(valid_low, weights_low, preferred_element_type=f32)
        attended.append(contract(values.astype(bf16), weights_low, 1, 1))
    attended = jnp.concatenate(attended, 0).astype(bf16)
    attended_sum = contract(valid_low, attended, 1, 1)
    attended_ref[...] = attended_sum
    high = attended_sum.astype(bf16)
    rest_low = (attended_sum - high.astype(f32)).astype(bf16)
    part = jnp.dot(high, out_weights_ref[...], preferred_element_type=f32)
    part = part + jnp.dot(rest_low, out_weights_ref[...], preferred_element_type=f32)
    slide_sum = contract(valid_low, low, 1, 1)
    pooled_ref[...] = (part + slide_sum * (1.0 / count)) / jnp.sum(valid)


def logits_row(parts_ref, reports_ref, unit_ref, report_ref, row_ref):
    pooled = jnp.sum(parts_ref[...], 0)
    inverse = lax.rsqrt(jnp.sum(pooled * pooled, -1, keepdims=True) + eps)
    unit = pooled * inverse
    unit_ref[...] = jnp.concatenate([unit, jnp.broadcast_to(inverse, unit.shape)], 0)
    reports = reports_ref[...].astype(f32)
    report = reports * lax.rsqrt(jnp.sum(reports * reports, -1, keepdims=True) + eps)
    report_ref[...] = report
    row = contract(unit, report, 1, 1, precision=exact) / contrast_divisor_factor
    pad = row_ref.shape[2] - row.shape[1]
    row = jnp.concatenate([row, jnp.zeros((1, pad), f32)], 1)
    row_ref[...] = jnp.broadcast_to(row[None], row_ref.shape)


def slide_backward(
    here,
    owner,
    logits_ref,
    pair_ref,
    unit_ref,
    report_ref,
    valid_ref,
    out_weights_ref,
    weights_ref,
    norm_ref,
    query_ref,
    key_ref,
    value_ref,
    scale_ref,
    attention_ref,
    mass_ref,
    loss_ref,
    grad_ref,
    up_ref,
    grads_ref,
    *outs,
):
    owners = report_ref.shape[0]
    valid = valid_ref[...]
    logits = logits_ref[...]
    shape = logits.shape
    columns = lax.broadcasted_iota(i32, shape, 1)
    rows = lax.broadcasted_iota(i32, shape, 0)
    real = columns < owners
    expo = jnp.where(real, jnp.exp(logits), 0.0)
    row_total = jnp.sum(expo, 1, keepdims=True)
    column_total = jnp.where(real[:1], jnp.sum(expo, 0, keepdims=True), 1.0)
    target = jnp.where(pair_ref[...] == columns, 1.0, 0.0)
    loss = jnp.sum(
        0.5 * jnp.log(row_total) - jnp.sum(logits * target, 1, keepdims=True), 0, keepdims=True
    )
    loss = loss + 0.5 * jnp.sum(jnp.log(column_total), 1, keepdims=True)
    loss_ref[...] = loss * (1.0 / owners)
    grad_logits = (0.5 * expo / row_total + 0.5 * expo / column_total - target) * (
        loss_scale / owners
    )
    grad_row = jnp.sum(jnp.where(rows == owner[0], grad_logits, 0.0), 0, keepdims=True)
    grad_unit = (
        jnp.dot(grad_row[:, :owners], report_ref[...], precision=exact, preferred_element_type=f32)
        / contrast_divisor_factor
    )
    unit = unit_ref[0:1]
    inverse = unit_ref[1:2]
    grad_pooled = (grad_unit - unit * jnp.sum(unit * grad_unit, -1, keepdims=True)) * inverse
    grad = grad_pooled / jnp.sum(valid)
    grad_ref[...] = grad
    low = grad.astype(bf16)
    out_weights = out_weights_ref[...]
    up_ref[...] = contract(low, out_weights, 1, 1)
    up = jnp.sum(out_weights.astype(f32) * low.astype(f32), 1, keepdims=True)
    heads = query_ref.shape[0]
    inner = heads * HEAD
    for h in range(heads):
        up_head = up[h * HEAD : (h + 1) * HEAD]
        values = value_ref[h]
        weights = attention_ref[h]
        pull = jnp.sum(up_head * values, 0, keepdims=True)
        pull_mean = jnp.sum(weights * pull, 1, keepdims=True)
        grad_scores = (weights * (pull - pull_mean) * (score_scale / HEAD)).astype(bf16)
        query_unit = query_ref[h]
        key_unit = key_ref[h]
        grad_query = contract(key_unit.astype(bf16), grad_scores, 1, 1) * valid
        grad_key = jnp.dot(query_unit.astype(bf16), grad_scores, preferred_element_type=f32)
        grad_query = scale_ref[h, 0:1] * (
            grad_query - query_unit * jnp.mean(query_unit * grad_query, 0, keepdims=True)
        )
        grad_key = scale_ref[h, 1:2] * (
            grad_key - key_unit * jnp.mean(key_unit * grad_key, 0, keepdims=True)
        )
        grad_value = up_head * mass_ref[h : h + 1]
        for part, values in enumerate((grad_query, grad_key, grad_value)):
            start = part * inner + h * HEAD
            grads_ref[start : start + HEAD, :] = values.astype(bf16)
    grads = grads_ref[...]
    count = len(outs)
    block = norm_ref.shape[0] // count
    first = jnp.zeros_like(valid)
    second = jnp.zeros_like(valid)
    for k in range(count):
        start = pl.multiple_of(lax.rem(here[0] + k, count) * block, 16)
        part = jnp.dot(weights_ref[pl.ds(start, block), :], grads, preferred_element_type=f32)
        outs[k][0:block, :] = part.astype(bf16)
        first = first + jnp.sum(part, 0, keepdims=True)
        second = second + jnp.sum(part * norm_ref[pl.ds(start, block), :].astype(f32), 0, keepdims=True)
    width = norm_ref.shape[0]
    stats = jnp.concatenate([first, second], 0) * (1.0 / width)
    high = stats.astype(bf16).astype(f32)
    stats = jnp.concatenate(
        [high, stats - high, jnp.zeros((EXTRA - 4, stats.shape[1]), f32)], 0
    ).astype(bf16)
    for k in range(count):
        outs[k][block : block + EXTRA, :] = stats


def slot_grads(own_ref, valid_ref, stat_ref, chunk_ref, select_ref, extra_ref, *rest):
    refs, out_ref = rest[:-1], rest[-1]
    total = refs[0][...].astype(f32)
    for ref in refs[1:]:
        total = total + ref[...].astype(f32)
    block = chunk_ref.shape[0]
    first = total[block : block + 1] + total[block + 2 : block + 3]
    second = total[block + 1 : block + 2] + total[block + 3 : block + 4]
    mean = stat_ref[0:1]
    inverse = stat_ref[1:2]
    normed = (chunk_ref[...].astype(f32) - mean) * inverse
    rows = own_ref[...] * valid_ref[...] + (total[:block] - first - normed * second) * inverse
    rows = contract(select_ref[...], rows.astype(bf16), 1, 1).astype(bf16)
    out_ref[...] = rows + extra_ref[...]


def tile_grads(back_ref, dispatch_ref, out_ref):
    out_ref[...] = pack(contract(back_ref[...], dispatch_ref[...], 0, 0).astype(bf16))


def other_grads(here, other, two_ref, slope_ref, norm_ref, hidden_ref, *rest):
    pieces, (grad_ref, hidden_grad_ref, out_ref) = rest[:9], rest[9:]
    rows = pieces[0].shape[0] // 3 * 2
    count = grad_ref.shape[0] // rows
    place(pieces, grad_ref, here[0], count, rows, unpack)
    grad_hidden = jnp.dot(two_ref[...], grad_ref[...], preferred_element_type=f32)
    hidden_grad_ref[...] = (grad_hidden * slope_ref[...]).astype(bf16)
    both_layers(other[0], norm_ref, hidden_ref, grad_ref, hidden_grad_ref, out_ref)


def own_grads(own, norm_ref, hidden_ref, grad_ref, hidden_grad_ref, out_ref):
    both_layers(own[0], norm_ref, hidden_ref, grad_ref, hidden_grad_ref, out_ref)


def both_layers(which, norm_ref, hidden_ref, grad_ref, hidden_grad_ref, out_ref):
    chips, share = out_ref.shape[0], out_ref.shape[1] // 2
    rows = [
        grad_ref[pl.ds(pl.multiple_of((CORES * chip + which) * share, 16), share), :]
        for chip in range(chips)
    ]
    two = jnp.dot(jnp.concatenate(rows, 0), hidden_ref[...], preferred_element_type=f32)
    one = contract(norm_ref[...], hidden_grad_ref[...], 1, 1)
    for chip in range(chips):
        start = chip * share
        out_ref[chip, 0:share, :] = one[start : start + share].astype(bf16)
        out_ref[chip, share : 2 * share, :] = two[start : start + share].astype(bf16)


def add_halves(own_ref, got_ref, out_ref):
    out_ref[...] = (own_ref[...].astype(f32) + got_ref[...].astype(f32)).astype(bf16)


def last_sums(values_ref, one_ref, two_ref):
    share = one_ref.shape[0]
    total = values_ref[0].astype(f32)
    for chip in range(1, values_ref.shape[0]):
        total = total + values_ref[chip].astype(f32)
    one_ref[...] = total[:share]
    two_ref[...] = total[share:].T


def per_device(
    tile_features, tile_slide, slide_pair, reports, w_one, w_two, w_query, w_key, w_value, w_out
):
    chips = lax.axis_size("chip")
    owners = chips * CORES
    parts = lax.axis_size("mp")
    core = lax.axis_index("core")
    owner = lax.axis_index(DP)
    here = lax.axis_index("mp")
    tiles, width = tile_features.shape
    units = w_one.shape[1]
    capacity = 2 * tiles // owners
    length = owners * capacity
    slots = owners * ROWS
    block = width // parts
    share = width // owners
    inner = w_query.shape[1]
    heads = inner // HEAD
    packed = (block // 2 * 3, 128)

    all_reports = spread(reports, DP, owners).reshape(owners, width)

    tile_norm, hidden, slope, *pieces = call(
        tile_forward,
        [((tiles, width), bf16), ((tiles, units), bf16), ((tiles, units), f32)]
        + [(packed, bf16)] * parts,
        tile_features,
        w_one,
        w_two,
        scalars=(here,),
        scratch=[((parts,) + packed, bf16)],
    )
    pieces = scatter_ring(pieces, parts)

    slide_ids = tile_slide[:, 0]
    matches = (slide_ids[:, None] == jnp.arange(owners, dtype=i32)[None, :]).astype(i32)
    ordinal = jnp.sum(matches * (jnp.cumsum(matches, 0) - 1), 1)
    position = slide_ids * ROWS + ordinal
    dispatch = jnp.arange(slots, dtype=i32)[:, None] == position[None, :]
    flags = jnp.sum(dispatch.astype(f32), 1, keepdims=True).astype(bf16)
    flags = jnp.pad(flags, ((0, 0), (0, 256 - block - 1)))
    dispatch = dispatch.astype(bf16)
    slot = jnp.arange(slots, dtype=i32)
    row_of_slot = jnp.where(slot % ROWS < capacity, slot // ROWS * capacity + slot % ROWS, -1)
    select = (row_of_slot[:, None] == jnp.arange(length, dtype=i32)[None, :]).astype(bf16)
    own_columns = pick(tile_features.reshape(tiles, parts, block), here, 1)
    weights_in = jnp.concatenate([w_query, w_key, w_value], 1)
    weights_across = weights_in.T

    (outgoing,) = call(
        tile_dispatch, [((slots, 256), bf16)], own_columns, dispatch, flags, *pieces
    )
    arrived = exchange(outgoing.reshape(owners, ROWS, 256), DP).reshape(slots, 256)
    chunk, valid = call(
        slot_rows, [((block, length), bf16), ((1, length), f32)], arrived, select
    )
    pieces = gather_ring(chunk, parts)

    slide_norm, stat, query, keys, values, scales, attention, mass, attended_sum, pooled = call(
        slide_forward,
        [
            ((width, length), bf16),
            ((2, length), f32),
            ((heads, HEAD, length), f32),
            ((heads, HEAD, length), f32),
            ((heads, HEAD, length), f32),
            ((heads, 2, length), f32),
            ((heads, length, length), f32),
            ((heads, length), f32),
            ((1, inner), f32),
            ((1, width), f32),
        ],
        valid,
        weights_across,
        w_out,
        *pieces,
        scalars=(here,),
        scratch=[((width, length), bf16)],
    )
    pooled = spread(pooled, "mp", parts)
    unit, report_unit, row = call(
        logits_row,
        [((2, width), f32), ((owners, width), f32), ((owners, 1, 128), f32)],
        pooled,
        all_reports,
    )
    logits = exchange(row, DP).reshape(owners, 128)
    loss, grad, up, grads, *pieces = call(
        slide_backward,
        [((1, 1), f32), ((1, width), f32), ((1, inner), f32), ((3 * inner, length), bf16)]
        + [((block + EXTRA, length), bf16)] * parts,
        logits,
        slide_pair[:, None],
        unit,
        report_unit,
        valid,
        w_out,
        weights_in,
        slide_norm,
        query,
        keys,
        values,
        scales,
        attention,
        mass,
        scalars=(here, owner),
    )
    pieces = scatter_ring(pieces, parts)

    def halves(values):
        rest = values.shape[1:]
        values = values.reshape((chips, CORES, share) + rest)
        own = pick(values, core, 1).reshape((chips * share,) + rest)
        other = pick(values, 1 - core, 1).reshape((chips * share,) + rest)
        return own, other

    norm_own, norm_other = halves(slide_norm)
    wide = (chips, share, 2 * inner)
    wide_other = contract(norm_other, grads[: 2 * inner], 1, 1).astype(bf16).reshape(wide)
    wide_got = lax.ppermute(wide_other, "core", [(0, 1), (1, 0)])
    wide_own = contract(norm_own, grads[: 2 * inner], 1, 1).reshape(wide)
    wide_sent = (wide_own + wide_got.astype(f32)).astype(bf16)
    grad_wide = jnp.sum(exchange(wide_sent, "chip").astype(f32), 0)
    value_rows = contract(mass.astype(bf16), slide_norm, 1, 1)
    extra = jnp.concatenate(
        [
            value_rows.reshape(heads, owners, share).transpose(1, 0, 2).reshape(owners, -1),
            grad.reshape(owners, share),
            jnp.broadcast_to(up, (owners, inner)),
            jnp.broadcast_to(attended_sum, (owners, inner)),
        ],
        1,
    ).astype(bf16)
    spare = ROWS - capacity
    extra = jnp.pad(extra, ((0, 0), (0, spare * block - extra.shape[1])))
    extra = extra.reshape(owners, spare, block)
    extra = jnp.pad(extra, ((0, 0), (capacity, 0), (0, 0))).reshape(slots, block)

    own_grad = lax.dynamic_slice_in_dim(grad, here * block, block, 1).reshape(block, 1)
    (going,) = call(
        slot_grads,
        [((slots, block), bf16)],
        own_grad,
        valid,
        stat,
        chunk,
        select,
        extra,
        *pieces,
    )
    back = exchange(going.reshape(owners, ROWS, block), DP).reshape(slots, block)
    (piece,) = call(tile_grads, [(packed, bf16)], back, dispatch)
    pieces = gather_ring(piece, parts)

    tile_own, tile_other = halves(tile_norm.T)
    size = (chips, 2 * share, units)
    grad_embedding, grad_hidden, sent = call(
        other_grads,
        [((width, tiles), bf16), ((units, tiles), bf16), (size, bf16)],
        w_two,
        slope.T,
        tile_other,
        hidden,
        *pieces,
        scalars=(here, 1 - core),
    )
    got = lax.ppermute(sent, "core", [(0, 1), (1, 0)])
    (own,) = call(
        own_grads, [(size, bf16)], tile_own, hidden, grad_embedding, grad_hidden, scalars=(core,)
    )
    (both,) = call(add_halves, [(size, bf16)], own, got)
    grad_one, grad_two = call(
        last_sums, [((share, units), f32), ((units, share), f32)], exchange(both, "chip")
    )

    terms = back.reshape(owners, ROWS, block)[:, capacity:].reshape(owners, -1).astype(f32)
    edge = heads * share
    from_values = terms[:, :edge].reshape(owners, heads, share)
    from_grads = terms[:, edge : edge + share]
    edge = edge + share
    from_up = terms[:, edge : edge + inner].reshape(owners, heads, HEAD)
    edge = edge + inner
    from_attended = terms[:, edge : edge + inner]
    grad_value = jnp.einsum("ohs,ohd->shd", from_values, from_up, precision=exact)
    grad_value = grad_value.reshape(share, inner)
    grad_out = contract(from_attended, from_grads, 0, 0, precision=exact)
    return (
        loss[0, 0],
        grad_one,
        grad_two,
        grad_wide[:, :inner],
        grad_wide[:, inner:],
        grad_value,
        grad_out,
    )


def solution(mesh):
    owners, parts = mesh.devices.shape
    split = Mesh(
        mesh.devices.reshape(owners // CORES, CORES, parts), ("chip", "core", "mp")
    )
    return jax.shard_map(
        per_device,
        mesh=split,
        in_specs=(
            P(DP, None),
            P(DP, None),
            P(),
            P(DP, None),
            P(None, "mp"),
            P("mp", None),
            P(None, "mp"),
            P(None, "mp"),
            P(None, "mp"),
            P("mp", None),
        ),
        out_specs=(
            P(),
            P(DP, "mp"),
            P("mp", DP),
            P(DP, "mp"),
            P(DP, "mp"),
            P(DP, "mp"),
            P("mp", DP),
        ),
        check_vma=False,
    )
```

```python
import jax
import jax.numpy as jnp
from jax import lax
from jax.experimental import pallas as pl
from jax.experimental.pallas import tpu as pltpu
from jax.sharding import Mesh, PartitionSpec as P

HEAD = 96
CORES = 2
ROWS = 16
EXTRA = 16

eps = 1e-05
contrast_divisor_factor = 0.07
score_scale = 10.0
loss_scale = 4096.0
exact = lax.Precision.HIGHEST
f32 = jnp.float32
bf16 = jnp.bfloat16
i32 = jnp.int32
DP = ("chip", "core")


def contract(left, right, left_dim, right_dim, **kw):
    return lax.dot_general(
        left, right, (((left_dim,), (right_dim,)), ((), ())), preferred_element_type=f32, **kw
    )


def exchange(values, axis):
    return lax.all_to_all(values, axis, 0, 0, tiled=True)


def pick(values, index, axis):
    return lax.dynamic_index_in_dim(values, index, axis, keepdims=False)


def call(body, outs, *args, scalars=(), scratch=(), anchors=(), limit=16):
    count = len(scalars)
    skip = len(anchors)

    def kernel(*refs):
        body(*refs[skip:])

    return pl.pallas_call(
        kernel if skip else body,
        out_shape=[jax.ShapeDtypeStruct(shape, kind) for shape, kind in outs],
        in_specs=[pl.BlockSpec(memory_space=pl.ANY)] * skip
        + [pl.BlockSpec(memory_space=pltpu.SMEM)] * count
        + [pl.BlockSpec(memory_space=pltpu.VMEM)] * len(args),
        out_specs=[pl.BlockSpec(memory_space=pltpu.VMEM)] * len(outs),
        scratch_shapes=[pltpu.VMEM(shape, kind) for shape, kind in scratch],
        compiler_params=pltpu.CompilerParams(vmem_limit_bytes=limit * 1024 * 1024),
    )(*anchors, *[jnp.reshape(s, (1,)).astype(i32) for s in scalars], *args)


def turn(count, step):
    return [(index, (index + step) % count) for index in range(count)]


def scatter_ring(pieces, count):
    return [pieces[0]] + [
        lax.ppermute(pieces[k], "mp", turn(count, k)) for k in range(1, count)
    ]


def gather_ring(piece, count):
    found = [piece]
    back = ahead = piece
    for _ in range(count // 2 - 1):
        back = lax.ppermute(back, "mp", turn(count, 1))
        ahead = lax.ppermute(ahead, "mp", turn(count, count - 1))
        found += [back, ahead]
    half = (piece.shape[0] // 2 + ROWS - 1) // ROWS * ROWS
    found.append(lax.ppermute(back[:half], "mp", turn(count, 1)))
    found.append(lax.ppermute(ahead[half:], "mp", turn(count, count - 1)))
    return found


def place(refs, here, count, store):
    half = count // 2
    store(here, refs[0][...])
    for step in range(1, half):
        for ref, sign in ((refs[2 * step - 1], -1), (refs[2 * step], 1)):
            store(lax.rem(here + sign * step + count, count), ref[...])
    store(
        lax.rem(here + half, count), jnp.concatenate([refs[-2][...], refs[-1][...]], 0)
    )


def pack(square):
    half = square.shape[0] // 2
    side = square[:, 128:]
    return jnp.concatenate(
        [square[:, :128], jnp.concatenate([side[:half], side[half:]], 1)], 0
    )


def unpack(packed):
    rows = packed.shape[0] // 3 * 2
    side = packed[rows:]
    return jnp.concatenate(
        [packed[:rows], jnp.concatenate([side[:, :64], side[:, 64:]], 0)], 1
    )


def tile_forward(x_ref, one_ref, two_ref, norm_ref, hidden_ref, slope_ref, out_ref):
    x = x_ref[...].astype(f32)
    centred = x - jnp.mean(x, -1, keepdims=True)
    normed = centred * lax.rsqrt(jnp.mean(centred * centred, -1, keepdims=True) + eps)
    normed = normed.astype(bf16)
    norm_ref[...] = normed
    pre = jnp.dot(normed, one_ref[...], preferred_element_type=f32)
    bell = 0.5 * (1.0 + lax.erf(pre * 0.7071067811865476))
    hidden = (pre * bell).astype(bf16)
    hidden_ref[...] = hidden
    slope_ref[...] = bell + pre * jnp.exp(-0.5 * pre * pre) * 0.3989422804014327
    partial = jnp.dot(hidden, two_ref[...], preferred_element_type=f32).astype(bf16)
    count = out_ref.shape[0]
    block = partial.shape[1] // count
    for j in range(count):
        out_ref[j] = pack(partial[:, j * block : (j + 1) * block])


def tile_dispatch(own_ref, report_ref, dispatch_ref, flags_ref, parts_ref, out_ref):
    total = parts_ref[0].astype(f32)
    for j in range(1, parts_ref.shape[0]):
        total = total + parts_ref[j].astype(f32)
    embedding = (own_ref[...].astype(f32) + unpack(total)).astype(bf16)
    rows = jnp.dot(dispatch_ref[...], embedding, preferred_element_type=f32)
    slot = lax.broadcasted_iota(i32, rows.shape, 0)
    rows = jnp.where(lax.rem(slot, ROWS) == ROWS - 1, report_ref[...].astype(f32), rows)
    out_ref[...] = jnp.concatenate([rows.astype(bf16), flags_ref[...]], 1)


def slot_rows(arrived_ref, select_ref, report_select_ref, chunk_ref, valid_ref):
    arrived = arrived_ref[...]
    chunk = contract(arrived, select_ref[...], 0, 0)
    block = chunk_ref.shape[0] - EXTRA
    chunk_ref[0:block, :] = chunk[:block].astype(bf16)
    valid_ref[...] = chunk[block : block + 1]
    reports = jnp.dot(report_select_ref[...], arrived, preferred_element_type=f32)
    reports = reports[:, :block].astype(bf16)
    chunk_ref[block : block + EXTRA, :] = jnp.concatenate(
        [reports[:EXTRA], reports[EXTRA:]], 1
    )


def slide_forward(
    here,
    valid_ref,
    query_weights_ref,
    key_weights_ref,
    value_weights_ref,
    out_weights_ref,
    *rest,
):
    pieces = rest[:9]
    (
        norm_ref,
        stat_ref,
        query_ref,
        key_ref,
        value_ref,
        scale_ref,
        attention_ref,
        mass_ref,
        attended_ref,
        pooled_ref,
        reports_ref,
        slide_ref,
    ) = rest[9:]
    count, owners, block = reports_ref.shape

    def store(index, piece):
        start = pl.multiple_of(index * block, 16)
        slide_ref[pl.ds(start, block), :] = piece[:block]
        reports = piece[block:]
        reports_ref[index] = jnp.concatenate([reports[:, :block], reports[:, block:]], 0)

    place(pieces, here[0], count, store)
    valid = valid_ref[...]
    valid_low = valid.astype(bf16)
    low = slide_ref[...]
    slide = low.astype(f32)
    mean = jnp.mean(slide, 0, keepdims=True)
    centred = slide - mean
    inverse = lax.rsqrt(jnp.mean(centred * centred, 0, keepdims=True) + eps)
    stat_ref[...] = jnp.concatenate([mean, inverse], 0)
    norm_ref[...] = (centred * inverse).astype(bf16)
    normed = norm_ref[...]
    all_query = jnp.dot(query_weights_ref[...], normed, preferred_element_type=f32)
    all_keys = jnp.dot(key_weights_ref[...], normed, preferred_element_type=f32)
    all_values = jnp.dot(value_weights_ref[...], normed, preferred_element_type=f32)
    heads = all_query.shape[0] // HEAD
    attended = []
    for h in range(heads):
        low_rows, high_rows = h * HEAD, (h + 1) * HEAD
        query = all_query[low_rows:high_rows]
        keys = all_keys[low_rows:high_rows]
        values = all_values[low_rows:high_rows]
        query_scale = lax.rsqrt(jnp.mean(query * query, 0, keepdims=True) + eps)
        key_scale = lax.rsqrt(jnp.mean(keys * keys, 0, keepdims=True) + eps)
        query_unit = query * query_scale
        key_unit = keys * key_scale
        query_ref[h] = query_unit
        key_ref[h] = key_unit
        value_ref[h] = values
        scale_ref[h] = jnp.concatenate([query_scale, key_scale], 0)
        scores = contract(query_unit.astype(bf16), key_unit.astype(bf16), 0, 0)
        weights = jnp.exp(scores * (score_scale / HEAD)) * valid
        weights = weights * (1.0 / jnp.sum(weights, 1, keepdims=True))
        attention_ref[h] = weights
        weights_low = weights.astype(bf16)
        mass_ref[h : h + 1, :] = jnp.dot(valid_low, weights_low, preferred_element_type=f32)
        attended.append(contract(values.astype(bf16), weights_low, 1, 1))
    attended = jnp.concatenate(attended, 0).astype(bf16)
    attended_sum = contract(valid_low, attended, 1, 1)
    attended_ref[...] = attended_sum
    high = attended_sum.astype(bf16)
    rest_low = (attended_sum - high.astype(f32)).astype(bf16)
    part = jnp.dot(high, out_weights_ref[...], preferred_element_type=f32)
    part = part + jnp.dot(rest_low, out_weights_ref[...], preferred_element_type=f32)
    slide_sum = contract(valid_low, low, 1, 1)
    pooled = (part + slide_sum * (1.0 / count)) / jnp.sum(valid)
    pooled_ref[...] = jnp.broadcast_to(pooled[None], pooled_ref.shape)


def logits_row(parts_ref, reports_ref, unit_ref, report_ref, row_ref):
    pooled = jnp.sum(parts_ref[...], 0)
    inverse = lax.rsqrt(jnp.sum(pooled * pooled, -1, keepdims=True) + eps)
    unit = pooled * inverse
    unit_ref[...] = jnp.concatenate([unit, jnp.broadcast_to(inverse, unit.shape)], 0)
    count, owners, block = reports_ref.shape
    squares = jnp.zeros((owners, 1), f32)
    for j in range(count):
        reports = reports_ref[j].astype(f32)
        report_ref[:, j * block : (j + 1) * block] = reports
        squares = squares + jnp.sum(reports * reports, -1, keepdims=True)
    report = report_ref[...] * lax.rsqrt(squares + eps)
    report_ref[...] = report
    row = contract(unit, report, 1, 1, precision=exact) / contrast_divisor_factor
    pad = row_ref.shape[2] - row.shape[1]
    row = jnp.concatenate([row, jnp.zeros((1, pad), f32)], 1)
    row_ref[...] = jnp.broadcast_to(row[None], row_ref.shape)


def slide_backward(
    here,
    owner,
    logits_ref,
    pair_ref,
    unit_ref,
    report_ref,
    valid_ref,
    out_weights_ref,
    query_weights_ref,
    key_weights_ref,
    value_weights_ref,
    norm_ref,
    query_ref,
    key_ref,
    value_ref,
    scale_ref,
    attention_ref,
    mass_ref,
    loss_ref,
    grad_ref,
    up_ref,
    grads_ref,
    *outs,
):
    owners = report_ref.shape[0]
    valid = valid_ref[...]
    logits = logits_ref[...]
    shape = logits.shape
    columns = lax.broadcasted_iota(i32, shape, 1)
    rows = lax.broadcasted_iota(i32, shape, 0)
    real = columns < owners
    expo = jnp.where(real, jnp.exp(logits), 0.0)
    row_total = jnp.sum(expo, 1, keepdims=True)
    column_total = jnp.where(real[:1], jnp.sum(expo, 0, keepdims=True), 1.0)
    target = jnp.where(pair_ref[...] == columns, 1.0, 0.0)
    loss = jnp.sum(
        0.5 * jnp.log(row_total) - jnp.sum(logits * target, 1, keepdims=True), 0, keepdims=True
    )
    loss = loss + 0.5 * jnp.sum(jnp.log(column_total), 1, keepdims=True)
    loss_ref[...] = loss * (1.0 / owners)
    grad_logits = (0.5 * expo / row_total + 0.5 * expo / column_total - target) * (
        loss_scale / owners
    )
    grad_row = jnp.sum(jnp.where(rows == owner[0], grad_logits, 0.0), 0, keepdims=True)
    grad_unit = (
        jnp.dot(grad_row[:, :owners], report_ref[...], precision=exact, preferred_element_type=f32)
        / contrast_divisor_factor
    )
    unit = unit_ref[0:1]
    inverse = unit_ref[1:2]
    grad_pooled = (grad_unit - unit * jnp.sum(unit * grad_unit, -1, keepdims=True)) * inverse
    grad = grad_pooled / jnp.sum(valid)
    grad_ref[...] = grad
    low = grad.astype(bf16)
    out_weights = out_weights_ref[...]
    up_ref[...] = contract(low, out_weights, 1, 1)
    up = jnp.sum(out_weights.astype(f32) * low.astype(f32), 1, keepdims=True)
    heads = query_ref.shape[0]
    inner = heads * HEAD
    for h in range(heads):
        up_head = up[h * HEAD : (h + 1) * HEAD]
        values = value_ref[h]
        weights = attention_ref[h]
        pull = jnp.sum(up_head * values, 0, keepdims=True)
        pull_mean = jnp.sum(weights * pull, 1, keepdims=True)
        grad_scores = (weights * (pull - pull_mean) * (score_scale / HEAD)).astype(bf16)
        query_unit = query_ref[h]
        key_unit = key_ref[h]
        grad_query = contract(key_unit.astype(bf16), grad_scores, 1, 1) * valid
        grad_key = jnp.dot(query_unit.astype(bf16), grad_scores, preferred_element_type=f32)
        grad_query = scale_ref[h, 0:1] * (
            grad_query - query_unit * jnp.mean(query_unit * grad_query, 0, keepdims=True)
        )
        grad_key = scale_ref[h, 1:2] * (
            grad_key - key_unit * jnp.mean(key_unit * grad_key, 0, keepdims=True)
        )
        grad_value = up_head * mass_ref[h : h + 1]
        for part, values in enumerate((grad_query, grad_key, grad_value)):
            start = part * inner + h * HEAD
            grads_ref[start : start + HEAD, :] = values.astype(bf16)
    grad_query = grads_ref[0:inner, :]
    grad_key = grads_ref[inner : 2 * inner, :]
    grad_value = grads_ref[2 * inner : 3 * inner, :]
    count = len(outs)
    block = norm_ref.shape[0] // count
    first = jnp.zeros_like(valid)
    second = jnp.zeros_like(valid)
    for k in range(count):
        start = pl.multiple_of(lax.rem(here[0] + k, count) * block, 16)
        rows = pl.ds(start, block)
        part = jnp.dot(query_weights_ref[rows, :], grad_query, preferred_element_type=f32)
        part = part + jnp.dot(key_weights_ref[rows, :], grad_key, preferred_element_type=f32)
        part = part + jnp.dot(value_weights_ref[rows, :], grad_value, preferred_element_type=f32)
        outs[k][0:block, :] = part.astype(bf16)
        first = first + jnp.sum(part, 0, keepdims=True)
        second = second + jnp.sum(part * norm_ref[rows, :].astype(f32), 0, keepdims=True)
    width = norm_ref.shape[0]
    stats = jnp.concatenate([first, second], 0) * (1.0 / width)
    high = stats.astype(bf16).astype(f32)
    stats = jnp.concatenate(
        [high, stats - high, jnp.zeros((EXTRA - 4, stats.shape[1]), f32)], 0
    ).astype(bf16)
    for k in range(count):
        outs[k][block : block + EXTRA, :] = stats


def slot_grads(own_ref, valid_ref, stat_ref, chunk_ref, select_ref, extra_ref, *rest):
    refs, out_ref = rest[:-1], rest[-1]
    total = refs[0][...].astype(f32)
    for ref in refs[1:]:
        total = total + ref[...].astype(f32)
    block = chunk_ref.shape[0] - EXTRA
    first = total[block : block + 1] + total[block + 2 : block + 3]
    second = total[block + 1 : block + 2] + total[block + 3 : block + 4]
    mean = stat_ref[0:1]
    inverse = stat_ref[1:2]
    normed = (chunk_ref[0:block, :].astype(f32) - mean) * inverse
    rows = own_ref[...] * valid_ref[...] + (total[:block] - first - normed * second) * inverse
    rows = contract(select_ref[...], rows.astype(bf16), 1, 1).astype(bf16)
    out_ref[...] = rows + extra_ref[...]


def tile_grads(back_ref, dispatch_ref, out_ref):
    piece = pack(contract(back_ref[...], dispatch_ref[...], 0, 0).astype(bf16))
    out_ref[...] = jnp.broadcast_to(piece[None], out_ref.shape)


def other_grads(
    other, two_ref, slope_ref, norm_ref, hidden_ref, parts_ref, grad_ref, hidden_grad_ref, out_ref
):
    count = parts_ref.shape[0]
    rows = grad_ref.shape[0] // count
    for j in range(count):
        grad_ref[j * rows : (j + 1) * rows, :] = unpack(parts_ref[j])
    grad_hidden = jnp.dot(two_ref[...], grad_ref[...], preferred_element_type=f32)
    hidden_grad_ref[...] = (grad_hidden * slope_ref[...]).astype(bf16)

    def store(rows, values):
        out_ref[rows] = values.astype(bf16)

    both_layers(other[0], norm_ref, hidden_ref, grad_ref, hidden_grad_ref, out_ref.shape, store)


def own_grads(own, norm_ref, hidden_ref, grad_ref, hidden_grad_ref, got_ref, out_ref):
    def store(rows, values):
        out_ref[rows] = (values + got_ref[rows].astype(f32)).astype(bf16)

    both_layers(own[0], norm_ref, hidden_ref, grad_ref, hidden_grad_ref, out_ref.shape, store)


def both_layers(which, norm_ref, hidden_ref, grad_ref, hidden_grad_ref, shape, store):
    chips, share = shape[0], shape[1] // 2
    rows = [
        grad_ref[pl.ds(pl.multiple_of((CORES * chip + which) * share, 16), share), :]
        for chip in range(chips)
    ]
    two = jnp.dot(jnp.concatenate(rows, 0), hidden_ref[...], preferred_element_type=f32)
    one = contract(norm_ref[...], hidden_grad_ref[...], 1, 1)
    for chip in range(chips):
        start = chip * share
        store((chip, slice(0, share)), one[start : start + share])
        store((chip, slice(share, 2 * share)), two[start : start + share])


def last_sums(values_ref, one_ref, two_ref):
    share = one_ref.shape[0]
    total = values_ref[0].astype(f32)
    for chip in range(1, values_ref.shape[0]):
        total = total + values_ref[chip].astype(f32)
    one_ref[...] = total[:share]
    two_ref[...] = total[share:]


def per_device(
    tile_features, tile_slide, slide_pair, reports, w_one, w_two, w_query, w_key, w_value, w_out
):
    chips = lax.axis_size("chip")
    owners = chips * CORES
    parts = lax.axis_size("mp")
    core = lax.axis_index("core")
    owner = lax.axis_index(DP)
    here = lax.axis_index("mp")
    tiles, width = tile_features.shape
    units = w_one.shape[1]
    capacity = 2 * tiles // owners
    length = owners * capacity
    slots = owners * ROWS
    block = width // parts
    share = width // owners
    inner = w_query.shape[1]
    heads = inner // HEAD
    packed = (block // 2 * 3, 128)

    def halves(values):
        rest = values.shape[1:]
        values = values.reshape((chips, CORES, share) + rest)
        own = pick(values, core, 1).reshape((chips * share,) + rest)
        other = pick(values, 1 - core, 1).reshape((chips * share,) + rest)
        return own, other

    tile_norm, hidden, slope, partial = call(
        tile_forward,
        [
            ((tiles, width), bf16),
            ((tiles, units), bf16),
            ((tiles, units), f32),
            ((parts,) + packed, bf16),
        ],
        tile_features,
        w_one,
        w_two,
        limit=24,
    )
    partial = exchange(partial, "mp")

    slide_ids = tile_slide[:, 0]
    matches = (slide_ids[:, None] == jnp.arange(owners, dtype=i32)[None, :]).astype(i32)
    ordinal = jnp.sum(matches * (jnp.cumsum(matches, 0) - 1), 1)
    position = slide_ids * ROWS + ordinal
    dispatch = jnp.arange(slots, dtype=i32)[:, None] == position[None, :]
    flags = jnp.sum(dispatch.astype(f32), 1, keepdims=True).astype(bf16)
    flags = jnp.pad(flags, ((0, 0), (0, 256 - block - 1)))
    dispatch = dispatch.astype(bf16)
    slot = jnp.arange(slots, dtype=i32)
    row_of_slot = jnp.where(slot % ROWS < capacity, slot // ROWS * capacity + slot % ROWS, -1)
    select = (row_of_slot[:, None] == jnp.arange(length, dtype=i32)[None, :]).astype(bf16)
    last_slot = jnp.arange(owners, dtype=i32)[:, None] * ROWS + ROWS - 1
    report_select = (last_slot == slot[None, :]).astype(bf16)
    own_columns = pick(tile_features.reshape(tiles, parts, block), here, 1)
    own_report = pick(reports.reshape(1, parts, block), here, 1)
    tile_own, tile_other = halves(tile_norm.T)
    slope = slope.T

    (outgoing,) = call(
        tile_dispatch,
        [((slots, 256), bf16)],
        own_columns,
        own_report,
        dispatch,
        flags,
        partial,
        anchors=(select, report_select, tile_own, tile_other, slope),
    )
    arrived = exchange(outgoing.reshape(owners, ROWS, 256), DP).reshape(slots, 256)
    chunk, valid = call(
        slot_rows,
        [((block + EXTRA, length), bf16), ((1, length), f32)],
        arrived,
        select,
        report_select,
    )
    pieces = gather_ring(chunk, parts)

    (
        slide_norm,
        stat,
        query,
        keys,
        values,
        scales,
        attention,
        mass,
        attended_sum,
        pooled,
        all_reports,
    ) = call(
        slide_forward,
        [
            ((width, length), bf16),
            ((2, length), f32),
            ((heads, HEAD, length), f32),
            ((heads, HEAD, length), f32),
            ((heads, HEAD, length), f32),
            ((heads, 2, length), f32),
            ((heads, length, length), f32),
            ((heads, length), f32),
            ((1, inner), f32),
            ((parts, 1, width), f32),
            ((parts, owners, block), bf16),
        ],
        valid,
        w_query.T,
        w_key.T,
        w_value.T,
        w_out,
        *pieces,
        scalars=(here,),
        scratch=[((width, length), bf16)],
        limit=28,
    )
    pooled = exchange(pooled, "mp")
    unit, report_unit, row = call(
        logits_row,
        [((2, width), f32), ((owners, width), f32), ((owners, 1, 128), f32)],
        pooled,
        all_reports,
    )
    logits = exchange(row, DP).reshape(owners, 128)
    loss, grad, up, grads, *pieces = call(
        slide_backward,
        [((1, 1), f32), ((1, width), f32), ((1, inner), f32), ((3 * inner, length), bf16)]
        + [((block + EXTRA, length), bf16)] * parts,
        logits,
        slide_pair[:, None],
        unit,
        report_unit,
        valid,
        w_out,
        w_query,
        w_key,
        w_value,
        slide_norm,
        query,
        keys,
        values,
        scales,
        attention,
        mass,
        scalars=(here, owner),
        limit=24,
    )
    pieces = scatter_ring(pieces, parts)

    norm_own, norm_other = halves(slide_norm)
    wide = (chips, share, 2 * inner)
    wide_other = contract(norm_other, grads[: 2 * inner], 1, 1).astype(bf16).reshape(wide)
    wide_got = lax.ppermute(wide_other, "core", [(0, 1), (1, 0)])
    wide_own = contract(norm_own, grads[: 2 * inner], 1, 1).reshape(wide)
    wide_sent = (wide_own + wide_got.astype(f32)).astype(bf16)
    grad_wide = jnp.sum(exchange(wide_sent, "chip").astype(f32), 0)
    value_rows = contract(mass.astype(bf16), slide_norm, 1, 1)
    extra = jnp.concatenate(
        [
            value_rows.reshape(heads, owners, share).transpose(1, 0, 2).reshape(owners, -1),
            grad.reshape(owners, share),
            jnp.broadcast_to(up, (owners, inner)),
            jnp.broadcast_to(attended_sum, (owners, inner)),
        ],
        1,
    ).astype(bf16)
    spare = ROWS - capacity
    extra = jnp.pad(extra, ((0, 0), (0, spare * block - extra.shape[1])))
    extra = extra.reshape(owners, spare, block)
    extra = jnp.pad(extra, ((0, 0), (capacity, 0), (0, 0))).reshape(slots, block)

    own_grad = lax.dynamic_slice_in_dim(grad, here * block, block, 1).reshape(block, 1)
    (going,) = call(
        slot_grads,
        [((slots, block), bf16)],
        own_grad,
        valid,
        stat,
        chunk,
        select,
        extra,
        *pieces,
        anchors=(grad_wide,),
    )
    back = exchange(going.reshape(owners, ROWS, block), DP).reshape(slots, block)
    (spreading,) = call(tile_grads, [((parts,) + packed, bf16)], back, dispatch)

    size = (chips, 2 * share, units)
    grad_embedding, grad_hidden, sent = call(
        other_grads,
        [((width, tiles), bf16), ((units, tiles), bf16), (size, bf16)],
        w_two,
        slope,
        tile_other,
        hidden,
        exchange(spreading, "mp"),
        scalars=(1 - core,),
        limit=24,
    )
    got = lax.ppermute(sent, "core", [(0, 1), (1, 0)])
    (both,) = call(
        own_grads,
        [(size, bf16)],
        tile_own,
        hidden,
        grad_embedding,
        grad_hidden,
        got,
        scalars=(core,),
        limit=24,
    )
    grad_one, grad_two = call(
        last_sums, [((share, units), f32), ((share, units), f32)], exchange(both, "chip")
    )
    grad_two = grad_two.T

    terms = back.reshape(owners, ROWS, block)[:, capacity:].reshape(owners, -1).astype(f32)
    edge = heads * share
    from_values = terms[:, :edge].reshape(owners, heads, share)
    from_grads = terms[:, edge : edge + share]
    edge = edge + share
    from_up = terms[:, edge : edge + inner].reshape(owners, heads, HEAD)
    edge = edge + inner
    from_attended = terms[:, edge : edge + inner]
    grad_value = jnp.einsum("ohs,ohd->shd", from_values, from_up, precision=exact)
    grad_value = grad_value.reshape(share, inner)
    grad_out = contract(from_attended, from_grads, 0, 0, precision=exact)
    return (
        loss[0, 0],
        grad_one,
        grad_two,
        grad_wide[:, :inner],
        grad_wide[:, inner:],
        grad_value,
        grad_out,
    )


def solution(mesh):
    owners, parts = mesh.devices.shape
    split = Mesh(
        mesh.devices.reshape(owners // CORES, CORES, parts), ("chip", "core", "mp")
    )
    return jax.shard_map(
        per_device,
        mesh=split,
        in_specs=(
            P(DP, None),
            P(DP, None),
            P(),
            P(DP, None),
            P(None, "mp"),
            P("mp", None),
            P(None, "mp"),
            P(None, "mp"),
            P(None, "mp"),
            P("mp", None),
        ),
        out_specs=(
            P(),
            P(DP, "mp"),
            P("mp", DP),
            P(DP, "mp"),
            P(DP, "mp"),
            P(DP, "mp"),
            P("mp", DP),
        ),
        check_vma=False,
    )
```

```python
import jax
import jax.numpy as jnp
from jax import lax
from jax.experimental import pallas as pl
from jax.experimental.pallas import tpu as pltpu
from jax.sharding import Mesh, PartitionSpec as P

HEAD = 96
CORES = 2
ROWS = 16
EXTRA = 16

eps = 1e-05
contrast_divisor_factor = 0.07
score_scale = 10.0
loss_scale = 4096.0
exact = lax.Precision.HIGHEST
f32 = jnp.float32
bf16 = jnp.bfloat16
i32 = jnp.int32
DP = ("chip", "core")


def contract(left, right, left_dim, right_dim, **kw):
    return lax.dot_general(
        left, right, (((left_dim,), (right_dim,)), ((), ())), preferred_element_type=f32, **kw
    )


def exchange(values, axis):
    return lax.all_to_all(values, axis, 0, 0, tiled=True)


def pick(values, index, axis):
    return lax.dynamic_index_in_dim(values, index, axis, keepdims=False)


def call(body, outs, *args, scalars=(), scratch=(), anchors=(), far=(), limit=16):
    count = len(scalars)
    skip = len(anchors)
    vmem = pl.BlockSpec(memory_space=pltpu.VMEM)
    away = pl.BlockSpec(memory_space=pl.ANY)

    def kernel(*refs):
        body(*refs[skip:])

    return pl.pallas_call(
        kernel if skip else body,
        out_shape=[jax.ShapeDtypeStruct(out[0], out[1]) for out in outs],
        in_specs=[away] * skip
        + [pl.BlockSpec(memory_space=pltpu.SMEM)] * count
        + [away if index in far else vmem for index in range(len(args))],
        out_specs=[vmem if len(out) == 2 else away for out in outs],
        scratch_shapes=[
            pltpu.VMEM(*part) if isinstance(part, tuple) else pltpu.SemaphoreType.DMA((part,))
            for part in scratch
        ],
        compiler_params=pltpu.CompilerParams(vmem_limit_bytes=limit * 1024 * 1024),
    )(*anchors, *[jnp.reshape(s, (1,)).astype(i32) for s in scalars], *args)


def fetch(sources, targets, semaphores):
    copies = [
        pltpu.make_async_copy(source, target, semaphores.at[index])
        for index, (source, target) in enumerate(zip(sources, targets))
    ]
    for copy in copies:
        copy.start()
    return copies


def turn(count, step):
    return [(index, (index + step) % count) for index in range(count)]


def scatter_ring(pieces, count):
    return [pieces[0]] + [
        lax.ppermute(pieces[k], "mp", turn(count, k)) for k in range(1, count)
    ]


def gather_ring(piece, count):
    found = [piece]
    back = ahead = piece
    for _ in range(count // 2 - 1):
        back = lax.ppermute(back, "mp", turn(count, 1))
        ahead = lax.ppermute(ahead, "mp", turn(count, count - 1))
        found += [back, ahead]
    half = (piece.shape[0] // 2 + ROWS - 1) // ROWS * ROWS
    found.append(lax.ppermute(back[:half], "mp", turn(count, 1)))
    found.append(lax.ppermute(ahead[half:], "mp", turn(count, count - 1)))
    return found


def place(refs, here, count, store):
    half = count // 2
    store(here, refs[0][...])
    for step in range(1, half):
        for ref, sign in ((refs[2 * step - 1], -1), (refs[2 * step], 1)):
            store(lax.rem(here + sign * step + count, count), ref[...])
    store(
        lax.rem(here + half, count), jnp.concatenate([refs[-2][...], refs[-1][...]], 0)
    )


def pack(square):
    half = square.shape[0] // 2
    side = square[:, 128:]
    return jnp.concatenate(
        [square[:, :128], jnp.concatenate([side[:half], side[half:]], 1)], 0
    )


def unpack(packed):
    rows = packed.shape[0] // 3 * 2
    side = packed[rows:]
    return jnp.concatenate(
        [packed[:rows], jnp.concatenate([side[:, :64], side[:, 64:]], 0)], 1
    )


def tile_forward(
    far_x, far_one, far_two, norm_ref, hidden_ref, slope_ref, out_ref, x_ref, one_ref, two_ref, sems
):
    copies = fetch((far_x, far_one, far_two), (x_ref, one_ref, two_ref), sems)
    copies[0].wait()
    x = x_ref[...].astype(f32)
    centred = x - jnp.mean(x, -1, keepdims=True)
    normed = centred * lax.rsqrt(jnp.mean(centred * centred, -1, keepdims=True) + eps)
    normed = normed.astype(bf16)
    norm_ref[...] = normed
    copies[1].wait()
    pre = jnp.dot(normed, one_ref[...], preferred_element_type=f32)
    bell = 0.5 * (1.0 + lax.erf(pre * 0.7071067811865476))
    hidden = (pre * bell).astype(bf16)
    hidden_ref[...] = hidden
    slope_ref[...] = bell + pre * jnp.exp(-0.5 * pre * pre) * 0.3989422804014327
    copies[2].wait()
    partial = jnp.dot(hidden, two_ref[...], preferred_element_type=f32).astype(bf16)
    count = out_ref.shape[0]
    block = partial.shape[1] // count
    for j in range(count):
        out_ref[j] = pack(partial[:, j * block : (j + 1) * block])


def tile_dispatch(own_ref, report_ref, dispatch_ref, flags_ref, parts_ref, out_ref):
    total = parts_ref[0].astype(f32)
    for j in range(1, parts_ref.shape[0]):
        total = total + parts_ref[j].astype(f32)
    embedding = (own_ref[...].astype(f32) + unpack(total)).astype(bf16)
    rows = jnp.dot(dispatch_ref[...], embedding, preferred_element_type=f32)
    slot = lax.broadcasted_iota(i32, rows.shape, 0)
    rows = jnp.where(lax.rem(slot, ROWS) == ROWS - 1, report_ref[...].astype(f32), rows)
    out_ref[...] = jnp.concatenate([rows.astype(bf16), flags_ref[...]], 1)


def slot_rows(arrived_ref, select_ref, report_select_ref, chunk_ref, valid_ref):
    arrived = arrived_ref[...]
    chunk = contract(arrived, select_ref[...], 0, 0)
    block = chunk_ref.shape[0] - EXTRA
    chunk_ref[0:block, :] = chunk[:block].astype(bf16)
    valid_ref[...] = chunk[block : block + 1]
    reports = jnp.dot(report_select_ref[...], arrived, preferred_element_type=f32)
    reports = reports[:, :block].astype(bf16)
    chunk_ref[block : block + EXTRA, :] = jnp.concatenate(
        [reports[:EXTRA], reports[EXTRA:]], 1
    )


def slide_forward(
    here,
    valid_ref,
    query_weights_ref,
    key_weights_ref,
    value_weights_ref,
    out_weights_ref,
    *rest,
):
    pieces = rest[:9]
    (
        far_norm,
        far_heads,
        far_attention,
        stat_ref,
        scale_ref,
        mass_ref,
        attended_ref,
        pooled_ref,
        reports_ref,
        slide_ref,
        norm_ref,
        heads_ref,
        attention_ref,
        sems,
    ) = rest[9:]
    count, owners, block = reports_ref.shape

    def store(index, piece):
        start = pl.multiple_of(index * block, 16)
        slide_ref[pl.ds(start, block), :] = piece[:block]
        reports = piece[block:]
        reports_ref[index] = jnp.concatenate([reports[:, :block], reports[:, block:]], 0)

    place(pieces, here[0], count, store)
    valid = valid_ref[...]
    valid_low = valid.astype(bf16)
    low = slide_ref[...]
    slide = low.astype(f32)
    mean = jnp.mean(slide, 0, keepdims=True)
    centred = slide - mean
    inverse = lax.rsqrt(jnp.mean(centred * centred, 0, keepdims=True) + eps)
    stat_ref[...] = jnp.concatenate([mean, inverse], 0)
    normed = (centred * inverse).astype(bf16)
    norm_ref[...] = normed
    copies = [pltpu.make_async_copy(norm_ref, far_norm, sems.at[0])]
    copies[0].start()
    all_query = jnp.dot(query_weights_ref[...], normed, preferred_element_type=f32)
    all_keys = jnp.dot(key_weights_ref[...], normed, preferred_element_type=f32)
    all_values = jnp.dot(value_weights_ref[...], normed, preferred_element_type=f32)
    heads = all_query.shape[0] // HEAD
    attended = []
    for h in range(heads):
        low_rows, high_rows = h * HEAD, (h + 1) * HEAD
        query = all_query[low_rows:high_rows]
        keys = all_keys[low_rows:high_rows]
        values = all_values[low_rows:high_rows]
        query_scale = lax.rsqrt(jnp.mean(query * query, 0, keepdims=True) + eps)
        key_scale = lax.rsqrt(jnp.mean(keys * keys, 0, keepdims=True) + eps)
        query_unit = query * query_scale
        key_unit = keys * key_scale
        heads_ref[h, 0] = query_unit
        heads_ref[h, 1] = key_unit
        heads_ref[h, 2] = values
        copies.append(pltpu.make_async_copy(heads_ref.at[h], far_heads.at[h], sems.at[1 + 2 * h]))
        copies[-1].start()
        scale_ref[h] = jnp.concatenate([query_scale, key_scale], 0)
        scores = contract(query_unit.astype(bf16), key_unit.astype(bf16), 0, 0)
        weights = jnp.exp(scores * (score_scale / HEAD)) * valid
        weights = weights * (1.0 / jnp.sum(weights, 1, keepdims=True))
        attention_ref[h] = weights
        copies.append(
            pltpu.make_async_copy(attention_ref.at[h], far_attention.at[h], sems.at[2 + 2 * h])
        )
        copies[-1].start()
        weights_low = weights.astype(bf16)
        mass_ref[h : h + 1, :] = jnp.dot(valid_low, weights_low, preferred_element_type=f32)
        attended.append(contract(values.astype(bf16), weights_low, 1, 1))
    attended = jnp.concatenate(attended, 0).astype(bf16)
    attended_sum = contract(valid_low, attended, 1, 1)
    attended_ref[...] = attended_sum
    high = attended_sum.astype(bf16)
    rest_low = (attended_sum - high.astype(f32)).astype(bf16)
    part = jnp.dot(high, out_weights_ref[...], preferred_element_type=f32)
    part = part + jnp.dot(rest_low, out_weights_ref[...], preferred_element_type=f32)
    slide_sum = contract(valid_low, low, 1, 1)
    pooled = (part + slide_sum * (1.0 / count)) / jnp.sum(valid)
    pooled_ref[...] = jnp.broadcast_to(pooled[None], pooled_ref.shape)
    for copy in copies:
        copy.wait()


def logits_row(parts_ref, reports_ref, unit_ref, report_ref, row_ref):
    pooled = jnp.sum(parts_ref[...], 0)
    inverse = lax.rsqrt(jnp.sum(pooled * pooled, -1, keepdims=True) + eps)
    unit = pooled * inverse
    unit_ref[...] = jnp.concatenate([unit, jnp.broadcast_to(inverse, unit.shape)], 0)
    count, owners, block = reports_ref.shape
    squares = jnp.zeros((owners, 1), f32)
    for j in range(count):
        reports = reports_ref[j].astype(f32)
        report_ref[:, j * block : (j + 1) * block] = reports
        squares = squares + jnp.sum(reports * reports, -1, keepdims=True)
    report = report_ref[...] * lax.rsqrt(squares + eps)
    report_ref[...] = report
    row = contract(unit, report, 1, 1, precision=exact) / contrast_divisor_factor
    pad = row_ref.shape[2] - row.shape[1]
    row = jnp.concatenate([row, jnp.zeros((1, pad), f32)], 1)
    row_ref[...] = jnp.broadcast_to(row[None], row_ref.shape)


def slide_backward(
    here,
    owner,
    logits_ref,
    pair_ref,
    unit_ref,
    report_ref,
    valid_ref,
    scale_ref,
    mass_ref,
    far_out_weights,
    far_heads,
    far_attention,
    far_query_weights,
    far_key_weights,
    far_value_weights,
    far_norm,
    loss_ref,
    grad_ref,
    up_ref,
    grads_ref,
    *rest,
):
    outs, fetched, sems = rest[:-8], rest[-8:-1], rest[-1]
    (
        out_weights_ref,
        heads_ref,
        attention_ref,
        query_weights_ref,
        key_weights_ref,
        value_weights_ref,
        norm_ref,
    ) = fetched
    copies = fetch(
        (
            far_out_weights,
            far_heads,
            far_attention,
            far_query_weights,
            far_key_weights,
            far_value_weights,
            far_norm,
        ),
        fetched,
        sems,
    )
    owners = report_ref.shape[0]
    valid = valid_ref[...]
    logits = logits_ref[...]
    shape = logits.shape
    columns = lax.broadcasted_iota(i32, shape, 1)
    rows = lax.broadcasted_iota(i32, shape, 0)
    real = columns < owners
    expo = jnp.where(real, jnp.exp(logits), 0.0)
    row_total = jnp.sum(expo, 1, keepdims=True)
    column_total = jnp.where(real[:1], jnp.sum(expo, 0, keepdims=True), 1.0)
    target = jnp.where(pair_ref[...] == columns, 1.0, 0.0)
    loss = jnp.sum(
        0.5 * jnp.log(row_total) - jnp.sum(logits * target, 1, keepdims=True), 0, keepdims=True
    )
    loss = loss + 0.5 * jnp.sum(jnp.log(column_total), 1, keepdims=True)
    loss_ref[...] = loss * (1.0 / owners)
    grad_logits = (0.5 * expo / row_total + 0.5 * expo / column_total - target) * (
        loss_scale / owners
    )
    grad_row = jnp.sum(jnp.where(rows == owner[0], grad_logits, 0.0), 0, keepdims=True)
    grad_unit = (
        jnp.dot(grad_row[:, :owners], report_ref[...], precision=exact, preferred_element_type=f32)
        / contrast_divisor_factor
    )
    unit = unit_ref[0:1]
    inverse = unit_ref[1:2]
    grad_pooled = (grad_unit - unit * jnp.sum(unit * grad_unit, -1, keepdims=True)) * inverse
    grad = grad_pooled / jnp.sum(valid)
    grad_ref[...] = grad
    low = grad.astype(bf16)
    copies[0].wait()
    out_weights = out_weights_ref[...]
    up_ref[...] = contract(low, out_weights, 1, 1)
    up = jnp.sum(out_weights.astype(f32) * low.astype(f32), 1, keepdims=True)
    heads = heads_ref.shape[0]
    inner = heads * HEAD
    copies[1].wait()
    copies[2].wait()
    for h in range(heads):
        up_head = up[h * HEAD : (h + 1) * HEAD]
        values = heads_ref[h, 2]
        weights = attention_ref[h]
        pull = jnp.sum(up_head * values, 0, keepdims=True)
        pull_mean = jnp.sum(weights * pull, 1, keepdims=True)
        grad_scores = (weights * (pull - pull_mean) * (score_scale / HEAD)).astype(bf16)
        query_unit = heads_ref[h, 0]
        key_unit = heads_ref[h, 1]
        grad_query = contract(key_unit.astype(bf16), grad_scores, 1, 1) * valid
        grad_key = jnp.dot(query_unit.astype(bf16), grad_scores, preferred_element_type=f32)
        grad_query = scale_ref[h, 0:1] * (
            grad_query - query_unit * jnp.mean(query_unit * grad_query, 0, keepdims=True)
        )
        grad_key = scale_ref[h, 1:2] * (
            grad_key - key_unit * jnp.mean(key_unit * grad_key, 0, keepdims=True)
        )
        grad_value = up_head * mass_ref[h : h + 1]
        for part, values in enumerate((grad_query, grad_key, grad_value)):
            start = part * inner + h * HEAD
            grads_ref[start : start + HEAD, :] = values.astype(bf16)
    grad_query = grads_ref[0:inner, :]
    grad_key = grads_ref[inner : 2 * inner, :]
    grad_value = grads_ref[2 * inner : 3 * inner, :]
    for copy in copies[3:]:
        copy.wait()
    count = len(outs)
    block = norm_ref.shape[0] // count
    first = jnp.zeros_like(valid)
    second = jnp.zeros_like(valid)
    for k in range(count):
        start = pl.multiple_of(lax.rem(here[0] + k, count) * block, 16)
        rows = pl.ds(start, block)
        part = jnp.dot(query_weights_ref[rows, :], grad_query, preferred_element_type=f32)
        part = part + jnp.dot(key_weights_ref[rows, :], grad_key, preferred_element_type=f32)
        part = part + jnp.dot(value_weights_ref[rows, :], grad_value, preferred_element_type=f32)
        outs[k][0:block, :] = part.astype(bf16)
        first = first + jnp.sum(part, 0, keepdims=True)
        second = second + jnp.sum(part * norm_ref[rows, :].astype(f32), 0, keepdims=True)
    width = norm_ref.shape[0]
    stats = jnp.concatenate([first, second], 0) * (1.0 / width)
    high = stats.astype(bf16).astype(f32)
    stats = jnp.concatenate(
        [high, stats - high, jnp.zeros((EXTRA - 4, stats.shape[1]), f32)], 0
    ).astype(bf16)
    for k in range(count):
        outs[k][block : block + EXTRA, :] = stats


def wide_grads(which, norm_ref, grads_ref, *rest):
    got, out_ref = rest[:-1], rest[-1]
    chips, share, columns = out_ref.shape
    rows = [
        norm_ref[pl.ds(pl.multiple_of((CORES * chip + which[0]) * share, 16), share), :]
        for chip in range(chips)
    ]
    values = contract(jnp.concatenate(rows, 0), grads_ref[0:columns, :], 1, 1)
    for chip in range(chips):
        part = values[chip * share : (chip + 1) * share]
        if got:
            part = part + got[0][chip].astype(f32)
        out_ref[chip] = part.astype(bf16)


def slot_grads(own_ref, valid_ref, stat_ref, chunk_ref, select_ref, extra_ref, *rest):
    refs, out_ref = rest[:-1], rest[-1]
    total = refs[0][...].astype(f32)
    for ref in refs[1:]:
        total = total + ref[...].astype(f32)
    block = chunk_ref.shape[0] - EXTRA
    first = total[block : block + 1] + total[block + 2 : block + 3]
    second = total[block + 1 : block + 2] + total[block + 3 : block + 4]
    mean = stat_ref[0:1]
    inverse = stat_ref[1:2]
    normed = (chunk_ref[0:block, :].astype(f32) - mean) * inverse
    rows = own_ref[...] * valid_ref[...] + (total[:block] - first - normed * second) * inverse
    rows = contract(select_ref[...], rows.astype(bf16), 1, 1).astype(bf16)
    out_ref[...] = rows + extra_ref[...]


def tile_grads(back_ref, dispatch_ref, out_ref):
    piece = pack(contract(back_ref[...], dispatch_ref[...], 0, 0).astype(bf16))
    out_ref[...] = jnp.broadcast_to(piece[None], out_ref.shape)


def other_grads(
    other, two_ref, slope_ref, norm_ref, hidden_ref, parts_ref, grad_ref, hidden_grad_ref, out_ref
):
    count = parts_ref.shape[0]
    rows = grad_ref.shape[0] // count
    for j in range(count):
        grad_ref[j * rows : (j + 1) * rows, :] = unpack(parts_ref[j])
    grad_hidden = jnp.dot(two_ref[...], grad_ref[...], preferred_element_type=f32)
    hidden_grad_ref[...] = (grad_hidden * slope_ref[...]).astype(bf16)

    def store(rows, values):
        out_ref[rows] = values.astype(bf16)

    both_layers(other[0], norm_ref, hidden_ref, grad_ref, hidden_grad_ref, out_ref.shape, store)


def own_grads(
    own, norm_ref, hidden_ref, grad_ref, hidden_grad_ref, got_ref, far_out, out_ref, sems
):
    copies = []

    def store(rows, values):
        out_ref[rows] = (values + got_ref[rows].astype(f32)).astype(bf16)
        chip = rows[0]
        if rows[1].start:
            copies.append(
                pltpu.make_async_copy(out_ref.at[chip], far_out.at[chip], sems.at[chip])
            )
            copies[-1].start()

    both_layers(own[0], norm_ref, hidden_ref, grad_ref, hidden_grad_ref, out_ref.shape, store)
    for copy in copies:
        copy.wait()


def both_layers(which, norm_ref, hidden_ref, grad_ref, hidden_grad_ref, shape, store):
    chips, share = shape[0], shape[1] // 2
    rows = [
        grad_ref[pl.ds(pl.multiple_of((CORES * chip + which) * share, 16), share), :]
        for chip in range(chips)
    ]
    two = jnp.dot(jnp.concatenate(rows, 0), hidden_ref[...], preferred_element_type=f32)
    one = contract(norm_ref[...], hidden_grad_ref[...], 1, 1)
    for chip in range(chips):
        start = chip * share
        store((chip, slice(0, share)), one[start : start + share])
        store((chip, slice(share, 2 * share)), two[start : start + share])


def last_sums(values_ref, one_ref, two_ref):
    share = one_ref.shape[0]
    total = values_ref[0].astype(f32)
    for chip in range(1, values_ref.shape[0]):
        total = total + values_ref[chip].astype(f32)
    one_ref[...] = total[:share]
    two_ref[...] = total[share:]


def per_device(
    tile_features, tile_slide, slide_pair, reports, w_one, w_two, w_query, w_key, w_value, w_out
):
    chips = lax.axis_size("chip")
    owners = chips * CORES
    parts = lax.axis_size("mp")
    core = lax.axis_index("core")
    owner = lax.axis_index(DP)
    here = lax.axis_index("mp")
    tiles, width = tile_features.shape
    units = w_one.shape[1]
    capacity = 2 * tiles // owners
    length = owners * capacity
    slots = owners * ROWS
    block = width // parts
    share = width // owners
    inner = w_query.shape[1]
    heads = inner // HEAD
    packed = (block // 2 * 3, 128)

    def halves(values):
        rest = values.shape[1:]
        values = values.reshape((chips, CORES, share) + rest)
        own = pick(values, core, 1).reshape((chips * share,) + rest)
        other = pick(values, 1 - core, 1).reshape((chips * share,) + rest)
        return own, other

    tile_norm, hidden, slope, partial = call(
        tile_forward,
        [
            ((tiles, width), bf16),
            ((tiles, units), bf16),
            ((tiles, units), f32),
            ((parts,) + packed, bf16),
        ],
        tile_features,
        w_one,
        w_two,
        far=(0, 1, 2),
        scratch=[
            (tile_features.shape, bf16),
            (w_one.shape, bf16),
            (w_two.shape, bf16),
            3,
        ],
        limit=24,
    )
    partial = exchange(partial, "mp")

    slide_ids = tile_slide[:, 0]
    matches = (slide_ids[:, None] == jnp.arange(owners, dtype=i32)[None, :]).astype(i32)
    ordinal = jnp.sum(matches * (jnp.cumsum(matches, 0) - 1), 1)
    position = slide_ids * ROWS + ordinal
    dispatch = jnp.arange(slots, dtype=i32)[:, None] == position[None, :]
    flags = jnp.sum(dispatch.astype(f32), 1, keepdims=True).astype(bf16)
    flags = jnp.pad(flags, ((0, 0), (0, 256 - block - 1)))
    dispatch = dispatch.astype(bf16)
    slot = jnp.arange(slots, dtype=i32)
    row_of_slot = jnp.where(slot % ROWS < capacity, slot // ROWS * capacity + slot % ROWS, -1)
    select = (row_of_slot[:, None] == jnp.arange(length, dtype=i32)[None, :]).astype(bf16)
    last_slot = jnp.arange(owners, dtype=i32)[:, None] * ROWS + ROWS - 1
    report_select = (last_slot == slot[None, :]).astype(bf16)
    own_columns = pick(tile_features.reshape(tiles, parts, block), here, 1)
    own_report = pick(reports.reshape(1, parts, block), here, 1)
    tile_own, tile_other = halves(tile_norm.T)
    slope = slope.T

    (outgoing,) = call(
        tile_dispatch,
        [((slots, 256), bf16)],
        own_columns,
        own_report,
        dispatch,
        flags,
        partial,
        anchors=(select, report_select, tile_own, tile_other, slope),
    )
    arrived = exchange(outgoing.reshape(owners, ROWS, 256), DP).reshape(slots, 256)
    chunk, valid = call(
        slot_rows,
        [((block + EXTRA, length), bf16), ((1, length), f32)],
        arrived,
        select,
        report_select,
    )
    pieces = gather_ring(chunk, parts)

    (
        slide_norm,
        by_head,
        attention,
        stat,
        scales,
        mass,
        attended_sum,
        pooled,
        all_reports,
    ) = call(
        slide_forward,
        [
            ((width, length), bf16, "far"),
            ((heads, 3, HEAD, length), f32, "far"),
            ((heads, length, length), f32, "far"),
            ((2, length), f32),
            ((heads, 2, length), f32),
            ((heads, length), f32),
            ((1, inner), f32),
            ((parts, 1, width), f32),
            ((parts, owners, block), bf16),
        ],
        valid,
        w_query.T,
        w_key.T,
        w_value.T,
        w_out,
        *pieces,
        scalars=(here,),
        scratch=[
            ((width, length), bf16),
            ((width, length), bf16),
            ((heads, 3, HEAD, length), f32),
            ((heads, length, length), f32),
            1 + 2 * heads,
        ],
        limit=28,
    )
    pooled = exchange(pooled, "mp")
    unit, report_unit, row = call(
        logits_row,
        [((2, width), f32), ((owners, width), f32), ((owners, 1, 128), f32)],
        pooled,
        all_reports,
    )
    logits = exchange(row, DP).reshape(owners, 128)
    loss, grad, up, grads, *pieces = call(
        slide_backward,
        [((1, 1), f32), ((1, width), f32), ((1, inner), f32), ((3 * inner, length), bf16)]
        + [((block + EXTRA, length), bf16)] * parts,
        logits,
        slide_pair[:, None],
        unit,
        report_unit,
        valid,
        scales,
        mass,
        w_out,
        by_head,
        attention,
        w_query,
        w_key,
        w_value,
        slide_norm,
        scalars=(here, owner),
        far=tuple(range(7, 14)),
        scratch=[
            (w_out.shape, bf16),
            (by_head.shape, f32),
            (attention.shape, f32),
            (w_query.shape, bf16),
            (w_key.shape, bf16),
            (w_value.shape, bf16),
            (slide_norm.shape, bf16),
            7,
        ],
        limit=28,
    )
    pieces = scatter_ring(pieces, parts)

    wide = (chips, share, 2 * inner)
    (wide_sent,) = call(
        wide_grads,
        [(wide, bf16)],
        slide_norm,
        grads,
        scalars=(1 - core,),
        anchors=(pieces[1],),
    )
    wide_got = lax.ppermute(wide_sent, "core", [(0, 1), (1, 0)])
    (wide_both,) = call(
        wide_grads, [(wide, bf16)], slide_norm, grads, wide_got, scalars=(core,)
    )
    grad_wide = jnp.sum(exchange(wide_both, "chip").astype(f32), 0)
    value_rows = contract(mass.astype(bf16), slide_norm, 1, 1)
    extra = jnp.concatenate(
        [
            value_rows.reshape(heads, owners, share).transpose(1, 0, 2).reshape(owners, -1),
            grad.reshape(owners, share),
            jnp.broadcast_to(up, (owners, inner)),
            jnp.broadcast_to(attended_sum, (owners, inner)),
        ],
        1,
    ).astype(bf16)
    spare = ROWS - capacity
    extra = jnp.pad(extra, ((0, 0), (0, spare * block - extra.shape[1])))
    extra = extra.reshape(owners, spare, block)
    extra = jnp.pad(extra, ((0, 0), (capacity, 0), (0, 0))).reshape(slots, block)

    own_grad = lax.dynamic_slice_in_dim(grad, here * block, block, 1).reshape(block, 1)
    (going,) = call(
        slot_grads,
        [((slots, block), bf16)],
        own_grad,
        valid,
        stat,
        chunk,
        select,
        extra,
        *pieces,
        anchors=(grad_wide,),
    )
    back = exchange(going.reshape(owners, ROWS, block), DP).reshape(slots, block)
    (spreading,) = call(tile_grads, [((parts,) + packed, bf16)], back, dispatch)

    size = (chips, 2 * share, units)
    grad_embedding, grad_hidden, sent = call(
        other_grads,
        [((width, tiles), bf16), ((units, tiles), bf16), (size, bf16)],
        w_two,
        slope,
        tile_other,
        hidden,
        exchange(spreading, "mp"),
        scalars=(1 - core,),
        limit=24,
    )
    got = lax.ppermute(sent, "core", [(0, 1), (1, 0)])
    (both,) = call(
        own_grads,
        [(size, bf16, "far")],
        tile_own,
        hidden,
        grad_embedding,
        grad_hidden,
        got,
        scalars=(core,),
        scratch=[(size, bf16), chips],
        limit=24,
    )
    grad_one, grad_two = call(
        last_sums, [((share, units), f32), ((share, units), f32)], exchange(both, "chip")
    )
    grad_two = grad_two.T

    terms = back.reshape(owners, ROWS, block)[:, capacity:].reshape(owners, -1).astype(f32)
    edge = heads * share
    from_values = terms[:, :edge].reshape(owners, heads, share)
    from_grads = terms[:, edge : edge + share]
    edge = edge + share
    from_up = terms[:, edge : edge + inner].reshape(owners, heads, HEAD)
    edge = edge + inner
    from_attended = terms[:, edge : edge + inner]
    grad_value = jnp.einsum("ohs,ohd->shd", from_values, from_up, precision=exact)
    grad_value = grad_value.reshape(share, inner)
    grad_out = contract(from_attended, from_grads, 0, 0, precision=exact)
    return (
        loss[0, 0],
        grad_one,
        grad_two,
        grad_wide[:, :inner],
        grad_wide[:, inner:],
        grad_value,
        grad_out,
    )


def solution(mesh):
    owners, parts = mesh.devices.shape
    split = Mesh(
        mesh.devices.reshape(owners // CORES, CORES, parts), ("chip", "core", "mp")
    )
    return jax.shard_map(
        per_device,
        mesh=split,
        in_specs=(
            P(DP, None),
            P(DP, None),
            P(),
            P(DP, None),
            P(None, "mp"),
            P("mp", None),
            P(None, "mp"),
            P(None, "mp"),
            P(None, "mp"),
            P("mp", None),
        ),
        out_specs=(
            P(),
            P(DP, "mp"),
            P("mp", DP),
            P(DP, "mp"),
            P(DP, "mp"),
            P(DP, "mp"),
            P("mp", DP),
        ),
        check_vma=False,
    )
```

```python
import math

import jax
import jax.numpy as jnp
from jax import lax
from jax.experimental import pallas as pl
from jax.experimental.pallas import tpu as pltpu
from jax.sharding import Mesh, PartitionSpec as P

HEAD = 96
CORES = 2
ROWS = 16
EXTRA = 16

eps = 1e-05
contrast_divisor_factor = 0.07
score_scale = 10.0
loss_scale = 4096.0
exact = lax.Precision.HIGHEST
f32 = jnp.float32
bf16 = jnp.bfloat16
i32 = jnp.int32
DP = ("chip", "core")


def contract(left, right, left_dim, right_dim, **kw):
    return lax.dot_general(
        left, right, (((left_dim,), (right_dim,)), ((), ())), preferred_element_type=f32, **kw
    )


def exchange(values, axis):
    return lax.all_to_all(values, axis, 0, 0, tiled=True)


def pick(values, index, axis):
    return lax.dynamic_index_in_dim(values, index, axis, keepdims=False)


def call(body, outs, *args, scalars=(), scratch=(), anchors=(), far=(), limit=16):
    count = len(scalars)
    skip = len(anchors)
    vmem = pl.BlockSpec(memory_space=pltpu.VMEM)
    away = pl.BlockSpec(memory_space=pltpu.HBM)

    def kernel(*refs):
        body(*refs[skip:])

    return pl.pallas_call(
        kernel if skip else body,
        out_shape=[jax.ShapeDtypeStruct(out[0], out[1]) for out in outs],
        in_specs=[pl.BlockSpec(memory_space=pl.ANY)] * skip
        + [pl.BlockSpec(memory_space=pltpu.SMEM)] * count
        + [away if index in far else vmem for index in range(len(args))],
        out_specs=[vmem if len(out) == 2 else away for out in outs],
        scratch_shapes=[
            pltpu.VMEM(*part) if isinstance(part, tuple) else pltpu.SemaphoreType.DMA((part,))
            for part in scratch
        ],
        compiler_params=pltpu.CompilerParams(vmem_limit_bytes=limit * 1024 * 1024),
    )(*anchors, *[jnp.reshape(s, (1,)).astype(i32) for s in scalars], *args)


def fetch(sources, targets, semaphores):
    copies = [
        pltpu.make_async_copy(source, target, semaphores.at[index])
        for index, (source, target) in enumerate(zip(sources, targets))
    ]
    for copy in copies:
        copy.start()
    return copies


def turn(count, step):
    return [(index, (index + step) % count) for index in range(count)]


def gather_ring(piece, count):
    found = [piece]
    back = ahead = piece
    for _ in range(count // 2 - 1):
        back = lax.ppermute(back, "mp", turn(count, 1))
        ahead = lax.ppermute(ahead, "mp", turn(count, count - 1))
        found += [back, ahead]
    half = (piece.shape[0] // 2 + ROWS - 1) // ROWS * ROWS
    found.append(lax.ppermute(back[:half], "mp", turn(count, 1)))
    found.append(lax.ppermute(ahead[half:], "mp", turn(count, count - 1)))
    return found


def place(refs, here, count, store):
    half = count // 2
    store(here, refs[0][...])
    for step in range(1, half):
        for ref, sign in ((refs[2 * step - 1], -1), (refs[2 * step], 1)):
            store(lax.rem(here + sign * step + count, count), ref[...])
    store(
        lax.rem(here + half, count), jnp.concatenate([refs[-2][...], refs[-1][...]], 0)
    )


def pack(square):
    half = square.shape[0] // 2
    side = square[:, 128:]
    return jnp.concatenate(
        [square[:, :128], jnp.concatenate([side[:half], side[half:]], 1)], 0
    )


def unpack(packed):
    rows = packed.shape[0] // 3 * 2
    side = packed[rows:]
    return jnp.concatenate(
        [packed[:rows], jnp.concatenate([side[:, :64], side[:, 64:]], 0)], 1
    )


def tile_forward(
    far_x, far_one, far_two, norm_ref, hidden_ref, slope_ref, out_ref, x_ref, one_ref, two_ref, sems
):
    copies = fetch((far_x, far_one, far_two), (x_ref, one_ref, two_ref), sems)
    copies[0].wait()
    x = x_ref[...].astype(f32)
    centred = x - jnp.mean(x, -1, keepdims=True)
    normed = centred * lax.rsqrt(jnp.mean(centred * centred, -1, keepdims=True) + eps)
    normed = normed.astype(bf16)
    norm_ref[...] = normed
    copies[1].wait()
    pre = jnp.dot(normed, one_ref[...], preferred_element_type=f32)
    bell = 0.5 * (1.0 + lax.erf(pre * 0.7071067811865476))
    hidden = (pre * bell).astype(bf16)
    hidden_ref[...] = hidden
    slope_ref[...] = bell + pre * jnp.exp(-0.5 * pre * pre) * 0.3989422804014327
    copies[2].wait()
    partial = jnp.dot(hidden, two_ref[...], preferred_element_type=f32).astype(bf16)
    count = out_ref.shape[0]
    block = partial.shape[1] // count
    for j in range(count):
        out_ref[j] = pack(partial[:, j * block : (j + 1) * block])


def tile_dispatch(own_ref, report_ref, dispatch_ref, flags_ref, parts_ref, out_ref):
    total = parts_ref[0].astype(f32)
    for j in range(1, parts_ref.shape[0]):
        total = total + parts_ref[j].astype(f32)
    embedding = (own_ref[...].astype(f32) + unpack(total)).astype(bf16)
    rows = jnp.dot(dispatch_ref[...], embedding, preferred_element_type=f32)
    slot = lax.broadcasted_iota(i32, rows.shape, 0)
    rows = jnp.where(lax.rem(slot, ROWS) == ROWS - 1, report_ref[...].astype(f32), rows)
    out_ref[...] = jnp.concatenate([rows.astype(bf16), flags_ref[...]], 1)


def slot_rows(arrived_ref, select_ref, report_select_ref, chunk_ref, valid_ref):
    arrived = arrived_ref[...]
    chunk = contract(arrived, select_ref[...], 0, 0)
    block = chunk_ref.shape[0] - EXTRA
    chunk_ref[0:block, :] = chunk[:block].astype(bf16)
    valid_ref[...] = chunk[block : block + 1]
    reports = jnp.dot(report_select_ref[...], arrived, preferred_element_type=f32)
    reports = reports[:, :block].astype(bf16)
    chunk_ref[block : block + EXTRA, :] = jnp.concatenate(
        [reports[:EXTRA], reports[EXTRA:]], 1
    )


def slide_forward(
    here,
    valid_ref,
    query_weights_ref,
    key_weights_ref,
    value_weights_ref,
    out_weights_ref,
    *rest,
):
    pieces = rest[:9]
    (
        far_norm,
        far_heads,
        far_attention,
        stat_ref,
        scale_ref,
        mass_ref,
        attended_ref,
        pooled_ref,
        reports_ref,
        slide_ref,
        norm_ref,
        heads_ref,
        attention_ref,
        sems,
    ) = rest[9:]
    count, owners, block = reports_ref.shape

    def store(index, piece):
        start = pl.multiple_of(index * block, 16)
        slide_ref[pl.ds(start, block), :] = piece[:block]
        reports = piece[block:]
        reports_ref[index] = jnp.concatenate([reports[:, :block], reports[:, block:]], 0)

    place(pieces, here[0], count, store)
    valid = valid_ref[...]
    valid_low = valid.astype(bf16)
    low = slide_ref[...]
    slide = low.astype(f32)
    mean = jnp.mean(slide, 0, keepdims=True)
    centred = slide - mean
    inverse = lax.rsqrt(jnp.mean(centred * centred, 0, keepdims=True) + eps)
    stat_ref[...] = jnp.concatenate([mean, inverse], 0)
    normed = (centred * inverse).astype(bf16)
    norm_ref[...] = normed
    copies = [pltpu.make_async_copy(norm_ref, far_norm, sems.at[0])]
    copies[0].start()
    all_query = jnp.dot(query_weights_ref[...], normed, preferred_element_type=f32)
    all_keys = jnp.dot(key_weights_ref[...], normed, preferred_element_type=f32)
    all_values = jnp.dot(value_weights_ref[...], normed, preferred_element_type=f32)
    heads = all_query.shape[0] // HEAD
    attended = []
    for h in range(heads):
        low_rows, high_rows = h * HEAD, (h + 1) * HEAD
        query = all_query[low_rows:high_rows]
        keys = all_keys[low_rows:high_rows]
        values = all_values[low_rows:high_rows]
        query_scale = lax.rsqrt(jnp.mean(query * query, 0, keepdims=True) + eps)
        key_scale = lax.rsqrt(jnp.mean(keys * keys, 0, keepdims=True) + eps)
        query_unit = query * query_scale
        key_unit = keys * key_scale
        heads_ref[h, 0] = query_unit
        heads_ref[h, 1] = key_unit
        heads_ref[h, 2] = values
        copies.append(pltpu.make_async_copy(heads_ref.at[h], far_heads.at[h], sems.at[1 + 2 * h]))
        copies[-1].start()
        scale_ref[h] = jnp.concatenate([query_scale, key_scale], 0)
        scores = contract(query_unit.astype(bf16), key_unit.astype(bf16), 0, 0)
        weights = jnp.exp(scores * (score_scale / HEAD)) * valid
        weights = weights * (1.0 / jnp.sum(weights, 1, keepdims=True))
        attention_ref[h] = weights
        copies.append(
            pltpu.make_async_copy(attention_ref.at[h], far_attention.at[h], sems.at[2 + 2 * h])
        )
        copies[-1].start()
        weights_low = weights.astype(bf16)
        mass_ref[h : h + 1, :] = jnp.dot(valid_low, weights_low, preferred_element_type=f32)
        attended.append(contract(values.astype(bf16), weights_low, 1, 1))
    attended = jnp.concatenate(attended, 0).astype(bf16)
    attended_sum = contract(valid_low, attended, 1, 1)
    attended_ref[...] = attended_sum
    high = attended_sum.astype(bf16)
    rest_low = (attended_sum - high.astype(f32)).astype(bf16)
    part = jnp.dot(high, out_weights_ref[...], preferred_element_type=f32)
    part = part + jnp.dot(rest_low, out_weights_ref[...], preferred_element_type=f32)
    slide_sum = contract(valid_low, low, 1, 1)
    pooled = (part + slide_sum * (1.0 / count)) / jnp.sum(valid)
    pooled_ref[...] = jnp.broadcast_to(pooled[None], pooled_ref.shape)
    for copy in copies:
        copy.wait()


def logits_row(parts_ref, reports_ref, unit_ref, report_ref, row_ref):
    pooled = jnp.sum(parts_ref[...], 0)
    inverse = lax.rsqrt(jnp.sum(pooled * pooled, -1, keepdims=True) + eps)
    unit = pooled * inverse
    unit_ref[...] = jnp.concatenate([unit, jnp.broadcast_to(inverse, unit.shape)], 0)
    count, owners, block = reports_ref.shape
    squares = jnp.zeros((owners, 1), f32)
    for j in range(count):
        reports = reports_ref[j].astype(f32)
        report_ref[:, j * block : (j + 1) * block] = reports
        squares = squares + jnp.sum(reports * reports, -1, keepdims=True)
    report = report_ref[...] * lax.rsqrt(squares + eps)
    report_ref[...] = report
    row = contract(unit, report, 1, 1, precision=exact) / contrast_divisor_factor
    pad = row_ref.shape[2] - row.shape[1]
    row = jnp.concatenate([row, jnp.zeros((1, pad), f32)], 1)
    row_ref[...] = jnp.broadcast_to(row[None], row_ref.shape)


def slide_backward(
    owner,
    logits_ref,
    pair_ref,
    unit_ref,
    report_ref,
    valid_ref,
    scale_ref,
    mass_ref,
    far_out_weights,
    far_heads,
    far_attention,
    far_query_weights,
    far_key_weights,
    far_value_weights,
    far_norm,
    loss_ref,
    grad_ref,
    up_ref,
    grads_ref,
    out_ref,
    *rest,
):
    fetched, sems = rest[:-1], rest[-1]
    (
        out_weights_ref,
        heads_ref,
        attention_ref,
        query_weights_ref,
        key_weights_ref,
        value_weights_ref,
        norm_ref,
    ) = fetched
    copies = fetch(
        (
            far_out_weights,
            far_heads,
            far_attention,
            far_query_weights,
            far_key_weights,
            far_value_weights,
            far_norm,
        ),
        fetched,
        sems,
    )
    owners = report_ref.shape[0]
    valid = valid_ref[...]
    logits = logits_ref[...]
    shape = logits.shape
    columns = lax.broadcasted_iota(i32, shape, 1)
    rows = lax.broadcasted_iota(i32, shape, 0)
    real = columns < owners
    expo = jnp.where(real, jnp.exp(logits), 0.0)
    row_total = jnp.sum(expo, 1, keepdims=True)
    column_total = jnp.where(real[:1], jnp.sum(expo, 0, keepdims=True), 1.0)
    target = jnp.where(pair_ref[...] == columns, 1.0, 0.0)
    loss = jnp.sum(
        0.5 * jnp.log(row_total) - jnp.sum(logits * target, 1, keepdims=True), 0, keepdims=True
    )
    loss = loss + 0.5 * jnp.sum(jnp.log(column_total), 1, keepdims=True)
    loss_ref[...] = loss * (1.0 / owners)
    grad_logits = (0.5 * expo / row_total + 0.5 * expo / column_total - target) * (
        loss_scale / owners
    )
    grad_row = jnp.sum(jnp.where(rows == owner[0], grad_logits, 0.0), 0, keepdims=True)
    grad_unit = (
        jnp.dot(grad_row[:, :owners], report_ref[...], precision=exact, preferred_element_type=f32)
        / contrast_divisor_factor
    )
    unit = unit_ref[0:1]
    inverse = unit_ref[1:2]
    grad_pooled = (grad_unit - unit * jnp.sum(unit * grad_unit, -1, keepdims=True)) * inverse
    grad = grad_pooled / jnp.sum(valid)
    grad_ref[...] = grad
    low = grad.astype(bf16)
    copies[0].wait()
    out_weights = out_weights_ref[...]
    up_ref[...] = contract(low, out_weights, 1, 1)
    up = jnp.sum(out_weights.astype(f32) * low.astype(f32), 1, keepdims=True)
    heads = heads_ref.shape[0]
    inner = heads * HEAD
    copies[1].wait()
    copies[2].wait()
    for h in range(heads):
        up_head = up[h * HEAD : (h + 1) * HEAD]
        values = heads_ref[h, 2]
        weights = attention_ref[h]
        pull = jnp.sum(up_head * values, 0, keepdims=True)
        pull_mean = jnp.sum(weights * pull, 1, keepdims=True)
        grad_scores = (weights * (pull - pull_mean) * (score_scale / HEAD)).astype(bf16)
        query_unit = heads_ref[h, 0]
        key_unit = heads_ref[h, 1]
        grad_query = contract(key_unit.astype(bf16), grad_scores, 1, 1) * valid
        grad_key = jnp.dot(query_unit.astype(bf16), grad_scores, preferred_element_type=f32)
        grad_query = scale_ref[h, 0:1] * (
            grad_query - query_unit * jnp.mean(query_unit * grad_query, 0, keepdims=True)
        )
        grad_key = scale_ref[h, 1:2] * (
            grad_key - key_unit * jnp.mean(key_unit * grad_key, 0, keepdims=True)
        )
        grad_value = up_head * mass_ref[h : h + 1]
        for part, values in enumerate((grad_query, grad_key, grad_value)):
            start = part * inner + h * HEAD
            grads_ref[start : start + HEAD, :] = values.astype(bf16)
    grad_query = grads_ref[0:inner, :]
    grad_key = grads_ref[inner : 2 * inner, :]
    grad_value = grads_ref[2 * inner : 3 * inner, :]
    for copy in copies[3:]:
        copy.wait()
    count = out_ref.shape[0]
    block = norm_ref.shape[0] // count
    first = jnp.zeros_like(valid)
    second = jnp.zeros_like(valid)
    for k in range(count):
        rows = slice(k * block, (k + 1) * block)
        part = jnp.dot(query_weights_ref[rows, :], grad_query, preferred_element_type=f32)
        part = part + jnp.dot(key_weights_ref[rows, :], grad_key, preferred_element_type=f32)
        part = part + jnp.dot(value_weights_ref[rows, :], grad_value, preferred_element_type=f32)
        out_ref[k, 0:block, :] = part.astype(bf16)
        first = first + jnp.sum(part, 0, keepdims=True)
        second = second + jnp.sum(part * norm_ref[rows, :].astype(f32), 0, keepdims=True)
    width = norm_ref.shape[0]
    stats = jnp.concatenate([first, second], 0) * (1.0 / width)
    high = stats.astype(bf16).astype(f32)
    stats = jnp.concatenate(
        [high, stats - high, jnp.zeros((EXTRA - 4, stats.shape[1]), f32)], 0
    ).astype(bf16)
    for k in range(count):
        out_ref[k, block : block + EXTRA, :] = stats


def wide_other(which, norm_ref, grads_ref, out_ref):
    chips, share, columns = out_ref.shape
    rows = [
        norm_ref[pl.ds(pl.multiple_of((CORES * chip + which[0]) * share, 16), share), :]
        for chip in range(chips)
    ]
    values = contract(jnp.concatenate(rows, 0), grads_ref[0:columns, :], 1, 1).astype(bf16)
    for chip in range(chips):
        out_ref[chip] = values[chip * share : (chip + 1) * share]


def wide_own(which, column, norm_ref, grads_ref, got_ref, *outs):
    side = len(outs)
    lines, share, columns = outs[0].shape
    chips = [
        line * side + lax.rem(column[0] + k, side) for k in range(side) for line in range(lines)
    ]
    rows = [
        norm_ref[pl.ds(pl.multiple_of((CORES * chip + which[0]) * share, 16), share), :]
        for chip in chips
    ]
    values = contract(jnp.concatenate(rows, 0), grads_ref[0:columns, :], 1, 1)
    for index, chip in enumerate(chips):
        part = values[index * share : (index + 1) * share] + got_ref[chip].astype(f32)
        outs[index // lines][index % lines] = part.astype(bf16)


def wide_line(line, *refs):
    side = len(refs) // 2
    for k in range(side):
        row = lax.rem(line[0] + k, side)
        total = refs[0][row].astype(f32)
        for ref in refs[1:side]:
            total = total + ref[row].astype(f32)
        refs[side + k][...] = total.astype(bf16)


def slot_grads(
    own_ref, valid_ref, stat_ref, chunk_ref, select_ref, extra_ref, parts_ref, out_ref
):
    total = parts_ref[0].astype(f32)
    for j in range(1, parts_ref.shape[0]):
        total = total + parts_ref[j].astype(f32)
    block = chunk_ref.shape[0] - EXTRA
    first = total[block : block + 1] + total[block + 2 : block + 3]
    second = total[block + 1 : block + 2] + total[block + 3 : block + 4]
    mean = stat_ref[0:1]
    inverse = stat_ref[1:2]
    normed = (chunk_ref[0:block, :].astype(f32) - mean) * inverse
    rows = own_ref[...] * valid_ref[...] + (total[:block] - first - normed * second) * inverse
    rows = contract(select_ref[...], rows.astype(bf16), 1, 1).astype(bf16)
    out_ref[...] = rows + extra_ref[...]


def tile_grads(back_ref, dispatch_ref, out_ref):
    piece = pack(contract(back_ref[...], dispatch_ref[...], 0, 0).astype(bf16))
    out_ref[...] = jnp.broadcast_to(piece[None], out_ref.shape)


def other_grads(
    other, two_ref, slope_ref, norm_ref, hidden_ref, parts_ref, grad_ref, hidden_grad_ref, out_ref
):
    count = parts_ref.shape[0]
    rows = grad_ref.shape[0] // count
    for j in range(count):
        grad_ref[j * rows : (j + 1) * rows, :] = unpack(parts_ref[j])
    grad_hidden = jnp.dot(two_ref[...], grad_ref[...], preferred_element_type=f32)
    hidden_grad_ref[...] = (grad_hidden * slope_ref[...]).astype(bf16)

    def store(rows, values):
        out_ref[rows] = values.astype(bf16)

    both_layers(other[0], norm_ref, hidden_ref, grad_ref, hidden_grad_ref, out_ref.shape, store)


def own_grads(
    own, norm_ref, hidden_ref, grad_ref, hidden_grad_ref, got_ref, far_out, out_ref, sems
):
    copies = []

    def store(rows, values):
        out_ref[rows] = (values + got_ref[rows].astype(f32)).astype(bf16)
        chip = rows[0]
        if rows[1].start:
            copies.append(
                pltpu.make_async_copy(out_ref.at[chip], far_out.at[chip], sems.at[chip])
            )
            copies[-1].start()

    both_layers(own[0], norm_ref, hidden_ref, grad_ref, hidden_grad_ref, out_ref.shape, store)
    for copy in copies:
        copy.wait()


def both_layers(which, norm_ref, hidden_ref, grad_ref, hidden_grad_ref, shape, store):
    chips, share = shape[0], shape[1] // 2
    rows = [
        grad_ref[pl.ds(pl.multiple_of((CORES * chip + which) * share, 16), share), :]
        for chip in range(chips)
    ]
    two = jnp.dot(jnp.concatenate(rows, 0), hidden_ref[...], preferred_element_type=f32)
    one = contract(norm_ref[...], hidden_grad_ref[...], 1, 1)
    for chip in range(chips):
        start = chip * share
        store((chip, slice(0, share)), one[start : start + share])
        store((chip, slice(share, 2 * share)), two[start : start + share])


def last_sums(values_ref, one_ref, two_ref):
    share = one_ref.shape[0]
    total = values_ref[0].astype(f32)
    for chip in range(1, values_ref.shape[0]):
        total = total + values_ref[chip].astype(f32)
    one_ref[...] = total[:share]
    two_ref[...] = total[share:]


def per_device(
    tile_features, tile_slide, slide_pair, reports, w_one, w_two, w_query, w_key, w_value, w_out
):
    chips = lax.axis_size("chip")
    owners = chips * CORES
    parts = lax.axis_size("mp")
    core = lax.axis_index("core")
    owner = lax.axis_index(DP)
    here = lax.axis_index("mp")
    tiles, width = tile_features.shape
    units = w_one.shape[1]
    capacity = 2 * tiles // owners
    length = owners * capacity
    slots = owners * ROWS
    block = width // parts
    share = width // owners
    inner = w_query.shape[1]
    heads = inner // HEAD
    packed = (block // 2 * 3, 128)

    def halves(values):
        rest = values.shape[1:]
        values = values.reshape((chips, CORES, share) + rest)
        own = pick(values, core, 1).reshape((chips * share,) + rest)
        other = pick(values, 1 - core, 1).reshape((chips * share,) + rest)
        return own, other

    tile_norm, hidden, slope, partial = call(
        tile_forward,
        [
            ((tiles, width), bf16),
            ((tiles, units), bf16),
            ((tiles, units), f32),
            ((parts,) + packed, bf16),
        ],
        tile_features,
        w_one,
        w_two,
        far=(0, 1, 2),
        scratch=[
            (tile_features.shape, bf16),
            (w_one.shape, bf16),
            (w_two.shape, bf16),
            3,
        ],
        limit=62,
    )
    partial = exchange(partial, "mp")

    slide_ids = tile_slide[:, 0]
    matches = (slide_ids[:, None] == jnp.arange(owners, dtype=i32)[None, :]).astype(i32)
    ordinal = jnp.sum(matches * (jnp.cumsum(matches, 0) - 1), 1)
    position = slide_ids * ROWS + ordinal
    dispatch = jnp.arange(slots, dtype=i32)[:, None] == position[None, :]
    flags = jnp.sum(dispatch.astype(f32), 1, keepdims=True).astype(bf16)
    flags = jnp.pad(flags, ((0, 0), (0, 256 - block - 1)))
    dispatch = dispatch.astype(bf16)
    slot = jnp.arange(slots, dtype=i32)
    row_of_slot = jnp.where(slot % ROWS < capacity, slot // ROWS * capacity + slot % ROWS, -1)
    select = (row_of_slot[:, None] == jnp.arange(length, dtype=i32)[None, :]).astype(bf16)
    last_slot = jnp.arange(owners, dtype=i32)[:, None] * ROWS + ROWS - 1
    report_select = (last_slot == slot[None, :]).astype(bf16)
    own_columns = pick(tile_features.reshape(tiles, parts, block), here, 1)
    own_report = pick(reports.reshape(1, parts, block), here, 1)
    tile_own, tile_other = halves(tile_norm.T)
    slope = slope.T

    (outgoing,) = call(
        tile_dispatch,
        [((slots, 256), bf16)],
        own_columns,
        own_report,
        dispatch,
        flags,
        partial,
        anchors=(select, report_select, tile_own, tile_other, slope),
    )
    arrived = exchange(outgoing.reshape(owners, ROWS, 256), DP).reshape(slots, 256)
    chunk, valid = call(
        slot_rows,
        [((block + EXTRA, length), bf16), ((1, length), f32)],
        arrived,
        select,
        report_select,
    )
    pieces = gather_ring(chunk, parts)

    (
        slide_norm,
        by_head,
        attention,
        stat,
        scales,
        mass,
        attended_sum,
        pooled,
        all_reports,
    ) = call(
        slide_forward,
        [
            ((width, length), bf16, "far"),
            ((heads, 3, HEAD, length), f32, "far"),
            ((heads, length, length), f32, "far"),
            ((2, length), f32),
            ((heads, 2, length), f32),
            ((heads, length), f32),
            ((1, inner), f32),
            ((parts, 1, width), f32),
            ((parts, owners, block), bf16),
        ],
        valid,
        w_query.T,
        w_key.T,
        w_value.T,
        w_out,
        *pieces,
        scalars=(here,),
        scratch=[
            ((width, length), bf16),
            ((width, length), bf16),
            ((heads, 3, HEAD, length), f32),
            ((heads, length, length), f32),
            1 + 2 * heads,
        ],
        limit=60,
    )
    pooled = exchange(pooled, "mp")
    unit, report_unit, row = call(
        logits_row,
        [((2, width), f32), ((owners, width), f32), ((owners, 1, 128), f32)],
        pooled,
        all_reports,
    )
    logits = exchange(row, DP).reshape(owners, 128)
    loss, grad, up, grads, sending = call(
        slide_backward,
        [((1, 1), f32), ((1, width), f32), ((1, inner), f32), ((3 * inner, length), bf16)]
        + [((parts, block + EXTRA, length), bf16)],
        logits,
        slide_pair[:, None],
        unit,
        report_unit,
        valid,
        scales,
        mass,
        w_out,
        by_head,
        attention,
        w_query,
        w_key,
        w_value,
        slide_norm,
        scalars=(owner,),
        far=tuple(range(7, 14)),
        scratch=[
            (w_out.shape, bf16),
            (by_head.shape, f32),
            (attention.shape, f32),
            (w_query.shape, bf16),
            (w_key.shape, bf16),
            (w_value.shape, bf16),
            (slide_norm.shape, bf16),
            7,
        ],
        limit=60,
    )
    received = exchange(sending, "mp")

    lines = math.isqrt(chips)
    side = chips // lines
    chip = lax.axis_index("chip")
    (wide_sent,) = call(
        wide_other,
        [((chips, share, 2 * inner), bf16)],
        slide_norm,
        grads,
        scalars=(1 - core,),
    )
    wide_got = lax.ppermute(wide_sent, "core", [(0, 1), (1, 0)])
    along = call(
        wide_own,
        [((lines, share, 2 * inner), bf16)] * side,
        slide_norm,
        grads,
        wide_got,
        scalars=(core, chip % side),
    )
    along = [along[0]] + [
        lax.ppermute(
            along[k], "chip", [(c, c // side * side + (c + k) % side) for c in range(chips)]
        )
        for k in range(1, side)
    ]
    across = call(
        wide_line, [((share, 2 * inner), bf16)] * lines, *along, scalars=(chip // side,)
    )
    across = [across[0]] + [
        lax.ppermute(across[k], "chip", [(c, (c + k * side) % chips) for c in range(chips)])
        for k in range(1, lines)
    ]
    grad_wide = sum(part.astype(f32) for part in across)
    value_rows = contract(mass.astype(bf16), slide_norm, 1, 1)
    extra = jnp.concatenate(
        [
            value_rows.reshape(heads, owners, share).transpose(1, 0, 2).reshape(owners, -1),
            grad.reshape(owners, share),
            jnp.broadcast_to(up, (owners, inner)),
            jnp.broadcast_to(attended_sum, (owners, inner)),
        ],
        1,
    ).astype(bf16)
    spare = ROWS - capacity
    extra = jnp.pad(extra, ((0, 0), (0, spare * block - extra.shape[1])))
    extra = extra.reshape(owners, spare, block)
    extra = jnp.pad(extra, ((0, 0), (capacity, 0), (0, 0))).reshape(slots, block)

    own_grad = lax.dynamic_slice_in_dim(grad, here * block, block, 1).reshape(block, 1)
    (going,) = call(
        slot_grads,
        [((slots, block), bf16)],
        own_grad,
        valid,
        stat,
        chunk,
        select,
        extra,
        received,
    )
    back = exchange(going.reshape(owners, ROWS, block), DP).reshape(slots, block)
    (spreading,) = call(tile_grads, [((parts,) + packed, bf16)], back, dispatch)

    size = (chips, 2 * share, units)
    grad_embedding, grad_hidden, sent = call(
        other_grads,
        [((width, tiles), bf16), ((units, tiles), bf16), (size, bf16)],
        w_two,
        slope,
        tile_other,
        hidden,
        exchange(spreading, "mp"),
        scalars=(1 - core,),
        anchors=(grad_wide,),
        limit=24,
    )
    got = lax.ppermute(sent, "core", [(0, 1), (1, 0)])
    (both,) = call(
        own_grads,
        [(size, bf16, "far")],
        tile_own,
        hidden,
        grad_embedding,
        grad_hidden,
        got,
        scalars=(core,),
        scratch=[(size, bf16), chips],
        limit=60,
    )
    grad_one, grad_two = call(
        last_sums, [((share, units), f32), ((share, units), f32)], exchange(both, "chip")
    )
    grad_two = grad_two.T

    terms = back.reshape(owners, ROWS, block)[:, capacity:].reshape(owners, -1).astype(f32)
    edge = heads * share
    from_values = terms[:, :edge].reshape(owners, heads, share)
    from_grads = terms[:, edge : edge + share]
    edge = edge + share
    from_up = terms[:, edge : edge + inner].reshape(owners, heads, HEAD)
    edge = edge + inner
    from_attended = terms[:, edge : edge + inner]
    grad_value = jnp.einsum("ohs,ohd->shd", from_values, from_up, precision=exact)
    grad_value = grad_value.reshape(share, inner)
    grad_out = contract(from_attended, from_grads, 0, 0, precision=exact)
    return (
        loss[0, 0],
        grad_one,
        grad_two,
        grad_wide[:, :inner],
        grad_wide[:, inner:],
        grad_value,
        grad_out,
    )


def solution(mesh):
    owners, parts = mesh.devices.shape
    split = Mesh(
        mesh.devices.reshape(owners // CORES, CORES, parts), ("chip", "core", "mp")
    )
    return jax.shard_map(
        per_device,
        mesh=split,
        in_specs=(
            P(DP, None),
            P(DP, None),
            P(),
            P(DP, None),
            P(None, "mp"),
            P("mp", None),
            P(None, "mp"),
            P(None, "mp"),
            P(None, "mp"),
            P("mp", None),
        ),
        out_specs=(
            P(),
            P(DP, "mp"),
            P("mp", DP),
            P(DP, "mp"),
            P(DP, "mp"),
            P(DP, "mp"),
            P("mp", DP),
        ),
        check_vma=False,
    )
```

```python
import math

import jax
import jax.numpy as jnp
from jax import lax
from jax.experimental import pallas as pl
from jax.experimental.pallas import tpu as pltpu
from jax.sharding import Mesh, PartitionSpec as P

HEAD = 96
CORES = 2
ROWS = 16
EXTRA = 16

eps = 1e-05
contrast_divisor_factor = 0.07
score_scale = 10.0
loss_scale = 4096.0
exact = lax.Precision.HIGHEST
f32 = jnp.float32
bf16 = jnp.bfloat16
i32 = jnp.int32
DP = ("chip", "core")


def contract(left, right, left_dim, right_dim, **kw):
    return lax.dot_general(
        left, right, (((left_dim,), (right_dim,)), ((), ())), preferred_element_type=f32, **kw
    )


def exchange(values, axis):
    return lax.all_to_all(values, axis, 0, 0, tiled=True)


def pick(values, index, axis):
    return lax.dynamic_index_in_dim(values, index, axis, keepdims=False)


def call(body, outs, *args, scalars=(), scratch=(), anchors=(), far=(), limit=16):
    count = len(scalars)
    skip = len(anchors)
    vmem = pl.BlockSpec(memory_space=pltpu.VMEM)
    away = pl.BlockSpec(memory_space=pltpu.HBM)

    def kernel(*refs):
        body(*refs[skip:])

    return pl.pallas_call(
        kernel if skip else body,
        out_shape=[jax.ShapeDtypeStruct(out[0], out[1]) for out in outs],
        in_specs=[pl.BlockSpec(memory_space=pl.ANY)] * skip
        + [pl.BlockSpec(memory_space=pltpu.SMEM)] * count
        + [away if index in far else vmem for index in range(len(args))],
        out_specs=[vmem if len(out) == 2 else away for out in outs],
        scratch_shapes=[
            pltpu.VMEM(*part) if isinstance(part, tuple) else pltpu.SemaphoreType.DMA((part,))
            for part in scratch
        ],
        compiler_params=pltpu.CompilerParams(vmem_limit_bytes=limit * 1024 * 1024),
    )(*anchors, *[jnp.reshape(s, (1,)).astype(i32) for s in scalars], *args)


def fetch(sources, targets, semaphores):
    copies = [
        pltpu.make_async_copy(source, target, semaphores.at[index])
        for index, (source, target) in enumerate(zip(sources, targets))
    ]
    for copy in copies:
        copy.start()
    return copies


def turn(count, step):
    return [(index, (index + step) % count) for index in range(count)]


def gather_ring(piece, count):
    found = [piece]
    back = ahead = piece
    for _ in range(count // 2 - 1):
        back = lax.ppermute(back, "mp", turn(count, 1))
        ahead = lax.ppermute(ahead, "mp", turn(count, count - 1))
        found += [back, ahead]
    half = (piece.shape[0] // 2 + ROWS - 1) // ROWS * ROWS
    found.append(lax.ppermute(back[:half], "mp", turn(count, 1)))
    found.append(lax.ppermute(ahead[half:], "mp", turn(count, count - 1)))
    return found


def place(refs, here, count, store):
    half = count // 2
    store(here, refs[0][...])
    for step in range(1, half):
        for ref, sign in ((refs[2 * step - 1], -1), (refs[2 * step], 1)):
            store(lax.rem(here + sign * step + count, count), ref[...])
    store(
        lax.rem(here + half, count), jnp.concatenate([refs[-2][...], refs[-1][...]], 0)
    )


def pack(square):
    half = square.shape[0] // 2
    side = square[:, 128:]
    return jnp.concatenate(
        [square[:, :128], jnp.concatenate([side[:half], side[half:]], 1)], 0
    )


def unpack(packed):
    rows = packed.shape[0] // 3 * 2
    side = packed[rows:]
    return jnp.concatenate(
        [packed[:rows], jnp.concatenate([side[:, :64], side[:, 64:]], 0)], 1
    )


def tile_forward(
    far_x, far_one, far_two, norm_ref, hidden_ref, slope_ref, out_ref, x_ref, one_ref, two_ref, sems
):
    copies = fetch((far_x, far_one, far_two), (x_ref, one_ref, two_ref), sems)
    copies[0].wait()
    x = x_ref[...].astype(f32)
    centred = x - jnp.mean(x, -1, keepdims=True)
    normed = centred * lax.rsqrt(jnp.mean(centred * centred, -1, keepdims=True) + eps)
    normed = normed.astype(bf16)
    norm_ref[...] = normed
    copies[1].wait()
    pre = jnp.dot(normed, one_ref[...], preferred_element_type=f32)
    bell = 0.5 * (1.0 + lax.erf(pre * 0.7071067811865476))
    hidden = (pre * bell).astype(bf16)
    hidden_ref[...] = hidden
    slope_ref[...] = bell + pre * jnp.exp(-0.5 * pre * pre) * 0.3989422804014327
    copies[2].wait()
    partial = jnp.dot(hidden, two_ref[...], preferred_element_type=f32).astype(bf16)
    count = out_ref.shape[0]
    block = partial.shape[1] // count
    for j in range(count):
        out_ref[j] = pack(partial[:, j * block : (j + 1) * block])


def tile_dispatch(own_ref, report_ref, dispatch_ref, flags_ref, parts_ref, out_ref):
    total = parts_ref[0].astype(f32)
    for j in range(1, parts_ref.shape[0]):
        total = total + parts_ref[j].astype(f32)
    embedding = (own_ref[...].astype(f32) + unpack(total)).astype(bf16)
    rows = jnp.dot(dispatch_ref[...], embedding, preferred_element_type=f32)
    slot = lax.broadcasted_iota(i32, rows.shape, 0)
    rows = jnp.where(lax.rem(slot, ROWS) == ROWS - 1, report_ref[...].astype(f32), rows)
    out_ref[...] = jnp.concatenate([rows.astype(bf16), flags_ref[...]], 1)


def slot_rows(arrived_ref, select_ref, report_select_ref, chunk_ref, valid_ref):
    arrived = arrived_ref[...]
    chunk = contract(arrived, select_ref[...], 0, 0)
    block = chunk_ref.shape[0] - EXTRA
    chunk_ref[0:block, :] = chunk[:block].astype(bf16)
    valid_ref[...] = chunk[block : block + 1]
    reports = jnp.dot(report_select_ref[...], arrived, preferred_element_type=f32)
    reports = reports[:, :block].astype(bf16)
    chunk_ref[block : block + EXTRA, :] = jnp.concatenate(
        [reports[:EXTRA], reports[EXTRA:]], 1
    )


def slide_forward(
    here,
    valid_ref,
    query_weights_ref,
    key_weights_ref,
    value_weights_ref,
    out_weights_ref,
    *rest,
):
    pieces = rest[:9]
    (
        far_norm,
        far_heads,
        far_attention,
        stat_ref,
        scale_ref,
        mass_ref,
        attended_ref,
        pooled_ref,
        reports_ref,
        slide_ref,
        norm_ref,
        heads_ref,
        attention_ref,
        sems,
    ) = rest[9:]
    count, owners, block = reports_ref.shape

    def store(index, piece):
        start = pl.multiple_of(index * block, 16)
        slide_ref[pl.ds(start, block), :] = piece[:block]
        reports = piece[block:]
        reports_ref[index] = jnp.concatenate([reports[:, :block], reports[:, block:]], 0)

    place(pieces, here[0], count, store)
    valid = valid_ref[...]
    valid_low = valid.astype(bf16)
    low = slide_ref[...]
    slide = low.astype(f32)
    mean = jnp.mean(slide, 0, keepdims=True)
    centred = slide - mean
    inverse = lax.rsqrt(jnp.mean(centred * centred, 0, keepdims=True) + eps)
    stat_ref[...] = jnp.concatenate([mean, inverse], 0)
    normed = (centred * inverse).astype(bf16)
    norm_ref[...] = normed
    copies = [pltpu.make_async_copy(norm_ref, far_norm, sems.at[0])]
    copies[0].start()
    all_query = jnp.dot(query_weights_ref[...], normed, preferred_element_type=f32)
    all_keys = jnp.dot(key_weights_ref[...], normed, preferred_element_type=f32)
    all_values = jnp.dot(value_weights_ref[...], normed, preferred_element_type=f32)
    heads = all_query.shape[0] // HEAD
    attended = []
    for h in range(heads):
        low_rows, high_rows = h * HEAD, (h + 1) * HEAD
        query = all_query[low_rows:high_rows]
        keys = all_keys[low_rows:high_rows]
        values = all_values[low_rows:high_rows]
        query_scale = lax.rsqrt(jnp.mean(query * query, 0, keepdims=True) + eps)
        key_scale = lax.rsqrt(jnp.mean(keys * keys, 0, keepdims=True) + eps)
        query_unit = query * query_scale
        key_unit = keys * key_scale
        heads_ref[h, 0] = query_unit
        heads_ref[h, 1] = key_unit
        heads_ref[h, 2] = values
        copies.append(pltpu.make_async_copy(heads_ref.at[h], far_heads.at[h], sems.at[1 + 2 * h]))
        copies[-1].start()
        scale_ref[h] = jnp.concatenate([query_scale, key_scale], 0)
        scores = contract(query_unit.astype(bf16), key_unit.astype(bf16), 0, 0)
        weights = jnp.exp(scores * (score_scale / HEAD)) * valid
        weights = weights * (1.0 / jnp.sum(weights, 1, keepdims=True))
        attention_ref[h] = weights
        copies.append(
            pltpu.make_async_copy(attention_ref.at[h], far_attention.at[h], sems.at[2 + 2 * h])
        )
        copies[-1].start()
        weights_low = weights.astype(bf16)
        mass_ref[h : h + 1, :] = jnp.dot(valid_low, weights_low, preferred_element_type=f32)
        attended.append(contract(values.astype(bf16), weights_low, 1, 1))
    attended = jnp.concatenate(attended, 0).astype(bf16)
    attended_sum = contract(valid_low, attended, 1, 1)
    attended_ref[...] = attended_sum
    high = attended_sum.astype(bf16)
    rest_low = (attended_sum - high.astype(f32)).astype(bf16)
    part = jnp.dot(high, out_weights_ref[...], preferred_element_type=f32)
    part = part + jnp.dot(rest_low, out_weights_ref[...], preferred_element_type=f32)
    slide_sum = contract(valid_low, low, 1, 1)
    pooled = (part + slide_sum * (1.0 / count)) / jnp.sum(valid)
    pooled_ref[...] = jnp.broadcast_to(pooled[None], pooled_ref.shape)
    for copy in copies:
        copy.wait()


def logits_row(parts_ref, reports_ref, unit_ref, report_ref, row_ref):
    pooled = jnp.sum(parts_ref[...], 0)
    inverse = lax.rsqrt(jnp.sum(pooled * pooled, -1, keepdims=True) + eps)
    unit = pooled * inverse
    unit_ref[...] = jnp.concatenate([unit, jnp.broadcast_to(inverse, unit.shape)], 0)
    count, owners, block = reports_ref.shape
    squares = jnp.zeros((owners, 1), f32)
    for j in range(count):
        reports = reports_ref[j].astype(f32)
        report_ref[:, j * block : (j + 1) * block] = reports
        squares = squares + jnp.sum(reports * reports, -1, keepdims=True)
    report = report_ref[...] * lax.rsqrt(squares + eps)
    report_ref[...] = report
    row = contract(unit, report, 1, 1, precision=exact) / contrast_divisor_factor
    pad = row_ref.shape[2] - row.shape[1]
    row = jnp.concatenate([row, jnp.zeros((1, pad), f32)], 1)
    row_ref[...] = jnp.broadcast_to(row[None], row_ref.shape)


def slide_backward(
    owner,
    logits_ref,
    pair_ref,
    unit_ref,
    report_ref,
    valid_ref,
    scale_ref,
    mass_ref,
    far_out_weights,
    far_heads,
    far_attention,
    far_query_weights,
    far_key_weights,
    far_value_weights,
    far_norm,
    loss_ref,
    grad_ref,
    up_ref,
    grads_ref,
    out_ref,
    *rest,
):
    fetched, sems = rest[:-1], rest[-1]
    (
        out_weights_ref,
        heads_ref,
        attention_ref,
        query_weights_ref,
        key_weights_ref,
        value_weights_ref,
        norm_ref,
    ) = fetched
    copies = fetch(
        (
            far_out_weights,
            far_heads,
            far_attention,
            far_query_weights,
            far_key_weights,
            far_value_weights,
            far_norm,
        ),
        fetched,
        sems,
    )
    owners = report_ref.shape[0]
    valid = valid_ref[...]
    logits = logits_ref[...]
    shape = logits.shape
    columns = lax.broadcasted_iota(i32, shape, 1)
    rows = lax.broadcasted_iota(i32, shape, 0)
    real = columns < owners
    expo = jnp.where(real, jnp.exp(logits), 0.0)
    row_total = jnp.sum(expo, 1, keepdims=True)
    column_total = jnp.where(real[:1], jnp.sum(expo, 0, keepdims=True), 1.0)
    target = jnp.where(pair_ref[...] == columns, 1.0, 0.0)
    loss = jnp.sum(
        0.5 * jnp.log(row_total) - jnp.sum(logits * target, 1, keepdims=True), 0, keepdims=True
    )
    loss = loss + 0.5 * jnp.sum(jnp.log(column_total), 1, keepdims=True)
    loss_ref[...] = loss * (1.0 / owners)
    grad_logits = (0.5 * expo / row_total + 0.5 * expo / column_total - target) * (
        loss_scale / owners
    )
    grad_row = jnp.sum(jnp.where(rows == owner[0], grad_logits, 0.0), 0, keepdims=True)
    grad_unit = (
        jnp.dot(grad_row[:, :owners], report_ref[...], precision=exact, preferred_element_type=f32)
        / contrast_divisor_factor
    )
    unit = unit_ref[0:1]
    inverse = unit_ref[1:2]
    grad_pooled = (grad_unit - unit * jnp.sum(unit * grad_unit, -1, keepdims=True)) * inverse
    grad = grad_pooled / jnp.sum(valid)
    grad_ref[...] = grad
    low = grad.astype(bf16)
    copies[0].wait()
    out_weights = out_weights_ref[...]
    up_ref[...] = contract(low, out_weights, 1, 1)
    up = jnp.sum(out_weights.astype(f32) * low.astype(f32), 1, keepdims=True)
    heads = heads_ref.shape[0]
    inner = heads * HEAD
    copies[1].wait()
    copies[2].wait()
    for h in range(heads):
        up_head = up[h * HEAD : (h + 1) * HEAD]
        values = heads_ref[h, 2]
        weights = attention_ref[h]
        pull = jnp.sum(up_head * values, 0, keepdims=True)
        pull_mean = jnp.sum(weights * pull, 1, keepdims=True)
        grad_scores = (weights * (pull - pull_mean) * (score_scale / HEAD)).astype(bf16)
        query_unit = heads_ref[h, 0]
        key_unit = heads_ref[h, 1]
        grad_query = contract(key_unit.astype(bf16), grad_scores, 1, 1) * valid
        grad_key = jnp.dot(query_unit.astype(bf16), grad_scores, preferred_element_type=f32)
        grad_query = scale_ref[h, 0:1] * (
            grad_query - query_unit * jnp.mean(query_unit * grad_query, 0, keepdims=True)
        )
        grad_key = scale_ref[h, 1:2] * (
            grad_key - key_unit * jnp.mean(key_unit * grad_key, 0, keepdims=True)
        )
        grad_value = up_head * mass_ref[h : h + 1]
        for part, values in enumerate((grad_query, grad_key, grad_value)):
            start = part * inner + h * HEAD
            grads_ref[start : start + HEAD, :] = values.astype(bf16)
    grad_query = grads_ref[0:inner, :]
    grad_key = grads_ref[inner : 2 * inner, :]
    grad_value = grads_ref[2 * inner : 3 * inner, :]
    for copy in copies[3:]:
        copy.wait()
    count = out_ref.shape[0]
    block = norm_ref.shape[0] // count
    first = jnp.zeros_like(valid)
    second = jnp.zeros_like(valid)
    for k in range(count):
        rows = slice(k * block, (k + 1) * block)
        part = jnp.dot(query_weights_ref[rows, :], grad_query, preferred_element_type=f32)
        part = part + jnp.dot(key_weights_ref[rows, :], grad_key, preferred_element_type=f32)
        part = part + jnp.dot(value_weights_ref[rows, :], grad_value, preferred_element_type=f32)
        out_ref[k, 0:block, :] = part.astype(bf16)
        first = first + jnp.sum(part, 0, keepdims=True)
        second = second + jnp.sum(part * norm_ref[rows, :].astype(f32), 0, keepdims=True)
    width = norm_ref.shape[0]
    stats = jnp.concatenate([first, second], 0) * (1.0 / width)
    high = stats.astype(bf16).astype(f32)
    stats = jnp.concatenate(
        [high, stats - high, jnp.zeros((EXTRA - 4, stats.shape[1]), f32)], 0
    ).astype(bf16)
    for k in range(count):
        out_ref[k, block : block + EXTRA, :] = stats


def wide_other(which, norm_ref, grads_ref, out_ref):
    chips, share, columns = out_ref.shape
    rows = [
        norm_ref[pl.ds(pl.multiple_of((CORES * chip + which[0]) * share, 16), share), :]
        for chip in range(chips)
    ]
    values = contract(jnp.concatenate(rows, 0), grads_ref[0:columns, :], 1, 1).astype(bf16)
    for chip in range(chips):
        out_ref[chip] = values[chip * share : (chip + 1) * share]


def wide_own(which, column, norm_ref, grads_ref, got_ref, *outs):
    side = len(outs)
    lines, share, columns = outs[0].shape
    chips = [
        line * side + lax.rem(column[0] + k, side) for k in range(side) for line in range(lines)
    ]
    rows = [
        norm_ref[pl.ds(pl.multiple_of((CORES * chip + which[0]) * share, 16), share), :]
        for chip in chips
    ]
    values = contract(jnp.concatenate(rows, 0), grads_ref[0:columns, :], 1, 1)
    for index, chip in enumerate(chips):
        part = values[index * share : (index + 1) * share] + got_ref[chip].astype(f32)
        outs[index // lines][index % lines] = part.astype(bf16)


def wide_line(line, *refs):
    side = len(refs) // 2
    for k in range(side):
        row = lax.rem(line[0] + k, side)
        total = refs[0][row].astype(f32)
        for ref in refs[1:side]:
            total = total + ref[row].astype(f32)
        refs[side + k][...] = total.astype(bf16)


def slot_grads(
    own_ref, valid_ref, stat_ref, chunk_ref, select_ref, extra_ref, parts_ref, out_ref
):
    total = parts_ref[0].astype(f32)
    for j in range(1, parts_ref.shape[0]):
        total = total + parts_ref[j].astype(f32)
    block = chunk_ref.shape[0] - EXTRA
    first = total[block : block + 1] + total[block + 2 : block + 3]
    second = total[block + 1 : block + 2] + total[block + 3 : block + 4]
    mean = stat_ref[0:1]
    inverse = stat_ref[1:2]
    normed = (chunk_ref[0:block, :].astype(f32) - mean) * inverse
    rows = own_ref[...] * valid_ref[...] + (total[:block] - first - normed * second) * inverse
    rows = contract(select_ref[...], rows.astype(bf16), 1, 1).astype(bf16)
    out_ref[...] = rows + extra_ref[...]


def tile_grads(back_ref, dispatch_ref, out_ref):
    piece = pack(contract(back_ref[...], dispatch_ref[...], 0, 0).astype(bf16))
    out_ref[...] = jnp.broadcast_to(piece[None], out_ref.shape)


def other_grads(
    other, two_ref, slope_ref, norm_ref, hidden_ref, parts_ref, grad_ref, hidden_grad_ref, out_ref
):
    count = parts_ref.shape[0]
    rows = grad_ref.shape[0] // count
    for j in range(count):
        grad_ref[j * rows : (j + 1) * rows, :] = unpack(parts_ref[j])
    grad_hidden = jnp.dot(two_ref[...], grad_ref[...], preferred_element_type=f32)
    hidden_grad_ref[...] = (grad_hidden * slope_ref[...]).astype(bf16)

    def store(rows, values):
        out_ref[rows] = values.astype(bf16)

    both_layers(other[0], norm_ref, hidden_ref, grad_ref, hidden_grad_ref, out_ref.shape, store)


def own_grads(own, norm_ref, hidden_ref, grad_ref, hidden_grad_ref, got_ref, out_ref):
    def store(rows, values):
        out_ref[rows] = (values + got_ref[rows].astype(f32)).astype(bf16)

    both_layers(own[0], norm_ref, hidden_ref, grad_ref, hidden_grad_ref, out_ref.shape, store)


def both_layers(which, norm_ref, hidden_ref, grad_ref, hidden_grad_ref, shape, store):
    chips, share = shape[0], shape[1] // 2
    rows = [
        grad_ref[pl.ds(pl.multiple_of((CORES * chip + which) * share, 16), share), :]
        for chip in range(chips)
    ]
    two = jnp.dot(jnp.concatenate(rows, 0), hidden_ref[...], preferred_element_type=f32)
    one = contract(norm_ref[...], hidden_grad_ref[...], 1, 1)
    for chip in range(chips):
        start = chip * share
        store((chip, slice(0, share)), one[start : start + share])
        store((chip, slice(share, 2 * share)), two[start : start + share])


def last_sums(values_ref, one_ref, two_ref):
    share = one_ref.shape[0]
    total = values_ref[0].astype(f32)
    for chip in range(1, values_ref.shape[0]):
        total = total + values_ref[chip].astype(f32)
    one_ref[...] = total[:share]
    two_ref[...] = total[share:]


def per_device(
    tile_features, tile_slide, slide_pair, reports, w_one, w_two, w_query, w_key, w_value, w_out
):
    chips = lax.axis_size("chip")
    owners = chips * CORES
    parts = lax.axis_size("mp")
    core = lax.axis_index("core")
    owner = lax.axis_index(DP)
    here = lax.axis_index("mp")
    tiles, width = tile_features.shape
    units = w_one.shape[1]
    capacity = 2 * tiles // owners
    length = owners * capacity
    slots = owners * ROWS
    block = width // parts
    share = width // owners
    inner = w_query.shape[1]
    heads = inner // HEAD
    packed = (block // 2 * 3, 128)

    def halves(values):
        rest = values.shape[1:]
        values = values.reshape((chips, CORES, share) + rest)
        own = pick(values, core, 1).reshape((chips * share,) + rest)
        other = pick(values, 1 - core, 1).reshape((chips * share,) + rest)
        return own, other

    tile_norm, hidden, slope, partial = call(
        tile_forward,
        [
            ((tiles, width), bf16),
            ((tiles, units), bf16),
            ((tiles, units), f32),
            ((parts,) + packed, bf16),
        ],
        tile_features,
        w_one,
        w_two,
        far=(0, 1, 2),
        scratch=[
            (tile_features.shape, bf16),
            (w_one.shape, bf16),
            (w_two.shape, bf16),
            3,
        ],
        limit=62,
    )
    partial = exchange(partial, "mp")

    slide_ids = tile_slide[:, 0]
    matches = (slide_ids[:, None] == jnp.arange(owners, dtype=i32)[None, :]).astype(i32)
    ordinal = jnp.sum(matches * (jnp.cumsum(matches, 0) - 1), 1)
    position = slide_ids * ROWS + ordinal
    dispatch = jnp.arange(slots, dtype=i32)[:, None] == position[None, :]
    flags = jnp.sum(dispatch.astype(f32), 1, keepdims=True).astype(bf16)
    flags = jnp.pad(flags, ((0, 0), (0, 256 - block - 1)))
    dispatch = dispatch.astype(bf16)
    slot = jnp.arange(slots, dtype=i32)
    row_of_slot = jnp.where(slot % ROWS < capacity, slot // ROWS * capacity + slot % ROWS, -1)
    select = (row_of_slot[:, None] == jnp.arange(length, dtype=i32)[None, :]).astype(bf16)
    last_slot = jnp.arange(owners, dtype=i32)[:, None] * ROWS + ROWS - 1
    report_select = (last_slot == slot[None, :]).astype(bf16)
    own_columns = pick(tile_features.reshape(tiles, parts, block), here, 1)
    own_report = pick(reports.reshape(1, parts, block), here, 1)
    tile_own, tile_other = halves(tile_norm.T)
    slope = slope.T

    (outgoing,) = call(
        tile_dispatch,
        [((slots, 256), bf16)],
        own_columns,
        own_report,
        dispatch,
        flags,
        partial,
        anchors=(select, report_select, tile_own, tile_other, slope),
    )
    arrived = exchange(outgoing.reshape(owners, ROWS, 256), DP).reshape(slots, 256)
    chunk, valid = call(
        slot_rows,
        [((block + EXTRA, length), bf16), ((1, length), f32)],
        arrived,
        select,
        report_select,
    )
    pieces = gather_ring(chunk, parts)

    (
        slide_norm,
        by_head,
        attention,
        stat,
        scales,
        mass,
        attended_sum,
        pooled,
        all_reports,
    ) = call(
        slide_forward,
        [
            ((width, length), bf16, "far"),
            ((heads, 3, HEAD, length), f32, "far"),
            ((heads, length, length), f32, "far"),
            ((2, length), f32),
            ((heads, 2, length), f32),
            ((heads, length), f32),
            ((1, inner), f32),
            ((parts, 1, width), f32),
            ((parts, owners, block), bf16),
        ],
        valid,
        w_query.T,
        w_key.T,
        w_value.T,
        w_out,
        *pieces,
        scalars=(here,),
        scratch=[
            ((width, length), bf16),
            ((width, length), bf16),
            ((heads, 3, HEAD, length), f32),
            ((heads, length, length), f32),
            1 + 2 * heads,
        ],
        limit=60,
    )
    pooled = exchange(pooled, "mp")
    unit, report_unit, row = call(
        logits_row,
        [((2, width), f32), ((owners, width), f32), ((owners, 1, 128), f32)],
        pooled,
        all_reports,
    )
    logits = exchange(row, DP).reshape(owners, 128)
    loss, grad, up, grads, sending = call(
        slide_backward,
        [((1, 1), f32), ((1, width), f32), ((1, inner), f32), ((3 * inner, length), bf16)]
        + [((parts, block + EXTRA, length), bf16)],
        logits,
        slide_pair[:, None],
        unit,
        report_unit,
        valid,
        scales,
        mass,
        w_out,
        by_head,
        attention,
        w_query,
        w_key,
        w_value,
        slide_norm,
        scalars=(owner,),
        far=tuple(range(7, 14)),
        scratch=[
            (w_out.shape, bf16),
            (by_head.shape, f32),
            (attention.shape, f32),
            (w_query.shape, bf16),
            (w_key.shape, bf16),
            (w_value.shape, bf16),
            (slide_norm.shape, bf16),
            7,
        ],
        limit=60,
    )
    received = exchange(sending, "mp")

    lines = math.isqrt(chips)
    side = chips // lines
    chip = lax.axis_index("chip")
    (wide_sent,) = call(
        wide_other,
        [((chips, share, 2 * inner), bf16)],
        slide_norm,
        grads,
        scalars=(1 - core,),
    )
    wide_got = lax.ppermute(wide_sent, "core", [(0, 1), (1, 0)])
    along = call(
        wide_own,
        [((lines, share, 2 * inner), bf16)] * side,
        slide_norm,
        grads,
        wide_got,
        scalars=(core, chip % side),
    )
    along = [along[0]] + [
        lax.ppermute(
            along[k], "chip", [(c, c // side * side + (c + k) % side) for c in range(chips)]
        )
        for k in range(1, side)
    ]
    across = call(
        wide_line, [((share, 2 * inner), bf16)] * lines, *along, scalars=(chip // side,)
    )
    across = [across[0]] + [
        lax.ppermute(across[k], "chip", [(c, (c + k * side) % chips) for c in range(chips)])
        for k in range(1, lines)
    ]
    grad_wide = sum(part.astype(f32) for part in across)
    value_rows = contract(mass.astype(bf16), slide_norm, 1, 1)
    extra = jnp.concatenate(
        [
            value_rows.reshape(heads, owners, share).transpose(1, 0, 2).reshape(owners, -1),
            grad.reshape(owners, share),
            jnp.broadcast_to(up, (owners, inner)),
            jnp.broadcast_to(attended_sum, (owners, inner)),
        ],
        1,
    ).astype(bf16)
    spare = ROWS - capacity
    extra = jnp.pad(extra, ((0, 0), (0, spare * block - extra.shape[1])))
    extra = extra.reshape(owners, spare, block)
    extra = jnp.pad(extra, ((0, 0), (capacity, 0), (0, 0))).reshape(slots, block)

    own_grad = lax.dynamic_slice_in_dim(grad, here * block, block, 1).reshape(block, 1)
    (going,) = call(
        slot_grads,
        [((slots, block), bf16)],
        own_grad,
        valid,
        stat,
        chunk,
        select,
        extra,
        received,
        anchors=(across[0],),
    )
    back = exchange(going.reshape(owners, ROWS, block), DP).reshape(slots, block)
    (spreading,) = call(tile_grads, [((parts,) + packed, bf16)], back, dispatch)

    size = (chips, 2 * share, units)
    grad_embedding, grad_hidden, sent = call(
        other_grads,
        [((width, tiles), bf16), ((units, tiles), bf16), (size, bf16)],
        w_two,
        slope,
        tile_other,
        hidden,
        exchange(spreading, "mp"),
        scalars=(1 - core,),
        limit=24,
    )
    got = lax.ppermute(sent, "core", [(0, 1), (1, 0)])
    (both,) = call(
        own_grads,
        [(size, bf16)],
        tile_own,
        hidden,
        grad_embedding,
        grad_hidden,
        got,
        scalars=(core,),
        limit=24,
    )
    grad_one, grad_two = call(
        last_sums, [((share, units), f32), ((share, units), f32)], exchange(both, "chip")
    )
    grad_two = grad_two.T

    terms = back.reshape(owners, ROWS, block)[:, capacity:].reshape(owners, -1).astype(f32)
    edge = heads * share
    from_values = terms[:, :edge].reshape(owners, heads, share)
    from_grads = terms[:, edge : edge + share]
    edge = edge + share
    from_up = terms[:, edge : edge + inner].reshape(owners, heads, HEAD)
    edge = edge + inner
    from_attended = terms[:, edge : edge + inner]
    grad_value = jnp.einsum("ohs,ohd->shd", from_values, from_up, precision=exact)
    grad_value = grad_value.reshape(share, inner)
    grad_out = contract(from_attended, from_grads, 0, 0, precision=exact)
    return (
        loss[0, 0],
        grad_one,
        grad_two,
        grad_wide[:, :inner],
        grad_wide[:, inner:],
        grad_value,
        grad_out,
    )


def solution(mesh):
    owners, parts = mesh.devices.shape
    split = Mesh(
        mesh.devices.reshape(owners // CORES, CORES, parts), ("chip", "core", "mp")
    )
    return jax.shard_map(
        per_device,
        mesh=split,
        in_specs=(
            P(DP, None),
            P(DP, None),
            P(),
            P(DP, None),
            P(None, "mp"),
            P("mp", None),
            P(None, "mp"),
            P(None, "mp"),
            P(None, "mp"),
            P("mp", None),
        ),
        out_specs=(
            P(),
            P(DP, "mp"),
            P("mp", DP),
            P(DP, "mp"),
            P(DP, "mp"),
            P(DP, "mp"),
            P("mp", DP),
        ),
        check_vma=False,
    )
```

```python
import math

import jax
import jax.numpy as jnp
from jax import lax
from jax.experimental import pallas as pl
from jax.experimental.pallas import tpu as pltpu
from jax.sharding import Mesh, PartitionSpec as P

HEAD = 96
CORES = 2
ROWS = 16
EXTRA = 16

eps = 1e-05
contrast_divisor_factor = 0.07
score_scale = 10.0
loss_scale = 4096.0
exact = lax.Precision.HIGHEST
f32 = jnp.float32
bf16 = jnp.bfloat16
i32 = jnp.int32
DP = ("chip", "core")


def contract(left, right, left_dim, right_dim, **kw):
    return lax.dot_general(
        left, right, (((left_dim,), (right_dim,)), ((), ())), preferred_element_type=f32, **kw
    )


def exchange(values, axis):
    return lax.all_to_all(values, axis, 0, 0, tiled=True)


def pick(values, index, axis):
    return lax.dynamic_index_in_dim(values, index, axis, keepdims=False)


def call(body, outs, *args, scalars=(), scratch=(), anchors=(), far=(), limit=16):
    count = len(scalars)
    skip = len(anchors)
    vmem = pl.BlockSpec(memory_space=pltpu.VMEM)
    away = pl.BlockSpec(memory_space=pltpu.HBM)

    def kernel(*refs):
        body(*refs[skip:])

    return pl.pallas_call(
        kernel if skip else body,
        out_shape=[jax.ShapeDtypeStruct(out[0], out[1]) for out in outs],
        in_specs=[pl.BlockSpec(memory_space=pl.ANY)] * skip
        + [pl.BlockSpec(memory_space=pltpu.SMEM)] * count
        + [away if index in far else vmem for index in range(len(args))],
        out_specs=[vmem if len(out) == 2 else away for out in outs],
        scratch_shapes=[
            pltpu.VMEM(*part) if isinstance(part, tuple) else pltpu.SemaphoreType.DMA((part,))
            for part in scratch
        ],
        compiler_params=pltpu.CompilerParams(vmem_limit_bytes=limit * 1024 * 1024),
    )(*anchors, *[jnp.reshape(s, (1,)).astype(i32) for s in scalars], *args)


def fetch(sources, targets, semaphores):
    copies = [
        pltpu.make_async_copy(source, target, semaphores.at[index])
        for index, (source, target) in enumerate(zip(sources, targets))
    ]
    for copy in copies:
        copy.start()
    return copies


def turn(count, step):
    return [(index, (index + step) % count) for index in range(count)]


def gather_ring(piece, count):
    found = [piece]
    back = ahead = piece
    for _ in range(count // 2 - 1):
        back = lax.ppermute(back, "mp", turn(count, 1))
        ahead = lax.ppermute(ahead, "mp", turn(count, count - 1))
        found += [back, ahead]
    half = (piece.shape[0] // 2 + ROWS - 1) // ROWS * ROWS
    found.append(lax.ppermute(back[:half], "mp", turn(count, 1)))
    found.append(lax.ppermute(ahead[half:], "mp", turn(count, count - 1)))
    return found


def place(refs, here, count, store):
    half = count // 2
    store(here, refs[0][...])
    for step in range(1, half):
        for ref, sign in ((refs[2 * step - 1], -1), (refs[2 * step], 1)):
            store(lax.rem(here + sign * step + count, count), ref[...])
    store(
        lax.rem(here + half, count), jnp.concatenate([refs[-2][...], refs[-1][...]], 0)
    )


def pack(square):
    half = square.shape[0] // 2
    side = square[:, 128:]
    return jnp.concatenate(
        [square[:, :128], jnp.concatenate([side[:half], side[half:]], 1)], 0
    )


def unpack(packed):
    rows = packed.shape[0] // 3 * 2
    side = packed[rows:]
    return jnp.concatenate(
        [packed[:rows], jnp.concatenate([side[:, :64], side[:, 64:]], 0)], 1
    )


def tile_forward(
    far_x, far_one, far_two, norm_ref, hidden_ref, slope_ref, out_ref, x_ref, one_ref, two_ref, sems
):
    copies = fetch((far_x, far_one, far_two), (x_ref, one_ref, two_ref), sems)
    copies[0].wait()
    x = x_ref[...].astype(f32)
    centred = x - jnp.mean(x, -1, keepdims=True)
    normed = centred * lax.rsqrt(jnp.mean(centred * centred, -1, keepdims=True) + eps)
    normed = normed.astype(bf16)
    norm_ref[...] = normed
    copies[1].wait()
    pre = jnp.dot(normed, one_ref[...], preferred_element_type=f32)
    bell = 0.5 * (1.0 + lax.erf(pre * 0.7071067811865476))
    hidden = (pre * bell).astype(bf16)
    hidden_ref[...] = hidden
    slope_ref[...] = bell + pre * jnp.exp(-0.5 * pre * pre) * 0.3989422804014327
    copies[2].wait()
    partial = jnp.dot(hidden, two_ref[...], preferred_element_type=f32).astype(bf16)
    count = out_ref.shape[0]
    block = partial.shape[1] // count
    for j in range(count):
        out_ref[j] = pack(partial[:, j * block : (j + 1) * block])


def tile_dispatch(own_ref, report_ref, dispatch_ref, flags_ref, parts_ref, out_ref):
    total = parts_ref[0].astype(f32)
    for j in range(1, parts_ref.shape[0]):
        total = total + parts_ref[j].astype(f32)
    embedding = (own_ref[...].astype(f32) + unpack(total)).astype(bf16)
    rows = jnp.dot(dispatch_ref[...], embedding, preferred_element_type=f32)
    slot = lax.broadcasted_iota(i32, rows.shape, 0)
    rows = jnp.where(lax.rem(slot, ROWS) == ROWS - 1, report_ref[...].astype(f32), rows)
    out_ref[...] = jnp.concatenate([rows.astype(bf16), flags_ref[...]], 1)


def slot_rows(arrived_ref, select_ref, report_select_ref, chunk_ref, valid_ref):
    arrived = arrived_ref[...]
    chunk = contract(arrived, select_ref[...], 0, 0)
    block = chunk_ref.shape[0] - EXTRA
    chunk_ref[0:block, :] = chunk[:block].astype(bf16)
    valid_ref[...] = chunk[block : block + 1]
    reports = jnp.dot(report_select_ref[...], arrived, preferred_element_type=f32)
    reports = reports[:, :block].astype(bf16)
    chunk_ref[block : block + EXTRA, :] = jnp.concatenate(
        [reports[:EXTRA], reports[EXTRA:]], 1
    )


def slide_forward(
    here,
    valid_ref,
    query_weights_ref,
    key_weights_ref,
    value_weights_ref,
    out_weights_ref,
    *rest,
):
    pieces = rest[:9]
    (
        far_norm,
        far_heads,
        far_attention,
        stat_ref,
        scale_ref,
        mass_ref,
        attended_ref,
        pooled_ref,
        reports_ref,
        slide_ref,
        norm_ref,
        heads_ref,
        attention_ref,
        sems,
    ) = rest[9:]
    count, owners, block = reports_ref.shape

    def store(index, piece):
        start = pl.multiple_of(index * block, 16)
        slide_ref[pl.ds(start, block), :] = piece[:block]
        reports = piece[block:]
        reports_ref[index] = jnp.concatenate([reports[:, :block], reports[:, block:]], 0)

    place(pieces, here[0], count, store)
    valid = valid_ref[...]
    valid_low = valid.astype(bf16)
    low = slide_ref[...]
    slide = low.astype(f32)
    mean = jnp.mean(slide, 0, keepdims=True)
    centred = slide - mean
    inverse = lax.rsqrt(jnp.mean(centred * centred, 0, keepdims=True) + eps)
    stat_ref[...] = jnp.concatenate([mean, inverse], 0)
    normed = (centred * inverse).astype(bf16)
    norm_ref[...] = normed
    copies = [pltpu.make_async_copy(norm_ref, far_norm, sems.at[0])]
    copies[0].start()
    all_query = jnp.dot(query_weights_ref[...], normed, preferred_element_type=f32)
    all_keys = jnp.dot(key_weights_ref[...], normed, preferred_element_type=f32)
    all_values = jnp.dot(value_weights_ref[...], normed, preferred_element_type=f32)
    heads = all_query.shape[0] // HEAD
    attended = []
    for h in range(heads):
        low_rows, high_rows = h * HEAD, (h + 1) * HEAD
        query = all_query[low_rows:high_rows]
        keys = all_keys[low_rows:high_rows]
        values = all_values[low_rows:high_rows]
        query_scale = lax.rsqrt(jnp.mean(query * query, 0, keepdims=True) + eps)
        key_scale = lax.rsqrt(jnp.mean(keys * keys, 0, keepdims=True) + eps)
        query_unit = query * query_scale
        key_unit = keys * key_scale
        heads_ref[h, 0] = query_unit
        heads_ref[h, 1] = key_unit
        heads_ref[h, 2] = values
        copies.append(pltpu.make_async_copy(heads_ref.at[h], far_heads.at[h], sems.at[1 + 2 * h]))
        copies[-1].start()
        scale_ref[h] = jnp.concatenate([query_scale, key_scale], 0)
        scores = contract(query_unit.astype(bf16), key_unit.astype(bf16), 0, 0)
        weights = jnp.exp(scores * (score_scale / HEAD)) * valid
        weights = weights * (1.0 / jnp.sum(weights, 1, keepdims=True))
        attention_ref[h] = weights
        copies.append(
            pltpu.make_async_copy(attention_ref.at[h], far_attention.at[h], sems.at[2 + 2 * h])
        )
        copies[-1].start()
        weights_low = weights.astype(bf16)
        mass_ref[h : h + 1, :] = jnp.dot(valid_low, weights_low, preferred_element_type=f32)
        attended.append(contract(values.astype(bf16), weights_low, 1, 1))
    attended = jnp.concatenate(attended, 0).astype(bf16)
    attended_sum = contract(valid_low, attended, 1, 1)
    attended_ref[...] = attended_sum
    high = attended_sum.astype(bf16)
    rest_low = (attended_sum - high.astype(f32)).astype(bf16)
    part = jnp.dot(high, out_weights_ref[...], preferred_element_type=f32)
    part = part + jnp.dot(rest_low, out_weights_ref[...], preferred_element_type=f32)
    slide_sum = contract(valid_low, low, 1, 1)
    pooled = (part + slide_sum * (1.0 / count)) / jnp.sum(valid)
    pooled_ref[...] = jnp.broadcast_to(pooled[None], pooled_ref.shape)
    for copy in copies:
        copy.wait()


def logits_row(parts_ref, reports_ref, unit_ref, report_ref, row_ref):
    pooled = jnp.sum(parts_ref[...], 0)
    inverse = lax.rsqrt(jnp.sum(pooled * pooled, -1, keepdims=True) + eps)
    unit = pooled * inverse
    unit_ref[...] = jnp.concatenate([unit, jnp.broadcast_to(inverse, unit.shape)], 0)
    count, owners, block = reports_ref.shape
    squares = jnp.zeros((owners, 1), f32)
    for j in range(count):
        reports = reports_ref[j].astype(f32)
        report_ref[:, j * block : (j + 1) * block] = reports
        squares = squares + jnp.sum(reports * reports, -1, keepdims=True)
    report = report_ref[...] * lax.rsqrt(squares + eps)
    report_ref[...] = report
    row = contract(unit, report, 1, 1, precision=exact) / contrast_divisor_factor
    pad = row_ref.shape[2] - row.shape[1]
    row = jnp.concatenate([row, jnp.zeros((1, pad), f32)], 1)
    row_ref[...] = jnp.broadcast_to(row[None], row_ref.shape)


def slide_backward(
    owner,
    logits_ref,
    pair_ref,
    unit_ref,
    report_ref,
    valid_ref,
    scale_ref,
    mass_ref,
    far_out_weights,
    far_heads,
    far_attention,
    far_query_weights,
    far_key_weights,
    far_value_weights,
    far_norm,
    loss_ref,
    grad_ref,
    up_ref,
    grads_ref,
    out_ref,
    *rest,
):
    fetched, sems = rest[:-1], rest[-1]
    (
        out_weights_ref,
        heads_ref,
        attention_ref,
        query_weights_ref,
        key_weights_ref,
        value_weights_ref,
        norm_ref,
    ) = fetched
    copies = fetch(
        (
            far_out_weights,
            far_heads,
            far_attention,
            far_query_weights,
            far_key_weights,
            far_value_weights,
            far_norm,
        ),
        fetched,
        sems,
    )
    owners = report_ref.shape[0]
    valid = valid_ref[...]
    logits = logits_ref[...]
    shape = logits.shape
    columns = lax.broadcasted_iota(i32, shape, 1)
    rows = lax.broadcasted_iota(i32, shape, 0)
    real = columns < owners
    expo = jnp.where(real, jnp.exp(logits), 0.0)
    row_total = jnp.sum(expo, 1, keepdims=True)
    column_total = jnp.where(real[:1], jnp.sum(expo, 0, keepdims=True), 1.0)
    target = jnp.where(pair_ref[...] == columns, 1.0, 0.0)
    loss = jnp.sum(
        0.5 * jnp.log(row_total) - jnp.sum(logits * target, 1, keepdims=True), 0, keepdims=True
    )
    loss = loss + 0.5 * jnp.sum(jnp.log(column_total), 1, keepdims=True)
    loss_ref[...] = loss * (1.0 / owners)
    grad_logits = (0.5 * expo / row_total + 0.5 * expo / column_total - target) * (
        loss_scale / owners
    )
    grad_row = jnp.sum(jnp.where(rows == owner[0], grad_logits, 0.0), 0, keepdims=True)
    grad_unit = (
        jnp.dot(grad_row[:, :owners], report_ref[...], precision=exact, preferred_element_type=f32)
        / contrast_divisor_factor
    )
    unit = unit_ref[0:1]
    inverse = unit_ref[1:2]
    grad_pooled = (grad_unit - unit * jnp.sum(unit * grad_unit, -1, keepdims=True)) * inverse
    grad = grad_pooled / jnp.sum(valid)
    grad_ref[...] = grad
    low = grad.astype(bf16)
    copies[0].wait()
    out_weights = out_weights_ref[...]
    up_ref[...] = contract(low, out_weights, 1, 1)
    up = jnp.sum(out_weights.astype(f32) * low.astype(f32), 1, keepdims=True)
    heads = heads_ref.shape[0]
    inner = heads * HEAD
    copies[1].wait()
    copies[2].wait()
    for h in range(heads):
        up_head = up[h * HEAD : (h + 1) * HEAD]
        values = heads_ref[h, 2]
        weights = attention_ref[h]
        pull = jnp.sum(up_head * values, 0, keepdims=True)
        pull_mean = jnp.sum(weights * pull, 1, keepdims=True)
        grad_scores = (weights * (pull - pull_mean) * (score_scale / HEAD)).astype(bf16)
        query_unit = heads_ref[h, 0]
        key_unit = heads_ref[h, 1]
        grad_query = contract(key_unit.astype(bf16), grad_scores, 1, 1) * valid
        grad_key = jnp.dot(query_unit.astype(bf16), grad_scores, preferred_element_type=f32)
        grad_query = scale_ref[h, 0:1] * (
            grad_query - query_unit * jnp.mean(query_unit * grad_query, 0, keepdims=True)
        )
        grad_key = scale_ref[h, 1:2] * (
            grad_key - key_unit * jnp.mean(key_unit * grad_key, 0, keepdims=True)
        )
        grad_value = up_head * mass_ref[h : h + 1]
        for part, values in enumerate((grad_query, grad_key, grad_value)):
            start = part * inner + h * HEAD
            grads_ref[start : start + HEAD, :] = values.astype(bf16)
    grad_query = grads_ref[0:inner, :]
    grad_key = grads_ref[inner : 2 * inner, :]
    grad_value = grads_ref[2 * inner : 3 * inner, :]
    for copy in copies[3:]:
        copy.wait()
    count = out_ref.shape[0]
    block = norm_ref.shape[0] // count
    first = jnp.zeros_like(valid)
    second = jnp.zeros_like(valid)
    for k in range(count):
        rows = slice(k * block, (k + 1) * block)
        part = jnp.dot(query_weights_ref[rows, :], grad_query, preferred_element_type=f32)
        part = part + jnp.dot(key_weights_ref[rows, :], grad_key, preferred_element_type=f32)
        part = part + jnp.dot(value_weights_ref[rows, :], grad_value, preferred_element_type=f32)
        out_ref[k, 0:block, :] = part.astype(bf16)
        first = first + jnp.sum(part, 0, keepdims=True)
        second = second + jnp.sum(part * norm_ref[rows, :].astype(f32), 0, keepdims=True)
    width = norm_ref.shape[0]
    stats = jnp.concatenate([first, second], 0) * (1.0 / width)
    high = stats.astype(bf16).astype(f32)
    stats = jnp.concatenate(
        [high, stats - high, jnp.zeros((EXTRA - 4, stats.shape[1]), f32)], 0
    ).astype(bf16)
    for k in range(count):
        out_ref[k, block : block + EXTRA, :] = stats


def wide_other(which, norm_ref, grads_ref, out_ref):
    chips, share, columns = out_ref.shape
    rows = [
        norm_ref[pl.ds(pl.multiple_of((CORES * chip + which[0]) * share, 16), share), :]
        for chip in range(chips)
    ]
    values = contract(jnp.concatenate(rows, 0), grads_ref[0:columns, :], 1, 1).astype(bf16)
    for chip in range(chips):
        out_ref[chip] = values[chip * share : (chip + 1) * share]


def wide_own(which, column, norm_ref, grads_ref, got_ref, *outs):
    side = len(outs)
    lines, share, columns = outs[0].shape
    chips = [
        line * side + lax.rem(column[0] + k, side) for k in range(side) for line in range(lines)
    ]
    rows = [
        norm_ref[pl.ds(pl.multiple_of((CORES * chip + which[0]) * share, 16), share), :]
        for chip in chips
    ]
    values = contract(jnp.concatenate(rows, 0), grads_ref[0:columns, :], 1, 1)
    for index, chip in enumerate(chips):
        part = values[index * share : (index + 1) * share] + got_ref[chip].astype(f32)
        outs[index // lines][index % lines] = part.astype(bf16)


def wide_line(line, *refs):
    side = len(refs) // 2
    for k in range(side):
        row = lax.rem(line[0] + k, side)
        total = refs[0][row].astype(f32)
        for ref in refs[1:side]:
            total = total + ref[row].astype(f32)
        refs[side + k][...] = total.astype(bf16)


def slot_grads(
    own_ref, valid_ref, stat_ref, chunk_ref, select_ref, extra_ref, parts_ref, out_ref
):
    total = parts_ref[0].astype(f32)
    for j in range(1, parts_ref.shape[0]):
        total = total + parts_ref[j].astype(f32)
    block = chunk_ref.shape[0] - EXTRA
    first = total[block : block + 1] + total[block + 2 : block + 3]
    second = total[block + 1 : block + 2] + total[block + 3 : block + 4]
    mean = stat_ref[0:1]
    inverse = stat_ref[1:2]
    normed = (chunk_ref[0:block, :].astype(f32) - mean) * inverse
    rows = own_ref[...] * valid_ref[...] + (total[:block] - first - normed * second) * inverse
    rows = contract(select_ref[...], rows.astype(bf16), 1, 1).astype(bf16)
    out_ref[...] = rows + extra_ref[...]


def tile_grads(back_ref, dispatch_ref, out_ref):
    piece = pack(contract(back_ref[...], dispatch_ref[...], 0, 0).astype(bf16))
    out_ref[...] = jnp.broadcast_to(piece[None], out_ref.shape)


def other_grads(
    other, two_ref, slope_ref, norm_ref, hidden_ref, parts_ref, grad_ref, hidden_grad_ref, out_ref
):
    count = parts_ref.shape[0]
    rows = grad_ref.shape[0] // count
    for j in range(count):
        grad_ref[j * rows : (j + 1) * rows, :] = unpack(parts_ref[j])
    grad_hidden = jnp.dot(two_ref[...], grad_ref[...], preferred_element_type=f32)
    hidden_grad_ref[...] = (grad_hidden * slope_ref[...]).astype(bf16)

    def store(rows, values):
        out_ref[rows] = values.astype(bf16)

    both_layers(other[0], norm_ref, hidden_ref, grad_ref, hidden_grad_ref, out_ref.shape, store)


def own_grads(
    own, line, column, norm_ref, hidden_ref, grad_ref, hidden_grad_ref, got_ref, *rest
):
    outs, both_ref = rest[:-1], rest[-1]
    side = len(outs) // 2
    lines, share = outs[0].shape[:2]

    def store(rows, values):
        both_ref[rows] = (values + got_ref[rows].astype(f32)).astype(bf16)

    both_layers(own[0], norm_ref, hidden_ref, grad_ref, hidden_grad_ref, both_ref.shape, store)
    for k in range(side):
        for index in range(lines):
            chip = index * side + lax.rem(column[0] + k, side)
            outs[k][index] = both_ref[chip, 0:share, :]
            chip = lax.rem(line[0] + k, lines) * side + index
            outs[side + k][index] = both_ref[chip, share : 2 * share, :]


def half_way(line, column, *refs):
    count = len(refs) // 2
    side = count // 2
    for k in range(side):
        for part, first in ((0, lax.rem(line[0] + k, side)), (side, lax.rem(column[0] + k, side))):
            total = refs[part][first].astype(f32)
            for ref in refs[part + 1 : part + side]:
                total = total + ref[first].astype(f32)
            refs[count + part + k][...] = total.astype(bf16)


def both_layers(which, norm_ref, hidden_ref, grad_ref, hidden_grad_ref, shape, store):
    chips, share = shape[0], shape[1] // 2
    rows = [
        grad_ref[pl.ds(pl.multiple_of((CORES * chip + which) * share, 16), share), :]
        for chip in range(chips)
    ]
    two = jnp.dot(jnp.concatenate(rows, 0), hidden_ref[...], preferred_element_type=f32)
    one = contract(norm_ref[...], hidden_grad_ref[...], 1, 1)
    for chip in range(chips):
        start = chip * share
        store((chip, slice(0, share)), one[start : start + share])
        store((chip, slice(share, 2 * share)), two[start : start + share])


def last_sums(*refs):
    side = len(refs) // 2 - 1
    for part in range(2):
        total = refs[part * side][...].astype(f32)
        for ref in refs[part * side + 1 : (part + 1) * side]:
            total = total + ref[...].astype(f32)
        refs[2 * side + part][...] = total


def per_device(
    tile_features, tile_slide, slide_pair, reports, w_one, w_two, w_query, w_key, w_value, w_out
):
    chips = lax.axis_size("chip")
    owners = chips * CORES
    parts = lax.axis_size("mp")
    core = lax.axis_index("core")
    owner = lax.axis_index(DP)
    here = lax.axis_index("mp")
    tiles, width = tile_features.shape
    units = w_one.shape[1]
    capacity = 2 * tiles // owners
    length = owners * capacity
    slots = owners * ROWS
    block = width // parts
    share = width // owners
    inner = w_query.shape[1]
    heads = inner // HEAD
    packed = (block // 2 * 3, 128)

    def halves(values):
        rest = values.shape[1:]
        values = values.reshape((chips, CORES, share) + rest)
        own = pick(values, core, 1).reshape((chips * share,) + rest)
        other = pick(values, 1 - core, 1).reshape((chips * share,) + rest)
        return own, other

    tile_norm, hidden, slope, partial = call(
        tile_forward,
        [
            ((tiles, width), bf16),
            ((tiles, units), bf16),
            ((tiles, units), f32),
            ((parts,) + packed, bf16),
        ],
        tile_features,
        w_one,
        w_two,
        far=(0, 1, 2),
        scratch=[
            (tile_features.shape, bf16),
            (w_one.shape, bf16),
            (w_two.shape, bf16),
            3,
        ],
        limit=62,
    )
    partial = exchange(partial, "mp")

    slide_ids = tile_slide[:, 0]
    matches = (slide_ids[:, None] == jnp.arange(owners, dtype=i32)[None, :]).astype(i32)
    ordinal = jnp.sum(matches * (jnp.cumsum(matches, 0) - 1), 1)
    position = slide_ids * ROWS + ordinal
    dispatch = jnp.arange(slots, dtype=i32)[:, None] == position[None, :]
    flags = jnp.sum(dispatch.astype(f32), 1, keepdims=True).astype(bf16)
    flags = jnp.pad(flags, ((0, 0), (0, 256 - block - 1)))
    dispatch = dispatch.astype(bf16)
    slot = jnp.arange(slots, dtype=i32)
    row_of_slot = jnp.where(slot % ROWS < capacity, slot // ROWS * capacity + slot % ROWS, -1)
    select = (row_of_slot[:, None] == jnp.arange(length, dtype=i32)[None, :]).astype(bf16)
    last_slot = jnp.arange(owners, dtype=i32)[:, None] * ROWS + ROWS - 1
    report_select = (last_slot == slot[None, :]).astype(bf16)
    own_columns = pick(tile_features.reshape(tiles, parts, block), here, 1)
    own_report = pick(reports.reshape(1, parts, block), here, 1)
    tile_own, tile_other = halves(tile_norm.T)
    slope = slope.T

    (outgoing,) = call(
        tile_dispatch,
        [((slots, 256), bf16)],
        own_columns,
        own_report,
        dispatch,
        flags,
        partial,
        anchors=(select, report_select, tile_own, tile_other, slope),
    )
    arrived = exchange(outgoing.reshape(owners, ROWS, 256), DP).reshape(slots, 256)
    chunk, valid = call(
        slot_rows,
        [((block + EXTRA, length), bf16), ((1, length), f32)],
        arrived,
        select,
        report_select,
    )
    pieces = gather_ring(chunk, parts)

    (
        slide_norm,
        by_head,
        attention,
        stat,
        scales,
        mass,
        attended_sum,
        pooled,
        all_reports,
    ) = call(
        slide_forward,
        [
            ((width, length), bf16, "far"),
            ((heads, 3, HEAD, length), f32, "far"),
            ((heads, length, length), f32, "far"),
            ((2, length), f32),
            ((heads, 2, length), f32),
            ((heads, length), f32),
            ((1, inner), f32),
            ((parts, 1, width), f32),
            ((parts, owners, block), bf16),
        ],
        valid,
        w_query.T,
        w_key.T,
        w_value.T,
        w_out,
        *pieces,
        scalars=(here,),
        scratch=[
            ((width, length), bf16),
            ((width, length), bf16),
            ((heads, 3, HEAD, length), f32),
            ((heads, length, length), f32),
            1 + 2 * heads,
        ],
        limit=60,
    )
    pooled = exchange(pooled, "mp")
    unit, report_unit, row = call(
        logits_row,
        [((2, width), f32), ((owners, width), f32), ((owners, 1, 128), f32)],
        pooled,
        all_reports,
    )
    logits = exchange(row, DP).reshape(owners, 128)
    loss, grad, up, grads, sending = call(
        slide_backward,
        [((1, 1), f32), ((1, width), f32), ((1, inner), f32), ((3 * inner, length), bf16)]
        + [((parts, block + EXTRA, length), bf16)],
        logits,
        slide_pair[:, None],
        unit,
        report_unit,
        valid,
        scales,
        mass,
        w_out,
        by_head,
        attention,
        w_query,
        w_key,
        w_value,
        slide_norm,
        scalars=(owner,),
        far=tuple(range(7, 14)),
        scratch=[
            (w_out.shape, bf16),
            (by_head.shape, f32),
            (attention.shape, f32),
            (w_query.shape, bf16),
            (w_key.shape, bf16),
            (w_value.shape, bf16),
            (slide_norm.shape, bf16),
            7,
        ],
        limit=60,
    )
    received = exchange(sending, "mp")

    side = math.isqrt(chips)
    lines = side
    chip = lax.axis_index("chip")
    (wide_sent,) = call(
        wide_other,
        [((chips, share, 2 * inner), bf16)],
        slide_norm,
        grads,
        scalars=(1 - core,),
    )
    wide_got = lax.ppermute(wide_sent, "core", [(0, 1), (1, 0)])
    along = call(
        wide_own,
        [((lines, share, 2 * inner), bf16)] * side,
        slide_norm,
        grads,
        wide_got,
        scalars=(core, chip % side),
    )
    def shift_columns(values):
        return [values[0]] + [
            lax.ppermute(
                values[k], "chip", [(c, c // side * side + (c + k) % side) for c in range(chips)]
            )
            for k in range(1, side)
        ]

    def shift_lines(values):
        return [values[0]] + [
            lax.ppermute(values[k], "chip", [(c, (c + k * side) % chips) for c in range(chips)])
            for k in range(1, lines)
        ]

    along = shift_columns(along)
    across = call(
        wide_line, [((share, 2 * inner), bf16)] * lines, *along, scalars=(chip // side,)
    )
    across = shift_lines(across)
    grad_wide = sum(part.astype(f32) for part in across)
    value_rows = contract(mass.astype(bf16), slide_norm, 1, 1)
    extra = jnp.concatenate(
        [
            value_rows.reshape(heads, owners, share).transpose(1, 0, 2).reshape(owners, -1),
            grad.reshape(owners, share),
            jnp.broadcast_to(up, (owners, inner)),
            jnp.broadcast_to(attended_sum, (owners, inner)),
        ],
        1,
    ).astype(bf16)
    spare = ROWS - capacity
    extra = jnp.pad(extra, ((0, 0), (0, spare * block - extra.shape[1])))
    extra = extra.reshape(owners, spare, block)
    extra = jnp.pad(extra, ((0, 0), (capacity, 0), (0, 0))).reshape(slots, block)

    own_grad = lax.dynamic_slice_in_dim(grad, here * block, block, 1).reshape(block, 1)
    (going,) = call(
        slot_grads,
        [((slots, block), bf16)],
        own_grad,
        valid,
        stat,
        chunk,
        select,
        extra,
        received,
        anchors=(grad_wide,),
    )
    back = exchange(going.reshape(owners, ROWS, block), DP).reshape(slots, block)
    (spreading,) = call(tile_grads, [((parts,) + packed, bf16)], back, dispatch)

    size = (chips, 2 * share, units)
    grad_embedding, grad_hidden, sent = call(
        other_grads,
        [((width, tiles), bf16), ((units, tiles), bf16), (size, bf16)],
        w_two,
        slope,
        tile_other,
        hidden,
        exchange(spreading, "mp"),
        scalars=(1 - core,),
        limit=24,
    )
    got = lax.ppermute(sent, "core", [(0, 1), (1, 0)])
    both = call(
        own_grads,
        [((lines, share, units), bf16)] * (2 * side),
        tile_own,
        hidden,
        grad_embedding,
        grad_hidden,
        got,
        scalars=(core, chip // side, chip % side),
        scratch=[(size, bf16)],
        limit=24,
    )
    both = call(
        half_way,
        [((share, units), bf16)] * (2 * side),
        *shift_columns(both[:side]),
        *shift_lines(both[side:]),
        scalars=(chip // side, chip % side),
    )
    grad_one, grad_two = call(
        last_sums,
        [((share, units), f32)] * 2,
        *shift_lines(both[:side]),
        *shift_columns(both[side:]),
    )
    grad_two = grad_two.T

    terms = back.reshape(owners, ROWS, block)[:, capacity:].reshape(owners, -1).astype(f32)
    edge = heads * share
    from_values = terms[:, :edge].reshape(owners, heads, share)
    from_grads = terms[:, edge : edge + share]
    edge = edge + share
    from_up = terms[:, edge : edge + inner].reshape(owners, heads, HEAD)
    edge = edge + inner
    from_attended = terms[:, edge : edge + inner]
    grad_value = jnp.einsum("ohs,ohd->shd", from_values, from_up, precision=exact)
    grad_value = grad_value.reshape(share, inner)
    grad_out = contract(from_attended, from_grads, 0, 0, precision=exact)
    return (
        loss[0, 0],
        grad_one,
        grad_two,
        grad_wide[:, :inner],
        grad_wide[:, inner:],
        grad_value,
        grad_out,
    )


def solution(mesh):
    owners, parts = mesh.devices.shape
    split = Mesh(
        mesh.devices.reshape(owners // CORES, CORES, parts), ("chip", "core", "mp")
    )
    return jax.shard_map(
        per_device,
        mesh=split,
        in_specs=(
            P(DP, None),
            P(DP, None),
            P(),
            P(DP, None),
            P(None, "mp"),
            P("mp", None),
            P(None, "mp"),
            P(None, "mp"),
            P(None, "mp"),
            P("mp", None),
        ),
        out_specs=(
            P(),
            P(DP, "mp"),
            P("mp", DP),
            P(DP, "mp"),
            P(DP, "mp"),
            P(DP, "mp"),
            P("mp", DP),
        ),
        check_vma=False,
    )
```

```python
import math

import jax
import jax.numpy as jnp
from jax import lax
from jax.experimental import pallas as pl
from jax.experimental.pallas import tpu as pltpu
from jax.sharding import Mesh, PartitionSpec as P

HEAD = 96
CORES = 2
ROWS = 16
EXTRA = 16

eps = 1e-05
contrast_divisor_factor = 0.07
score_scale = 10.0
loss_scale = 4096.0
exact = lax.Precision.HIGHEST
f32 = jnp.float32
bf16 = jnp.bfloat16
i32 = jnp.int32
DP = ("line", "column", "core")


def contract(left, right, left_dim, right_dim, **kw):
    return lax.dot_general(
        left, right, (((left_dim,), (right_dim,)), ((), ())), preferred_element_type=f32, **kw
    )


def exchange(values, axis):
    return lax.all_to_all(values, axis, 0, 0, tiled=True)


def pick(values, index, axis):
    return lax.dynamic_index_in_dim(values, index, axis, keepdims=False)


def call(body, outs, *args, scalars=(), scratch=(), anchors=(), far=(), limit=16):
    count = len(scalars)
    skip = len(anchors)
    vmem = pl.BlockSpec(memory_space=pltpu.VMEM)
    away = pl.BlockSpec(memory_space=pltpu.HBM)

    def kernel(*refs):
        body(*refs[skip:])

    return pl.pallas_call(
        kernel if skip else body,
        out_shape=[jax.ShapeDtypeStruct(out[0], out[1]) for out in outs],
        in_specs=[pl.BlockSpec(memory_space=pl.ANY)] * skip
        + [pl.BlockSpec(memory_space=pltpu.SMEM)] * count
        + [away if index in far else vmem for index in range(len(args))],
        out_specs=[vmem if len(out) == 2 else away for out in outs],
        scratch_shapes=[
            pltpu.VMEM(*part) if isinstance(part, tuple) else pltpu.SemaphoreType.DMA((part,))
            for part in scratch
        ],
        compiler_params=pltpu.CompilerParams(vmem_limit_bytes=limit * 1024 * 1024),
    )(*anchors, *[jnp.reshape(s, (1,)).astype(i32) for s in scalars], *args)


def fetch(sources, targets, semaphores):
    copies = [
        pltpu.make_async_copy(source, target, semaphores.at[index])
        for index, (source, target) in enumerate(zip(sources, targets))
    ]
    for copy in copies:
        copy.start()
    return copies


def turn(count, step):
    return [(index, (index + step) % count) for index in range(count)]


def gather_ring(piece, count):
    found = [piece]
    back = ahead = piece
    for _ in range(count // 2 - 1):
        back = lax.ppermute(back, "mp", turn(count, 1))
        ahead = lax.ppermute(ahead, "mp", turn(count, count - 1))
        found += [back, ahead]
    half = (piece.shape[0] // 2 + ROWS - 1) // ROWS * ROWS
    found.append(lax.ppermute(back[:half], "mp", turn(count, 1)))
    found.append(lax.ppermute(ahead[half:], "mp", turn(count, count - 1)))
    return found


def place(refs, here, count, store):
    half = count // 2
    store(here, refs[0][...])
    for step in range(1, half):
        for ref, sign in ((refs[2 * step - 1], -1), (refs[2 * step], 1)):
            store(lax.rem(here + sign * step + count, count), ref[...])
    store(
        lax.rem(here + half, count), jnp.concatenate([refs[-2][...], refs[-1][...]], 0)
    )


def pack(square):
    half = square.shape[0] // 2
    side = square[:, 128:]
    return jnp.concatenate(
        [square[:, :128], jnp.concatenate([side[:half], side[half:]], 1)], 0
    )


def unpack(packed):
    rows = packed.shape[0] // 3 * 2
    side = packed[rows:]
    return jnp.concatenate(
        [packed[:rows], jnp.concatenate([side[:, :64], side[:, 64:]], 0)], 1
    )


def tile_forward(
    far_x, far_one, far_two, norm_ref, hidden_ref, slope_ref, out_ref, x_ref, one_ref, two_ref, sems
):
    copies = fetch((far_x, far_one, far_two), (x_ref, one_ref, two_ref), sems)
    copies[0].wait()
    x = x_ref[...].astype(f32)
    centred = x - jnp.mean(x, -1, keepdims=True)
    normed = centred * lax.rsqrt(jnp.mean(centred * centred, -1, keepdims=True) + eps)
    normed = normed.astype(bf16)
    norm_ref[...] = normed
    copies[1].wait()
    pre = jnp.dot(normed, one_ref[...], preferred_element_type=f32)
    bell = 0.5 * (1.0 + lax.erf(pre * 0.7071067811865476))
    hidden = (pre * bell).astype(bf16)
    hidden_ref[...] = hidden
    slope_ref[...] = bell + pre * jnp.exp(-0.5 * pre * pre) * 0.3989422804014327
    copies[2].wait()
    partial = jnp.dot(hidden, two_ref[...], preferred_element_type=f32).astype(bf16)
    count = out_ref.shape[0]
    block = partial.shape[1] // count
    for j in range(count):
        out_ref[j] = pack(partial[:, j * block : (j + 1) * block])


def tile_dispatch(own_ref, report_ref, dispatch_ref, flags_ref, parts_ref, out_ref):
    total = parts_ref[0].astype(f32)
    for j in range(1, parts_ref.shape[0]):
        total = total + parts_ref[j].astype(f32)
    embedding = (own_ref[...].astype(f32) + unpack(total)).astype(bf16)
    rows = jnp.dot(dispatch_ref[...], embedding, preferred_element_type=f32)
    slot = lax.broadcasted_iota(i32, rows.shape, 0)
    rows = jnp.where(lax.rem(slot, ROWS) == ROWS - 1, report_ref[...].astype(f32), rows)
    out_ref[...] = jnp.concatenate([rows.astype(bf16), flags_ref[...]], 1)


def slot_rows(arrived_ref, select_ref, report_select_ref, chunk_ref, valid_ref):
    arrived = arrived_ref[...]
    chunk = contract(arrived, select_ref[...], 0, 0)
    block = chunk_ref.shape[0] - EXTRA
    chunk_ref[0:block, :] = chunk[:block].astype(bf16)
    valid_ref[...] = chunk[block : block + 1]
    reports = jnp.dot(report_select_ref[...], arrived, preferred_element_type=f32)
    reports = reports[:, :block].astype(bf16)
    chunk_ref[block : block + EXTRA, :] = jnp.concatenate(
        [reports[:EXTRA], reports[EXTRA:]], 1
    )


def slide_forward(
    here,
    valid_ref,
    query_weights_ref,
    key_weights_ref,
    value_weights_ref,
    out_weights_ref,
    *rest,
):
    pieces = rest[:9]
    (
        far_norm,
        far_heads,
        far_attention,
        stat_ref,
        scale_ref,
        mass_ref,
        attended_ref,
        pooled_ref,
        reports_ref,
        slide_ref,
        norm_ref,
        heads_ref,
        attention_ref,
        sems,
    ) = rest[9:]
    count, owners, block = reports_ref.shape

    def store(index, piece):
        start = pl.multiple_of(index * block, 16)
        slide_ref[pl.ds(start, block), :] = piece[:block]
        reports = piece[block:]
        reports_ref[index] = jnp.concatenate([reports[:, :block], reports[:, block:]], 0)

    place(pieces, here[0], count, store)
    valid = valid_ref[...]
    valid_low = valid.astype(bf16)
    low = slide_ref[...]
    slide = low.astype(f32)
    mean = jnp.mean(slide, 0, keepdims=True)
    centred = slide - mean
    inverse = lax.rsqrt(jnp.mean(centred * centred, 0, keepdims=True) + eps)
    stat_ref[...] = jnp.concatenate([mean, inverse], 0)
    normed = (centred * inverse).astype(bf16)
    norm_ref[...] = normed
    copies = [pltpu.make_async_copy(norm_ref, far_norm, sems.at[0])]
    copies[0].start()
    all_query = jnp.dot(query_weights_ref[...], normed, preferred_element_type=f32)
    all_keys = jnp.dot(key_weights_ref[...], normed, preferred_element_type=f32)
    all_values = jnp.dot(value_weights_ref[...], normed, preferred_element_type=f32)
    heads = all_query.shape[0] // HEAD
    attended = []
    for h in range(heads):
        low_rows, high_rows = h * HEAD, (h + 1) * HEAD
        query = all_query[low_rows:high_rows]
        keys = all_keys[low_rows:high_rows]
        values = all_values[low_rows:high_rows]
        query_scale = lax.rsqrt(jnp.mean(query * query, 0, keepdims=True) + eps)
        key_scale = lax.rsqrt(jnp.mean(keys * keys, 0, keepdims=True) + eps)
        query_unit = query * query_scale
        key_unit = keys * key_scale
        heads_ref[h, 0] = query_unit
        heads_ref[h, 1] = key_unit
        heads_ref[h, 2] = values
        copies.append(pltpu.make_async_copy(heads_ref.at[h], far_heads.at[h], sems.at[1 + 2 * h]))
        copies[-1].start()
        scale_ref[h] = jnp.concatenate([query_scale, key_scale], 0)
        scores = contract(query_unit.astype(bf16), key_unit.astype(bf16), 0, 0)
        weights = jnp.exp(scores * (score_scale / HEAD)) * valid
        weights = weights * (1.0 / jnp.sum(weights, 1, keepdims=True))
        attention_ref[h] = weights
        copies.append(
            pltpu.make_async_copy(attention_ref.at[h], far_attention.at[h], sems.at[2 + 2 * h])
        )
        copies[-1].start()
        weights_low = weights.astype(bf16)
        mass_ref[h : h + 1, :] = jnp.dot(valid_low, weights_low, preferred_element_type=f32)
        attended.append(contract(values.astype(bf16), weights_low, 1, 1))
    attended = jnp.concatenate(attended, 0).astype(bf16)
    attended_sum = contract(valid_low, attended, 1, 1)
    attended_ref[...] = attended_sum
    high = attended_sum.astype(bf16)
    rest_low = (attended_sum - high.astype(f32)).astype(bf16)
    part = jnp.dot(high, out_weights_ref[...], preferred_element_type=f32)
    part = part + jnp.dot(rest_low, out_weights_ref[...], preferred_element_type=f32)
    slide_sum = contract(valid_low, low, 1, 1)
    pooled = (part + slide_sum * (1.0 / count)) / jnp.sum(valid)
    pooled_ref[...] = jnp.broadcast_to(pooled[None], pooled_ref.shape)
    for copy in copies:
        copy.wait()


def logits_row(parts_ref, reports_ref, unit_ref, report_ref, row_ref):
    pooled = jnp.sum(parts_ref[...], 0)
    inverse = lax.rsqrt(jnp.sum(pooled * pooled, -1, keepdims=True) + eps)
    unit = pooled * inverse
    unit_ref[...] = jnp.concatenate([unit, jnp.broadcast_to(inverse, unit.shape)], 0)
    count, owners, block = reports_ref.shape
    squares = jnp.zeros((owners, 1), f32)
    for j in range(count):
        reports = reports_ref[j].astype(f32)
        report_ref[:, j * block : (j + 1) * block] = reports
        squares = squares + jnp.sum(reports * reports, -1, keepdims=True)
    report = report_ref[...] * lax.rsqrt(squares + eps)
    report_ref[...] = report
    row = contract(unit, report, 1, 1, precision=exact) / contrast_divisor_factor
    pad = row_ref.shape[2] - row.shape[1]
    row = jnp.concatenate([row, jnp.zeros((1, pad), f32)], 1)
    row_ref[...] = jnp.broadcast_to(row[None], row_ref.shape)


def slide_backward(
    owner,
    logits_ref,
    pair_ref,
    unit_ref,
    report_ref,
    valid_ref,
    scale_ref,
    mass_ref,
    far_out_weights,
    far_heads,
    far_attention,
    far_query_weights,
    far_key_weights,
    far_value_weights,
    far_norm,
    loss_ref,
    grad_ref,
    up_ref,
    grads_ref,
    out_ref,
    *rest,
):
    fetched, sems = rest[:-1], rest[-1]
    (
        out_weights_ref,
        heads_ref,
        attention_ref,
        query_weights_ref,
        key_weights_ref,
        value_weights_ref,
        norm_ref,
    ) = fetched
    copies = fetch(
        (
            far_out_weights,
            far_heads,
            far_attention,
            far_query_weights,
            far_key_weights,
            far_value_weights,
            far_norm,
        ),
        fetched,
        sems,
    )
    owners = report_ref.shape[0]
    valid = valid_ref[...]
    logits = logits_ref[...]
    shape = logits.shape
    columns = lax.broadcasted_iota(i32, shape, 1)
    rows = lax.broadcasted_iota(i32, shape, 0)
    real = columns < owners
    expo = jnp.where(real, jnp.exp(logits), 0.0)
    row_total = jnp.sum(expo, 1, keepdims=True)
    column_total = jnp.where(real[:1], jnp.sum(expo, 0, keepdims=True), 1.0)
    target = jnp.where(pair_ref[...] == columns, 1.0, 0.0)
    loss = jnp.sum(
        0.5 * jnp.log(row_total) - jnp.sum(logits * target, 1, keepdims=True), 0, keepdims=True
    )
    loss = loss + 0.5 * jnp.sum(jnp.log(column_total), 1, keepdims=True)
    loss_ref[...] = loss * (1.0 / owners)
    grad_logits = (0.5 * expo / row_total + 0.5 * expo / column_total - target) * (
        loss_scale / owners
    )
    grad_row = jnp.sum(jnp.where(rows == owner[0], grad_logits, 0.0), 0, keepdims=True)
    grad_unit = (
        jnp.dot(grad_row[:, :owners], report_ref[...], precision=exact, preferred_element_type=f32)
        / contrast_divisor_factor
    )
    unit = unit_ref[0:1]
    inverse = unit_ref[1:2]
    grad_pooled = (grad_unit - unit * jnp.sum(unit * grad_unit, -1, keepdims=True)) * inverse
    grad = grad_pooled / jnp.sum(valid)
    grad_ref[...] = grad
    low = grad.astype(bf16)
    copies[0].wait()
    out_weights = out_weights_ref[...]
    up_ref[...] = contract(low, out_weights, 1, 1)
    up = jnp.sum(out_weights.astype(f32) * low.astype(f32), 1, keepdims=True)
    heads = heads_ref.shape[0]
    inner = heads * HEAD
    copies[1].wait()
    copies[2].wait()
    for h in range(heads):
        up_head = up[h * HEAD : (h + 1) * HEAD]
        values = heads_ref[h, 2]
        weights = attention_ref[h]
        pull = jnp.sum(up_head * values, 0, keepdims=True)
        pull_mean = jnp.sum(weights * pull, 1, keepdims=True)
        grad_scores = (weights * (pull - pull_mean) * (score_scale / HEAD)).astype(bf16)
        query_unit = heads_ref[h, 0]
        key_unit = heads_ref[h, 1]
        grad_query = contract(key_unit.astype(bf16), grad_scores, 1, 1) * valid
        grad_key = jnp.dot(query_unit.astype(bf16), grad_scores, preferred_element_type=f32)
        grad_query = scale_ref[h, 0:1] * (
            grad_query - query_unit * jnp.mean(query_unit * grad_query, 0, keepdims=True)
        )
        grad_key = scale_ref[h, 1:2] * (
            grad_key - key_unit * jnp.mean(key_unit * grad_key, 0, keepdims=True)
        )
        grad_value = up_head * mass_ref[h : h + 1]
        for part, values in enumerate((grad_query, grad_key, grad_value)):
            start = part * inner + h * HEAD
            grads_ref[start : start + HEAD, :] = values.astype(bf16)
    grad_query = grads_ref[0:inner, :]
    grad_key = grads_ref[inner : 2 * inner, :]
    grad_value = grads_ref[2 * inner : 3 * inner, :]
    for copy in copies[3:]:
        copy.wait()
    count = out_ref.shape[0]
    block = norm_ref.shape[0] // count
    first = jnp.zeros_like(valid)
    second = jnp.zeros_like(valid)
    for k in range(count):
        rows = slice(k * block, (k + 1) * block)
        part = jnp.dot(query_weights_ref[rows, :], grad_query, preferred_element_type=f32)
        part = part + jnp.dot(key_weights_ref[rows, :], grad_key, preferred_element_type=f32)
        part = part + jnp.dot(value_weights_ref[rows, :], grad_value, preferred_element_type=f32)
        out_ref[k, 0:block, :] = part.astype(bf16)
        first = first + jnp.sum(part, 0, keepdims=True)
        second = second + jnp.sum(part * norm_ref[rows, :].astype(f32), 0, keepdims=True)
    width = norm_ref.shape[0]
    stats = jnp.concatenate([first, second], 0) * (1.0 / width)
    high = stats.astype(bf16).astype(f32)
    stats = jnp.concatenate(
        [high, stats - high, jnp.zeros((EXTRA - 4, stats.shape[1]), f32)], 0
    ).astype(bf16)
    for k in range(count):
        out_ref[k, block : block + EXTRA, :] = stats


def wide_other(which, norm_ref, grads_ref, out_ref):
    chips, share, columns = out_ref.shape
    rows = [
        norm_ref[pl.ds(pl.multiple_of((CORES * chip + which[0]) * share, 16), share), :]
        for chip in range(chips)
    ]
    values = contract(jnp.concatenate(rows, 0), grads_ref[0:columns, :], 1, 1).astype(bf16)
    for chip in range(chips):
        out_ref[chip] = values[chip * share : (chip + 1) * share]


def wide_own(which, column, norm_ref, grads_ref, got_ref, *outs):
    side = len(outs)
    lines, share, columns = outs[0].shape
    chips = [
        line * side + lax.rem(column[0] + k, side) for k in range(side) for line in range(lines)
    ]
    rows = [
        norm_ref[pl.ds(pl.multiple_of((CORES * chip + which[0]) * share, 16), share), :]
        for chip in chips
    ]
    values = contract(jnp.concatenate(rows, 0), grads_ref[0:columns, :], 1, 1)
    for index, chip in enumerate(chips):
        part = values[index * share : (index + 1) * share] + got_ref[chip].astype(f32)
        outs[index // lines][index % lines] = part.astype(bf16)


def wide_line(line, *refs):
    side = len(refs) // 2
    for k in range(side):
        row = lax.rem(line[0] + k, side)
        total = refs[0][row].astype(f32)
        for ref in refs[1:side]:
            total = total + ref[row].astype(f32)
        refs[side + k][...] = total.astype(bf16)


def slot_grads(
    own_ref, valid_ref, stat_ref, chunk_ref, select_ref, extra_ref, parts_ref, out_ref
):
    total = parts_ref[0].astype(f32)
    for j in range(1, parts_ref.shape[0]):
        total = total + parts_ref[j].astype(f32)
    block = chunk_ref.shape[0] - EXTRA
    first = total[block : block + 1] + total[block + 2 : block + 3]
    second = total[block + 1 : block + 2] + total[block + 3 : block + 4]
    mean = stat_ref[0:1]
    inverse = stat_ref[1:2]
    normed = (chunk_ref[0:block, :].astype(f32) - mean) * inverse
    rows = own_ref[...] * valid_ref[...] + (total[:block] - first - normed * second) * inverse
    rows = contract(select_ref[...], rows.astype(bf16), 1, 1).astype(bf16)
    out_ref[...] = rows + extra_ref[...]


def tile_grads(back_ref, dispatch_ref, out_ref):
    piece = pack(contract(back_ref[...], dispatch_ref[...], 0, 0).astype(bf16))
    out_ref[...] = jnp.broadcast_to(piece[None], out_ref.shape)


def other_grads(
    other, two_ref, slope_ref, norm_ref, hidden_ref, parts_ref, grad_ref, hidden_grad_ref, out_ref
):
    count = parts_ref.shape[0]
    rows = grad_ref.shape[0] // count
    for j in range(count):
        grad_ref[j * rows : (j + 1) * rows, :] = unpack(parts_ref[j])
    grad_hidden = jnp.dot(two_ref[...], grad_ref[...], preferred_element_type=f32)
    hidden_grad_ref[...] = (grad_hidden * slope_ref[...]).astype(bf16)

    def store(rows, values):
        out_ref[rows] = values.astype(bf16)

    both_layers(other[0], norm_ref, hidden_ref, grad_ref, hidden_grad_ref, out_ref.shape, store)


def own_grads(own, column, norm_ref, hidden_ref, grad_ref, hidden_grad_ref, got_ref, *rest):
    outs, line_ref, one_ref = rest[:-2], rest[-2], rest[-1]
    side = len(outs)

    def store(rows, values):
        values = (values + got_ref[rows].astype(f32)).astype(bf16)
        line, place = divmod(rows[0], side)
        if rows[1].start:
            line_ref[line, place] = values
        else:
            one_ref[place, line] = values

    both_layers(own[0], norm_ref, hidden_ref, grad_ref, hidden_grad_ref, got_ref.shape, store)
    for k in range(side):
        outs[k][...] = one_ref[lax.rem(column[0] + k, side)]


def half_way(column, *refs):
    side = (len(refs) - 2) // 2
    lines_ref, out_ref = refs[side], refs[side + 1]
    total = refs[0][...].astype(f32)
    for ref in refs[1:side]:
        total = total + ref[...].astype(f32)
    out_ref[...] = total.astype(bf16)
    for k in range(side):
        place = lax.rem(column[0] + k, side)
        total = lines_ref[0, place].astype(f32)
        for line in range(1, lines_ref.shape[0]):
            total = total + lines_ref[line, place].astype(f32)
        refs[side + 2 + k][...] = total.astype(bf16)


def both_layers(which, norm_ref, hidden_ref, grad_ref, hidden_grad_ref, shape, store):
    chips, share = shape[0], shape[1] // 2
    rows = [
        grad_ref[pl.ds(pl.multiple_of((CORES * chip + which) * share, 16), share), :]
        for chip in range(chips)
    ]
    two = jnp.dot(jnp.concatenate(rows, 0), hidden_ref[...], preferred_element_type=f32)
    one = contract(norm_ref[...], hidden_grad_ref[...], 1, 1)
    for chip in range(chips):
        start = chip * share
        store((chip, slice(0, share)), one[start : start + share])
        store((chip, slice(share, 2 * share)), two[start : start + share])


def last_sums(lines_ref, *refs):
    one_ref, two_ref = refs[-2:]
    total = lines_ref[0].astype(f32)
    for line in range(1, lines_ref.shape[0]):
        total = total + lines_ref[line].astype(f32)
    one_ref[...] = total
    total = refs[0][...].astype(f32)
    for ref in refs[1:-2]:
        total = total + ref[...].astype(f32)
    two_ref[...] = total


def per_device(
    tile_features, tile_slide, slide_pair, reports, w_one, w_two, w_query, w_key, w_value, w_out
):
    lines = lax.axis_size("line")
    side = lax.axis_size("column")
    line = lax.axis_index("line")
    column = lax.axis_index("column")
    chips = lines * side
    owners = chips * CORES
    parts = lax.axis_size("mp")
    core = lax.axis_index("core")
    owner = lax.axis_index(DP)
    here = lax.axis_index("mp")
    tiles, width = tile_features.shape
    units = w_one.shape[1]
    capacity = 2 * tiles // owners
    length = owners * capacity
    slots = owners * ROWS
    block = width // parts
    share = width // owners
    inner = w_query.shape[1]
    heads = inner // HEAD
    packed = (block // 2 * 3, 128)

    def halves(values):
        rest = values.shape[1:]
        values = values.reshape((chips, CORES, share) + rest)
        own = pick(values, core, 1).reshape((chips * share,) + rest)
        other = pick(values, 1 - core, 1).reshape((chips * share,) + rest)
        return own, other

    tile_norm, hidden, slope, partial = call(
        tile_forward,
        [
            ((tiles, width), bf16),
            ((tiles, units), bf16),
            ((tiles, units), f32),
            ((parts,) + packed, bf16),
        ],
        tile_features,
        w_one,
        w_two,
        far=(0, 1, 2),
        scratch=[
            (tile_features.shape, bf16),
            (w_one.shape, bf16),
            (w_two.shape, bf16),
            3,
        ],
        limit=62,
    )
    partial = exchange(partial, "mp")

    slide_ids = tile_slide[:, 0]
    matches = (slide_ids[:, None] == jnp.arange(owners, dtype=i32)[None, :]).astype(i32)
    ordinal = jnp.sum(matches * (jnp.cumsum(matches, 0) - 1), 1)
    position = slide_ids * ROWS + ordinal
    dispatch = jnp.arange(slots, dtype=i32)[:, None] == position[None, :]
    flags = jnp.sum(dispatch.astype(f32), 1, keepdims=True).astype(bf16)
    flags = jnp.pad(flags, ((0, 0), (0, 256 - block - 1)))
    dispatch = dispatch.astype(bf16)
    slot = jnp.arange(slots, dtype=i32)
    row_of_slot = jnp.where(slot % ROWS < capacity, slot // ROWS * capacity + slot % ROWS, -1)
    select = (row_of_slot[:, None] == jnp.arange(length, dtype=i32)[None, :]).astype(bf16)
    last_slot = jnp.arange(owners, dtype=i32)[:, None] * ROWS + ROWS - 1
    report_select = (last_slot == slot[None, :]).astype(bf16)
    own_columns = pick(tile_features.reshape(tiles, parts, block), here, 1)
    own_report = pick(reports.reshape(1, parts, block), here, 1)
    tile_own, tile_other = halves(tile_norm.T)
    slope = slope.T

    (outgoing,) = call(
        tile_dispatch,
        [((slots, 256), bf16)],
        own_columns,
        own_report,
        dispatch,
        flags,
        partial,
        anchors=(select, report_select, tile_own, tile_other, slope),
    )
    arrived = exchange(outgoing.reshape(owners, ROWS, 256), DP).reshape(slots, 256)
    chunk, valid = call(
        slot_rows,
        [((block + EXTRA, length), bf16), ((1, length), f32)],
        arrived,
        select,
        report_select,
    )
    pieces = gather_ring(chunk, parts)

    (
        slide_norm,
        by_head,
        attention,
        stat,
        scales,
        mass,
        attended_sum,
        pooled,
        all_reports,
    ) = call(
        slide_forward,
        [
            ((width, length), bf16, "far"),
            ((heads, 3, HEAD, length), f32, "far"),
            ((heads, length, length), f32, "far"),
            ((2, length), f32),
            ((heads, 2, length), f32),
            ((heads, length), f32),
            ((1, inner), f32),
            ((parts, 1, width), f32),
            ((parts, owners, block), bf16),
        ],
        valid,
        w_query.T,
        w_key.T,
        w_value.T,
        w_out,
        *pieces,
        scalars=(here,),
        scratch=[
            ((width, length), bf16),
            ((width, length), bf16),
            ((heads, 3, HEAD, length), f32),
            ((heads, length, length), f32),
            1 + 2 * heads,
        ],
        limit=60,
    )
    pooled = exchange(pooled, "mp")
    unit, report_unit, row = call(
        logits_row,
        [((2, width), f32), ((owners, width), f32), ((owners, 1, 128), f32)],
        pooled,
        all_reports,
    )
    logits = exchange(row, DP).reshape(owners, 128)
    loss, grad, up, grads, sending = call(
        slide_backward,
        [((1, 1), f32), ((1, width), f32), ((1, inner), f32), ((3 * inner, length), bf16)]
        + [((parts, block + EXTRA, length), bf16)],
        logits,
        slide_pair[:, None],
        unit,
        report_unit,
        valid,
        scales,
        mass,
        w_out,
        by_head,
        attention,
        w_query,
        w_key,
        w_value,
        slide_norm,
        scalars=(owner,),
        far=tuple(range(7, 14)),
        scratch=[
            (w_out.shape, bf16),
            (by_head.shape, f32),
            (attention.shape, f32),
            (w_query.shape, bf16),
            (w_key.shape, bf16),
            (w_value.shape, bf16),
            (slide_norm.shape, bf16),
            7,
        ],
        limit=60,
    )
    received = exchange(sending, "mp")

    (wide_sent,) = call(
        wide_other,
        [((chips, share, 2 * inner), bf16)],
        slide_norm,
        grads,
        scalars=(1 - core,),
    )
    wide_got = lax.ppermute(wide_sent, "core", [(0, 1), (1, 0)])
    along = call(
        wide_own,
        [((lines, share, 2 * inner), bf16)] * side,
        slide_norm,
        grads,
        wide_got,
        scalars=(core, column),
    )
    def shift(values, axis):
        return [values[0]] + [
            lax.ppermute(values[k], axis, turn(len(values), k)) for k in range(1, len(values))
        ]

    along = shift(along, "column")
    across = call(
        wide_line, [((share, 2 * inner), bf16)] * lines, *along, scalars=(line,)
    )
    across = shift(across, "line")
    grad_wide = sum(part.astype(f32) for part in across)
    value_rows = contract(mass.astype(bf16), slide_norm, 1, 1)
    extra = jnp.concatenate(
        [
            value_rows.reshape(heads, owners, share).transpose(1, 0, 2).reshape(owners, -1),
            grad.reshape(owners, share),
            jnp.broadcast_to(up, (owners, inner)),
            jnp.broadcast_to(attended_sum, (owners, inner)),
        ],
        1,
    ).astype(bf16)
    spare = ROWS - capacity
    extra = jnp.pad(extra, ((0, 0), (0, spare * block - extra.shape[1])))
    extra = extra.reshape(owners, spare, block)
    extra = jnp.pad(extra, ((0, 0), (capacity, 0), (0, 0))).reshape(slots, block)

    own_grad = lax.dynamic_slice_in_dim(grad, here * block, block, 1).reshape(block, 1)
    (going,) = call(
        slot_grads,
        [((slots, block), bf16)],
        own_grad,
        valid,
        stat,
        chunk,
        select,
        extra,
        received,
        anchors=(grad_wide,),
    )
    back = exchange(going.reshape(owners, ROWS, block), DP).reshape(slots, block)
    (spreading,) = call(tile_grads, [((parts,) + packed, bf16)], back, dispatch)

    size = (chips, 2 * share, units)
    grad_embedding, grad_hidden, sent = call(
        other_grads,
        [((width, tiles), bf16), ((units, tiles), bf16), (size, bf16)],
        w_two,
        slope,
        tile_other,
        hidden,
        exchange(spreading, "mp"),
        scalars=(1 - core,),
        limit=24,
    )
    got = lax.ppermute(sent, "core", [(0, 1), (1, 0)])
    *along, across = call(
        own_grads,
        [((lines, share, units), bf16)] * side + [((lines, side, share, units), bf16)],
        tile_own,
        hidden,
        grad_embedding,
        grad_hidden,
        got,
        scalars=(core, column),
        scratch=[((side, lines, share, units), bf16)],
        limit=24,
    )
    across, *along = call(
        half_way,
        [((lines, share, units), bf16)] + [((share, units), bf16)] * side,
        *shift(along, "column"),
        exchange(across, "line"),
        scalars=(column,),
    )
    grad_one, grad_two = call(
        last_sums,
        [((share, units), f32)] * 2,
        exchange(across, "line"),
        *shift(along, "column"),
    )
    grad_two = grad_two.T

    terms = back.reshape(owners, ROWS, block)[:, capacity:].reshape(owners, -1).astype(f32)
    edge = heads * share
    from_values = terms[:, :edge].reshape(owners, heads, share)
    from_grads = terms[:, edge : edge + share]
    edge = edge + share
    from_up = terms[:, edge : edge + inner].reshape(owners, heads, HEAD)
    edge = edge + inner
    from_attended = terms[:, edge : edge + inner]
    grad_value = jnp.einsum("ohs,ohd->shd", from_values, from_up, precision=exact)
    grad_value = grad_value.reshape(share, inner)
    grad_out = contract(from_attended, from_grads, 0, 0, precision=exact)
    return (
        loss[0, 0],
        grad_one,
        grad_two,
        grad_wide[:, :inner],
        grad_wide[:, inner:],
        grad_value,
        grad_out,
    )


def solution(mesh):
    owners, parts = mesh.devices.shape
    side = math.isqrt(owners // CORES)
    split = Mesh(
        mesh.devices.reshape(owners // CORES // side, side, CORES, parts),
        ("line", "column", "core", "mp"),
    )
    return jax.shard_map(
        per_device,
        mesh=split,
        in_specs=(
            P(DP, None),
            P(DP, None),
            P(),
            P(DP, None),
            P(None, "mp"),
            P("mp", None),
            P(None, "mp"),
            P(None, "mp"),
            P(None, "mp"),
            P("mp", None),
        ),
        out_specs=(
            P(),
            P(DP, "mp"),
            P("mp", DP),
            P(DP, "mp"),
            P(DP, "mp"),
            P(DP, "mp"),
            P("mp", DP),
        ),
        check_vma=False,
    )
```

```python
import math

import jax
import jax.numpy as jnp
from jax import lax
from jax.experimental import pallas as pl
from jax.experimental.pallas import tpu as pltpu
from jax.sharding import Mesh, PartitionSpec as P

HEAD = 96
CORES = 2
ROWS = 16
EXTRA = 16

eps = 1e-05
contrast_divisor_factor = 0.07
score_scale = 10.0
loss_scale = 4096.0
exact = lax.Precision.HIGHEST
f32 = jnp.float32
bf16 = jnp.bfloat16
i32 = jnp.int32
DP = ("line", "column", "core")


def contract(left, right, left_dim, right_dim, **kw):
    return lax.dot_general(
        left, right, (((left_dim,), (right_dim,)), ((), ())), preferred_element_type=f32, **kw
    )


def exchange(values, axis):
    return lax.all_to_all(values, axis, 0, 0, tiled=True)


def pick(values, index, axis):
    return lax.dynamic_index_in_dim(values, index, axis, keepdims=False)


def call(body, outs, *args, scalars=(), scratch=(), anchors=(), far=(), limit=16):
    count = len(scalars)
    skip = len(anchors)
    vmem = pl.BlockSpec(memory_space=pltpu.VMEM)
    away = pl.BlockSpec(memory_space=pltpu.HBM)

    def kernel(*refs):
        body(*refs[skip:])

    return pl.pallas_call(
        kernel if skip else body,
        out_shape=[jax.ShapeDtypeStruct(out[0], out[1]) for out in outs],
        in_specs=[pl.BlockSpec(memory_space=pl.ANY)] * skip
        + [pl.BlockSpec(memory_space=pltpu.SMEM)] * count
        + [away if index in far else vmem for index in range(len(args))],
        out_specs=[vmem if len(out) == 2 else away for out in outs],
        scratch_shapes=[
            pltpu.VMEM(*part) if isinstance(part, tuple) else pltpu.SemaphoreType.DMA((part,))
            for part in scratch
        ],
        compiler_params=pltpu.CompilerParams(vmem_limit_bytes=limit * 1024 * 1024),
    )(*anchors, *[jnp.reshape(s, (1,)).astype(i32) for s in scalars], *args)


def fetch(sources, targets, semaphores):
    copies = [
        pltpu.make_async_copy(source, target, semaphores.at[index])
        for index, (source, target) in enumerate(zip(sources, targets))
    ]
    for copy in copies:
        copy.start()
    return copies


def turn(count, step):
    return [(index, (index + step) % count) for index in range(count)]


def gather_ring(piece, count):
    found = [piece]
    back = ahead = piece
    for _ in range(count // 2 - 1):
        back = lax.ppermute(back, "mp", turn(count, 1))
        ahead = lax.ppermute(ahead, "mp", turn(count, count - 1))
        found += [back, ahead]
    half = (piece.shape[0] // 2 + ROWS - 1) // ROWS * ROWS
    found.append(lax.ppermute(back[:half], "mp", turn(count, 1)))
    found.append(lax.ppermute(ahead[half:], "mp", turn(count, count - 1)))
    return found


def place(refs, here, count, store):
    half = count // 2
    store(here, refs[0][...])
    for step in range(1, half):
        for ref, sign in ((refs[2 * step - 1], -1), (refs[2 * step], 1)):
            store(lax.rem(here + sign * step + count, count), ref[...])
    store(
        lax.rem(here + half, count), jnp.concatenate([refs[-2][...], refs[-1][...]], 0)
    )


def pack(square):
    half = square.shape[0] // 2
    side = square[:, 128:]
    return jnp.concatenate(
        [square[:, :128], jnp.concatenate([side[:half], side[half:]], 1)], 0
    )


def unpack(packed):
    rows = packed.shape[0] // 3 * 2
    side = packed[rows:]
    return jnp.concatenate(
        [packed[:rows], jnp.concatenate([side[:, :64], side[:, 64:]], 0)], 1
    )


def tile_forward(
    far_x, far_one, far_two, norm_ref, hidden_ref, slope_ref, out_ref, x_ref, one_ref, two_ref, sems
):
    copies = fetch((far_x, far_one, far_two), (x_ref, one_ref, two_ref), sems)
    copies[0].wait()
    x = x_ref[...].astype(f32)
    centred = x - jnp.mean(x, -1, keepdims=True)
    normed = centred * lax.rsqrt(jnp.mean(centred * centred, -1, keepdims=True) + eps)
    normed = normed.astype(bf16)
    norm_ref[...] = normed
    copies[1].wait()
    pre = jnp.dot(normed, one_ref[...], preferred_element_type=f32)
    bell = 0.5 * (1.0 + lax.erf(pre * 0.7071067811865476))
    hidden = (pre * bell).astype(bf16)
    hidden_ref[...] = hidden
    slope_ref[...] = bell + pre * jnp.exp(-0.5 * pre * pre) * 0.3989422804014327
    copies[2].wait()
    partial = jnp.dot(hidden, two_ref[...], preferred_element_type=f32).astype(bf16)
    count = out_ref.shape[0]
    block = partial.shape[1] // count
    for j in range(count):
        out_ref[j] = pack(partial[:, j * block : (j + 1) * block])


def tile_dispatch(own_ref, report_ref, dispatch_ref, flags_ref, parts_ref, out_ref):
    total = parts_ref[0].astype(f32)
    for j in range(1, parts_ref.shape[0]):
        total = total + parts_ref[j].astype(f32)
    embedding = (own_ref[...].astype(f32) + unpack(total)).astype(bf16)
    rows = jnp.dot(dispatch_ref[...], embedding, preferred_element_type=f32)
    slot = lax.broadcasted_iota(i32, rows.shape, 0)
    rows = jnp.where(lax.rem(slot, ROWS) == ROWS - 1, report_ref[...].astype(f32), rows)
    out_ref[...] = jnp.concatenate([rows.astype(bf16), flags_ref[...]], 1)


def slot_rows(arrived_ref, select_ref, report_select_ref, chunk_ref, valid_ref):
    arrived = arrived_ref[...]
    chunk = contract(arrived, select_ref[...], 0, 0)
    block = chunk_ref.shape[0] - EXTRA
    chunk_ref[0:block, :] = chunk[:block].astype(bf16)
    valid_ref[...] = chunk[block : block + 1]
    reports = jnp.dot(report_select_ref[...], arrived, preferred_element_type=f32)
    reports = reports[:, :block].astype(bf16)
    chunk_ref[block : block + EXTRA, :] = jnp.concatenate(
        [reports[:EXTRA], reports[EXTRA:]], 1
    )


def slide_forward(
    here,
    valid_ref,
    query_weights_ref,
    key_weights_ref,
    value_weights_ref,
    out_weights_ref,
    *rest,
):
    pieces = rest[:9]
    (
        far_norm,
        far_heads,
        far_attention,
        stat_ref,
        scale_ref,
        mass_ref,
        attended_ref,
        pooled_ref,
        reports_ref,
        slide_ref,
        norm_ref,
        heads_ref,
        attention_ref,
        sems,
    ) = rest[9:]
    count, owners, block = reports_ref.shape

    def store(index, piece):
        start = pl.multiple_of(index * block, 16)
        slide_ref[pl.ds(start, block), :] = piece[:block]
        reports = piece[block:]
        reports_ref[index] = jnp.concatenate([reports[:, :block], reports[:, block:]], 0)

    place(pieces, here[0], count, store)
    valid = valid_ref[...]
    valid_low = valid.astype(bf16)
    low = slide_ref[...]
    slide = low.astype(f32)
    mean = jnp.mean(slide, 0, keepdims=True)
    centred = slide - mean
    inverse = lax.rsqrt(jnp.mean(centred * centred, 0, keepdims=True) + eps)
    stat_ref[...] = jnp.concatenate([mean, inverse], 0)
    normed = (centred * inverse).astype(bf16)
    norm_ref[...] = normed
    copies = [pltpu.make_async_copy(norm_ref, far_norm, sems.at[0])]
    copies[0].start()
    all_query = jnp.dot(query_weights_ref[...], normed, preferred_element_type=f32)
    all_keys = jnp.dot(key_weights_ref[...], normed, preferred_element_type=f32)
    all_values = jnp.dot(value_weights_ref[...], normed, preferred_element_type=f32)
    heads = all_query.shape[0] // HEAD
    attended = []
    for h in range(heads):
        low_rows, high_rows = h * HEAD, (h + 1) * HEAD
        query = all_query[low_rows:high_rows]
        keys = all_keys[low_rows:high_rows]
        values = all_values[low_rows:high_rows]
        query_scale = lax.rsqrt(jnp.mean(query * query, 0, keepdims=True) + eps)
        key_scale = lax.rsqrt(jnp.mean(keys * keys, 0, keepdims=True) + eps)
        query_unit = query * query_scale
        key_unit = keys * key_scale
        heads_ref[h, 0] = query_unit
        heads_ref[h, 1] = key_unit
        heads_ref[h, 2] = values
        copies.append(pltpu.make_async_copy(heads_ref.at[h], far_heads.at[h], sems.at[1 + 2 * h]))
        copies[-1].start()
        scale_ref[h] = jnp.concatenate([query_scale, key_scale], 0)
        scores = contract(query_unit.astype(bf16), key_unit.astype(bf16), 0, 0)
        weights = jnp.exp(scores * (score_scale / HEAD)) * valid
        weights = weights * (1.0 / jnp.sum(weights, 1, keepdims=True))
        attention_ref[h] = weights
        copies.append(
            pltpu.make_async_copy(attention_ref.at[h], far_attention.at[h], sems.at[2 + 2 * h])
        )
        copies[-1].start()
        weights_low = weights.astype(bf16)
        mass_ref[h : h + 1, :] = jnp.dot(valid_low, weights_low, preferred_element_type=f32)
        attended.append(contract(values.astype(bf16), weights_low, 1, 1))
    attended = jnp.concatenate(attended, 0).astype(bf16)
    attended_sum = contract(valid_low, attended, 1, 1)
    attended_ref[...] = attended_sum
    high = attended_sum.astype(bf16)
    rest_low = (attended_sum - high.astype(f32)).astype(bf16)
    part = jnp.dot(high, out_weights_ref[...], preferred_element_type=f32)
    part = part + jnp.dot(rest_low, out_weights_ref[...], preferred_element_type=f32)
    slide_sum = contract(valid_low, low, 1, 1)
    pooled = (part + slide_sum * (1.0 / count)) / jnp.sum(valid)
    pooled_ref[...] = jnp.broadcast_to(pooled[None], pooled_ref.shape)
    for copy in copies:
        copy.wait()


def unit_vectors(parts_ref, reports_ref, report_ref):
    pooled = jnp.sum(parts_ref[...], 0)
    inverse = lax.rsqrt(jnp.sum(pooled * pooled, -1, keepdims=True) + eps)
    count, owners, block = reports_ref.shape
    squares = jnp.zeros((owners, 1), f32)
    for j in range(count):
        reports = reports_ref[j].astype(f32)
        report_ref[:, j * block : (j + 1) * block] = reports
        squares = squares + jnp.sum(reports * reports, -1, keepdims=True)
    report = report_ref[...] * lax.rsqrt(squares + eps)
    return pooled * inverse, inverse, report


def logits_row(parts_ref, reports_ref, row_ref, report_ref):
    unit, inverse, report = unit_vectors(parts_ref, reports_ref, report_ref)
    row = contract(unit, report, 1, 1, precision=exact) / contrast_divisor_factor
    pad = row_ref.shape[2] - row.shape[1]
    row = jnp.concatenate([row, jnp.zeros((1, pad), f32)], 1)
    row_ref[...] = jnp.broadcast_to(row[None], row_ref.shape)


def slide_backward(
    owner,
    logits_ref,
    pair_ref,
    parts_ref,
    reports_ref,
    valid_ref,
    scale_ref,
    mass_ref,
    far_out_weights,
    far_heads,
    far_attention,
    far_query_weights,
    far_key_weights,
    far_value_weights,
    far_norm,
    loss_ref,
    grad_ref,
    up_ref,
    grads_ref,
    out_ref,
    *rest,
):
    fetched, report_ref, sems = rest[:-2], rest[-2], rest[-1]
    (
        out_weights_ref,
        heads_ref,
        attention_ref,
        query_weights_ref,
        key_weights_ref,
        value_weights_ref,
        norm_ref,
    ) = fetched
    copies = fetch(
        (
            far_out_weights,
            far_heads,
            far_attention,
            far_query_weights,
            far_key_weights,
            far_value_weights,
            far_norm,
        ),
        fetched,
        sems,
    )
    unit, inverse, report = unit_vectors(parts_ref, reports_ref, report_ref)
    owners = report.shape[0]
    valid = valid_ref[...]
    logits = logits_ref[...]
    shape = logits.shape
    columns = lax.broadcasted_iota(i32, shape, 1)
    rows = lax.broadcasted_iota(i32, shape, 0)
    real = columns < owners
    expo = jnp.where(real, jnp.exp(logits), 0.0)
    row_total = jnp.sum(expo, 1, keepdims=True)
    column_total = jnp.where(real[:1], jnp.sum(expo, 0, keepdims=True), 1.0)
    target = jnp.where(pair_ref[...] == columns, 1.0, 0.0)
    loss = jnp.sum(
        0.5 * jnp.log(row_total) - jnp.sum(logits * target, 1, keepdims=True), 0, keepdims=True
    )
    loss = loss + 0.5 * jnp.sum(jnp.log(column_total), 1, keepdims=True)
    loss_ref[...] = loss * (1.0 / owners)
    grad_logits = (0.5 * expo / row_total + 0.5 * expo / column_total - target) * (
        loss_scale / owners
    )
    grad_row = jnp.sum(jnp.where(rows == owner[0], grad_logits, 0.0), 0, keepdims=True)
    grad_unit = (
        jnp.dot(grad_row[:, :owners], report, precision=exact, preferred_element_type=f32)
        / contrast_divisor_factor
    )
    grad_pooled = (grad_unit - unit * jnp.sum(unit * grad_unit, -1, keepdims=True)) * inverse
    grad = grad_pooled / jnp.sum(valid)
    grad_ref[...] = grad
    low = grad.astype(bf16)
    copies[0].wait()
    out_weights = out_weights_ref[...]
    up_ref[...] = contract(low, out_weights, 1, 1)
    up = jnp.sum(out_weights.astype(f32) * low.astype(f32), 1, keepdims=True)
    heads = heads_ref.shape[0]
    inner = heads * HEAD
    copies[1].wait()
    copies[2].wait()
    for h in range(heads):
        up_head = up[h * HEAD : (h + 1) * HEAD]
        values = heads_ref[h, 2]
        weights = attention_ref[h]
        pull = jnp.sum(up_head * values, 0, keepdims=True)
        pull_mean = jnp.sum(weights * pull, 1, keepdims=True)
        grad_scores = (weights * (pull - pull_mean) * (score_scale / HEAD)).astype(bf16)
        query_unit = heads_ref[h, 0]
        key_unit = heads_ref[h, 1]
        grad_query = contract(key_unit.astype(bf16), grad_scores, 1, 1) * valid
        grad_key = jnp.dot(query_unit.astype(bf16), grad_scores, preferred_element_type=f32)
        grad_query = scale_ref[h, 0:1] * (
            grad_query - query_unit * jnp.mean(query_unit * grad_query, 0, keepdims=True)
        )
        grad_key = scale_ref[h, 1:2] * (
            grad_key - key_unit * jnp.mean(key_unit * grad_key, 0, keepdims=True)
        )
        grad_value = up_head * mass_ref[h : h + 1]
        for part, values in enumerate((grad_query, grad_key, grad_value)):
            start = part * inner + h * HEAD
            grads_ref[start : start + HEAD, :] = values.astype(bf16)
    grad_query = grads_ref[0:inner, :]
    grad_key = grads_ref[inner : 2 * inner, :]
    grad_value = grads_ref[2 * inner : 3 * inner, :]
    for copy in copies[3:]:
        copy.wait()
    count = out_ref.shape[0]
    block = norm_ref.shape[0] // count
    first = jnp.zeros_like(valid)
    second = jnp.zeros_like(valid)
    for k in range(count):
        rows = slice(k * block, (k + 1) * block)
        part = jnp.dot(query_weights_ref[rows, :], grad_query, preferred_element_type=f32)
        part = part + jnp.dot(key_weights_ref[rows, :], grad_key, preferred_element_type=f32)
        part = part + jnp.dot(value_weights_ref[rows, :], grad_value, preferred_element_type=f32)
        out_ref[k, 0:block, :] = part.astype(bf16)
        first = first + jnp.sum(part, 0, keepdims=True)
        second = second + jnp.sum(part * norm_ref[rows, :].astype(f32), 0, keepdims=True)
    width = norm_ref.shape[0]
    stats = jnp.concatenate([first, second], 0) * (1.0 / width)
    high = stats.astype(bf16).astype(f32)
    stats = jnp.concatenate(
        [high, stats - high, jnp.zeros((EXTRA - 4, stats.shape[1]), f32)], 0
    ).astype(bf16)
    for k in range(count):
        out_ref[k, block : block + EXTRA, :] = stats


def wide_other(which, norm_ref, grads_ref, out_ref):
    chips, share, columns = out_ref.shape
    rows = [
        norm_ref[pl.ds(pl.multiple_of((CORES * chip + which[0]) * share, 16), share), :]
        for chip in range(chips)
    ]
    values = contract(jnp.concatenate(rows, 0), grads_ref[0:columns, :], 1, 1).astype(bf16)
    for chip in range(chips):
        out_ref[chip] = values[chip * share : (chip + 1) * share]


def wide_own(which, column, norm_ref, grads_ref, got_ref, *outs):
    side = len(outs)
    lines, share, columns = outs[0].shape
    chips = [
        line * side + lax.rem(column[0] + k, side) for k in range(side) for line in range(lines)
    ]
    rows = [
        norm_ref[pl.ds(pl.multiple_of((CORES * chip + which[0]) * share, 16), share), :]
        for chip in chips
    ]
    values = contract(jnp.concatenate(rows, 0), grads_ref[0:columns, :], 1, 1)
    for index, chip in enumerate(chips):
        part = values[index * share : (index + 1) * share] + got_ref[chip].astype(f32)
        outs[index // lines][index % lines] = part.astype(bf16)


def wide_line(line, *refs):
    side = len(refs) // 2
    for k in range(side):
        row = lax.rem(line[0] + k, side)
        total = refs[0][row].astype(f32)
        for ref in refs[1:side]:
            total = total + ref[row].astype(f32)
        refs[side + k][...] = total.astype(bf16)


def slot_grads(
    own_ref, valid_ref, stat_ref, chunk_ref, select_ref, extra_ref, parts_ref, out_ref
):
    total = parts_ref[0].astype(f32)
    for j in range(1, parts_ref.shape[0]):
        total = total + parts_ref[j].astype(f32)
    block = chunk_ref.shape[0] - EXTRA
    first = total[block : block + 1] + total[block + 2 : block + 3]
    second = total[block + 1 : block + 2] + total[block + 3 : block + 4]
    mean = stat_ref[0:1]
    inverse = stat_ref[1:2]
    normed = (chunk_ref[0:block, :].astype(f32) - mean) * inverse
    rows = own_ref[...] * valid_ref[...] + (total[:block] - first - normed * second) * inverse
    rows = contract(select_ref[...], rows.astype(bf16), 1, 1).astype(bf16)
    out_ref[...] = rows + extra_ref[...]


def tile_grads(back_ref, dispatch_ref, out_ref):
    piece = pack(contract(back_ref[...], dispatch_ref[...], 0, 0).astype(bf16))
    out_ref[...] = jnp.broadcast_to(piece[None], out_ref.shape)


def rows_of(which, ref, chips, share):
    rows = [
        ref[pl.ds(pl.multiple_of((CORES * chip + which) * share, 16), share), :]
        for chip in range(chips)
    ]
    return jnp.concatenate(rows, 0)


def other_two(other, hidden_ref, parts_ref, grad_ref, out_ref):
    count = parts_ref.shape[0]
    rows = grad_ref.shape[0] // count
    for j in range(count):
        grad_ref[j * rows : (j + 1) * rows, :] = unpack(parts_ref[j])
    chips, share = out_ref.shape[:2]
    rows = rows_of(other[0], grad_ref, chips, share)
    two = jnp.dot(rows, hidden_ref[...], preferred_element_type=f32).astype(bf16)
    for chip in range(chips):
        out_ref[chip] = two[chip * share : (chip + 1) * share]


def other_one(two_ref, slope_ref, norm_ref, grad_ref, hidden_grad_ref, out_ref):
    grad_hidden = jnp.dot(two_ref[...], grad_ref[...], preferred_element_type=f32)
    hidden_grad_ref[...] = (grad_hidden * slope_ref[...]).astype(bf16)
    one = contract(norm_ref[...], hidden_grad_ref[...], 1, 1).astype(bf16)
    chips, share = out_ref.shape[:2]
    for chip in range(chips):
        out_ref[chip] = one[chip * share : (chip + 1) * share]


def own_two(own, hidden_ref, grad_ref, got_ref, out_ref):
    chips, share = got_ref.shape[:2]
    side = out_ref.shape[1]
    rows = rows_of(own[0], grad_ref, chips, share)
    two = jnp.dot(rows, hidden_ref[...], preferred_element_type=f32)
    for chip in range(chips):
        part = two[chip * share : (chip + 1) * share] + got_ref[chip].astype(f32)
        out_ref[chip // side, chip % side] = part.astype(bf16)


def own_one(column, norm_ref, hidden_grad_ref, got_ref, *rest):
    outs, one_ref = rest[:-1], rest[-1]
    chips, share = got_ref.shape[:2]
    side = len(outs)
    one = contract(norm_ref[...], hidden_grad_ref[...], 1, 1)
    for chip in range(chips):
        part = one[chip * share : (chip + 1) * share] + got_ref[chip].astype(f32)
        one_ref[chip % side, chip // side] = part.astype(bf16)
    for k in range(side):
        outs[k][...] = one_ref[lax.rem(column[0] + k, side)]


def half_way_one(*refs):
    out_ref = refs[-1]
    total = refs[0][...].astype(f32)
    for ref in refs[1:-1]:
        total = total + ref[...].astype(f32)
    out_ref[...] = total.astype(bf16)


def half_way_two(column, lines_ref, *outs):
    side = len(outs)
    for k in range(side):
        place = lax.rem(column[0] + k, side)
        total = lines_ref[0, place].astype(f32)
        for line in range(1, lines_ref.shape[0]):
            total = total + lines_ref[line, place].astype(f32)
        outs[k][...] = total.astype(bf16)


def last_sums(lines_ref, *refs):
    one_ref, two_ref = refs[-2:]
    total = lines_ref[0].astype(f32)
    for line in range(1, lines_ref.shape[0]):
        total = total + lines_ref[line].astype(f32)
    one_ref[...] = total
    total = refs[0][...].astype(f32)
    for ref in refs[1:-2]:
        total = total + ref[...].astype(f32)
    two_ref[...] = total


def per_device(
    tile_features, tile_slide, slide_pair, reports, w_one, w_two, w_query, w_key, w_value, w_out
):
    lines = lax.axis_size("line")
    side = lax.axis_size("column")
    line = lax.axis_index("line")
    column = lax.axis_index("column")
    chips = lines * side
    owners = chips * CORES
    parts = lax.axis_size("mp")
    core = lax.axis_index("core")
    owner = lax.axis_index(DP)
    here = lax.axis_index("mp")
    tiles, width = tile_features.shape
    units = w_one.shape[1]
    capacity = 2 * tiles // owners
    length = owners * capacity
    slots = owners * ROWS
    block = width // parts
    share = width // owners
    inner = w_query.shape[1]
    heads = inner // HEAD
    packed = (block // 2 * 3, 128)

    def halves(values):
        rest = values.shape[1:]
        values = values.reshape((chips, CORES, share) + rest)
        own = pick(values, core, 1).reshape((chips * share,) + rest)
        other = pick(values, 1 - core, 1).reshape((chips * share,) + rest)
        return own, other

    tile_norm, hidden, slope, partial = call(
        tile_forward,
        [
            ((tiles, width), bf16),
            ((tiles, units), bf16),
            ((tiles, units), f32),
            ((parts,) + packed, bf16),
        ],
        tile_features,
        w_one,
        w_two,
        far=(0, 1, 2),
        scratch=[
            (tile_features.shape, bf16),
            (w_one.shape, bf16),
            (w_two.shape, bf16),
            3,
        ],
        limit=62,
    )
    partial = exchange(partial, "mp")

    slide_ids = tile_slide[:, 0]
    matches = (slide_ids[:, None] == jnp.arange(owners, dtype=i32)[None, :]).astype(i32)
    ordinal = jnp.sum(matches * (jnp.cumsum(matches, 0) - 1), 1)
    position = slide_ids * ROWS + ordinal
    dispatch = jnp.arange(slots, dtype=i32)[:, None] == position[None, :]
    flags = jnp.sum(dispatch.astype(f32), 1, keepdims=True).astype(bf16)
    flags = jnp.pad(flags, ((0, 0), (0, 256 - block - 1)))
    dispatch = dispatch.astype(bf16)
    slot = jnp.arange(slots, dtype=i32)
    row_of_slot = jnp.where(slot % ROWS < capacity, slot // ROWS * capacity + slot % ROWS, -1)
    select = (row_of_slot[:, None] == jnp.arange(length, dtype=i32)[None, :]).astype(bf16)
    last_slot = jnp.arange(owners, dtype=i32)[:, None] * ROWS + ROWS - 1
    report_select = (last_slot == slot[None, :]).astype(bf16)
    own_columns = pick(tile_features.reshape(tiles, parts, block), here, 1)
    own_report = pick(reports.reshape(1, parts, block), here, 1)
    tile_own, tile_other = halves(tile_norm.T)
    slope = slope.T

    (outgoing,) = call(
        tile_dispatch,
        [((slots, 256), bf16)],
        own_columns,
        own_report,
        dispatch,
        flags,
        partial,
        anchors=(select, report_select, tile_own, tile_other, slope),
    )
    arrived = exchange(outgoing.reshape(owners, ROWS, 256), DP).reshape(slots, 256)
    chunk, valid = call(
        slot_rows,
        [((block + EXTRA, length), bf16), ((1, length), f32)],
        arrived,
        select,
        report_select,
    )
    pieces = gather_ring(chunk, parts)

    (
        slide_norm,
        by_head,
        attention,
        stat,
        scales,
        mass,
        attended_sum,
        pooled,
        all_reports,
    ) = call(
        slide_forward,
        [
            ((width, length), bf16, "far"),
            ((heads, 3, HEAD, length), f32, "far"),
            ((heads, length, length), f32, "far"),
            ((2, length), f32),
            ((heads, 2, length), f32),
            ((heads, length), f32),
            ((1, inner), f32),
            ((parts, 1, width), f32),
            ((parts, owners, block), bf16),
        ],
        valid,
        w_query.T,
        w_key.T,
        w_value.T,
        w_out,
        *pieces,
        scalars=(here,),
        scratch=[
            ((width, length), bf16),
            ((width, length), bf16),
            ((heads, 3, HEAD, length), f32),
            ((heads, length, length), f32),
            1 + 2 * heads,
        ],
        limit=60,
    )
    pooled = exchange(pooled, "mp")
    (row,) = call(
        logits_row,
        [((owners, 1, 128), f32)],
        pooled,
        all_reports,
        scratch=[((owners, width), f32)],
    )
    logits = exchange(row, DP).reshape(owners, 128)
    loss, grad, up, grads, sending = call(
        slide_backward,
        [((1, 1), f32), ((1, width), f32), ((1, inner), f32), ((3 * inner, length), bf16)]
        + [((parts, block + EXTRA, length), bf16)],
        logits,
        slide_pair[:, None],
        pooled,
        all_reports,
        valid,
        scales,
        mass,
        w_out,
        by_head,
        attention,
        w_query,
        w_key,
        w_value,
        slide_norm,
        scalars=(owner,),
        far=tuple(range(7, 14)),
        scratch=[
            (w_out.shape, bf16),
            (by_head.shape, f32),
            (attention.shape, f32),
            (w_query.shape, bf16),
            (w_key.shape, bf16),
            (w_value.shape, bf16),
            (slide_norm.shape, bf16),
            ((owners, width), f32),
            7,
        ],
        limit=60,
    )
    received = exchange(sending, "mp")

    (wide_sent,) = call(
        wide_other,
        [((chips, share, 2 * inner), bf16)],
        slide_norm,
        grads,
        scalars=(1 - core,),
    )
    wide_got = lax.ppermute(wide_sent, "core", [(0, 1), (1, 0)])
    along = call(
        wide_own,
        [((lines, share, 2 * inner), bf16)] * side,
        slide_norm,
        grads,
        wide_got,
        scalars=(core, column),
    )
    def shift(values, axis):
        return [values[0]] + [
            lax.ppermute(values[k], axis, turn(len(values), k)) for k in range(1, len(values))
        ]

    along = shift(along, "column")
    across = call(
        wide_line, [((share, 2 * inner), bf16)] * lines, *along, scalars=(line,)
    )
    across = shift(across, "line")
    grad_wide = sum(part.astype(f32) for part in across)
    value_rows = contract(mass.astype(bf16), slide_norm, 1, 1)
    extra = jnp.concatenate(
        [
            value_rows.reshape(heads, owners, share).transpose(1, 0, 2).reshape(owners, -1),
            grad.reshape(owners, share),
            jnp.broadcast_to(up, (owners, inner)),
            jnp.broadcast_to(attended_sum, (owners, inner)),
        ],
        1,
    ).astype(bf16)
    spare = ROWS - capacity
    extra = jnp.pad(extra, ((0, 0), (0, spare * block - extra.shape[1])))
    extra = extra.reshape(owners, spare, block)
    extra = jnp.pad(extra, ((0, 0), (capacity, 0), (0, 0))).reshape(slots, block)

    own_grad = lax.dynamic_slice_in_dim(grad, here * block, block, 1).reshape(block, 1)
    (going,) = call(
        slot_grads,
        [((slots, block), bf16)],
        own_grad,
        valid,
        stat,
        chunk,
        select,
        extra,
        received,
        anchors=(grad_wide,),
    )
    back = exchange(going.reshape(owners, ROWS, block), DP).reshape(slots, block)
    (spreading,) = call(tile_grads, [((parts,) + packed, bf16)], back, dispatch)

    size = (chips, share, units)
    swap = [(0, 1), (1, 0)]
    grad_embedding, two_sent = call(
        other_two,
        [((width, tiles), bf16), (size, bf16)],
        hidden,
        exchange(spreading, "mp"),
        scalars=(1 - core,),
    )
    two_got = lax.ppermute(two_sent, "core", swap)
    grad_hidden, one_sent = call(
        other_one,
        [((units, tiles), bf16), (size, bf16)],
        w_two,
        slope,
        tile_other,
        grad_embedding,
    )
    one_got = lax.ppermute(one_sent, "core", swap)
    (across,) = call(
        own_two,
        [((lines, side, share, units), bf16)],
        hidden,
        grad_embedding,
        two_got,
        scalars=(core,),
    )
    across = exchange(across, "line")
    along = call(
        own_one,
        [((lines, share, units), bf16)] * side,
        tile_own,
        grad_hidden,
        one_got,
        scalars=(column,),
        scratch=[((side, lines, share, units), bf16)],
    )
    (one_lines,) = call(
        half_way_one, [((lines, share, units), bf16)], *shift(along, "column")
    )
    two_columns = call(
        half_way_two, [((share, units), bf16)] * side, across, scalars=(column,)
    )
    grad_one, grad_two = call(
        last_sums,
        [((share, units), f32)] * 2,
        exchange(one_lines, "line"),
        *shift(two_columns, "column"),
    )
    grad_two = grad_two.T

    terms = back.reshape(owners, ROWS, block)[:, capacity:].reshape(owners, -1).astype(f32)
    edge = heads * share
    from_values = terms[:, :edge].reshape(owners, heads, share)
    from_grads = terms[:, edge : edge + share]
    edge = edge + share
    from_up = terms[:, edge : edge + inner].reshape(owners, heads, HEAD)
    edge = edge + inner
    from_attended = terms[:, edge : edge + inner]
    grad_value = jnp.einsum("ohs,ohd->shd", from_values, from_up, precision=exact)
    grad_value = grad_value.reshape(share, inner)
    grad_out = contract(from_attended, from_grads, 0, 0, precision=exact)
    return (
        loss[0, 0],
        grad_one,
        grad_two,
        grad_wide[:, :inner],
        grad_wide[:, inner:],
        grad_value,
        grad_out,
    )


def solution(mesh):
    owners, parts = mesh.devices.shape
    side = math.isqrt(owners // CORES)
    split = Mesh(
        mesh.devices.reshape(owners // CORES // side, side, CORES, parts),
        ("line", "column", "core", "mp"),
    )
    return jax.shard_map(
        per_device,
        mesh=split,
        in_specs=(
            P(DP, None),
            P(DP, None),
            P(),
            P(DP, None),
            P(None, "mp"),
            P("mp", None),
            P(None, "mp"),
            P(None, "mp"),
            P(None, "mp"),
            P("mp", None),
        ),
        out_specs=(
            P(),
            P(DP, "mp"),
            P("mp", DP),
            P(DP, "mp"),
            P(DP, "mp"),
            P(DP, "mp"),
            P("mp", DP),
        ),
        check_vma=False,
    )
```

```python
import math

import jax
import jax.numpy as jnp
from jax import lax
from jax.experimental import pallas as pl
from jax.experimental.pallas import tpu as pltpu
from jax.sharding import Mesh, PartitionSpec as P

HEAD = 96
CORES = 2
ROWS = 16
EXTRA = 16

eps = 1e-05
contrast_divisor_factor = 0.07
score_scale = 10.0
loss_scale = 4096.0
exact = lax.Precision.HIGHEST
f32 = jnp.float32
bf16 = jnp.bfloat16
i32 = jnp.int32
DP = ("line", "column", "core")


def contract(left, right, left_dim, right_dim, **kw):
    return lax.dot_general(
        left, right, (((left_dim,), (right_dim,)), ((), ())), preferred_element_type=f32, **kw
    )


def exchange(values, axis):
    return lax.all_to_all(values, axis, 0, 0, tiled=True)


def pick(values, index, axis):
    return lax.dynamic_index_in_dim(values, index, axis, keepdims=False)


def call(body, outs, *args, scalars=(), scratch=(), anchors=(), far=(), limit=16):
    count = len(scalars)
    skip = len(anchors)
    vmem = pl.BlockSpec(memory_space=pltpu.VMEM)
    away = pl.BlockSpec(memory_space=pltpu.HBM)

    def kernel(*refs):
        body(*refs[skip:])

    return pl.pallas_call(
        kernel if skip else body,
        out_shape=[jax.ShapeDtypeStruct(out[0], out[1]) for out in outs],
        in_specs=[pl.BlockSpec(memory_space=pl.ANY)] * skip
        + [pl.BlockSpec(memory_space=pltpu.SMEM)] * count
        + [away if index in far else vmem for index in range(len(args))],
        out_specs=[vmem if len(out) == 2 else away for out in outs],
        scratch_shapes=[
            pltpu.VMEM(*part) if isinstance(part, tuple) else pltpu.SemaphoreType.DMA((part,))
            for part in scratch
        ],
        compiler_params=pltpu.CompilerParams(vmem_limit_bytes=limit * 1024 * 1024),
    )(*anchors, *[jnp.reshape(s, (1,)).astype(i32) for s in scalars], *args)


def fetch(sources, targets, semaphores):
    copies = [
        pltpu.make_async_copy(source, target, semaphores.at[index])
        for index, (source, target) in enumerate(zip(sources, targets))
    ]
    for copy in copies:
        copy.start()
    return copies


def turn(count, step):
    return [(index, (index + step) % count) for index in range(count)]


def gather_ring(piece, count):
    found = [piece]
    back = ahead = piece
    for _ in range(count // 2 - 1):
        back = lax.ppermute(back, "mp", turn(count, 1))
        ahead = lax.ppermute(ahead, "mp", turn(count, count - 1))
        found += [back, ahead]
    half = (piece.shape[0] // 2 + ROWS - 1) // ROWS * ROWS
    found.append(lax.ppermute(back[:half], "mp", turn(count, 1)))
    found.append(lax.ppermute(ahead[half:], "mp", turn(count, count - 1)))
    return found


def place(refs, here, count, store):
    half = count // 2
    store(here, refs[0][...])
    for step in range(1, half):
        for ref, sign in ((refs[2 * step - 1], -1), (refs[2 * step], 1)):
            store(lax.rem(here + sign * step + count, count), ref[...])
    store(
        lax.rem(here + half, count), jnp.concatenate([refs[-2][...], refs[-1][...]], 0)
    )


def pack(square):
    half = square.shape[0] // 2
    side = square[:, 128:]
    return jnp.concatenate(
        [square[:, :128], jnp.concatenate([side[:half], side[half:]], 1)], 0
    )


def unpack(packed):
    rows = packed.shape[0] // 3 * 2
    side = packed[rows:]
    return jnp.concatenate(
        [packed[:rows], jnp.concatenate([side[:, :64], side[:, 64:]], 0)], 1
    )


def tile_forward(
    far_x, far_one, far_two, norm_ref, hidden_ref, slope_ref, out_ref, x_ref, one_ref, two_ref, sems
):
    copies = fetch((far_x, far_one, far_two), (x_ref, one_ref, two_ref), sems)
    copies[0].wait()
    x = x_ref[...].astype(f32)
    centred = x - jnp.mean(x, -1, keepdims=True)
    normed = centred * lax.rsqrt(jnp.mean(centred * centred, -1, keepdims=True) + eps)
    normed = normed.astype(bf16)
    norm_ref[...] = normed
    copies[1].wait()
    pre = jnp.dot(normed, one_ref[...], preferred_element_type=f32)
    bell = 0.5 * (1.0 + lax.erf(pre * 0.7071067811865476))
    hidden = (pre * bell).astype(bf16)
    hidden_ref[...] = hidden
    slope_ref[...] = bell + pre * jnp.exp(-0.5 * pre * pre) * 0.3989422804014327
    copies[2].wait()
    partial = jnp.dot(hidden, two_ref[...], preferred_element_type=f32).astype(bf16)
    count = out_ref.shape[0]
    block = partial.shape[1] // count
    for j in range(count):
        out_ref[j] = pack(partial[:, j * block : (j + 1) * block])


def tile_dispatch(own_ref, report_ref, dispatch_ref, flags_ref, parts_ref, out_ref):
    total = parts_ref[0].astype(f32)
    for j in range(1, parts_ref.shape[0]):
        total = total + parts_ref[j].astype(f32)
    embedding = (own_ref[...].astype(f32) + unpack(total)).astype(bf16)
    rows = jnp.dot(dispatch_ref[...], embedding, preferred_element_type=f32)
    slot = lax.broadcasted_iota(i32, rows.shape, 0)
    rows = jnp.where(lax.rem(slot, ROWS) == ROWS - 1, report_ref[...].astype(f32), rows)
    out_ref[...] = jnp.concatenate([rows.astype(bf16), flags_ref[...]], 1)


def slot_rows(arrived_ref, select_ref, report_select_ref, chunk_ref, valid_ref):
    arrived = arrived_ref[...]
    chunk = contract(arrived, select_ref[...], 0, 0)
    block = chunk_ref.shape[0] - EXTRA
    chunk_ref[0:block, :] = chunk[:block].astype(bf16)
    valid_ref[...] = chunk[block : block + 1]
    reports = jnp.dot(report_select_ref[...], arrived, preferred_element_type=f32)
    reports = reports[:, :block].astype(bf16)
    chunk_ref[block : block + EXTRA, :] = jnp.concatenate(
        [reports[:EXTRA], reports[EXTRA:]], 1
    )


def slide_forward(
    here,
    valid_ref,
    far_query_weights,
    far_key_weights,
    far_value_weights,
    far_out_weights,
    *rest,
):
    pieces = rest[:9]
    (
        far_norm,
        far_heads,
        far_attention,
        stat_ref,
        scale_ref,
        mass_ref,
        attended_ref,
        pooled_ref,
        reports_ref,
        slide_ref,
        norm_ref,
        heads_ref,
        attention_ref,
        query_weights_ref,
        key_weights_ref,
        value_weights_ref,
        out_weights_ref,
        weight_sems,
        sems,
    ) = rest[9:]
    fetched = fetch(
        (far_query_weights, far_key_weights, far_value_weights, far_out_weights),
        (query_weights_ref, key_weights_ref, value_weights_ref, out_weights_ref),
        weight_sems,
    )
    count, owners, block = reports_ref.shape

    def store(index, piece):
        start = pl.multiple_of(index * block, 16)
        slide_ref[pl.ds(start, block), :] = piece[:block]
        reports = piece[block:]
        reports_ref[index] = jnp.concatenate([reports[:, :block], reports[:, block:]], 0)

    place(pieces, here[0], count, store)
    valid = valid_ref[...]
    valid_low = valid.astype(bf16)
    low = slide_ref[...]
    slide = low.astype(f32)
    mean = jnp.mean(slide, 0, keepdims=True)
    centred = slide - mean
    inverse = lax.rsqrt(jnp.mean(centred * centred, 0, keepdims=True) + eps)
    stat_ref[...] = jnp.concatenate([mean, inverse], 0)
    normed = (centred * inverse).astype(bf16)
    norm_ref[...] = normed
    copies = [pltpu.make_async_copy(norm_ref, far_norm, sems.at[0])]
    copies[0].start()
    for copy in fetched:
        copy.wait()
    all_query = jnp.dot(query_weights_ref[...], normed, preferred_element_type=f32)
    all_keys = jnp.dot(key_weights_ref[...], normed, preferred_element_type=f32)
    all_values = jnp.dot(value_weights_ref[...], normed, preferred_element_type=f32)
    heads = all_query.shape[0] // HEAD
    attended = []
    for h in range(heads):
        low_rows, high_rows = h * HEAD, (h + 1) * HEAD
        query = all_query[low_rows:high_rows]
        keys = all_keys[low_rows:high_rows]
        values = all_values[low_rows:high_rows]
        query_scale = lax.rsqrt(jnp.mean(query * query, 0, keepdims=True) + eps)
        key_scale = lax.rsqrt(jnp.mean(keys * keys, 0, keepdims=True) + eps)
        query_unit = query * query_scale
        key_unit = keys * key_scale
        heads_ref[h, 0] = query_unit
        heads_ref[h, 1] = key_unit
        heads_ref[h, 2] = values
        copies.append(pltpu.make_async_copy(heads_ref.at[h], far_heads.at[h], sems.at[1 + 2 * h]))
        copies[-1].start()
        scale_ref[h] = jnp.concatenate([query_scale, key_scale], 0)
        scores = contract(query_unit.astype(bf16), key_unit.astype(bf16), 0, 0)
        weights = jnp.exp(scores * (score_scale / HEAD)) * valid
        weights = weights * (1.0 / jnp.sum(weights, 1, keepdims=True))
        attention_ref[h] = weights
        copies.append(
            pltpu.make_async_copy(attention_ref.at[h], far_attention.at[h], sems.at[2 + 2 * h])
        )
        copies[-1].start()
        weights_low = weights.astype(bf16)
        mass_ref[h : h + 1, :] = jnp.dot(valid_low, weights_low, preferred_element_type=f32)
        attended.append(contract(values.astype(bf16), weights_low, 1, 1))
    attended = jnp.concatenate(attended, 0).astype(bf16)
    attended_sum = contract(valid_low, attended, 1, 1)
    attended_ref[...] = attended_sum
    high = attended_sum.astype(bf16)
    rest_low = (attended_sum - high.astype(f32)).astype(bf16)
    part = jnp.dot(high, out_weights_ref[...], preferred_element_type=f32)
    part = part + jnp.dot(rest_low, out_weights_ref[...], preferred_element_type=f32)
    slide_sum = contract(valid_low, low, 1, 1)
    pooled = (part + slide_sum * (1.0 / count)) / jnp.sum(valid)
    pooled_ref[...] = jnp.broadcast_to(pooled[None], pooled_ref.shape)
    for copy in copies:
        copy.wait()


def unit_vectors(parts_ref, reports_ref, report_ref):
    pooled = jnp.sum(parts_ref[...], 0)
    inverse = lax.rsqrt(jnp.sum(pooled * pooled, -1, keepdims=True) + eps)
    count, owners, block = reports_ref.shape
    squares = jnp.zeros((owners, 1), f32)
    for j in range(count):
        reports = reports_ref[j].astype(f32)
        report_ref[:, j * block : (j + 1) * block] = reports
        squares = squares + jnp.sum(reports * reports, -1, keepdims=True)
    report = report_ref[...] * lax.rsqrt(squares + eps)
    return pooled * inverse, inverse, report


def logits_row(parts_ref, reports_ref, row_ref, report_ref):
    unit, inverse, report = unit_vectors(parts_ref, reports_ref, report_ref)
    row = contract(unit, report, 1, 1, precision=exact) / contrast_divisor_factor
    pad = row_ref.shape[2] - row.shape[1]
    row = jnp.concatenate([row, jnp.zeros((1, pad), f32)], 1)
    row_ref[...] = jnp.broadcast_to(row[None], row_ref.shape)


def slide_backward(
    owner,
    logits_ref,
    pair_ref,
    parts_ref,
    reports_ref,
    valid_ref,
    scale_ref,
    mass_ref,
    far_out_weights,
    far_heads,
    far_attention,
    far_query_weights,
    far_key_weights,
    far_value_weights,
    far_norm,
    loss_ref,
    grad_ref,
    up_ref,
    grads_ref,
    far_out,
    *rest,
):
    fetched, report_ref, out_ref, sems, out_sems = rest[:-4], *rest[-4:]
    (
        out_weights_ref,
        heads_ref,
        attention_ref,
        query_weights_ref,
        key_weights_ref,
        value_weights_ref,
        norm_ref,
    ) = fetched
    copies = fetch(
        (
            far_out_weights,
            far_heads,
            far_attention,
            far_query_weights,
            far_key_weights,
            far_value_weights,
            far_norm,
        ),
        fetched,
        sems,
    )
    unit, inverse, report = unit_vectors(parts_ref, reports_ref, report_ref)
    owners = report.shape[0]
    valid = valid_ref[...]
    logits = logits_ref[...]
    shape = logits.shape
    columns = lax.broadcasted_iota(i32, shape, 1)
    rows = lax.broadcasted_iota(i32, shape, 0)
    real = columns < owners
    expo = jnp.where(real, jnp.exp(logits), 0.0)
    row_total = jnp.sum(expo, 1, keepdims=True)
    column_total = jnp.where(real[:1], jnp.sum(expo, 0, keepdims=True), 1.0)
    target = jnp.where(pair_ref[...] == columns, 1.0, 0.0)
    loss = jnp.sum(
        0.5 * jnp.log(row_total) - jnp.sum(logits * target, 1, keepdims=True), 0, keepdims=True
    )
    loss = loss + 0.5 * jnp.sum(jnp.log(column_total), 1, keepdims=True)
    loss_ref[...] = loss * (1.0 / owners)
    grad_logits = (0.5 * expo / row_total + 0.5 * expo / column_total - target) * (
        loss_scale / owners
    )
    grad_row = jnp.sum(jnp.where(rows == owner[0], grad_logits, 0.0), 0, keepdims=True)
    grad_unit = (
        jnp.dot(grad_row[:, :owners], report, precision=exact, preferred_element_type=f32)
        / contrast_divisor_factor
    )
    grad_pooled = (grad_unit - unit * jnp.sum(unit * grad_unit, -1, keepdims=True)) * inverse
    grad = grad_pooled / jnp.sum(valid)
    grad_ref[...] = grad
    low = grad.astype(bf16)
    copies[0].wait()
    out_weights = out_weights_ref[...]
    up_ref[...] = contract(low, out_weights, 1, 1)
    up = jnp.sum(out_weights.astype(f32) * low.astype(f32), 1, keepdims=True)
    heads = heads_ref.shape[0]
    inner = heads * HEAD
    copies[1].wait()
    copies[2].wait()
    for h in range(heads):
        up_head = up[h * HEAD : (h + 1) * HEAD]
        values = heads_ref[h, 2]
        weights = attention_ref[h]
        pull = jnp.sum(up_head * values, 0, keepdims=True)
        pull_mean = jnp.sum(weights * pull, 1, keepdims=True)
        grad_scores = (weights * (pull - pull_mean) * (score_scale / HEAD)).astype(bf16)
        query_unit = heads_ref[h, 0]
        key_unit = heads_ref[h, 1]
        grad_query = contract(key_unit.astype(bf16), grad_scores, 1, 1) * valid
        grad_key = jnp.dot(query_unit.astype(bf16), grad_scores, preferred_element_type=f32)
        grad_query = scale_ref[h, 0:1] * (
            grad_query - query_unit * jnp.mean(query_unit * grad_query, 0, keepdims=True)
        )
        grad_key = scale_ref[h, 1:2] * (
            grad_key - key_unit * jnp.mean(key_unit * grad_key, 0, keepdims=True)
        )
        grad_value = up_head * mass_ref[h : h + 1]
        for part, values in enumerate((grad_query, grad_key, grad_value)):
            start = part * inner + h * HEAD
            grads_ref[start : start + HEAD, :] = values.astype(bf16)
    grad_query = grads_ref[0:inner, :]
    grad_key = grads_ref[inner : 2 * inner, :]
    grad_value = grads_ref[2 * inner : 3 * inner, :]
    for copy in copies[3:]:
        copy.wait()
    count = out_ref.shape[0]
    block = norm_ref.shape[0] // count
    sending = []
    first = jnp.zeros_like(valid)
    second = jnp.zeros_like(valid)
    for k in range(count):
        rows = slice(k * block, (k + 1) * block)
        part = jnp.dot(query_weights_ref[rows, :], grad_query, preferred_element_type=f32)
        part = part + jnp.dot(key_weights_ref[rows, :], grad_key, preferred_element_type=f32)
        part = part + jnp.dot(value_weights_ref[rows, :], grad_value, preferred_element_type=f32)
        out_ref[k, 0:block, :] = part.astype(bf16)
        sending.append(
            pltpu.make_async_copy(
                out_ref.at[k, pl.ds(0, block)], far_out.at[k, pl.ds(0, block)], out_sems.at[k]
            )
        )
        sending[-1].start()
        first = first + jnp.sum(part, 0, keepdims=True)
        second = second + jnp.sum(part * norm_ref[rows, :].astype(f32), 0, keepdims=True)
    width = norm_ref.shape[0]
    stats = jnp.concatenate([first, second], 0) * (1.0 / width)
    high = stats.astype(bf16).astype(f32)
    stats = jnp.concatenate(
        [high, stats - high, jnp.zeros((EXTRA - 4, stats.shape[1]), f32)], 0
    ).astype(bf16)
    for k in range(count):
        out_ref[k, block : block + EXTRA, :] = stats
        tail = pl.ds(block, EXTRA)
        sending.append(
            pltpu.make_async_copy(out_ref.at[k, tail], far_out.at[k, tail], out_sems.at[count + k])
        )
        sending[-1].start()
    for copy in sending:
        copy.wait()


def wide_other(which, norm_ref, grads_ref, out_ref):
    chips, share, columns = out_ref.shape
    rows = [
        norm_ref[pl.ds(pl.multiple_of((CORES * chip + which[0]) * share, 16), share), :]
        for chip in range(chips)
    ]
    values = contract(jnp.concatenate(rows, 0), grads_ref[0:columns, :], 1, 1).astype(bf16)
    for chip in range(chips):
        out_ref[chip] = values[chip * share : (chip + 1) * share]


def wide_own(which, column, norm_ref, grads_ref, got_ref, *outs):
    side = len(outs)
    lines, share, columns = outs[0].shape
    chips = [
        line * side + lax.rem(column[0] + k, side) for k in range(side) for line in range(lines)
    ]
    rows = [
        norm_ref[pl.ds(pl.multiple_of((CORES * chip + which[0]) * share, 16), share), :]
        for chip in chips
    ]
    values = contract(jnp.concatenate(rows, 0), grads_ref[0:columns, :], 1, 1)
    for index, chip in enumerate(chips):
        part = values[index * share : (index + 1) * share] + got_ref[chip].astype(f32)
        outs[index // lines][index % lines] = part.astype(bf16)


def wide_line(line, *refs):
    side = len(refs) // 2
    for k in range(side):
        row = lax.rem(line[0] + k, side)
        total = refs[0][row].astype(f32)
        for ref in refs[1:side]:
            total = total + ref[row].astype(f32)
        refs[side + k][...] = total.astype(bf16)


def slot_grads(
    own_ref, valid_ref, stat_ref, chunk_ref, select_ref, extra_ref, parts_ref, out_ref
):
    total = parts_ref[0].astype(f32)
    for j in range(1, parts_ref.shape[0]):
        total = total + parts_ref[j].astype(f32)
    block = chunk_ref.shape[0] - EXTRA
    first = total[block : block + 1] + total[block + 2 : block + 3]
    second = total[block + 1 : block + 2] + total[block + 3 : block + 4]
    mean = stat_ref[0:1]
    inverse = stat_ref[1:2]
    normed = (chunk_ref[0:block, :].astype(f32) - mean) * inverse
    rows = own_ref[...] * valid_ref[...] + (total[:block] - first - normed * second) * inverse
    rows = contract(select_ref[...], rows.astype(bf16), 1, 1).astype(bf16)
    out_ref[...] = rows + extra_ref[...]


def tile_grads(back_ref, dispatch_ref, out_ref):
    piece = pack(contract(back_ref[...], dispatch_ref[...], 0, 0).astype(bf16))
    out_ref[...] = jnp.broadcast_to(piece[None], out_ref.shape)


def rows_of(which, ref, chips, share):
    rows = [
        ref[pl.ds(pl.multiple_of((CORES * chip + which) * share, 16), share), :]
        for chip in range(chips)
    ]
    return jnp.concatenate(rows, 0)


def other_two(other, hidden_ref, parts_ref, grad_ref, out_ref):
    count = parts_ref.shape[0]
    rows = grad_ref.shape[0] // count
    for j in range(count):
        grad_ref[j * rows : (j + 1) * rows, :] = unpack(parts_ref[j])
    chips, share = out_ref.shape[:2]
    rows = rows_of(other[0], grad_ref, chips, share)
    two = jnp.dot(rows, hidden_ref[...], preferred_element_type=f32).astype(bf16)
    for chip in range(chips):
        out_ref[chip] = two[chip * share : (chip + 1) * share]


def both_one(
    two_ref, slope_ref, other_norm_ref, own_norm_ref, grad_ref, out_ref, own_ref, hidden_grad_ref
):
    grad_hidden = jnp.dot(two_ref[...], grad_ref[...], preferred_element_type=f32)
    hidden_grad_ref[...] = (grad_hidden * slope_ref[...]).astype(bf16)
    chips, share = out_ref.shape[:2]
    for norm_ref, target_ref in ((other_norm_ref, out_ref), (own_norm_ref, own_ref)):
        one = contract(norm_ref[...], hidden_grad_ref[...], 1, 1).astype(bf16)
        for chip in range(chips):
            target_ref[chip] = one[chip * share : (chip + 1) * share]


def own_two(own, column, hidden_ref, grad_ref, got_ref, *rest):
    outs, two_ref = rest[:-1], rest[-1]
    chips, share = got_ref.shape[:2]
    side = len(outs)
    rows = rows_of(own[0], grad_ref, chips, share)
    two = jnp.dot(rows, hidden_ref[...], preferred_element_type=f32)
    for chip in range(chips):
        part = two[chip * share : (chip + 1) * share] + got_ref[chip].astype(f32)
        two_ref[chip % side, chip // side] = part.astype(bf16)
    for k in range(side):
        outs[k][...] = two_ref[lax.rem(column[0] + k, side)]


def own_one(own_ref, got_ref, out_ref):
    side = out_ref.shape[1]
    for chip in range(got_ref.shape[0]):
        part = own_ref[chip].astype(f32) + got_ref[chip].astype(f32)
        out_ref[chip // side, chip % side] = part.astype(bf16)


def add_up(*refs):
    total = refs[0][...].astype(f32)
    for ref in refs[1:-1]:
        total = total + ref[...].astype(f32)
    refs[-1][...] = total.astype(refs[-1].dtype)


def add_lines(column, lines_ref, *outs):
    side = len(outs)
    for k in range(side):
        place = lax.rem(column[0] + k, side)
        total = lines_ref[0, place].astype(f32)
        for line in range(1, lines_ref.shape[0]):
            total = total + lines_ref[line, place].astype(f32)
        outs[k][...] = total.astype(bf16)


def last_sums(lines_ref, *refs):
    one_ref, two_ref = refs[-2:]
    total = lines_ref[0].astype(f32)
    for line in range(1, lines_ref.shape[0]):
        total = total + lines_ref[line].astype(f32)
    two_ref[...] = total
    total = refs[0][...].astype(f32)
    for ref in refs[1:-2]:
        total = total + ref[...].astype(f32)
    one_ref[...] = total


def per_device(
    tile_features, tile_slide, slide_pair, reports, w_one, w_two, w_query, w_key, w_value, w_out
):
    lines = lax.axis_size("line")
    side = lax.axis_size("column")
    line = lax.axis_index("line")
    column = lax.axis_index("column")
    chips = lines * side
    owners = chips * CORES
    parts = lax.axis_size("mp")
    core = lax.axis_index("core")
    owner = lax.axis_index(DP)
    here = lax.axis_index("mp")
    tiles, width = tile_features.shape
    units = w_one.shape[1]
    capacity = 2 * tiles // owners
    length = owners * capacity
    slots = owners * ROWS
    block = width // parts
    share = width // owners
    inner = w_query.shape[1]
    heads = inner // HEAD
    packed = (block // 2 * 3, 128)

    def halves(values):
        rest = values.shape[1:]
        values = values.reshape((chips, CORES, share) + rest)
        own = pick(values, core, 1).reshape((chips * share,) + rest)
        other = pick(values, 1 - core, 1).reshape((chips * share,) + rest)
        return own, other

    tile_norm, hidden, slope, partial = call(
        tile_forward,
        [
            ((tiles, width), bf16),
            ((tiles, units), bf16),
            ((tiles, units), f32),
            ((parts,) + packed, bf16),
        ],
        tile_features,
        w_one,
        w_two,
        far=(0, 1, 2),
        scratch=[
            (tile_features.shape, bf16),
            (w_one.shape, bf16),
            (w_two.shape, bf16),
            3,
        ],
        limit=62,
    )
    partial = exchange(partial, "mp")

    slide_ids = tile_slide[:, 0]
    matches = (slide_ids[:, None] == jnp.arange(owners, dtype=i32)[None, :]).astype(i32)
    ordinal = jnp.sum(matches * (jnp.cumsum(matches, 0) - 1), 1)
    position = slide_ids * ROWS + ordinal
    dispatch = jnp.arange(slots, dtype=i32)[:, None] == position[None, :]
    flags = jnp.sum(dispatch.astype(f32), 1, keepdims=True).astype(bf16)
    flags = jnp.pad(flags, ((0, 0), (0, 256 - block - 1)))
    dispatch = dispatch.astype(bf16)
    slot = jnp.arange(slots, dtype=i32)
    row_of_slot = jnp.where(slot % ROWS < capacity, slot // ROWS * capacity + slot % ROWS, -1)
    select = (row_of_slot[:, None] == jnp.arange(length, dtype=i32)[None, :]).astype(bf16)
    last_slot = jnp.arange(owners, dtype=i32)[:, None] * ROWS + ROWS - 1
    report_select = (last_slot == slot[None, :]).astype(bf16)
    own_columns = pick(tile_features.reshape(tiles, parts, block), here, 1)
    own_report = pick(reports.reshape(1, parts, block), here, 1)
    tile_own, tile_other = halves(tile_norm.T)
    slope = slope.T

    (outgoing,) = call(
        tile_dispatch,
        [((slots, 256), bf16)],
        own_columns,
        own_report,
        dispatch,
        flags,
        partial,
        anchors=(select, report_select, tile_own, tile_other, slope),
    )
    arrived = exchange(outgoing.reshape(owners, ROWS, 256), DP).reshape(slots, 256)
    chunk, valid = call(
        slot_rows,
        [((block + EXTRA, length), bf16), ((1, length), f32)],
        arrived,
        select,
        report_select,
    )
    pieces = gather_ring(chunk, parts)

    (
        slide_norm,
        by_head,
        attention,
        stat,
        scales,
        mass,
        attended_sum,
        pooled,
        all_reports,
    ) = call(
        slide_forward,
        [
            ((width, length), bf16, "far"),
            ((heads, 3, HEAD, length), f32, "far"),
            ((heads, length, length), f32, "far"),
            ((2, length), f32),
            ((heads, 2, length), f32),
            ((heads, length), f32),
            ((1, inner), f32),
            ((parts, 1, width), f32),
            ((parts, owners, block), bf16),
        ],
        valid,
        w_query.T,
        w_key.T,
        w_value.T,
        w_out,
        *pieces,
        scalars=(here,),
        far=(1, 2, 3, 4),
        scratch=[
            ((width, length), bf16),
            ((width, length), bf16),
            ((heads, 3, HEAD, length), f32),
            ((heads, length, length), f32),
            ((inner, width), bf16),
            ((inner, width), bf16),
            ((inner, width), bf16),
            ((inner, width), bf16),
            4,
            1 + 2 * heads,
        ],
        limit=60,
    )
    pooled = exchange(pooled, "mp")
    (row,) = call(
        logits_row,
        [((owners, 1, 128), f32)],
        pooled,
        all_reports,
        scratch=[((owners, width), f32)],
    )
    logits = exchange(row, DP).reshape(owners, 128)
    loss, grad, up, grads, sending = call(
        slide_backward,
        [((1, 1), f32), ((1, width), f32), ((1, inner), f32), ((3 * inner, length), bf16)]
        + [((parts, block + EXTRA, length), bf16, "far")],
        logits,
        slide_pair[:, None],
        pooled,
        all_reports,
        valid,
        scales,
        mass,
        w_out,
        by_head,
        attention,
        w_query,
        w_key,
        w_value,
        slide_norm,
        scalars=(owner,),
        far=tuple(range(7, 14)),
        scratch=[
            (w_out.shape, bf16),
            (by_head.shape, f32),
            (attention.shape, f32),
            (w_query.shape, bf16),
            (w_key.shape, bf16),
            (w_value.shape, bf16),
            (slide_norm.shape, bf16),
            ((owners, width), f32),
            ((parts, block + EXTRA, length), bf16),
            7,
            2 * parts,
        ],
        limit=60,
    )
    received = exchange(sending, "mp")

    (wide_sent,) = call(
        wide_other,
        [((chips, share, 2 * inner), bf16)],
        slide_norm,
        grads,
        scalars=(1 - core,),
    )
    wide_got = lax.ppermute(wide_sent, "core", [(0, 1), (1, 0)])
    along = call(
        wide_own,
        [((lines, share, 2 * inner), bf16)] * side,
        slide_norm,
        grads,
        wide_got,
        scalars=(core, column),
    )
    def shift(values, axis):
        return [values[0]] + [
            lax.ppermute(values[k], axis, turn(len(values), k)) for k in range(1, len(values))
        ]

    along = shift(along, "column")
    across = call(
        wide_line, [((share, 2 * inner), bf16)] * lines, *along, scalars=(line,)
    )
    across = shift(across, "line")
    grad_wide = sum(part.astype(f32) for part in across)
    value_rows = contract(mass.astype(bf16), slide_norm, 1, 1)
    extra = jnp.concatenate(
        [
            value_rows.reshape(heads, owners, share).transpose(1, 0, 2).reshape(owners, -1),
            grad.reshape(owners, share),
            jnp.broadcast_to(up, (owners, inner)),
            jnp.broadcast_to(attended_sum, (owners, inner)),
        ],
        1,
    ).astype(bf16)
    spare = ROWS - capacity
    extra = jnp.pad(extra, ((0, 0), (0, spare * block - extra.shape[1])))
    extra = extra.reshape(owners, spare, block)
    extra = jnp.pad(extra, ((0, 0), (capacity, 0), (0, 0))).reshape(slots, block)

    own_grad = lax.dynamic_slice_in_dim(grad, here * block, block, 1).reshape(block, 1)
    (going,) = call(
        slot_grads,
        [((slots, block), bf16)],
        own_grad,
        valid,
        stat,
        chunk,
        select,
        extra,
        received,
        anchors=(grad_wide,),
    )
    back = exchange(going.reshape(owners, ROWS, block), DP).reshape(slots, block)
    (spreading,) = call(tile_grads, [((parts,) + packed, bf16)], back, dispatch)

    size = (chips, share, units)
    swap = [(0, 1), (1, 0)]
    grad_embedding, two_sent = call(
        other_two,
        [((width, tiles), bf16), (size, bf16)],
        hidden,
        exchange(spreading, "mp"),
        scalars=(1 - core,),
    )
    two_got = lax.ppermute(two_sent, "core", swap)
    one_sent, one_own = call(
        both_one,
        [(size, bf16), (size, bf16)],
        w_two,
        slope,
        tile_other,
        tile_own,
        grad_embedding,
        scratch=[((units, tiles), bf16)],
    )
    one_got = lax.ppermute(one_sent, "core", swap)
    two_along = call(
        own_two,
        [((lines, share, units), bf16)] * side,
        hidden,
        grad_embedding,
        two_got,
        scalars=(core, column),
        scratch=[((side, lines, share, units), bf16)],
    )
    two_along = shift(two_along, "column")
    (one_across,) = call(own_one, [((lines, side, share, units), bf16)], one_own, one_got)
    one_across = exchange(one_across, "line")
    (two_across,) = call(add_up, [((lines, share, units), bf16)], *two_along)
    one_along = call(add_lines, [((share, units), bf16)] * side, one_across, scalars=(column,))
    grad_one, grad_two = call(
        last_sums,
        [((share, units), f32)] * 2,
        exchange(two_across, "line"),
        *shift(one_along, "column"),
    )
    grad_two = grad_two.T

    terms = back.reshape(owners, ROWS, block)[:, capacity:].reshape(owners, -1).astype(f32)
    edge = heads * share
    from_values = terms[:, :edge].reshape(owners, heads, share)
    from_grads = terms[:, edge : edge + share]
    edge = edge + share
    from_up = terms[:, edge : edge + inner].reshape(owners, heads, HEAD)
    edge = edge + inner
    from_attended = terms[:, edge : edge + inner]
    grad_value = jnp.einsum("ohs,ohd->shd", from_values, from_up, precision=exact)
    grad_value = grad_value.reshape(share, inner)
    grad_out = contract(from_attended, from_grads, 0, 0, precision=exact)
    return (
        loss[0, 0],
        grad_one,
        grad_two,
        grad_wide[:, :inner],
        grad_wide[:, inner:],
        grad_value,
        grad_out,
    )


def solution(mesh):
    owners, parts = mesh.devices.shape
    side = math.isqrt(owners // CORES)
    split = Mesh(
        mesh.devices.reshape(owners // CORES // side, side, CORES, parts),
        ("line", "column", "core", "mp"),
    )
    return jax.shard_map(
        per_device,
        mesh=split,
        in_specs=(
            P(DP, None),
            P(DP, None),
            P(),
            P(DP, None),
            P(None, "mp"),
            P("mp", None),
            P(None, "mp"),
            P(None, "mp"),
            P(None, "mp"),
            P("mp", None),
        ),
        out_specs=(
            P(),
            P(DP, "mp"),
            P("mp", DP),
            P(DP, "mp"),
            P(DP, "mp"),
            P(DP, "mp"),
            P("mp", DP),
        ),
        check_vma=False,
    )
```

```python
import math

import jax
import jax.numpy as jnp
from jax import lax
from jax.experimental import pallas as pl
from jax.experimental.pallas import tpu as pltpu
from jax.sharding import Mesh, PartitionSpec as P

HEAD = 96
CORES = 2
ROWS = 16
EXTRA = 16

eps = 1e-05
contrast_divisor_factor = 0.07
score_scale = 10.0
loss_scale = 4096.0
exact = lax.Precision.HIGHEST
f32 = jnp.float32
bf16 = jnp.bfloat16
i32 = jnp.int32
DP = ("line", "column", "core")


def contract(left, right, left_dim, right_dim, **kw):
    return lax.dot_general(
        left, right, (((left_dim,), (right_dim,)), ((), ())), preferred_element_type=f32, **kw
    )


def exchange(values, axis):
    return lax.all_to_all(values, axis, 0, 0, tiled=True)


def pick(values, index, axis):
    return lax.dynamic_index_in_dim(values, index, axis, keepdims=False)


def call(body, outs, *args, scalars=(), scratch=(), anchors=(), far=(), limit=16):
    count = len(scalars)
    skip = len(anchors)
    vmem = pl.BlockSpec(memory_space=pltpu.VMEM)
    away = pl.BlockSpec(memory_space=pltpu.HBM)

    def kernel(*refs):
        body(*refs[skip:])

    return pl.pallas_call(
        kernel if skip else body,
        out_shape=[jax.ShapeDtypeStruct(out[0], out[1]) for out in outs],
        in_specs=[pl.BlockSpec(memory_space=pl.ANY)] * skip
        + [pl.BlockSpec(memory_space=pltpu.SMEM)] * count
        + [away if index in far else vmem for index in range(len(args))],
        out_specs=[vmem if len(out) == 2 else away for out in outs],
        scratch_shapes=[
            pltpu.VMEM(*part) if isinstance(part, tuple) else pltpu.SemaphoreType.DMA((part,))
            for part in scratch
        ],
        compiler_params=pltpu.CompilerParams(vmem_limit_bytes=limit * 1024 * 1024),
    )(*anchors, *[jnp.reshape(s, (1,)).astype(i32) for s in scalars], *args)


def fetch(sources, targets, semaphores):
    copies = [
        pltpu.make_async_copy(source, target, semaphores.at[index])
        for index, (source, target) in enumerate(zip(sources, targets))
    ]
    for copy in copies:
        copy.start()
    return copies


def turn(count, step):
    return [(index, (index + step) % count) for index in range(count)]


def gather_ring(piece, count):
    found = [piece]
    back = ahead = piece
    for _ in range(count // 2 - 1):
        back = lax.ppermute(back, "mp", turn(count, 1))
        ahead = lax.ppermute(ahead, "mp", turn(count, count - 1))
        found += [back, ahead]
    half = (piece.shape[0] // 2 + ROWS - 1) // ROWS * ROWS
    found.append(lax.ppermute(back[:half], "mp", turn(count, 1)))
    found.append(lax.ppermute(ahead[half:], "mp", turn(count, count - 1)))
    return found


def place(refs, here, count, store):
    half = count // 2
    store(here, refs[0][...])
    for step in range(1, half):
        for ref, sign in ((refs[2 * step - 1], -1), (refs[2 * step], 1)):
            store(lax.rem(here + sign * step + count, count), ref[...])
    store(
        lax.rem(here + half, count), jnp.concatenate([refs[-2][...], refs[-1][...]], 0)
    )


def pack(square):
    half = square.shape[0] // 2
    side = square[:, 128:]
    return jnp.concatenate(
        [square[:, :128], jnp.concatenate([side[:half], side[half:]], 1)], 0
    )


def unpack(packed):
    rows = packed.shape[0] // 3 * 2
    side = packed[rows:]
    return jnp.concatenate(
        [packed[:rows], jnp.concatenate([side[:, :64], side[:, 64:]], 0)], 1
    )


def tile_forward(
    far_x, far_one, far_two, norm_ref, hidden_ref, slope_ref, out_ref, x_ref, one_ref, two_ref, sems
):
    copies = fetch((far_x, far_one, far_two), (x_ref, one_ref, two_ref), sems)
    copies[0].wait()
    x = x_ref[...].astype(f32)
    centred = x - jnp.mean(x, -1, keepdims=True)
    normed = centred * lax.rsqrt(jnp.mean(centred * centred, -1, keepdims=True) + eps)
    normed = normed.astype(bf16)
    norm_ref[...] = normed
    copies[1].wait()
    pre = jnp.dot(normed, one_ref[...], preferred_element_type=f32)
    bell = 0.5 * (1.0 + lax.erf(pre * 0.7071067811865476))
    hidden = (pre * bell).astype(bf16)
    hidden_ref[...] = hidden
    slope_ref[...] = bell + pre * jnp.exp(-0.5 * pre * pre) * 0.3989422804014327
    copies[2].wait()
    partial = jnp.dot(hidden, two_ref[...], preferred_element_type=f32).astype(bf16)
    count = out_ref.shape[0]
    block = partial.shape[1] // count
    for j in range(count):
        out_ref[j] = pack(partial[:, j * block : (j + 1) * block])


def tile_dispatch(own_ref, report_ref, dispatch_ref, flags_ref, parts_ref, out_ref):
    total = parts_ref[0].astype(f32)
    for j in range(1, parts_ref.shape[0]):
        total = total + parts_ref[j].astype(f32)
    embedding = (own_ref[...].astype(f32) + unpack(total)).astype(bf16)
    rows = jnp.dot(dispatch_ref[...], embedding, preferred_element_type=f32)
    slot = lax.broadcasted_iota(i32, rows.shape, 0)
    rows = jnp.where(lax.rem(slot, ROWS) == ROWS - 1, report_ref[...].astype(f32), rows)
    out_ref[...] = jnp.concatenate([rows.astype(bf16), flags_ref[...]], 1)


def slot_rows(arrived_ref, select_ref, report_select_ref, chunk_ref, valid_ref):
    arrived = arrived_ref[...]
    chunk = contract(arrived, select_ref[...], 0, 0)
    block = chunk_ref.shape[0] - EXTRA
    chunk_ref[0:block, :] = chunk[:block].astype(bf16)
    valid_ref[...] = chunk[block : block + 1]
    reports = jnp.dot(report_select_ref[...], arrived, preferred_element_type=f32)
    reports = reports[:, :block].astype(bf16)
    chunk_ref[block : block + EXTRA, :] = jnp.concatenate(
        [reports[:EXTRA], reports[EXTRA:]], 1
    )


def slide_forward(
    here,
    valid_ref,
    far_query_weights,
    far_key_weights,
    far_value_weights,
    far_out_weights,
    *rest,
):
    pieces = rest[:9]
    (
        far_norm,
        far_heads,
        far_attention,
        stat_ref,
        scale_ref,
        mass_ref,
        attended_ref,
        pooled_ref,
        reports_ref,
        slide_ref,
        norm_ref,
        heads_ref,
        attention_ref,
        query_weights_ref,
        key_weights_ref,
        value_weights_ref,
        out_weights_ref,
        weight_sems,
        sems,
    ) = rest[9:]
    fetched = fetch(
        (far_query_weights, far_key_weights, far_value_weights, far_out_weights),
        (query_weights_ref, key_weights_ref, value_weights_ref, out_weights_ref),
        weight_sems,
    )
    count, owners, block = reports_ref.shape

    def store(index, piece):
        start = pl.multiple_of(index * block, 16)
        slide_ref[pl.ds(start, block), :] = piece[:block]
        reports = piece[block:]
        reports_ref[index] = jnp.concatenate([reports[:, :block], reports[:, block:]], 0)

    place(pieces, here[0], count, store)
    valid = valid_ref[...]
    valid_low = valid.astype(bf16)
    low = slide_ref[...]
    slide = low.astype(f32)
    mean = jnp.mean(slide, 0, keepdims=True)
    centred = slide - mean
    inverse = lax.rsqrt(jnp.mean(centred * centred, 0, keepdims=True) + eps)
    stat_ref[...] = jnp.concatenate([mean, inverse], 0)
    normed = (centred * inverse).astype(bf16)
    norm_ref[...] = normed
    copies = [pltpu.make_async_copy(norm_ref, far_norm, sems.at[0])]
    copies[0].start()
    for copy in fetched:
        copy.wait()
    all_query = jnp.dot(query_weights_ref[...], normed, preferred_element_type=f32)
    all_keys = jnp.dot(key_weights_ref[...], normed, preferred_element_type=f32)
    all_values = jnp.dot(value_weights_ref[...], normed, preferred_element_type=f32)
    heads = all_query.shape[0] // HEAD
    attended = []
    for h in range(heads):
        low_rows, high_rows = h * HEAD, (h + 1) * HEAD
        query = all_query[low_rows:high_rows]
        keys = all_keys[low_rows:high_rows]
        values = all_values[low_rows:high_rows]
        query_scale = lax.rsqrt(jnp.mean(query * query, 0, keepdims=True) + eps)
        key_scale = lax.rsqrt(jnp.mean(keys * keys, 0, keepdims=True) + eps)
        query_unit = query * query_scale
        key_unit = keys * key_scale
        heads_ref[h, 0] = query_unit
        heads_ref[h, 1] = key_unit
        heads_ref[h, 2] = values
        copies.append(pltpu.make_async_copy(heads_ref.at[h], far_heads.at[h], sems.at[1 + 2 * h]))
        copies[-1].start()
        scale_ref[h] = jnp.concatenate([query_scale, key_scale], 0)
        scores = contract(query_unit.astype(bf16), key_unit.astype(bf16), 0, 0)
        weights = jnp.exp(scores * (score_scale / HEAD)) * valid
        weights = weights * (1.0 / jnp.sum(weights, 1, keepdims=True))
        attention_ref[h] = weights
        copies.append(
            pltpu.make_async_copy(attention_ref.at[h], far_attention.at[h], sems.at[2 + 2 * h])
        )
        copies[-1].start()
        weights_low = weights.astype(bf16)
        mass_ref[h : h + 1, :] = jnp.dot(valid_low, weights_low, preferred_element_type=f32)
        attended.append(contract(values.astype(bf16), weights_low, 1, 1))
    attended = jnp.concatenate(attended, 0).astype(bf16)
    attended_sum = contract(valid_low, attended, 1, 1)
    attended_ref[...] = attended_sum
    high = attended_sum.astype(bf16)
    rest_low = (attended_sum - high.astype(f32)).astype(bf16)
    part = jnp.dot(high, out_weights_ref[...], preferred_element_type=f32)
    part = part + jnp.dot(rest_low, out_weights_ref[...], preferred_element_type=f32)
    slide_sum = contract(valid_low, low, 1, 1)
    pooled = (part + slide_sum * (1.0 / count)) / jnp.sum(valid)
    pooled_ref[...] = jnp.broadcast_to(pooled[None], pooled_ref.shape)
    for copy in copies:
        copy.wait()


def unit_vectors(parts_ref, reports_ref, report_ref):
    pooled = jnp.sum(parts_ref[...], 0)
    inverse = lax.rsqrt(jnp.sum(pooled * pooled, -1, keepdims=True) + eps)
    count, owners, block = reports_ref.shape
    squares = jnp.zeros((owners, 1), f32)
    for j in range(count):
        reports = reports_ref[j].astype(f32)
        report_ref[:, j * block : (j + 1) * block] = reports
        squares = squares + jnp.sum(reports * reports, -1, keepdims=True)
    report = report_ref[...] * lax.rsqrt(squares + eps)
    return pooled * inverse, inverse, report


def logits_row(parts_ref, reports_ref, row_ref, report_ref):
    unit, inverse, report = unit_vectors(parts_ref, reports_ref, report_ref)
    row = contract(unit, report, 1, 1, precision=exact) / contrast_divisor_factor
    pad = row_ref.shape[2] - row.shape[1]
    row = jnp.concatenate([row, jnp.zeros((1, pad), f32)], 1)
    row_ref[...] = jnp.broadcast_to(row[None], row_ref.shape)


def slide_backward(
    owner,
    logits_ref,
    pair_ref,
    parts_ref,
    reports_ref,
    valid_ref,
    scale_ref,
    mass_ref,
    far_out_weights,
    far_heads,
    far_attention,
    far_query_weights,
    far_key_weights,
    far_value_weights,
    far_norm,
    loss_ref,
    grad_ref,
    up_ref,
    grads_ref,
    out_ref,
    *rest,
):
    fetched, report_ref, sems = rest[:-2], rest[-2], rest[-1]
    (
        out_weights_ref,
        heads_ref,
        attention_ref,
        query_weights_ref,
        key_weights_ref,
        value_weights_ref,
        norm_ref,
    ) = fetched
    copies = fetch(
        (
            far_out_weights,
            far_heads,
            far_attention,
            far_query_weights,
            far_key_weights,
            far_value_weights,
            far_norm,
        ),
        fetched,
        sems,
    )
    unit, inverse, report = unit_vectors(parts_ref, reports_ref, report_ref)
    owners = report.shape[0]
    valid = valid_ref[...]
    logits = logits_ref[...]
    shape = logits.shape
    columns = lax.broadcasted_iota(i32, shape, 1)
    rows = lax.broadcasted_iota(i32, shape, 0)
    real = columns < owners
    expo = jnp.where(real, jnp.exp(logits), 0.0)
    row_total = jnp.sum(expo, 1, keepdims=True)
    column_total = jnp.where(real[:1], jnp.sum(expo, 0, keepdims=True), 1.0)
    target = jnp.where(pair_ref[...] == columns, 1.0, 0.0)
    loss = jnp.sum(
        0.5 * jnp.log(row_total) - jnp.sum(logits * target, 1, keepdims=True), 0, keepdims=True
    )
    loss = loss + 0.5 * jnp.sum(jnp.log(column_total), 1, keepdims=True)
    loss_ref[...] = loss * (1.0 / owners)
    grad_logits = (0.5 * expo / row_total + 0.5 * expo / column_total - target) * (
        loss_scale / owners
    )
    grad_row = jnp.sum(jnp.where(rows == owner[0], grad_logits, 0.0), 0, keepdims=True)
    grad_unit = (
        jnp.dot(grad_row[:, :owners], report, precision=exact, preferred_element_type=f32)
        / contrast_divisor_factor
    )
    grad_pooled = (grad_unit - unit * jnp.sum(unit * grad_unit, -1, keepdims=True)) * inverse
    grad = grad_pooled / jnp.sum(valid)
    grad_ref[...] = grad
    low = grad.astype(bf16)
    copies[0].wait()
    out_weights = out_weights_ref[...]
    up_ref[...] = contract(low, out_weights, 1, 1)
    up = jnp.sum(out_weights.astype(f32) * low.astype(f32), 1, keepdims=True)
    heads = heads_ref.shape[0]
    inner = heads * HEAD
    copies[1].wait()
    copies[2].wait()
    for h in range(heads):
        up_head = up[h * HEAD : (h + 1) * HEAD]
        values = heads_ref[h, 2]
        weights = attention_ref[h]
        pull = jnp.sum(up_head * values, 0, keepdims=True)
        pull_mean = jnp.sum(weights * pull, 1, keepdims=True)
        grad_scores = (weights * (pull - pull_mean) * (score_scale / HEAD)).astype(bf16)
        query_unit = heads_ref[h, 0]
        key_unit = heads_ref[h, 1]
        grad_query = contract(key_unit.astype(bf16), grad_scores, 1, 1) * valid
        grad_key = jnp.dot(query_unit.astype(bf16), grad_scores, preferred_element_type=f32)
        grad_query = scale_ref[h, 0:1] * (
            grad_query - query_unit * jnp.mean(query_unit * grad_query, 0, keepdims=True)
        )
        grad_key = scale_ref[h, 1:2] * (
            grad_key - key_unit * jnp.mean(key_unit * grad_key, 0, keepdims=True)
        )
        grad_value = up_head * mass_ref[h : h + 1]
        for part, values in enumerate((grad_query, grad_key, grad_value)):
            start = part * inner + h * HEAD
            grads_ref[start : start + HEAD, :] = values.astype(bf16)
    grad_query = grads_ref[0:inner, :]
    grad_key = grads_ref[inner : 2 * inner, :]
    grad_value = grads_ref[2 * inner : 3 * inner, :]
    for copy in copies[3:]:
        copy.wait()
    count = out_ref.shape[0]
    block = norm_ref.shape[0] // count
    first = jnp.zeros_like(valid)
    second = jnp.zeros_like(valid)
    for k in range(count):
        rows = slice(k * block, (k + 1) * block)
        part = jnp.dot(query_weights_ref[rows, :], grad_query, preferred_element_type=f32)
        part = part + jnp.dot(key_weights_ref[rows, :], grad_key, preferred_element_type=f32)
        part = part + jnp.dot(value_weights_ref[rows, :], grad_value, preferred_element_type=f32)
        out_ref[k, 0:block, :] = part.astype(bf16)
        first = first + jnp.sum(part, 0, keepdims=True)
        second = second + jnp.sum(part * norm_ref[rows, :].astype(f32), 0, keepdims=True)
    width = norm_ref.shape[0]
    stats = jnp.concatenate([first, second], 0) * (1.0 / width)
    high = stats.astype(bf16).astype(f32)
    stats = jnp.concatenate(
        [high, stats - high, jnp.zeros((EXTRA - 4, stats.shape[1]), f32)], 0
    ).astype(bf16)
    for k in range(count):
        out_ref[k, block : block + EXTRA, :] = stats


def wide_other(which, norm_ref, grads_ref, out_ref):
    chips, share, columns = out_ref.shape
    rows = [
        norm_ref[pl.ds(pl.multiple_of((CORES * chip + which[0]) * share, 16), share), :]
        for chip in range(chips)
    ]
    values = contract(jnp.concatenate(rows, 0), grads_ref[0:columns, :], 1, 1).astype(bf16)
    for chip in range(chips):
        out_ref[chip] = values[chip * share : (chip + 1) * share]


def wide_own(which, column, norm_ref, grads_ref, got_ref, *outs):
    side = len(outs)
    lines, share, columns = outs[0].shape
    chips = [
        line * side + lax.rem(column[0] + k, side) for k in range(side) for line in range(lines)
    ]
    rows = [
        norm_ref[pl.ds(pl.multiple_of((CORES * chip + which[0]) * share, 16), share), :]
        for chip in chips
    ]
    values = contract(jnp.concatenate(rows, 0), grads_ref[0:columns, :], 1, 1)
    for index, chip in enumerate(chips):
        part = values[index * share : (index + 1) * share] + got_ref[chip].astype(f32)
        outs[index // lines][index % lines] = part.astype(bf16)


def wide_line(line, *refs):
    side = len(refs) // 2
    for k in range(side):
        row = lax.rem(line[0] + k, side)
        total = refs[0][row].astype(f32)
        for ref in refs[1:side]:
            total = total + ref[row].astype(f32)
        refs[side + k][...] = total.astype(bf16)


def slot_grads(
    own_ref, valid_ref, stat_ref, chunk_ref, select_ref, extra_ref, parts_ref, out_ref
):
    total = parts_ref[0].astype(f32)
    for j in range(1, parts_ref.shape[0]):
        total = total + parts_ref[j].astype(f32)
    block = chunk_ref.shape[0] - EXTRA
    first = total[block : block + 1] + total[block + 2 : block + 3]
    second = total[block + 1 : block + 2] + total[block + 3 : block + 4]
    mean = stat_ref[0:1]
    inverse = stat_ref[1:2]
    normed = (chunk_ref[0:block, :].astype(f32) - mean) * inverse
    rows = own_ref[...] * valid_ref[...] + (total[:block] - first - normed * second) * inverse
    rows = contract(select_ref[...], rows.astype(bf16), 1, 1).astype(bf16)
    out_ref[...] = rows + extra_ref[...]


def tile_grads(back_ref, dispatch_ref, out_ref):
    piece = pack(contract(back_ref[...], dispatch_ref[...], 0, 0).astype(bf16))
    out_ref[...] = jnp.broadcast_to(piece[None], out_ref.shape)


def rows_of(which, ref, chips, share):
    rows = [
        ref[pl.ds(pl.multiple_of((CORES * chip + which) * share, 16), share), :]
        for chip in range(chips)
    ]
    return jnp.concatenate(rows, 0)


def other_two(other, hidden_ref, parts_ref, grad_ref, out_ref):
    count = parts_ref.shape[0]
    rows = grad_ref.shape[0] // count
    for j in range(count):
        grad_ref[j * rows : (j + 1) * rows, :] = unpack(parts_ref[j])
    chips, share = out_ref.shape[:2]
    rows = rows_of(other[0], grad_ref, chips, share)
    two = jnp.dot(rows, hidden_ref[...], preferred_element_type=f32).astype(bf16)
    for chip in range(chips):
        out_ref[chip] = two[chip * share : (chip + 1) * share]


def both_one(
    two_ref, slope_ref, other_norm_ref, own_norm_ref, grad_ref, out_ref, own_ref, hidden_grad_ref
):
    grad_hidden = jnp.dot(two_ref[...], grad_ref[...], preferred_element_type=f32)
    hidden_grad_ref[...] = (grad_hidden * slope_ref[...]).astype(bf16)
    chips, share = out_ref.shape[:2]
    for norm_ref, target_ref in ((other_norm_ref, out_ref), (own_norm_ref, own_ref)):
        one = contract(norm_ref[...], hidden_grad_ref[...], 1, 1).astype(bf16)
        for chip in range(chips):
            target_ref[chip] = one[chip * share : (chip + 1) * share]


def own_two(own, column, hidden_ref, grad_ref, got_ref, *outs):
    side = len(outs)
    lines, share = outs[0].shape[:2]
    for k in range(side):
        place = lax.rem(column[0] + k, side)
        chips = [line * side + place for line in range(lines)]
        rows = [
            grad_ref[pl.ds(pl.multiple_of((CORES * chip + own[0]) * share, 16), share), :]
            for chip in chips
        ]
        two = jnp.dot(jnp.concatenate(rows, 0), hidden_ref[...], preferred_element_type=f32)
        for line, chip in enumerate(chips):
            part = two[line * share : (line + 1) * share] + got_ref[chip].astype(f32)
            outs[k][line] = part.astype(bf16)


def own_one(own_ref, got_ref, out_ref):
    side = out_ref.shape[1]
    for chip in range(got_ref.shape[0]):
        part = own_ref[chip].astype(f32) + got_ref[chip].astype(f32)
        out_ref[chip // side, chip % side] = part.astype(bf16)


def add_up(*refs):
    total = refs[0][...].astype(f32)
    for ref in refs[1:-1]:
        total = total + ref[...].astype(f32)
    refs[-1][...] = total.astype(refs[-1].dtype)


def add_lines(column, lines_ref, *outs):
    side = len(outs)
    for k in range(side):
        place = lax.rem(column[0] + k, side)
        total = lines_ref[0, place].astype(f32)
        for line in range(1, lines_ref.shape[0]):
            total = total + lines_ref[line, place].astype(f32)
        outs[k][...] = total.astype(bf16)


def last_sums(lines_ref, *refs):
    one_ref, two_ref = refs[-2:]
    total = lines_ref[0].astype(f32)
    for line in range(1, lines_ref.shape[0]):
        total = total + lines_ref[line].astype(f32)
    two_ref[...] = total
    total = refs[0][...].astype(f32)
    for ref in refs[1:-2]:
        total = total + ref[...].astype(f32)
    one_ref[...] = total


def per_device(
    tile_features, tile_slide, slide_pair, reports, w_one, w_two, w_query, w_key, w_value, w_out
):
    lines = lax.axis_size("line")
    side = lax.axis_size("column")
    line = lax.axis_index("line")
    column = lax.axis_index("column")
    chips = lines * side
    owners = chips * CORES
    parts = lax.axis_size("mp")
    core = lax.axis_index("core")
    owner = lax.axis_index(DP)
    here = lax.axis_index("mp")
    tiles, width = tile_features.shape
    units = w_one.shape[1]
    capacity = 2 * tiles // owners
    length = owners * capacity
    slots = owners * ROWS
    block = width // parts
    share = width // owners
    inner = w_query.shape[1]
    heads = inner // HEAD
    packed = (block // 2 * 3, 128)

    def halves(values):
        rest = values.shape[1:]
        values = values.reshape((chips, CORES, share) + rest)
        own = pick(values, core, 1).reshape((chips * share,) + rest)
        other = pick(values, 1 - core, 1).reshape((chips * share,) + rest)
        return own, other

    tile_norm, hidden, slope, partial = call(
        tile_forward,
        [
            ((tiles, width), bf16),
            ((tiles, units), bf16),
            ((tiles, units), f32),
            ((parts,) + packed, bf16),
        ],
        tile_features,
        w_one,
        w_two,
        far=(0, 1, 2),
        scratch=[
            (tile_features.shape, bf16),
            (w_one.shape, bf16),
            (w_two.shape, bf16),
            3,
        ],
        limit=62,
    )
    partial = exchange(partial, "mp")

    slide_ids = tile_slide[:, 0]
    matches = (slide_ids[:, None] == jnp.arange(owners, dtype=i32)[None, :]).astype(i32)
    ordinal = jnp.sum(matches * (jnp.cumsum(matches, 0) - 1), 1)
    position = slide_ids * ROWS + ordinal
    dispatch = jnp.arange(slots, dtype=i32)[:, None] == position[None, :]
    flags = jnp.sum(dispatch.astype(f32), 1, keepdims=True).astype(bf16)
    flags = jnp.pad(flags, ((0, 0), (0, 256 - block - 1)))
    dispatch = dispatch.astype(bf16)
    slot = jnp.arange(slots, dtype=i32)
    row_of_slot = jnp.where(slot % ROWS < capacity, slot // ROWS * capacity + slot % ROWS, -1)
    select = (row_of_slot[:, None] == jnp.arange(length, dtype=i32)[None, :]).astype(bf16)
    last_slot = jnp.arange(owners, dtype=i32)[:, None] * ROWS + ROWS - 1
    report_select = (last_slot == slot[None, :]).astype(bf16)
    own_columns = pick(tile_features.reshape(tiles, parts, block), here, 1)
    own_report = pick(reports.reshape(1, parts, block), here, 1)
    tile_own, tile_other = halves(tile_norm.T)
    slope = slope.T

    (outgoing,) = call(
        tile_dispatch,
        [((slots, 256), bf16)],
        own_columns,
        own_report,
        dispatch,
        flags,
        partial,
        anchors=(select, report_select, tile_own, tile_other, slope),
    )
    arrived = exchange(outgoing.reshape(owners, ROWS, 256), DP).reshape(slots, 256)
    chunk, valid = call(
        slot_rows,
        [((block + EXTRA, length), bf16), ((1, length), f32)],
        arrived,
        select,
        report_select,
    )
    pieces = gather_ring(chunk, parts)

    (
        slide_norm,
        by_head,
        attention,
        stat,
        scales,
        mass,
        attended_sum,
        pooled,
        all_reports,
    ) = call(
        slide_forward,
        [
            ((width, length), bf16, "far"),
            ((heads, 3, HEAD, length), f32, "far"),
            ((heads, length, length), f32, "far"),
            ((2, length), f32),
            ((heads, 2, length), f32),
            ((heads, length), f32),
            ((1, inner), f32),
            ((parts, 1, width), f32),
            ((parts, owners, block), bf16),
        ],
        valid,
        w_query.T,
        w_key.T,
        w_value.T,
        w_out,
        *pieces,
        scalars=(here,),
        far=(1, 2, 3, 4),
        scratch=[
            ((width, length), bf16),
            ((width, length), bf16),
            ((heads, 3, HEAD, length), f32),
            ((heads, length, length), f32),
            ((inner, width), bf16),
            ((inner, width), bf16),
            ((inner, width), bf16),
            ((inner, width), bf16),
            4,
            1 + 2 * heads,
        ],
        limit=60,
    )
    pooled = exchange(pooled, "mp")
    (row,) = call(
        logits_row,
        [((owners, 1, 128), f32)],
        pooled,
        all_reports,
        scratch=[((owners, width), f32)],
    )
    logits = exchange(row, DP).reshape(owners, 128)
    loss, grad, up, grads, sending = call(
        slide_backward,
        [((1, 1), f32), ((1, width), f32), ((1, inner), f32), ((3 * inner, length), bf16)]
        + [((parts, block + EXTRA, length), bf16)],
        logits,
        slide_pair[:, None],
        pooled,
        all_reports,
        valid,
        scales,
        mass,
        w_out,
        by_head,
        attention,
        w_query,
        w_key,
        w_value,
        slide_norm,
        scalars=(owner,),
        far=tuple(range(7, 14)),
        scratch=[
            (w_out.shape, bf16),
            (by_head.shape, f32),
            (attention.shape, f32),
            (w_query.shape, bf16),
            (w_key.shape, bf16),
            (w_value.shape, bf16),
            (slide_norm.shape, bf16),
            ((owners, width), f32),
            7,
        ],
        limit=60,
    )
    received = exchange(sending, "mp")

    (wide_sent,) = call(
        wide_other,
        [((chips, share, 2 * inner), bf16)],
        slide_norm,
        grads,
        scalars=(1 - core,),
    )
    wide_got = lax.ppermute(wide_sent, "core", [(0, 1), (1, 0)])
    along = call(
        wide_own,
        [((lines, share, 2 * inner), bf16)] * side,
        slide_norm,
        grads,
        wide_got,
        scalars=(core, column),
    )
    def shift(values, axis):
        return [values[0]] + [
            lax.ppermute(values[k], axis, turn(len(values), k)) for k in range(1, len(values))
        ]

    along = shift(along, "column")
    across = call(
        wide_line, [((share, 2 * inner), bf16)] * lines, *along, scalars=(line,)
    )
    across = shift(across, "line")
    grad_wide = sum(part.astype(f32) for part in across)
    value_rows = contract(mass.astype(bf16), slide_norm, 1, 1)
    extra = jnp.concatenate(
        [
            value_rows.reshape(heads, owners, share).transpose(1, 0, 2).reshape(owners, -1),
            grad.reshape(owners, share),
            jnp.broadcast_to(up, (owners, inner)),
            jnp.broadcast_to(attended_sum, (owners, inner)),
        ],
        1,
    ).astype(bf16)
    spare = ROWS - capacity
    extra = jnp.pad(extra, ((0, 0), (0, spare * block - extra.shape[1])))
    extra = extra.reshape(owners, spare, block)
    extra = jnp.pad(extra, ((0, 0), (capacity, 0), (0, 0))).reshape(slots, block)

    own_grad = lax.dynamic_slice_in_dim(grad, here * block, block, 1).reshape(block, 1)
    (going,) = call(
        slot_grads,
        [((slots, block), bf16)],
        own_grad,
        valid,
        stat,
        chunk,
        select,
        extra,
        received,
        anchors=(grad_wide,),
    )
    back = exchange(going.reshape(owners, ROWS, block), DP).reshape(slots, block)
    (spreading,) = call(tile_grads, [((parts,) + packed, bf16)], back, dispatch)

    size = (chips, share, units)
    swap = [(0, 1), (1, 0)]
    grad_embedding, two_sent = call(
        other_two,
        [((width, tiles), bf16), (size, bf16)],
        hidden,
        exchange(spreading, "mp"),
        scalars=(1 - core,),
    )
    two_got = lax.ppermute(two_sent, "core", swap)
    one_sent, one_own = call(
        both_one,
        [(size, bf16), (size, bf16)],
        w_two,
        slope,
        tile_other,
        tile_own,
        grad_embedding,
        scratch=[((units, tiles), bf16)],
    )
    one_got = lax.ppermute(one_sent, "core", swap)
    two_along = call(
        own_two,
        [((lines, share, units), bf16)] * side,
        hidden,
        grad_embedding,
        two_got,
        scalars=(core, column),
    )
    (one_across,) = call(
        own_one,
        [((lines, side, share, units), bf16)],
        one_own,
        one_got,
        anchors=(two_along[0],),
    )
    two_along = shift(two_along, "column")
    one_across = exchange(one_across, "line")
    (two_across,) = call(add_up, [((lines, share, units), bf16)], *two_along)
    one_along = call(add_lines, [((share, units), bf16)] * side, one_across, scalars=(column,))
    grad_one, grad_two = call(
        last_sums,
        [((share, units), f32)] * 2,
        exchange(two_across, "line"),
        *shift(one_along, "column"),
    )
    grad_two = grad_two.T

    terms = back.reshape(owners, ROWS, block)[:, capacity:].reshape(owners, -1).astype(f32)
    edge = heads * share
    from_values = terms[:, :edge].reshape(owners, heads, share)
    from_grads = terms[:, edge : edge + share]
    edge = edge + share
    from_up = terms[:, edge : edge + inner].reshape(owners, heads, HEAD)
    edge = edge + inner
    from_attended = terms[:, edge : edge + inner]
    grad_value = jnp.einsum("ohs,ohd->shd", from_values, from_up, precision=exact)
    grad_value = grad_value.reshape(share, inner)
    grad_out = contract(from_attended, from_grads, 0, 0, precision=exact)
    return (
        loss[0, 0],
        grad_one,
        grad_two,
        grad_wide[:, :inner],
        grad_wide[:, inner:],
        grad_value,
        grad_out,
    )


def solution(mesh):
    owners, parts = mesh.devices.shape
    side = math.isqrt(owners // CORES)
    split = Mesh(
        mesh.devices.reshape(owners // CORES // side, side, CORES, parts),
        ("line", "column", "core", "mp"),
    )
    return jax.shard_map(
        per_device,
        mesh=split,
        in_specs=(
            P(DP, None),
            P(DP, None),
            P(),
            P(DP, None),
            P(None, "mp"),
            P("mp", None),
            P(None, "mp"),
            P(None, "mp"),
            P(None, "mp"),
            P("mp", None),
        ),
        out_specs=(
            P(),
            P(DP, "mp"),
            P("mp", DP),
            P(DP, "mp"),
            P(DP, "mp"),
            P(DP, "mp"),
            P("mp", DP),
        ),
        check_vma=False,
    )
```

```python
import math

import jax
import jax.numpy as jnp
from jax import lax
from jax.experimental import pallas as pl
from jax.experimental.pallas import tpu as pltpu
from jax.sharding import Mesh, PartitionSpec as P

HEAD = 96
CORES = 2
ROWS = 16
EXTRA = 16

eps = 1e-05
contrast_divisor_factor = 0.07
score_scale = 10.0
loss_scale = 4096.0
exact = lax.Precision.HIGHEST
f32 = jnp.float32
bf16 = jnp.bfloat16
i32 = jnp.int32
DP = ("line", "column", "core")


def contract(left, right, left_dim, right_dim, **kw):
    return lax.dot_general(
        left, right, (((left_dim,), (right_dim,)), ((), ())), preferred_element_type=f32, **kw
    )


def exchange(values, axis):
    return lax.all_to_all(values, axis, 0, 0, tiled=True)


def pick(values, index, axis):
    return lax.dynamic_index_in_dim(values, index, axis, keepdims=False)


def call(body, outs, *args, scalars=(), scratch=(), anchors=(), far=(), limit=16):
    count = len(scalars)
    skip = len(anchors)
    vmem = pl.BlockSpec(memory_space=pltpu.VMEM)
    away = pl.BlockSpec(memory_space=pltpu.HBM)

    def kernel(*refs):
        body(*refs[skip:])

    return pl.pallas_call(
        kernel if skip else body,
        out_shape=[jax.ShapeDtypeStruct(out[0], out[1]) for out in outs],
        in_specs=[pl.BlockSpec(memory_space=pl.ANY)] * skip
        + [pl.BlockSpec(memory_space=pltpu.SMEM)] * count
        + [away if index in far else vmem for index in range(len(args))],
        out_specs=[vmem if len(out) == 2 else away for out in outs],
        scratch_shapes=[
            pltpu.VMEM(*part) if isinstance(part, tuple) else pltpu.SemaphoreType.DMA((part,))
            for part in scratch
        ],
        compiler_params=pltpu.CompilerParams(vmem_limit_bytes=limit * 1024 * 1024),
    )(*anchors, *[jnp.reshape(s, (1,)).astype(i32) for s in scalars], *args)


def fetch(sources, targets, semaphores):
    copies = [
        pltpu.make_async_copy(source, target, semaphores.at[index])
        for index, (source, target) in enumerate(zip(sources, targets))
    ]
    for copy in copies:
        copy.start()
    return copies


def turn(count, step):
    return [(index, (index + step) % count) for index in range(count)]


def gather_ring(piece, count):
    found = [piece]
    back = ahead = piece
    for _ in range(count // 2 - 1):
        back = lax.ppermute(back, "mp", turn(count, 1))
        ahead = lax.ppermute(ahead, "mp", turn(count, count - 1))
        found += [back, ahead]
    half = (piece.shape[0] // 2 + ROWS - 1) // ROWS * ROWS
    found.append(lax.ppermute(back[:half], "mp", turn(count, 1)))
    found.append(lax.ppermute(ahead[half:], "mp", turn(count, count - 1)))
    return found


def place(refs, here, count, store):
    half = count // 2
    store(here, refs[0][...])
    for step in range(1, half):
        for ref, sign in ((refs[2 * step - 1], -1), (refs[2 * step], 1)):
            store(lax.rem(here + sign * step + count, count), ref[...])
    store(
        lax.rem(here + half, count), jnp.concatenate([refs[-2][...], refs[-1][...]], 0)
    )


def pack(square):
    half = square.shape[0] // 2
    side = square[:, 128:]
    return jnp.concatenate(
        [square[:, :128], jnp.concatenate([side[:half], side[half:]], 1)], 0
    )


def unpack(packed):
    rows = packed.shape[0] // 3 * 2
    side = packed[rows:]
    return jnp.concatenate(
        [packed[:rows], jnp.concatenate([side[:, :64], side[:, 64:]], 0)], 1
    )


def tile_forward(
    far_x, far_one, far_two, norm_ref, hidden_ref, slope_ref, out_ref, x_ref, one_ref, two_ref, sems
):
    copies = fetch((far_x, far_one, far_two), (x_ref, one_ref, two_ref), sems)
    copies[0].wait()
    x = x_ref[...].astype(f32)
    centred = x - jnp.mean(x, -1, keepdims=True)
    normed = centred * lax.rsqrt(jnp.mean(centred * centred, -1, keepdims=True) + eps)
    normed = normed.astype(bf16)
    norm_ref[...] = normed
    copies[1].wait()
    pre = jnp.dot(normed, one_ref[...], preferred_element_type=f32)
    bell = 0.5 * (1.0 + lax.erf(pre * 0.7071067811865476))
    hidden = (pre * bell).astype(bf16)
    hidden_ref[...] = hidden
    slope_ref[...] = bell + pre * jnp.exp(-0.5 * pre * pre) * 0.3989422804014327
    copies[2].wait()
    partial = jnp.dot(hidden, two_ref[...], preferred_element_type=f32).astype(bf16)
    count = out_ref.shape[0]
    block = partial.shape[1] // count
    for j in range(count):
        out_ref[j] = pack(partial[:, j * block : (j + 1) * block])


def tile_dispatch(own_ref, report_ref, dispatch_ref, flags_ref, parts_ref, out_ref):
    total = parts_ref[0].astype(f32)
    for j in range(1, parts_ref.shape[0]):
        total = total + parts_ref[j].astype(f32)
    embedding = (own_ref[...].astype(f32) + unpack(total)).astype(bf16)
    rows = jnp.dot(dispatch_ref[...], embedding, preferred_element_type=f32)
    slot = lax.broadcasted_iota(i32, rows.shape, 0)
    rows = jnp.where(lax.rem(slot, ROWS) == ROWS - 1, report_ref[...].astype(f32), rows)
    out_ref[...] = jnp.concatenate([rows.astype(bf16), flags_ref[...]], 1)


def slot_rows(arrived_ref, select_ref, report_select_ref, chunk_ref, valid_ref):
    arrived = arrived_ref[...]
    chunk = contract(arrived, select_ref[...], 0, 0)
    block = chunk_ref.shape[0] - EXTRA
    chunk_ref[0:block, :] = chunk[:block].astype(bf16)
    valid_ref[...] = chunk[block : block + 1]
    reports = jnp.dot(report_select_ref[...], arrived, preferred_element_type=f32)
    reports = reports[:, :block].astype(bf16)
    chunk_ref[block : block + EXTRA, :] = jnp.concatenate(
        [reports[:EXTRA], reports[EXTRA:]], 1
    )


def slide_forward(
    here,
    valid_ref,
    far_query_weights,
    far_key_weights,
    far_value_weights,
    far_out_weights,
    *rest,
):
    pieces = rest[:9]
    (
        far_norm,
        far_heads,
        far_attention,
        stat_ref,
        scale_ref,
        mass_ref,
        attended_ref,
        pooled_ref,
        reports_ref,
        slide_ref,
        norm_ref,
        heads_ref,
        attention_ref,
        query_weights_ref,
        key_weights_ref,
        value_weights_ref,
        out_weights_ref,
        weight_sems,
        sems,
    ) = rest[9:]
    fetched = fetch(
        (far_query_weights, far_key_weights, far_value_weights, far_out_weights),
        (query_weights_ref, key_weights_ref, value_weights_ref, out_weights_ref),
        weight_sems,
    )
    count, owners, block = reports_ref.shape

    def store(index, piece):
        start = pl.multiple_of(index * block, 16)
        slide_ref[pl.ds(start, block), :] = piece[:block]
        reports = piece[block:]
        reports_ref[index] = jnp.concatenate([reports[:, :block], reports[:, block:]], 0)

    place(pieces, here[0], count, store)
    valid = valid_ref[...]
    valid_low = valid.astype(bf16)
    low = slide_ref[...]
    slide = low.astype(f32)
    mean = jnp.mean(slide, 0, keepdims=True)
    centred = slide - mean
    inverse = lax.rsqrt(jnp.mean(centred * centred, 0, keepdims=True) + eps)
    stat_ref[...] = jnp.concatenate([mean, inverse], 0)
    normed = (centred * inverse).astype(bf16)
    norm_ref[...] = normed
    copies = [pltpu.make_async_copy(norm_ref, far_norm, sems.at[0])]
    copies[0].start()
    for copy in fetched:
        copy.wait()
    all_query = jnp.dot(query_weights_ref[...], normed, preferred_element_type=f32)
    all_keys = jnp.dot(key_weights_ref[...], normed, preferred_element_type=f32)
    all_values = jnp.dot(value_weights_ref[...], normed, preferred_element_type=f32)
    heads = all_query.shape[0] // HEAD
    attended = []
    for h in range(heads):
        low_rows, high_rows = h * HEAD, (h + 1) * HEAD
        query = all_query[low_rows:high_rows]
        keys = all_keys[low_rows:high_rows]
        values = all_values[low_rows:high_rows]
        query_scale = lax.rsqrt(jnp.mean(query * query, 0, keepdims=True) + eps)
        key_scale = lax.rsqrt(jnp.mean(keys * keys, 0, keepdims=True) + eps)
        query_unit = query * query_scale
        key_unit = keys * key_scale
        heads_ref[h, 0] = query_unit
        heads_ref[h, 1] = key_unit
        heads_ref[h, 2] = values
        copies.append(pltpu.make_async_copy(heads_ref.at[h], far_heads.at[h], sems.at[1 + 2 * h]))
        copies[-1].start()
        scale_ref[h] = jnp.concatenate([query_scale, key_scale], 0)
        scores = contract(query_unit.astype(bf16), key_unit.astype(bf16), 0, 0)
        weights = jnp.exp(scores * (score_scale / HEAD)) * valid
        weights = weights * (1.0 / jnp.sum(weights, 1, keepdims=True))
        attention_ref[h] = weights
        copies.append(
            pltpu.make_async_copy(attention_ref.at[h], far_attention.at[h], sems.at[2 + 2 * h])
        )
        copies[-1].start()
        weights_low = weights.astype(bf16)
        mass_ref[h : h + 1, :] = jnp.dot(valid_low, weights_low, preferred_element_type=f32)
        attended.append(contract(values.astype(bf16), weights_low, 1, 1))
    attended = jnp.concatenate(attended, 0).astype(bf16)
    attended_sum = contract(valid_low, attended, 1, 1)
    attended_ref[...] = attended_sum
    high = attended_sum.astype(bf16)
    rest_low = (attended_sum - high.astype(f32)).astype(bf16)
    part = jnp.dot(high, out_weights_ref[...], preferred_element_type=f32)
    part = part + jnp.dot(rest_low, out_weights_ref[...], preferred_element_type=f32)
    slide_sum = contract(valid_low, low, 1, 1)
    pooled = (part + slide_sum * (1.0 / count)) / jnp.sum(valid)
    pooled_ref[...] = jnp.broadcast_to(pooled[None], pooled_ref.shape)
    for copy in copies:
        copy.wait()


def unit_vectors(parts_ref, reports_ref, report_ref):
    pooled = jnp.sum(parts_ref[...], 0)
    inverse = lax.rsqrt(jnp.sum(pooled * pooled, -1, keepdims=True) + eps)
    count, owners, block = reports_ref.shape
    squares = jnp.zeros((owners, 1), f32)
    for j in range(count):
        reports = reports_ref[j].astype(f32)
        report_ref[:, j * block : (j + 1) * block] = reports
        squares = squares + jnp.sum(reports * reports, -1, keepdims=True)
    report = report_ref[...] * lax.rsqrt(squares + eps)
    return pooled * inverse, inverse, report


def logits_row(parts_ref, reports_ref, row_ref, report_ref):
    unit, inverse, report = unit_vectors(parts_ref, reports_ref, report_ref)
    row = contract(unit, report, 1, 1, precision=exact) / contrast_divisor_factor
    pad = row_ref.shape[2] - row.shape[1]
    row = jnp.concatenate([row, jnp.zeros((1, pad), f32)], 1)
    row_ref[...] = jnp.broadcast_to(row[None], row_ref.shape)


def slide_backward(
    owner,
    logits_ref,
    pair_ref,
    parts_ref,
    reports_ref,
    valid_ref,
    scale_ref,
    mass_ref,
    far_out_weights,
    far_heads,
    far_attention,
    far_query_weights,
    far_key_weights,
    far_value_weights,
    far_norm,
    loss_ref,
    grad_ref,
    up_ref,
    grads_ref,
    out_ref,
    *rest,
):
    fetched, report_ref, sems = rest[:-2], rest[-2], rest[-1]
    (
        out_weights_ref,
        heads_ref,
        attention_ref,
        query_weights_ref,
        key_weights_ref,
        value_weights_ref,
        norm_ref,
    ) = fetched
    copies = fetch(
        (
            far_out_weights,
            far_heads,
            far_attention,
            far_query_weights,
            far_key_weights,
            far_value_weights,
            far_norm,
        ),
        fetched,
        sems,
    )
    unit, inverse, report = unit_vectors(parts_ref, reports_ref, report_ref)
    owners = report.shape[0]
    valid = valid_ref[...]
    logits = logits_ref[...]
    shape = logits.shape
    columns = lax.broadcasted_iota(i32, shape, 1)
    rows = lax.broadcasted_iota(i32, shape, 0)
    real = columns < owners
    expo = jnp.where(real, jnp.exp(logits), 0.0)
    row_total = jnp.sum(expo, 1, keepdims=True)
    column_total = jnp.where(real[:1], jnp.sum(expo, 0, keepdims=True), 1.0)
    target = jnp.where(pair_ref[...] == columns, 1.0, 0.0)
    loss = jnp.sum(
        0.5 * jnp.log(row_total) - jnp.sum(logits * target, 1, keepdims=True), 0, keepdims=True
    )
    loss = loss + 0.5 * jnp.sum(jnp.log(column_total), 1, keepdims=True)
    loss_ref[...] = loss * (1.0 / owners)
    grad_logits = (0.5 * expo / row_total + 0.5 * expo / column_total - target) * (
        loss_scale / owners
    )
    grad_row = jnp.sum(jnp.where(rows == owner[0], grad_logits, 0.0), 0, keepdims=True)
    grad_unit = (
        jnp.dot(grad_row[:, :owners], report, precision=exact, preferred_element_type=f32)
        / contrast_divisor_factor
    )
    grad_pooled = (grad_unit - unit * jnp.sum(unit * grad_unit, -1, keepdims=True)) * inverse
    grad = grad_pooled / jnp.sum(valid)
    grad_ref[...] = grad
    low = grad.astype(bf16)
    copies[0].wait()
    out_weights = out_weights_ref[...]
    up_ref[...] = contract(low, out_weights, 1, 1)
    up = jnp.sum(out_weights.astype(f32) * low.astype(f32), 1, keepdims=True)
    heads = heads_ref.shape[0]
    inner = heads * HEAD
    copies[1].wait()
    copies[2].wait()
    for h in range(heads):
        up_head = up[h * HEAD : (h + 1) * HEAD]
        values = heads_ref[h, 2]
        weights = attention_ref[h]
        pull = jnp.sum(up_head * values, 0, keepdims=True)
        pull_mean = jnp.sum(weights * pull, 1, keepdims=True)
        grad_scores = (weights * (pull - pull_mean) * (score_scale / HEAD)).astype(bf16)
        query_unit = heads_ref[h, 0]
        key_unit = heads_ref[h, 1]
        grad_query = contract(key_unit.astype(bf16), grad_scores, 1, 1) * valid
        grad_key = jnp.dot(query_unit.astype(bf16), grad_scores, preferred_element_type=f32)
        grad_query = scale_ref[h, 0:1] * (
            grad_query - query_unit * jnp.mean(query_unit * grad_query, 0, keepdims=True)
        )
        grad_key = scale_ref[h, 1:2] * (
            grad_key - key_unit * jnp.mean(key_unit * grad_key, 0, keepdims=True)
        )
        grad_value = up_head * mass_ref[h : h + 1]
        for part, values in enumerate((grad_query, grad_key, grad_value)):
            start = part * inner + h * HEAD
            grads_ref[start : start + HEAD, :] = values.astype(bf16)
    grad_query = grads_ref[0:inner, :]
    grad_key = grads_ref[inner : 2 * inner, :]
    grad_value = grads_ref[2 * inner : 3 * inner, :]
    for copy in copies[3:]:
        copy.wait()
    count = out_ref.shape[0]
    block = norm_ref.shape[0] // count
    first = jnp.zeros_like(valid)
    second = jnp.zeros_like(valid)
    for k in range(count):
        rows = slice(k * block, (k + 1) * block)
        part = jnp.dot(query_weights_ref[rows, :], grad_query, preferred_element_type=f32)
        part = part + jnp.dot(key_weights_ref[rows, :], grad_key, preferred_element_type=f32)
        part = part + jnp.dot(value_weights_ref[rows, :], grad_value, preferred_element_type=f32)
        out_ref[k, 0:block, :] = part.astype(bf16)
        first = first + jnp.sum(part, 0, keepdims=True)
        second = second + jnp.sum(part * norm_ref[rows, :].astype(f32), 0, keepdims=True)
    width = norm_ref.shape[0]
    stats = jnp.concatenate([first, second], 0) * (1.0 / width)
    high = stats.astype(bf16).astype(f32)
    stats = jnp.concatenate(
        [high, stats - high, jnp.zeros((EXTRA - 4, stats.shape[1]), f32)], 0
    ).astype(bf16)
    for k in range(count):
        out_ref[k, block : block + EXTRA, :] = stats


def wide_other(which, norm_ref, grads_ref, out_ref):
    chips, share, columns = out_ref.shape
    rows = [
        norm_ref[pl.ds(pl.multiple_of((CORES * chip + which[0]) * share, 16), share), :]
        for chip in range(chips)
    ]
    values = contract(jnp.concatenate(rows, 0), grads_ref[0:columns, :], 1, 1).astype(bf16)
    for chip in range(chips):
        out_ref[chip] = values[chip * share : (chip + 1) * share]


def wide_own(which, column, norm_ref, grads_ref, got_ref, *outs):
    side = len(outs)
    lines, share, columns = outs[0].shape
    chips = [
        line * side + lax.rem(column[0] + k, side) for k in range(side) for line in range(lines)
    ]
    rows = [
        norm_ref[pl.ds(pl.multiple_of((CORES * chip + which[0]) * share, 16), share), :]
        for chip in chips
    ]
    values = contract(jnp.concatenate(rows, 0), grads_ref[0:columns, :], 1, 1)
    for index, chip in enumerate(chips):
        part = values[index * share : (index + 1) * share] + got_ref[chip].astype(f32)
        outs[index // lines][index % lines] = part.astype(bf16)


def wide_line(line, *refs):
    side = len(refs) // 2
    for k in range(side):
        row = lax.rem(line[0] + k, side)
        total = refs[0][row].astype(f32)
        for ref in refs[1:side]:
            total = total + ref[row].astype(f32)
        refs[side + k][...] = total.astype(bf16)


def slot_grads(
    own_ref, valid_ref, stat_ref, chunk_ref, select_ref, extra_ref, parts_ref, out_ref
):
    total = parts_ref[0].astype(f32)
    for j in range(1, parts_ref.shape[0]):
        total = total + parts_ref[j].astype(f32)
    block = chunk_ref.shape[0] - EXTRA
    first = total[block : block + 1] + total[block + 2 : block + 3]
    second = total[block + 1 : block + 2] + total[block + 3 : block + 4]
    mean = stat_ref[0:1]
    inverse = stat_ref[1:2]
    normed = (chunk_ref[0:block, :].astype(f32) - mean) * inverse
    rows = own_ref[...] * valid_ref[...] + (total[:block] - first - normed * second) * inverse
    rows = contract(select_ref[...], rows.astype(bf16), 1, 1).astype(bf16)
    out_ref[...] = rows + extra_ref[...]


def tile_grads(back_ref, dispatch_ref, out_ref):
    piece = pack(contract(back_ref[...], dispatch_ref[...], 0, 0).astype(bf16))
    out_ref[...] = jnp.broadcast_to(piece[None], out_ref.shape)


def rows_of(which, ref, chips, share):
    rows = [
        ref[pl.ds(pl.multiple_of((CORES * chip + which) * share, 16), share), :]
        for chip in range(chips)
    ]
    return jnp.concatenate(rows, 0)


def other_two(other, hidden_ref, parts_ref, grad_ref, out_ref):
    count = parts_ref.shape[0]
    rows = grad_ref.shape[0] // count
    for j in range(count):
        grad_ref[j * rows : (j + 1) * rows, :] = unpack(parts_ref[j])
    chips, share = out_ref.shape[:2]
    rows = rows_of(other[0], grad_ref, chips, share)
    two = jnp.dot(rows, hidden_ref[...], preferred_element_type=f32).astype(bf16)
    for chip in range(chips):
        out_ref[chip] = two[chip * share : (chip + 1) * share]


def both_one(
    two_ref, slope_ref, other_norm_ref, own_norm_ref, grad_ref, out_ref, own_ref, hidden_grad_ref
):
    grad_hidden = jnp.dot(two_ref[...], grad_ref[...], preferred_element_type=f32)
    hidden_grad_ref[...] = (grad_hidden * slope_ref[...]).astype(bf16)
    chips, share = out_ref.shape[:2]
    for norm_ref, target_ref in ((other_norm_ref, out_ref), (own_norm_ref, own_ref)):
        one = contract(norm_ref[...], hidden_grad_ref[...], 1, 1).astype(bf16)
        for chip in range(chips):
            target_ref[chip] = one[chip * share : (chip + 1) * share]


def own_two(own, column, hidden_ref, grad_ref, got_ref, *outs):
    side = len(outs)
    lines, share = outs[0].shape[:2]
    for k in range(side):
        place = lax.rem(column[0] + k, side)
        chips = [line * side + place for line in range(lines)]
        rows = [
            grad_ref[pl.ds(pl.multiple_of((CORES * chip + own[0]) * share, 16), share), :]
            for chip in chips
        ]
        two = jnp.dot(jnp.concatenate(rows, 0), hidden_ref[...], preferred_element_type=f32)
        for line, chip in enumerate(chips):
            part = two[line * share : (line + 1) * share] + got_ref[chip].astype(f32)
            outs[k][line] = part.astype(bf16)


def own_one(own_ref, got_ref, out_ref):
    side = out_ref.shape[1]
    for chip in range(got_ref.shape[0]):
        part = own_ref[chip].astype(f32) + got_ref[chip].astype(f32)
        out_ref[chip // side, chip % side] = part.astype(bf16)


def add_lines(column, lines_ref, *outs):
    side = len(outs)
    for k in range(side):
        place = lax.rem(column[0] + k, side)
        total = lines_ref[0, place].astype(f32)
        for line in range(1, lines_ref.shape[0]):
            total = total + lines_ref[line, place].astype(f32)
        outs[k][...] = total.astype(bf16)


def last_sums(*refs):
    side = len(refs) // 2 - 1
    for part in range(2):
        total = refs[part * side][...].astype(f32)
        for ref in refs[part * side + 1 : (part + 1) * side]:
            total = total + ref[...].astype(f32)
        refs[2 * side + part][...] = total


def per_device(
    tile_features, tile_slide, slide_pair, reports, w_one, w_two, w_query, w_key, w_value, w_out
):
    lines = lax.axis_size("line")
    side = lax.axis_size("column")
    line = lax.axis_index("line")
    column = lax.axis_index("column")
    chips = lines * side
    owners = chips * CORES
    parts = lax.axis_size("mp")
    core = lax.axis_index("core")
    owner = lax.axis_index(DP)
    here = lax.axis_index("mp")
    tiles, width = tile_features.shape
    units = w_one.shape[1]
    capacity = 2 * tiles // owners
    length = owners * capacity
    slots = owners * ROWS
    block = width // parts
    share = width // owners
    inner = w_query.shape[1]
    heads = inner // HEAD
    packed = (block // 2 * 3, 128)

    def halves(values):
        rest = values.shape[1:]
        values = values.reshape((chips, CORES, share) + rest)
        own = pick(values, core, 1).reshape((chips * share,) + rest)
        other = pick(values, 1 - core, 1).reshape((chips * share,) + rest)
        return own, other

    tile_norm, hidden, slope, partial = call(
        tile_forward,
        [
            ((tiles, width), bf16),
            ((tiles, units), bf16),
            ((tiles, units), f32),
            ((parts,) + packed, bf16),
        ],
        tile_features,
        w_one,
        w_two,
        far=(0, 1, 2),
        scratch=[
            (tile_features.shape, bf16),
            (w_one.shape, bf16),
            (w_two.shape, bf16),
            3,
        ],
        limit=62,
    )
    partial = exchange(partial, "mp")

    slide_ids = tile_slide[:, 0]
    matches = (slide_ids[:, None] == jnp.arange(owners, dtype=i32)[None, :]).astype(i32)
    ordinal = jnp.sum(matches * (jnp.cumsum(matches, 0) - 1), 1)
    position = slide_ids * ROWS + ordinal
    dispatch = jnp.arange(slots, dtype=i32)[:, None] == position[None, :]
    flags = jnp.sum(dispatch.astype(f32), 1, keepdims=True).astype(bf16)
    flags = jnp.pad(flags, ((0, 0), (0, 256 - block - 1)))
    dispatch = dispatch.astype(bf16)
    slot = jnp.arange(slots, dtype=i32)
    row_of_slot = jnp.where(slot % ROWS < capacity, slot // ROWS * capacity + slot % ROWS, -1)
    select = (row_of_slot[:, None] == jnp.arange(length, dtype=i32)[None, :]).astype(bf16)
    last_slot = jnp.arange(owners, dtype=i32)[:, None] * ROWS + ROWS - 1
    report_select = (last_slot == slot[None, :]).astype(bf16)
    own_columns = pick(tile_features.reshape(tiles, parts, block), here, 1)
    own_report = pick(reports.reshape(1, parts, block), here, 1)
    tile_own, tile_other = halves(tile_norm.T)
    slope = slope.T

    (outgoing,) = call(
        tile_dispatch,
        [((slots, 256), bf16)],
        own_columns,
        own_report,
        dispatch,
        flags,
        partial,
        anchors=(select, report_select, tile_own, tile_other, slope),
    )
    arrived = exchange(outgoing.reshape(owners, ROWS, 256), DP).reshape(slots, 256)
    chunk, valid = call(
        slot_rows,
        [((block + EXTRA, length), bf16), ((1, length), f32)],
        arrived,
        select,
        report_select,
    )
    pieces = gather_ring(chunk, parts)

    (
        slide_norm,
        by_head,
        attention,
        stat,
        scales,
        mass,
        attended_sum,
        pooled,
        all_reports,
    ) = call(
        slide_forward,
        [
            ((width, length), bf16, "far"),
            ((heads, 3, HEAD, length), f32, "far"),
            ((heads, length, length), f32, "far"),
            ((2, length), f32),
            ((heads, 2, length), f32),
            ((heads, length), f32),
            ((1, inner), f32),
            ((parts, 1, width), f32),
            ((parts, owners, block), bf16),
        ],
        valid,
        w_query.T,
        w_key.T,
        w_value.T,
        w_out,
        *pieces,
        scalars=(here,),
        far=(1, 2, 3, 4),
        scratch=[
            ((width, length), bf16),
            ((width, length), bf16),
            ((heads, 3, HEAD, length), f32),
            ((heads, length, length), f32),
            ((inner, width), bf16),
            ((inner, width), bf16),
            ((inner, width), bf16),
            ((inner, width), bf16),
            4,
            1 + 2 * heads,
        ],
        limit=60,
    )
    pooled = exchange(pooled, "mp")
    (row,) = call(
        logits_row,
        [((owners, 1, 128), f32)],
        pooled,
        all_reports,
        scratch=[((owners, width), f32)],
    )
    logits = exchange(row, DP).reshape(owners, 128)
    loss, grad, up, grads, sending = call(
        slide_backward,
        [((1, 1), f32), ((1, width), f32), ((1, inner), f32), ((3 * inner, length), bf16)]
        + [((parts, block + EXTRA, length), bf16)],
        logits,
        slide_pair[:, None],
        pooled,
        all_reports,
        valid,
        scales,
        mass,
        w_out,
        by_head,
        attention,
        w_query,
        w_key,
        w_value,
        slide_norm,
        scalars=(owner,),
        far=tuple(range(7, 14)),
        scratch=[
            (w_out.shape, bf16),
            (by_head.shape, f32),
            (attention.shape, f32),
            (w_query.shape, bf16),
            (w_key.shape, bf16),
            (w_value.shape, bf16),
            (slide_norm.shape, bf16),
            ((owners, width), f32),
            7,
        ],
        limit=60,
    )
    received = exchange(sending, "mp")

    (wide_sent,) = call(
        wide_other,
        [((chips, share, 2 * inner), bf16)],
        slide_norm,
        grads,
        scalars=(1 - core,),
    )
    wide_got = lax.ppermute(wide_sent, "core", [(0, 1), (1, 0)])
    along = call(
        wide_own,
        [((lines, share, 2 * inner), bf16)] * side,
        slide_norm,
        grads,
        wide_got,
        scalars=(core, column),
    )
    def shift(values, axis):
        return [values[0]] + [
            lax.ppermute(values[k], axis, turn(len(values), k)) for k in range(1, len(values))
        ]

    along = shift(along, "column")
    across = call(
        wide_line, [((share, 2 * inner), bf16)] * lines, *along, scalars=(line,)
    )
    across = shift(across, "line")
    grad_wide = sum(part.astype(f32) for part in across)
    value_rows = contract(mass.astype(bf16), slide_norm, 1, 1)
    extra = jnp.concatenate(
        [
            value_rows.reshape(heads, owners, share).transpose(1, 0, 2).reshape(owners, -1),
            grad.reshape(owners, share),
            jnp.broadcast_to(up, (owners, inner)),
            jnp.broadcast_to(attended_sum, (owners, inner)),
        ],
        1,
    ).astype(bf16)
    spare = ROWS - capacity
    extra = jnp.pad(extra, ((0, 0), (0, spare * block - extra.shape[1])))
    extra = extra.reshape(owners, spare, block)
    extra = jnp.pad(extra, ((0, 0), (capacity, 0), (0, 0))).reshape(slots, block)

    own_grad = lax.dynamic_slice_in_dim(grad, here * block, block, 1).reshape(block, 1)
    (going,) = call(
        slot_grads,
        [((slots, block), bf16)],
        own_grad,
        valid,
        stat,
        chunk,
        select,
        extra,
        received,
        anchors=(grad_wide,),
    )
    back = exchange(going.reshape(owners, ROWS, block), DP).reshape(slots, block)
    (spreading,) = call(tile_grads, [((parts,) + packed, bf16)], back, dispatch)

    size = (chips, share, units)
    swap = [(0, 1), (1, 0)]
    grad_embedding, two_sent = call(
        other_two,
        [((width, tiles), bf16), (size, bf16)],
        hidden,
        exchange(spreading, "mp"),
        scalars=(1 - core,),
    )
    two_got = lax.ppermute(two_sent, "core", swap)
    one_sent, one_own = call(
        both_one,
        [(size, bf16), (size, bf16)],
        w_two,
        slope,
        tile_other,
        tile_own,
        grad_embedding,
        scratch=[((units, tiles), bf16)],
    )
    one_got = lax.ppermute(one_sent, "core", swap)
    two_along = call(
        own_two,
        [((lines, share, units), bf16)] * side,
        hidden,
        grad_embedding,
        two_got,
        scalars=(core, column),
    )
    (one_across,) = call(
        own_one,
        [((lines, side, share, units), bf16)],
        one_own,
        one_got,
        anchors=(two_along[0],),
    )
    two_along = shift(two_along, "column")
    one_across = exchange(one_across, "line")
    one_along = call(add_lines, [((share, units), bf16)] * side, one_across, scalars=(column,))
    two_across = call(wide_line, [((share, units), bf16)] * lines, *two_along, scalars=(line,))
    grad_one, grad_two = call(
        last_sums,
        [((share, units), f32)] * 2,
        *shift(one_along, "column"),
        *shift(two_across, "line"),
    )
    grad_two = grad_two.T

    terms = back.reshape(owners, ROWS, block)[:, capacity:].reshape(owners, -1).astype(f32)
    edge = heads * share
    from_values = terms[:, :edge].reshape(owners, heads, share)
    from_grads = terms[:, edge : edge + share]
    edge = edge + share
    from_up = terms[:, edge : edge + inner].reshape(owners, heads, HEAD)
    edge = edge + inner
    from_attended = terms[:, edge : edge + inner]
    grad_value = jnp.einsum("ohs,ohd->shd", from_values, from_up, precision=exact)
    grad_value = grad_value.reshape(share, inner)
    grad_out = contract(from_attended, from_grads, 0, 0, precision=exact)
    return (
        loss[0, 0],
        grad_one,
        grad_two,
        grad_wide[:, :inner],
        grad_wide[:, inner:],
        grad_value,
        grad_out,
    )


def solution(mesh):
    owners, parts = mesh.devices.shape
    side = math.isqrt(owners // CORES)
    split = Mesh(
        mesh.devices.reshape(owners // CORES // side, side, CORES, parts),
        ("line", "column", "core", "mp"),
    )
    return jax.shard_map(
        per_device,
        mesh=split,
        in_specs=(
            P(DP, None),
            P(DP, None),
            P(),
            P(DP, None),
            P(None, "mp"),
            P("mp", None),
            P(None, "mp"),
            P(None, "mp"),
            P(None, "mp"),
            P("mp", None),
        ),
        out_specs=(
            P(),
            P(DP, "mp"),
            P("mp", DP),
            P(DP, "mp"),
            P(DP, "mp"),
            P(DP, "mp"),
            P("mp", DP),
        ),
        check_vma=False,
    )
```

```python
import math

import jax
import jax.numpy as jnp
from jax import lax
from jax.experimental import pallas as pl
from jax.experimental.pallas import tpu as pltpu
from jax.sharding import Mesh, PartitionSpec as P

HEAD = 96
CORES = 2
ROWS = 16
EXTRA = 16

eps = 1e-05
contrast_divisor_factor = 0.07
score_scale = 10.0
loss_scale = 4096.0
exact = lax.Precision.HIGHEST
f32 = jnp.float32
bf16 = jnp.bfloat16
i32 = jnp.int32
DP = ("line", "column", "core")


def contract(left, right, left_dim, right_dim, **kw):
    return lax.dot_general(
        left, right, (((left_dim,), (right_dim,)), ((), ())), preferred_element_type=f32, **kw
    )


def exchange(values, axis):
    return lax.all_to_all(values, axis, 0, 0, tiled=True)


def pick(values, index, axis):
    return lax.dynamic_index_in_dim(values, index, axis, keepdims=False)


def call(body, outs, *args, scalars=(), scratch=(), anchors=(), far=(), limit=16):
    count = len(scalars)
    skip = len(anchors)
    vmem = pl.BlockSpec(memory_space=pltpu.VMEM)
    away = pl.BlockSpec(memory_space=pltpu.HBM)

    def kernel(*refs):
        body(*refs[skip:])

    return pl.pallas_call(
        kernel if skip else body,
        out_shape=[jax.ShapeDtypeStruct(out[0], out[1]) for out in outs],
        in_specs=[pl.BlockSpec(memory_space=pl.ANY)] * skip
        + [pl.BlockSpec(memory_space=pltpu.SMEM)] * count
        + [away if index in far else vmem for index in range(len(args))],
        out_specs=[vmem if len(out) == 2 else away for out in outs],
        scratch_shapes=[
            pltpu.VMEM(*part) if isinstance(part, tuple) else pltpu.SemaphoreType.DMA((part,))
            for part in scratch
        ],
        compiler_params=pltpu.CompilerParams(vmem_limit_bytes=limit * 1024 * 1024),
    )(*anchors, *[jnp.reshape(s, (1,)).astype(i32) for s in scalars], *args)


def fetch(sources, targets, semaphores):
    copies = [
        pltpu.make_async_copy(source, target, semaphores.at[index])
        for index, (source, target) in enumerate(zip(sources, targets))
    ]
    for copy in copies:
        copy.start()
    return copies


def turn(count, step):
    return [(index, (index + step) % count) for index in range(count)]


def gather_ring(piece, count):
    found = [piece]
    back = ahead = piece
    for _ in range(count // 2 - 1):
        back = lax.ppermute(back, "mp", turn(count, 1))
        ahead = lax.ppermute(ahead, "mp", turn(count, count - 1))
        found += [back, ahead]
    half = (piece.shape[0] // 2 + ROWS - 1) // ROWS * ROWS
    found.append(lax.ppermute(back[:half], "mp", turn(count, 1)))
    found.append(lax.ppermute(ahead[half:], "mp", turn(count, count - 1)))
    return found


def place(refs, here, count, store):
    half = count // 2
    store(here, refs[0][...])
    for step in range(1, half):
        for ref, sign in ((refs[2 * step - 1], -1), (refs[2 * step], 1)):
            store(lax.rem(here + sign * step + count, count), ref[...])
    store(
        lax.rem(here + half, count), jnp.concatenate([refs[-2][...], refs[-1][...]], 0)
    )


def pack(square):
    half = square.shape[0] // 2
    side = square[:, 128:]
    return jnp.concatenate(
        [square[:, :128], jnp.concatenate([side[:half], side[half:]], 1)], 0
    )


def unpack(packed):
    rows = packed.shape[0] // 3 * 2
    side = packed[rows:]
    return jnp.concatenate(
        [packed[:rows], jnp.concatenate([side[:, :64], side[:, 64:]], 0)], 1
    )


def tile_forward(
    far_x, far_one, far_two, norm_ref, hidden_ref, slope_ref, out_ref, x_ref, one_ref, two_ref, sems
):
    copies = fetch((far_x, far_one, far_two), (x_ref, one_ref, two_ref), sems)
    copies[0].wait()
    x = x_ref[...].astype(f32)
    centred = x - jnp.mean(x, -1, keepdims=True)
    normed = centred * lax.rsqrt(jnp.mean(centred * centred, -1, keepdims=True) + eps)
    normed = normed.astype(bf16)
    norm_ref[...] = normed
    copies[1].wait()
    pre = jnp.dot(normed, one_ref[...], preferred_element_type=f32)
    bell = 0.5 * (1.0 + lax.erf(pre * 0.7071067811865476))
    hidden = (pre * bell).astype(bf16)
    hidden_ref[...] = hidden
    slope_ref[...] = bell + pre * jnp.exp(-0.5 * pre * pre) * 0.3989422804014327
    copies[2].wait()
    partial = jnp.dot(hidden, two_ref[...], preferred_element_type=f32).astype(bf16)
    count = out_ref.shape[0]
    block = partial.shape[1] // count
    for j in range(count):
        out_ref[j] = pack(partial[:, j * block : (j + 1) * block])


def tile_dispatch(own_ref, report_ref, dispatch_ref, flags_ref, parts_ref, out_ref):
    total = parts_ref[0].astype(f32)
    for j in range(1, parts_ref.shape[0]):
        total = total + parts_ref[j].astype(f32)
    embedding = (own_ref[...].astype(f32) + unpack(total)).astype(bf16)
    rows = jnp.dot(dispatch_ref[...], embedding, preferred_element_type=f32)
    slot = lax.broadcasted_iota(i32, rows.shape, 0)
    rows = jnp.where(lax.rem(slot, ROWS) == ROWS - 1, report_ref[...].astype(f32), rows)
    out_ref[...] = jnp.concatenate([rows.astype(bf16), flags_ref[...]], 1)


def slot_rows(arrived_ref, select_ref, report_select_ref, chunk_ref, valid_ref):
    arrived = arrived_ref[...]
    chunk = contract(arrived, select_ref[...], 0, 0)
    block = chunk_ref.shape[0] - EXTRA
    chunk_ref[0:block, :] = chunk[:block].astype(bf16)
    valid_ref[...] = chunk[block : block + 1]
    reports = jnp.dot(report_select_ref[...], arrived, preferred_element_type=f32)
    reports = reports[:, :block].astype(bf16)
    chunk_ref[block : block + EXTRA, :] = jnp.concatenate(
        [reports[:EXTRA], reports[EXTRA:]], 1
    )


def slide_forward(
    here,
    valid_ref,
    far_query_weights,
    far_key_weights,
    far_value_weights,
    far_out_weights,
    *rest,
):
    pieces = rest[:9]
    (
        far_norm,
        far_heads,
        far_attention,
        stat_ref,
        scale_ref,
        mass_ref,
        attended_ref,
        pooled_ref,
        reports_ref,
        slide_ref,
        norm_ref,
        heads_ref,
        attention_ref,
        query_weights_ref,
        key_weights_ref,
        value_weights_ref,
        out_weights_ref,
        weight_sems,
        sems,
    ) = rest[9:]
    fetched = fetch(
        (far_query_weights, far_key_weights, far_value_weights, far_out_weights),
        (query_weights_ref, key_weights_ref, value_weights_ref, out_weights_ref),
        weight_sems,
    )
    count, owners, block = reports_ref.shape

    def store(index, piece):
        start = pl.multiple_of(index * block, 16)
        slide_ref[pl.ds(start, block), :] = piece[:block]
        reports = piece[block:]
        reports_ref[index] = jnp.concatenate([reports[:, :block], reports[:, block:]], 0)

    place(pieces, here[0], count, store)
    valid = valid_ref[...]
    valid_low = valid.astype(bf16)
    low = slide_ref[...]
    slide = low.astype(f32)
    mean = jnp.mean(slide, 0, keepdims=True)
    centred = slide - mean
    inverse = lax.rsqrt(jnp.mean(centred * centred, 0, keepdims=True) + eps)
    stat_ref[...] = jnp.concatenate([mean, inverse], 0)
    normed = (centred * inverse).astype(bf16)
    norm_ref[...] = normed
    copies = [pltpu.make_async_copy(norm_ref, far_norm, sems.at[0])]
    copies[0].start()
    for copy in fetched:
        copy.wait()
    all_query = jnp.dot(query_weights_ref[...], normed, preferred_element_type=f32)
    all_keys = jnp.dot(key_weights_ref[...], normed, preferred_element_type=f32)
    all_values = jnp.dot(value_weights_ref[...], normed, preferred_element_type=f32)
    heads = all_query.shape[0] // HEAD
    attended = []
    for h in range(heads):
        low_rows, high_rows = h * HEAD, (h + 1) * HEAD
        query = all_query[low_rows:high_rows]
        keys = all_keys[low_rows:high_rows]
        values = all_values[low_rows:high_rows]
        query_scale = lax.rsqrt(jnp.mean(query * query, 0, keepdims=True) + eps)
        key_scale = lax.rsqrt(jnp.mean(keys * keys, 0, keepdims=True) + eps)
        query_unit = query * query_scale
        key_unit = keys * key_scale
        heads_ref[h, 0] = query_unit
        heads_ref[h, 1] = key_unit
        heads_ref[h, 2] = values
        copies.append(pltpu.make_async_copy(heads_ref.at[h], far_heads.at[h], sems.at[1 + 2 * h]))
        copies[-1].start()
        scale_ref[h] = jnp.concatenate([query_scale, key_scale], 0)
        scores = contract(query_unit.astype(bf16), key_unit.astype(bf16), 0, 0)
        weights = jnp.exp(scores * (score_scale / HEAD)) * valid
        weights = weights * (1.0 / jnp.sum(weights, 1, keepdims=True))
        attention_ref[h] = weights
        copies.append(
            pltpu.make_async_copy(attention_ref.at[h], far_attention.at[h], sems.at[2 + 2 * h])
        )
        copies[-1].start()
        weights_low = weights.astype(bf16)
        mass_ref[h : h + 1, :] = jnp.dot(valid_low, weights_low, preferred_element_type=f32)
        attended.append(contract(values.astype(bf16), weights_low, 1, 1))
    attended = jnp.concatenate(attended, 0).astype(bf16)
    attended_sum = contract(valid_low, attended, 1, 1)
    attended_ref[...] = attended_sum
    high = attended_sum.astype(bf16)
    rest_low = (attended_sum - high.astype(f32)).astype(bf16)
    part = jnp.dot(high, out_weights_ref[...], preferred_element_type=f32)
    part = part + jnp.dot(rest_low, out_weights_ref[...], preferred_element_type=f32)
    slide_sum = contract(valid_low, low, 1, 1)
    pooled = (part + slide_sum * (1.0 / count)) / jnp.sum(valid)
    pooled_ref[...] = jnp.broadcast_to(pooled[None], pooled_ref.shape)
    for copy in copies:
        copy.wait()


def unit_vectors(parts_ref, reports_ref, report_ref):
    pooled = jnp.sum(parts_ref[...], 0)
    inverse = lax.rsqrt(jnp.sum(pooled * pooled, -1, keepdims=True) + eps)
    count, owners, block = reports_ref.shape
    squares = jnp.zeros((owners, 1), f32)
    for j in range(count):
        reports = reports_ref[j].astype(f32)
        report_ref[:, j * block : (j + 1) * block] = reports
        squares = squares + jnp.sum(reports * reports, -1, keepdims=True)
    report = report_ref[...] * lax.rsqrt(squares + eps)
    return pooled * inverse, inverse, report


def logits_row(parts_ref, reports_ref, row_ref, report_ref):
    unit, inverse, report = unit_vectors(parts_ref, reports_ref, report_ref)
    row = contract(unit, report, 1, 1, precision=exact) / contrast_divisor_factor
    pad = row_ref.shape[2] - row.shape[1]
    row = jnp.concatenate([row, jnp.zeros((1, pad), f32)], 1)
    row_ref[...] = jnp.broadcast_to(row[None], row_ref.shape)


def slide_backward(
    owner,
    logits_ref,
    pair_ref,
    parts_ref,
    reports_ref,
    valid_ref,
    scale_ref,
    mass_ref,
    far_out_weights,
    far_heads,
    far_attention,
    far_query_weights,
    far_key_weights,
    far_value_weights,
    far_norm,
    loss_ref,
    grad_ref,
    up_ref,
    grads_ref,
    out_ref,
    *rest,
):
    fetched, report_ref, sems = rest[:-2], rest[-2], rest[-1]
    (
        out_weights_ref,
        heads_ref,
        attention_ref,
        query_weights_ref,
        key_weights_ref,
        value_weights_ref,
        norm_ref,
    ) = fetched
    copies = fetch(
        (
            far_out_weights,
            far_heads,
            far_attention,
            far_query_weights,
            far_key_weights,
            far_value_weights,
            far_norm,
        ),
        fetched,
        sems,
    )
    unit, inverse, report = unit_vectors(parts_ref, reports_ref, report_ref)
    owners = report.shape[0]
    valid = valid_ref[...]
    logits = logits_ref[...]
    shape = logits.shape
    columns = lax.broadcasted_iota(i32, shape, 1)
    rows = lax.broadcasted_iota(i32, shape, 0)
    real = columns < owners
    expo = jnp.where(real, jnp.exp(logits), 0.0)
    row_total = jnp.sum(expo, 1, keepdims=True)
    column_total = jnp.where(real[:1], jnp.sum(expo, 0, keepdims=True), 1.0)
    target = jnp.where(pair_ref[...] == columns, 1.0, 0.0)
    loss = jnp.sum(
        0.5 * jnp.log(row_total) - jnp.sum(logits * target, 1, keepdims=True), 0, keepdims=True
    )
    loss = loss + 0.5 * jnp.sum(jnp.log(column_total), 1, keepdims=True)
    loss_ref[...] = loss * (1.0 / owners)
    grad_logits = (0.5 * expo / row_total + 0.5 * expo / column_total - target) * (
        loss_scale / owners
    )
    grad_row = jnp.sum(jnp.where(rows == owner[0], grad_logits, 0.0), 0, keepdims=True)
    grad_unit = (
        jnp.dot(grad_row[:, :owners], report, precision=exact, preferred_element_type=f32)
        / contrast_divisor_factor
    )
    grad_pooled = (grad_unit - unit * jnp.sum(unit * grad_unit, -1, keepdims=True)) * inverse
    grad = grad_pooled / jnp.sum(valid)
    grad_ref[...] = grad
    low = grad.astype(bf16)
    copies[0].wait()
    out_weights = out_weights_ref[...]
    up_ref[...] = contract(low, out_weights, 1, 1)
    up = jnp.sum(out_weights.astype(f32) * low.astype(f32), 1, keepdims=True)
    heads = heads_ref.shape[0]
    inner = heads * HEAD
    copies[1].wait()
    copies[2].wait()
    for h in range(heads):
        up_head = up[h * HEAD : (h + 1) * HEAD]
        values = heads_ref[h, 2]
        weights = attention_ref[h]
        pull = jnp.sum(up_head * values, 0, keepdims=True)
        pull_mean = jnp.sum(weights * pull, 1, keepdims=True)
        grad_scores = (weights * (pull - pull_mean) * (score_scale / HEAD)).astype(bf16)
        query_unit = heads_ref[h, 0]
        key_unit = heads_ref[h, 1]
        grad_query = contract(key_unit.astype(bf16), grad_scores, 1, 1) * valid
        grad_key = jnp.dot(query_unit.astype(bf16), grad_scores, preferred_element_type=f32)
        grad_query = scale_ref[h, 0:1] * (
            grad_query - query_unit * jnp.mean(query_unit * grad_query, 0, keepdims=True)
        )
        grad_key = scale_ref[h, 1:2] * (
            grad_key - key_unit * jnp.mean(key_unit * grad_key, 0, keepdims=True)
        )
        grad_value = up_head * mass_ref[h : h + 1]
        for part, values in enumerate((grad_query, grad_key, grad_value)):
            start = part * inner + h * HEAD
            grads_ref[start : start + HEAD, :] = values.astype(bf16)
    grad_query = grads_ref[0:inner, :]
    grad_key = grads_ref[inner : 2 * inner, :]
    grad_value = grads_ref[2 * inner : 3 * inner, :]
    for copy in copies[3:]:
        copy.wait()
    count = out_ref.shape[0]
    block = norm_ref.shape[0] // count
    first = jnp.zeros_like(valid)
    second = jnp.zeros_like(valid)
    for k in range(count):
        rows = slice(k * block, (k + 1) * block)
        part = jnp.dot(query_weights_ref[rows, :], grad_query, preferred_element_type=f32)
        part = part + jnp.dot(key_weights_ref[rows, :], grad_key, preferred_element_type=f32)
        part = part + jnp.dot(value_weights_ref[rows, :], grad_value, preferred_element_type=f32)
        out_ref[k, 0:block, :] = part.astype(bf16)
        first = first + jnp.sum(part, 0, keepdims=True)
        second = second + jnp.sum(part * norm_ref[rows, :].astype(f32), 0, keepdims=True)
    width = norm_ref.shape[0]
    stats = jnp.concatenate([first, second], 0) * (1.0 / width)
    high = stats.astype(bf16).astype(f32)
    stats = jnp.concatenate(
        [high, stats - high, jnp.zeros((EXTRA - 4, stats.shape[1]), f32)], 0
    ).astype(bf16)
    for k in range(count):
        out_ref[k, block : block + EXTRA, :] = stats


def wide_other(which, norm_ref, grads_ref, out_ref):
    chips, share, columns = out_ref.shape
    rows = [
        norm_ref[pl.ds(pl.multiple_of((CORES * chip + which[0]) * share, 16), share), :]
        for chip in range(chips)
    ]
    values = contract(jnp.concatenate(rows, 0), grads_ref[0:columns, :], 1, 1).astype(bf16)
    for chip in range(chips):
        out_ref[chip] = values[chip * share : (chip + 1) * share]


def wide_own(which, column, norm_ref, grads_ref, got_ref, *outs):
    side = len(outs)
    lines, share, columns = outs[0].shape
    chips = [
        line * side + lax.rem(column[0] + k, side) for k in range(side) for line in range(lines)
    ]
    rows = [
        norm_ref[pl.ds(pl.multiple_of((CORES * chip + which[0]) * share, 16), share), :]
        for chip in chips
    ]
    values = contract(jnp.concatenate(rows, 0), grads_ref[0:columns, :], 1, 1)
    for index, chip in enumerate(chips):
        part = values[index * share : (index + 1) * share] + got_ref[chip].astype(f32)
        outs[index // lines][index % lines] = part.astype(bf16)


def wide_line(line, *refs):
    side = len(refs) // 2
    for k in range(side):
        row = lax.rem(line[0] + k, side)
        total = refs[0][row].astype(f32)
        for ref in refs[1:side]:
            total = total + ref[row].astype(f32)
        refs[side + k][...] = total.astype(bf16)


def slot_grads(
    own_ref, valid_ref, stat_ref, chunk_ref, select_ref, extra_ref, parts_ref, out_ref
):
    total = parts_ref[0].astype(f32)
    for j in range(1, parts_ref.shape[0]):
        total = total + parts_ref[j].astype(f32)
    block = chunk_ref.shape[0] - EXTRA
    first = total[block : block + 1] + total[block + 2 : block + 3]
    second = total[block + 1 : block + 2] + total[block + 3 : block + 4]
    mean = stat_ref[0:1]
    inverse = stat_ref[1:2]
    normed = (chunk_ref[0:block, :].astype(f32) - mean) * inverse
    rows = own_ref[...] * valid_ref[...] + (total[:block] - first - normed * second) * inverse
    rows = contract(select_ref[...], rows.astype(bf16), 1, 1).astype(bf16)
    out_ref[...] = rows + extra_ref[...]


def tile_grads(back_ref, dispatch_ref, out_ref):
    piece = pack(contract(back_ref[...], dispatch_ref[...], 0, 0).astype(bf16))
    out_ref[...] = jnp.broadcast_to(piece[None], out_ref.shape)


def rows_of(which, ref, chips, share):
    rows = [
        ref[pl.ds(pl.multiple_of((CORES * chip + which) * share, 16), share), :]
        for chip in range(chips)
    ]
    return jnp.concatenate(rows, 0)


def other_two(other, hidden_ref, parts_ref, grad_ref, out_ref):
    count = parts_ref.shape[0]
    rows = grad_ref.shape[0] // count
    for j in range(count):
        grad_ref[j * rows : (j + 1) * rows, :] = unpack(parts_ref[j])
    chips, share = out_ref.shape[:2]
    rows = rows_of(other[0], grad_ref, chips, share)
    two = jnp.dot(rows, hidden_ref[...], preferred_element_type=f32).astype(bf16)
    for chip in range(chips):
        out_ref[chip] = two[chip * share : (chip + 1) * share]


def both_one(
    two_ref, slope_ref, other_norm_ref, own_norm_ref, grad_ref, out_ref, own_ref, hidden_grad_ref
):
    grad_hidden = jnp.dot(two_ref[...], grad_ref[...], preferred_element_type=f32)
    hidden_grad_ref[...] = (grad_hidden * slope_ref[...]).astype(bf16)
    chips, share = out_ref.shape[:2]
    for norm_ref, target_ref in ((other_norm_ref, out_ref), (own_norm_ref, own_ref)):
        one = contract(norm_ref[...], hidden_grad_ref[...], 1, 1).astype(bf16)
        for chip in range(chips):
            target_ref[chip] = one[chip * share : (chip + 1) * share]


def own_two(own, hidden_ref, grad_ref, got_ref, out_ref):
    chips, share = got_ref.shape[:2]
    side = out_ref.shape[1]
    rows = rows_of(own[0], grad_ref, chips, share)
    two = jnp.dot(rows, hidden_ref[...], preferred_element_type=f32)
    for chip in range(chips):
        part = two[chip * share : (chip + 1) * share] + got_ref[chip].astype(f32)
        out_ref[chip // side, chip % side] = part.astype(bf16)


def own_one(column, own_ref, got_ref, *outs):
    side = len(outs)
    for k in range(side):
        place = lax.rem(column[0] + k, side)
        for line in range(outs[k].shape[0]):
            chip = line * side + place
            part = own_ref[chip].astype(f32) + got_ref[chip].astype(f32)
            outs[k][line] = part.astype(bf16)


def add_up(*refs):
    total = refs[0][...].astype(f32)
    for ref in refs[1:-1]:
        total = total + ref[...].astype(f32)
    refs[-1][...] = total.astype(refs[-1].dtype)


def add_lines(column, lines_ref, *outs):
    side = len(outs)
    for k in range(side):
        place = lax.rem(column[0] + k, side)
        total = lines_ref[0, place].astype(f32)
        for line in range(1, lines_ref.shape[0]):
            total = total + lines_ref[line, place].astype(f32)
        outs[k][...] = total.astype(bf16)


def last_sums(lines_ref, *refs):
    one_ref, two_ref = refs[-2:]
    total = lines_ref[0].astype(f32)
    for line in range(1, lines_ref.shape[0]):
        total = total + lines_ref[line].astype(f32)
    one_ref[...] = total
    total = refs[0][...].astype(f32)
    for ref in refs[1:-2]:
        total = total + ref[...].astype(f32)
    two_ref[...] = total


def per_device(
    tile_features, tile_slide, slide_pair, reports, w_one, w_two, w_query, w_key, w_value, w_out
):
    lines = lax.axis_size("line")
    side = lax.axis_size("column")
    line = lax.axis_index("line")
    column = lax.axis_index("column")
    chips = lines * side
    owners = chips * CORES
    parts = lax.axis_size("mp")
    core = lax.axis_index("core")
    owner = lax.axis_index(DP)
    here = lax.axis_index("mp")
    tiles, width = tile_features.shape
    units = w_one.shape[1]
    capacity = 2 * tiles // owners
    length = owners * capacity
    slots = owners * ROWS
    block = width // parts
    share = width // owners
    inner = w_query.shape[1]
    heads = inner // HEAD
    packed = (block // 2 * 3, 128)

    def halves(values):
        rest = values.shape[1:]
        values = values.reshape((chips, CORES, share) + rest)
        own = pick(values, core, 1).reshape((chips * share,) + rest)
        other = pick(values, 1 - core, 1).reshape((chips * share,) + rest)
        return own, other

    tile_norm, hidden, slope, partial = call(
        tile_forward,
        [
            ((tiles, width), bf16),
            ((tiles, units), bf16),
            ((tiles, units), f32),
            ((parts,) + packed, bf16),
        ],
        tile_features,
        w_one,
        w_two,
        far=(0, 1, 2),
        scratch=[
            (tile_features.shape, bf16),
            (w_one.shape, bf16),
            (w_two.shape, bf16),
            3,
        ],
        limit=62,
    )
    partial = exchange(partial, "mp")

    slide_ids = tile_slide[:, 0]
    matches = (slide_ids[:, None] == jnp.arange(owners, dtype=i32)[None, :]).astype(i32)
    ordinal = jnp.sum(matches * (jnp.cumsum(matches, 0) - 1), 1)
    position = slide_ids * ROWS + ordinal
    dispatch = jnp.arange(slots, dtype=i32)[:, None] == position[None, :]
    flags = jnp.sum(dispatch.astype(f32), 1, keepdims=True).astype(bf16)
    flags = jnp.pad(flags, ((0, 0), (0, 256 - block - 1)))
    dispatch = dispatch.astype(bf16)
    slot = jnp.arange(slots, dtype=i32)
    row_of_slot = jnp.where(slot % ROWS < capacity, slot // ROWS * capacity + slot % ROWS, -1)
    select = (row_of_slot[:, None] == jnp.arange(length, dtype=i32)[None, :]).astype(bf16)
    last_slot = jnp.arange(owners, dtype=i32)[:, None] * ROWS + ROWS - 1
    report_select = (last_slot == slot[None, :]).astype(bf16)
    own_columns = pick(tile_features.reshape(tiles, parts, block), here, 1)
    own_report = pick(reports.reshape(1, parts, block), here, 1)
    tile_own, tile_other = halves(tile_norm.T)
    slope = slope.T

    (outgoing,) = call(
        tile_dispatch,
        [((slots, 256), bf16)],
        own_columns,
        own_report,
        dispatch,
        flags,
        partial,
        anchors=(select, report_select, tile_own, tile_other, slope),
    )
    arrived = exchange(outgoing.reshape(owners, ROWS, 256), DP).reshape(slots, 256)
    chunk, valid = call(
        slot_rows,
        [((block + EXTRA, length), bf16), ((1, length), f32)],
        arrived,
        select,
        report_select,
    )
    pieces = gather_ring(chunk, parts)

    (
        slide_norm,
        by_head,
        attention,
        stat,
        scales,
        mass,
        attended_sum,
        pooled,
        all_reports,
    ) = call(
        slide_forward,
        [
            ((width, length), bf16, "far"),
            ((heads, 3, HEAD, length), f32, "far"),
            ((heads, length, length), f32, "far"),
            ((2, length), f32),
            ((heads, 2, length), f32),
            ((heads, length), f32),
            ((1, inner), f32),
            ((parts, 1, width), f32),
            ((parts, owners, block), bf16),
        ],
        valid,
        w_query.T,
        w_key.T,
        w_value.T,
        w_out,
        *pieces,
        scalars=(here,),
        far=(1, 2, 3, 4),
        scratch=[
            ((width, length), bf16),
            ((width, length), bf16),
            ((heads, 3, HEAD, length), f32),
            ((heads, length, length), f32),
            ((inner, width), bf16),
            ((inner, width), bf16),
            ((inner, width), bf16),
            ((inner, width), bf16),
            4,
            1 + 2 * heads,
        ],
        limit=60,
    )
    pooled = exchange(pooled, "mp")
    (row,) = call(
        logits_row,
        [((owners, 1, 128), f32)],
        pooled,
        all_reports,
        scratch=[((owners, width), f32)],
    )
    logits = exchange(row, DP).reshape(owners, 128)
    loss, grad, up, grads, sending = call(
        slide_backward,
        [((1, 1), f32), ((1, width), f32), ((1, inner), f32), ((3 * inner, length), bf16)]
        + [((parts, block + EXTRA, length), bf16)],
        logits,
        slide_pair[:, None],
        pooled,
        all_reports,
        valid,
        scales,
        mass,
        w_out,
        by_head,
        attention,
        w_query,
        w_key,
        w_value,
        slide_norm,
        scalars=(owner,),
        far=tuple(range(7, 14)),
        scratch=[
            (w_out.shape, bf16),
            (by_head.shape, f32),
            (attention.shape, f32),
            (w_query.shape, bf16),
            (w_key.shape, bf16),
            (w_value.shape, bf16),
            (slide_norm.shape, bf16),
            ((owners, width), f32),
            7,
        ],
        limit=60,
    )
    received = exchange(sending, "mp")

    (wide_sent,) = call(
        wide_other,
        [((chips, share, 2 * inner), bf16)],
        slide_norm,
        grads,
        scalars=(1 - core,),
    )
    wide_got = lax.ppermute(wide_sent, "core", [(0, 1), (1, 0)])
    along = call(
        wide_own,
        [((lines, share, 2 * inner), bf16)] * side,
        slide_norm,
        grads,
        wide_got,
        scalars=(core, column),
    )
    def shift(values, axis):
        return [values[0]] + [
            lax.ppermute(values[k], axis, turn(len(values), k)) for k in range(1, len(values))
        ]

    along = shift(along, "column")
    across = call(
        wide_line, [((share, 2 * inner), bf16)] * lines, *along, scalars=(line,)
    )
    across = shift(across, "line")
    grad_wide = sum(part.astype(f32) for part in across)
    value_rows = contract(mass.astype(bf16), slide_norm, 1, 1)
    extra = jnp.concatenate(
        [
            value_rows.reshape(heads, owners, share).transpose(1, 0, 2).reshape(owners, -1),
            grad.reshape(owners, share),
            jnp.broadcast_to(up, (owners, inner)),
            jnp.broadcast_to(attended_sum, (owners, inner)),
        ],
        1,
    ).astype(bf16)
    spare = ROWS - capacity
    extra = jnp.pad(extra, ((0, 0), (0, spare * block - extra.shape[1])))
    extra = extra.reshape(owners, spare, block)
    extra = jnp.pad(extra, ((0, 0), (capacity, 0), (0, 0))).reshape(slots, block)

    own_grad = lax.dynamic_slice_in_dim(grad, here * block, block, 1).reshape(block, 1)
    (going,) = call(
        slot_grads,
        [((slots, block), bf16)],
        own_grad,
        valid,
        stat,
        chunk,
        select,
        extra,
        received,
        anchors=(grad_wide,),
    )
    back = exchange(going.reshape(owners, ROWS, block), DP).reshape(slots, block)
    (spreading,) = call(tile_grads, [((parts,) + packed, bf16)], back, dispatch)

    size = (chips, share, units)
    swap = [(0, 1), (1, 0)]
    grad_embedding, two_sent = call(
        other_two,
        [((width, tiles), bf16), (size, bf16)],
        hidden,
        exchange(spreading, "mp"),
        scalars=(1 - core,),
    )
    two_got = lax.ppermute(two_sent, "core", swap)
    one_sent, one_own = call(
        both_one,
        [(size, bf16), (size, bf16)],
        w_two,
        slope,
        tile_other,
        tile_own,
        grad_embedding,
        scratch=[((units, tiles), bf16)],
    )
    one_got = lax.ppermute(one_sent, "core", swap)
    (two_across,) = call(
        own_two,
        [((lines, side, share, units), bf16)],
        hidden,
        grad_embedding,
        two_got,
        scalars=(core,),
    )
    two_across = exchange(two_across, "line")
    one_along = call(
        own_one,
        [((lines, share, units), bf16)] * side,
        one_own,
        one_got,
        scalars=(column,),
    )
    (one_across,) = call(
        add_up, [((lines, share, units), bf16)], *shift(one_along, "column")
    )
    two_along = call(add_lines, [((share, units), bf16)] * side, two_across, scalars=(column,))
    grad_one, grad_two = call(
        last_sums,
        [((share, units), f32)] * 2,
        exchange(one_across, "line"),
        *shift(two_along, "column"),
    )
    grad_two = grad_two.T

    terms = back.reshape(owners, ROWS, block)[:, capacity:].reshape(owners, -1).astype(f32)
    edge = heads * share
    from_values = terms[:, :edge].reshape(owners, heads, share)
    from_grads = terms[:, edge : edge + share]
    edge = edge + share
    from_up = terms[:, edge : edge + inner].reshape(owners, heads, HEAD)
    edge = edge + inner
    from_attended = terms[:, edge : edge + inner]
    grad_value = jnp.einsum("ohs,ohd->shd", from_values, from_up, precision=exact)
    grad_value = grad_value.reshape(share, inner)
    grad_out = contract(from_attended, from_grads, 0, 0, precision=exact)
    return (
        loss[0, 0],
        grad_one,
        grad_two,
        grad_wide[:, :inner],
        grad_wide[:, inner:],
        grad_value,
        grad_out,
    )


def solution(mesh):
    owners, parts = mesh.devices.shape
    side = math.isqrt(owners // CORES)
    split = Mesh(
        mesh.devices.reshape(owners // CORES // side, side, CORES, parts),
        ("line", "column", "core", "mp"),
    )
    return jax.shard_map(
        per_device,
        mesh=split,
        in_specs=(
            P(DP, None),
            P(DP, None),
            P(),
            P(DP, None),
            P(None, "mp"),
            P("mp", None),
            P(None, "mp"),
            P(None, "mp"),
            P(None, "mp"),
            P("mp", None),
        ),
        out_specs=(
            P(),
            P(DP, "mp"),
            P("mp", DP),
            P(DP, "mp"),
            P(DP, "mp"),
            P(DP, "mp"),
            P("mp", DP),
        ),
        check_vma=False,
    )
```

```python
import math

import jax
import jax.numpy as jnp
from jax import lax
from jax.experimental import pallas as pl
from jax.experimental.pallas import tpu as pltpu
from jax.sharding import Mesh, PartitionSpec as P

HEAD = 96
CORES = 2
ROWS = 16
EXTRA = 16

eps = 1e-05
contrast_divisor_factor = 0.07
score_scale = 10.0
loss_scale = 4096.0
exact = lax.Precision.HIGHEST
f32 = jnp.float32
bf16 = jnp.bfloat16
i32 = jnp.int32
DP = ("line", "column", "core")


def contract(left, right, left_dim, right_dim, **kw):
    return lax.dot_general(
        left, right, (((left_dim,), (right_dim,)), ((), ())), preferred_element_type=f32, **kw
    )


def exchange(values, axis):
    return lax.all_to_all(values, axis, 0, 0, tiled=True)


def pick(values, index, axis):
    return lax.dynamic_index_in_dim(values, index, axis, keepdims=False)


def call(body, outs, *args, scalars=(), scratch=(), anchors=(), far=(), limit=16):
    count = len(scalars)
    skip = len(anchors)
    vmem = pl.BlockSpec(memory_space=pltpu.VMEM)
    away = pl.BlockSpec(memory_space=pltpu.HBM)

    def kernel(*refs):
        body(*refs[skip:])

    return pl.pallas_call(
        kernel if skip else body,
        out_shape=[jax.ShapeDtypeStruct(out[0], out[1]) for out in outs],
        in_specs=[pl.BlockSpec(memory_space=pl.ANY)] * skip
        + [pl.BlockSpec(memory_space=pltpu.SMEM)] * count
        + [away if index in far else vmem for index in range(len(args))],
        out_specs=[vmem if len(out) == 2 else away for out in outs],
        scratch_shapes=[
            pltpu.VMEM(*part) if isinstance(part, tuple) else pltpu.SemaphoreType.DMA((part,))
            for part in scratch
        ],
        compiler_params=pltpu.CompilerParams(vmem_limit_bytes=limit * 1024 * 1024),
    )(*anchors, *[jnp.reshape(s, (1,)).astype(i32) for s in scalars], *args)


def fetch(sources, targets, semaphores):
    copies = [
        pltpu.make_async_copy(source, target, semaphores.at[index])
        for index, (source, target) in enumerate(zip(sources, targets))
    ]
    for copy in copies:
        copy.start()
    return copies


def turn(count, step):
    return [(index, (index + step) % count) for index in range(count)]


def gather_ring(piece, count):
    found = [piece]
    back = ahead = piece
    for _ in range(count // 2 - 1):
        back = lax.ppermute(back, "mp", turn(count, 1))
        ahead = lax.ppermute(ahead, "mp", turn(count, count - 1))
        found += [back, ahead]
    half = (piece.shape[0] // 2 + ROWS - 1) // ROWS * ROWS
    found.append(lax.ppermute(back[:half], "mp", turn(count, 1)))
    found.append(lax.ppermute(ahead[half:], "mp", turn(count, count - 1)))
    return found


def place(refs, here, count, store):
    half = count // 2
    store(here, refs[0][...])
    for step in range(1, half):
        for ref, sign in ((refs[2 * step - 1], -1), (refs[2 * step], 1)):
            store(lax.rem(here + sign * step + count, count), ref[...])
    store(
        lax.rem(here + half, count), jnp.concatenate([refs[-2][...], refs[-1][...]], 0)
    )


def pack(square):
    half = square.shape[0] // 2
    side = square[:, 128:]
    return jnp.concatenate(
        [square[:, :128], jnp.concatenate([side[:half], side[half:]], 1)], 0
    )


def unpack(packed):
    rows = packed.shape[0] // 3 * 2
    side = packed[rows:]
    return jnp.concatenate(
        [packed[:rows], jnp.concatenate([side[:, :64], side[:, 64:]], 0)], 1
    )


def tile_forward(
    far_x, far_one, far_two, norm_ref, hidden_ref, slope_ref, out_ref, x_ref, one_ref, two_ref, sems
):
    copies = fetch((far_x, far_one, far_two), (x_ref, one_ref, two_ref), sems)
    copies[0].wait()
    x = x_ref[...].astype(f32)
    centred = x - jnp.mean(x, -1, keepdims=True)
    normed = centred * lax.rsqrt(jnp.mean(centred * centred, -1, keepdims=True) + eps)
    normed = normed.astype(bf16)
    norm_ref[...] = normed
    copies[1].wait()
    pre = jnp.dot(normed, one_ref[...], preferred_element_type=f32)
    bell = 0.5 * (1.0 + lax.erf(pre * 0.7071067811865476))
    hidden = (pre * bell).astype(bf16)
    hidden_ref[...] = hidden
    slope_ref[...] = bell + pre * jnp.exp(-0.5 * pre * pre) * 0.3989422804014327
    copies[2].wait()
    partial = jnp.dot(hidden, two_ref[...], preferred_element_type=f32).astype(bf16)
    count = out_ref.shape[0]
    block = partial.shape[1] // count
    for j in range(count):
        out_ref[j] = pack(partial[:, j * block : (j + 1) * block])


def tile_dispatch(own_ref, report_ref, dispatch_ref, flags_ref, parts_ref, out_ref):
    total = parts_ref[0].astype(f32)
    for j in range(1, parts_ref.shape[0]):
        total = total + parts_ref[j].astype(f32)
    embedding = (own_ref[...].astype(f32) + unpack(total)).astype(bf16)
    rows = jnp.dot(dispatch_ref[...], embedding, preferred_element_type=f32)
    slot = lax.broadcasted_iota(i32, rows.shape, 0)
    rows = jnp.where(lax.rem(slot, ROWS) == ROWS - 1, report_ref[...].astype(f32), rows)
    out_ref[...] = jnp.concatenate([rows.astype(bf16), flags_ref[...]], 1)


def slot_rows(arrived_ref, select_ref, report_select_ref, chunk_ref, valid_ref):
    arrived = arrived_ref[...]
    chunk = contract(arrived, select_ref[...], 0, 0)
    block = chunk_ref.shape[0] - EXTRA
    chunk_ref[0:block, :] = chunk[:block].astype(bf16)
    valid_ref[...] = chunk[block : block + 1]
    reports = jnp.dot(report_select_ref[...], arrived, preferred_element_type=f32)
    reports = reports[:, :block].astype(bf16)
    chunk_ref[block : block + EXTRA, :] = jnp.concatenate(
        [reports[:EXTRA], reports[EXTRA:]], 1
    )


def slide_forward(
    here,
    valid_ref,
    far_query_weights,
    far_key_weights,
    far_value_weights,
    far_out_weights,
    *rest,
):
    pieces = rest[:9]
    (
        far_norm,
        far_heads,
        far_attention,
        stat_ref,
        scale_ref,
        mass_ref,
        attended_ref,
        pooled_ref,
        reports_ref,
        slide_ref,
        norm_ref,
        heads_ref,
        attention_ref,
        query_weights_ref,
        key_weights_ref,
        value_weights_ref,
        out_weights_ref,
        weight_sems,
        sems,
    ) = rest[9:]
    fetched = fetch(
        (far_query_weights, far_key_weights, far_value_weights, far_out_weights),
        (query_weights_ref, key_weights_ref, value_weights_ref, out_weights_ref),
        weight_sems,
    )
    count, owners, block = reports_ref.shape

    def store(index, piece):
        start = pl.multiple_of(index * block, 16)
        slide_ref[pl.ds(start, block), :] = piece[:block]
        reports = piece[block:]
        reports_ref[index] = jnp.concatenate([reports[:, :block], reports[:, block:]], 0)

    place(pieces, here[0], count, store)
    valid = valid_ref[...]
    valid_low = valid.astype(bf16)
    low = slide_ref[...]
    slide = low.astype(f32)
    mean = jnp.mean(slide, 0, keepdims=True)
    centred = slide - mean
    inverse = lax.rsqrt(jnp.mean(centred * centred, 0, keepdims=True) + eps)
    stat_ref[...] = jnp.concatenate([mean, inverse], 0)
    normed = (centred * inverse).astype(bf16)
    norm_ref[...] = normed
    copies = [pltpu.make_async_copy(norm_ref, far_norm, sems.at[0])]
    copies[0].start()
    for copy in fetched:
        copy.wait()
    all_query = jnp.dot(query_weights_ref[...], normed, preferred_element_type=f32)
    all_keys = jnp.dot(key_weights_ref[...], normed, preferred_element_type=f32)
    all_values = jnp.dot(value_weights_ref[...], normed, preferred_element_type=f32)
    heads = all_query.shape[0] // HEAD
    attended = []
    for h in range(heads):
        low_rows, high_rows = h * HEAD, (h + 1) * HEAD
        query = all_query[low_rows:high_rows]
        keys = all_keys[low_rows:high_rows]
        values = all_values[low_rows:high_rows]
        query_scale = lax.rsqrt(jnp.mean(query * query, 0, keepdims=True) + eps)
        key_scale = lax.rsqrt(jnp.mean(keys * keys, 0, keepdims=True) + eps)
        query_unit = query * query_scale
        key_unit = keys * key_scale
        heads_ref[h, 0] = query_unit
        heads_ref[h, 1] = key_unit
        heads_ref[h, 2] = values
        copies.append(pltpu.make_async_copy(heads_ref.at[h], far_heads.at[h], sems.at[1 + 2 * h]))
        copies[-1].start()
        scale_ref[h] = jnp.concatenate([query_scale, key_scale], 0)
        scores = contract(query_unit.astype(bf16), key_unit.astype(bf16), 0, 0)
        weights = jnp.exp(scores * (score_scale / HEAD)) * valid
        weights = weights * (1.0 / jnp.sum(weights, 1, keepdims=True))
        attention_ref[h] = weights
        copies.append(
            pltpu.make_async_copy(attention_ref.at[h], far_attention.at[h], sems.at[2 + 2 * h])
        )
        copies[-1].start()
        weights_low = weights.astype(bf16)
        mass_ref[h : h + 1, :] = jnp.dot(valid_low, weights_low, preferred_element_type=f32)
        attended.append(contract(values.astype(bf16), weights_low, 1, 1))
    attended = jnp.concatenate(attended, 0).astype(bf16)
    attended_sum = contract(valid_low, attended, 1, 1)
    attended_ref[...] = attended_sum
    high = attended_sum.astype(bf16)
    rest_low = (attended_sum - high.astype(f32)).astype(bf16)
    part = jnp.dot(high, out_weights_ref[...], preferred_element_type=f32)
    part = part + jnp.dot(rest_low, out_weights_ref[...], preferred_element_type=f32)
    slide_sum = contract(valid_low, low, 1, 1)
    pooled = (part + slide_sum * (1.0 / count)) / jnp.sum(valid)
    pooled_ref[...] = jnp.broadcast_to(pooled[None], pooled_ref.shape)
    for copy in copies:
        copy.wait()


def unit_vectors(parts_ref, reports_ref, report_ref):
    pooled = jnp.sum(parts_ref[...], 0)
    inverse = lax.rsqrt(jnp.sum(pooled * pooled, -1, keepdims=True) + eps)
    count, owners, block = reports_ref.shape
    squares = jnp.zeros((owners, 1), f32)
    for j in range(count):
        reports = reports_ref[j].astype(f32)
        report_ref[:, j * block : (j + 1) * block] = reports
        squares = squares + jnp.sum(reports * reports, -1, keepdims=True)
    report = report_ref[...] * lax.rsqrt(squares + eps)
    return pooled * inverse, inverse, report


def logits_row(parts_ref, reports_ref, row_ref, report_ref):
    unit, inverse, report = unit_vectors(parts_ref, reports_ref, report_ref)
    row = contract(unit, report, 1, 1, precision=exact) / contrast_divisor_factor
    pad = row_ref.shape[2] - row.shape[1]
    row = jnp.concatenate([row, jnp.zeros((1, pad), f32)], 1)
    row_ref[...] = jnp.broadcast_to(row[None], row_ref.shape)


def slide_backward(
    owner,
    logits_ref,
    pair_ref,
    parts_ref,
    reports_ref,
    valid_ref,
    scale_ref,
    mass_ref,
    far_out_weights,
    far_heads,
    far_attention,
    far_query_weights,
    far_key_weights,
    far_value_weights,
    far_norm,
    loss_ref,
    grad_ref,
    up_ref,
    grads_ref,
    out_ref,
    *rest,
):
    fetched, report_ref, sems = rest[:-2], rest[-2], rest[-1]
    (
        out_weights_ref,
        heads_ref,
        attention_ref,
        query_weights_ref,
        key_weights_ref,
        value_weights_ref,
        norm_ref,
    ) = fetched
    copies = fetch(
        (
            far_out_weights,
            far_heads,
            far_attention,
            far_query_weights,
            far_key_weights,
            far_value_weights,
            far_norm,
        ),
        fetched,
        sems,
    )
    unit, inverse, report = unit_vectors(parts_ref, reports_ref, report_ref)
    owners = report.shape[0]
    valid = valid_ref[...]
    logits = logits_ref[...]
    shape = logits.shape
    columns = lax.broadcasted_iota(i32, shape, 1)
    rows = lax.broadcasted_iota(i32, shape, 0)
    real = columns < owners
    expo = jnp.where(real, jnp.exp(logits), 0.0)
    row_total = jnp.sum(expo, 1, keepdims=True)
    column_total = jnp.where(real[:1], jnp.sum(expo, 0, keepdims=True), 1.0)
    target = jnp.where(pair_ref[...] == columns, 1.0, 0.0)
    loss = jnp.sum(
        0.5 * jnp.log(row_total) - jnp.sum(logits * target, 1, keepdims=True), 0, keepdims=True
    )
    loss = loss + 0.5 * jnp.sum(jnp.log(column_total), 1, keepdims=True)
    loss_ref[...] = loss * (1.0 / owners)
    grad_logits = (0.5 * expo / row_total + 0.5 * expo / column_total - target) * (
        loss_scale / owners
    )
    grad_row = jnp.sum(jnp.where(rows == owner[0], grad_logits, 0.0), 0, keepdims=True)
    grad_unit = (
        jnp.dot(grad_row[:, :owners], report, precision=exact, preferred_element_type=f32)
        / contrast_divisor_factor
    )
    grad_pooled = (grad_unit - unit * jnp.sum(unit * grad_unit, -1, keepdims=True)) * inverse
    grad = grad_pooled / jnp.sum(valid)
    grad_ref[...] = grad
    low = grad.astype(bf16)
    copies[0].wait()
    out_weights = out_weights_ref[...]
    up_ref[...] = contract(low, out_weights, 1, 1)
    up = jnp.sum(out_weights.astype(f32) * low.astype(f32), 1, keepdims=True)
    heads = heads_ref.shape[0]
    inner = heads * HEAD
    copies[1].wait()
    copies[2].wait()
    for h in range(heads):
        up_head = up[h * HEAD : (h + 1) * HEAD]
        values = heads_ref[h, 2]
        weights = attention_ref[h]
        pull = jnp.sum(up_head * values, 0, keepdims=True)
        pull_mean = jnp.sum(weights * pull, 1, keepdims=True)
        grad_scores = (weights * (pull - pull_mean) * (score_scale / HEAD)).astype(bf16)
        query_unit = heads_ref[h, 0]
        key_unit = heads_ref[h, 1]
        grad_query = contract(key_unit.astype(bf16), grad_scores, 1, 1) * valid
        grad_key = jnp.dot(query_unit.astype(bf16), grad_scores, preferred_element_type=f32)
        grad_query = scale_ref[h, 0:1] * (
            grad_query - query_unit * jnp.mean(query_unit * grad_query, 0, keepdims=True)
        )
        grad_key = scale_ref[h, 1:2] * (
            grad_key - key_unit * jnp.mean(key_unit * grad_key, 0, keepdims=True)
        )
        grad_value = up_head * mass_ref[h : h + 1]
        for part, values in enumerate((grad_query, grad_key, grad_value)):
            start = part * inner + h * HEAD
            grads_ref[start : start + HEAD, :] = values.astype(bf16)
    grad_query = grads_ref[0:inner, :]
    grad_key = grads_ref[inner : 2 * inner, :]
    grad_value = grads_ref[2 * inner : 3 * inner, :]
    for copy in copies[3:]:
        copy.wait()
    count = out_ref.shape[0]
    block = norm_ref.shape[0] // count
    first = jnp.zeros_like(valid)
    second = jnp.zeros_like(valid)
    for k in range(count):
        rows = slice(k * block, (k + 1) * block)
        part = jnp.dot(query_weights_ref[rows, :], grad_query, preferred_element_type=f32)
        part = part + jnp.dot(key_weights_ref[rows, :], grad_key, preferred_element_type=f32)
        part = part + jnp.dot(value_weights_ref[rows, :], grad_value, preferred_element_type=f32)
        out_ref[k, 0:block, :] = part.astype(bf16)
        first = first + jnp.sum(part, 0, keepdims=True)
        second = second + jnp.sum(part * norm_ref[rows, :].astype(f32), 0, keepdims=True)
    width = norm_ref.shape[0]
    stats = jnp.concatenate([first, second], 0) * (1.0 / width)
    high = stats.astype(bf16).astype(f32)
    stats = jnp.concatenate(
        [high, stats - high, jnp.zeros((EXTRA - 4, stats.shape[1]), f32)], 0
    ).astype(bf16)
    for k in range(count):
        out_ref[k, block : block + EXTRA, :] = stats


def wide_other(which, norm_ref, grads_ref, out_ref):
    chips, share, columns = out_ref.shape
    rows = [
        norm_ref[pl.ds(pl.multiple_of((CORES * chip + which[0]) * share, 16), share), :]
        for chip in range(chips)
    ]
    values = contract(jnp.concatenate(rows, 0), grads_ref[0:columns, :], 1, 1).astype(bf16)
    for chip in range(chips):
        out_ref[chip] = values[chip * share : (chip + 1) * share]


def wide_own(which, column, norm_ref, grads_ref, got_ref, *outs):
    side = len(outs)
    lines, share, columns = outs[0].shape
    chips = [
        line * side + lax.rem(column[0] + k, side) for k in range(side) for line in range(lines)
    ]
    rows = [
        norm_ref[pl.ds(pl.multiple_of((CORES * chip + which[0]) * share, 16), share), :]
        for chip in chips
    ]
    values = contract(jnp.concatenate(rows, 0), grads_ref[0:columns, :], 1, 1)
    for index, chip in enumerate(chips):
        part = values[index * share : (index + 1) * share] + got_ref[chip].astype(f32)
        outs[index // lines][index % lines] = part.astype(bf16)


def wide_line(line, *refs):
    side = len(refs) // 2
    for k in range(side):
        row = lax.rem(line[0] + k, side)
        total = refs[0][row].astype(f32)
        for ref in refs[1:side]:
            total = total + ref[row].astype(f32)
        refs[side + k][...] = total.astype(bf16)


def slot_grads(
    own_ref, valid_ref, stat_ref, chunk_ref, select_ref, extra_ref, parts_ref, out_ref
):
    total = parts_ref[0].astype(f32)
    for j in range(1, parts_ref.shape[0]):
        total = total + parts_ref[j].astype(f32)
    block = chunk_ref.shape[0] - EXTRA
    first = total[block : block + 1] + total[block + 2 : block + 3]
    second = total[block + 1 : block + 2] + total[block + 3 : block + 4]
    mean = stat_ref[0:1]
    inverse = stat_ref[1:2]
    normed = (chunk_ref[0:block, :].astype(f32) - mean) * inverse
    rows = own_ref[...] * valid_ref[...] + (total[:block] - first - normed * second) * inverse
    rows = contract(select_ref[...], rows.astype(bf16), 1, 1).astype(bf16)
    out_ref[...] = rows + extra_ref[...]


def tile_grads(back_ref, dispatch_ref, out_ref):
    piece = pack(contract(back_ref[...], dispatch_ref[...], 0, 0).astype(bf16))
    out_ref[...] = jnp.broadcast_to(piece[None], out_ref.shape)


def rows_of(which, ref, chips, share):
    rows = [
        ref[pl.ds(pl.multiple_of((CORES * chip + which) * share, 16), share), :]
        for chip in range(chips)
    ]
    return jnp.concatenate(rows, 0)


def other_two(other, hidden_ref, parts_ref, grad_ref, out_ref):
    count = parts_ref.shape[0]
    rows = grad_ref.shape[0] // count
    for j in range(count):
        grad_ref[j * rows : (j + 1) * rows, :] = unpack(parts_ref[j])
    chips, share = out_ref.shape[:2]
    rows = rows_of(other[0], grad_ref, chips, share)
    two = jnp.dot(rows, hidden_ref[...], preferred_element_type=f32).astype(bf16)
    for chip in range(chips):
        out_ref[chip] = two[chip * share : (chip + 1) * share]


def both_one(
    two_ref, slope_ref, other_norm_ref, own_norm_ref, grad_ref, out_ref, own_ref, hidden_grad_ref
):
    grad_hidden = jnp.dot(two_ref[...], grad_ref[...], preferred_element_type=f32)
    hidden_grad_ref[...] = (grad_hidden * slope_ref[...]).astype(bf16)
    chips, share = out_ref.shape[:2]
    for norm_ref, target_ref in ((other_norm_ref, out_ref), (own_norm_ref, own_ref)):
        one = contract(norm_ref[...], hidden_grad_ref[...], 1, 1).astype(bf16)
        for chip in range(chips):
            target_ref[chip] = one[chip * share : (chip + 1) * share]


def own_two(own, column, hidden_ref, grad_ref, got_ref, *outs):
    side = len(outs)
    lines, share = outs[0].shape[:2]
    for k in range(side):
        place = lax.rem(column[0] + k, side)
        chips = [line * side + place for line in range(lines)]
        rows = [
            grad_ref[pl.ds(pl.multiple_of((CORES * chip + own[0]) * share, 16), share), :]
            for chip in chips
        ]
        two = jnp.dot(jnp.concatenate(rows, 0), hidden_ref[...], preferred_element_type=f32)
        for line, chip in enumerate(chips):
            part = two[line * share : (line + 1) * share] + got_ref[chip].astype(f32)
            outs[k][line] = part.astype(bf16)


def own_one(own_ref, got_ref, out_ref):
    side = out_ref.shape[1]
    for chip in range(got_ref.shape[0]):
        part = own_ref[chip].astype(f32) + got_ref[chip].astype(f32)
        out_ref[chip // side, chip % side] = part.astype(bf16)


def add_up(*refs):
    total = refs[0][...].astype(f32)
    for ref in refs[1:-1]:
        total = total + ref[...].astype(f32)
    refs[-1][...] = total.astype(refs[-1].dtype)


def add_lines(column, lines_ref, *outs):
    side = len(outs)
    for k in range(side):
        place = lax.rem(column[0] + k, side)
        total = lines_ref[0, place].astype(f32)
        for line in range(1, lines_ref.shape[0]):
            total = total + lines_ref[line, place].astype(f32)
        outs[k][...] = total.astype(bf16)


def last_sums(lines_ref, *refs):
    one_ref, two_ref = refs[-2:]
    total = lines_ref[0].astype(f32)
    for line in range(1, lines_ref.shape[0]):
        total = total + lines_ref[line].astype(f32)
    two_ref[...] = total
    total = refs[0][...].astype(f32)
    for ref in refs[1:-2]:
        total = total + ref[...].astype(f32)
    one_ref[...] = total


def per_device(
    tile_features, tile_slide, slide_pair, reports, w_one, w_two, w_query, w_key, w_value, w_out
):
    lines = lax.axis_size("line")
    side = lax.axis_size("column")
    line = lax.axis_index("line")
    column = lax.axis_index("column")
    chips = lines * side
    owners = chips * CORES
    parts = lax.axis_size("mp")
    core = lax.axis_index("core")
    owner = lax.axis_index(DP)
    here = lax.axis_index("mp")
    tiles, width = tile_features.shape
    units = w_one.shape[1]
    capacity = 2 * tiles // owners
    length = owners * capacity
    slots = owners * ROWS
    block = width // parts
    share = width // owners
    inner = w_query.shape[1]
    heads = inner // HEAD
    packed = (block // 2 * 3, 128)

    def halves(values):
        rest = values.shape[1:]
        values = values.reshape((chips, CORES, share) + rest)
        own = pick(values, core, 1).reshape((chips * share,) + rest)
        other = pick(values, 1 - core, 1).reshape((chips * share,) + rest)
        return own, other

    tile_norm, hidden, slope, partial = call(
        tile_forward,
        [
            ((tiles, width), bf16),
            ((tiles, units), bf16),
            ((tiles, units), f32),
            ((parts,) + packed, bf16),
        ],
        tile_features,
        w_one,
        w_two,
        far=(0, 1, 2),
        scratch=[
            (tile_features.shape, bf16),
            (w_one.shape, bf16),
            (w_two.shape, bf16),
            3,
        ],
        limit=62,
    )
    partial = exchange(partial, "mp")

    slide_ids = tile_slide[:, 0]
    matches = (slide_ids[:, None] == jnp.arange(owners, dtype=i32)[None, :]).astype(i32)
    ordinal = jnp.sum(matches * (jnp.cumsum(matches, 0) - 1), 1)
    position = slide_ids * ROWS + ordinal
    dispatch = jnp.arange(slots, dtype=i32)[:, None] == position[None, :]
    flags = jnp.sum(dispatch.astype(f32), 1, keepdims=True).astype(bf16)
    flags = jnp.pad(flags, ((0, 0), (0, 256 - block - 1)))
    dispatch = dispatch.astype(bf16)
    slot = jnp.arange(slots, dtype=i32)
    row_of_slot = jnp.where(slot % ROWS < capacity, slot // ROWS * capacity + slot % ROWS, -1)
    select = (row_of_slot[:, None] == jnp.arange(length, dtype=i32)[None, :]).astype(bf16)
    last_slot = jnp.arange(owners, dtype=i32)[:, None] * ROWS + ROWS - 1
    report_select = (last_slot == slot[None, :]).astype(bf16)
    own_columns = pick(tile_features.reshape(tiles, parts, block), here, 1)
    own_report = pick(reports.reshape(1, parts, block), here, 1)
    tile_own, tile_other = halves(tile_norm.T)
    slope = slope.T

    (outgoing,) = call(
        tile_dispatch,
        [((slots, 256), bf16)],
        own_columns,
        own_report,
        dispatch,
        flags,
        partial,
        anchors=(select, report_select, tile_own, tile_other, slope),
    )
    arrived = exchange(outgoing.reshape(owners, ROWS, 256), DP).reshape(slots, 256)
    chunk, valid = call(
        slot_rows,
        [((block + EXTRA, length), bf16), ((1, length), f32)],
        arrived,
        select,
        report_select,
    )
    pieces = gather_ring(chunk, parts)

    (
        slide_norm,
        by_head,
        attention,
        stat,
        scales,
        mass,
        attended_sum,
        pooled,
        all_reports,
    ) = call(
        slide_forward,
        [
            ((width, length), bf16, "far"),
            ((heads, 3, HEAD, length), f32, "far"),
            ((heads, length, length), f32, "far"),
            ((2, length), f32),
            ((heads, 2, length), f32),
            ((heads, length), f32),
            ((1, inner), f32),
            ((parts, 1, width), f32),
            ((parts, owners, block), bf16),
        ],
        valid,
        w_query.T,
        w_key.T,
        w_value.T,
        w_out,
        *pieces,
        scalars=(here,),
        far=(1, 2, 3, 4),
        scratch=[
            ((width, length), bf16),
            ((width, length), bf16),
            ((heads, 3, HEAD, length), f32),
            ((heads, length, length), f32),
            ((inner, width), bf16),
            ((inner, width), bf16),
            ((inner, width), bf16),
            ((inner, width), bf16),
            4,
            1 + 2 * heads,
        ],
        limit=60,
    )
    pooled = exchange(pooled, "mp")
    (row,) = call(
        logits_row,
        [((owners, 1, 128), f32)],
        pooled,
        all_reports,
        scratch=[((owners, width), f32)],
        limit=60,
    )
    logits = exchange(row, DP).reshape(owners, 128)
    loss, grad, up, grads, sending = call(
        slide_backward,
        [((1, 1), f32), ((1, width), f32), ((1, inner), f32), ((3 * inner, length), bf16)]
        + [((parts, block + EXTRA, length), bf16)],
        logits,
        slide_pair[:, None],
        pooled,
        all_reports,
        valid,
        scales,
        mass,
        w_out,
        by_head,
        attention,
        w_query,
        w_key,
        w_value,
        slide_norm,
        scalars=(owner,),
        far=tuple(range(7, 14)),
        scratch=[
            (w_out.shape, bf16),
            (by_head.shape, f32),
            (attention.shape, f32),
            (w_query.shape, bf16),
            (w_key.shape, bf16),
            (w_value.shape, bf16),
            (slide_norm.shape, bf16),
            ((owners, width), f32),
            7,
        ],
        limit=60,
    )
    received = exchange(sending, "mp")

    (wide_sent,) = call(
        wide_other,
        [((chips, share, 2 * inner), bf16)],
        slide_norm,
        grads,
        scalars=(1 - core,),
    )
    wide_got = lax.ppermute(wide_sent, "core", [(0, 1), (1, 0)])
    along = call(
        wide_own,
        [((lines, share, 2 * inner), bf16)] * side,
        slide_norm,
        grads,
        wide_got,
        scalars=(core, column),
    )
    def shift(values, axis):
        return [values[0]] + [
            lax.ppermute(values[k], axis, turn(len(values), k)) for k in range(1, len(values))
        ]

    along = shift(along, "column")
    across = call(
        wide_line, [((share, 2 * inner), bf16)] * lines, *along, scalars=(line,)
    )
    across = shift(across, "line")
    grad_wide = sum(part.astype(f32) for part in across)
    value_rows = contract(mass.astype(bf16), slide_norm, 1, 1)
    extra = jnp.concatenate(
        [
            value_rows.reshape(heads, owners, share).transpose(1, 0, 2).reshape(owners, -1),
            grad.reshape(owners, share),
            jnp.broadcast_to(up, (owners, inner)),
            jnp.broadcast_to(attended_sum, (owners, inner)),
        ],
        1,
    ).astype(bf16)
    spare = ROWS - capacity
    extra = jnp.pad(extra, ((0, 0), (0, spare * block - extra.shape[1])))
    extra = extra.reshape(owners, spare, block)
    extra = jnp.pad(extra, ((0, 0), (capacity, 0), (0, 0))).reshape(slots, block)

    own_grad = lax.dynamic_slice_in_dim(grad, here * block, block, 1).reshape(block, 1)
    (going,) = call(
        slot_grads,
        [((slots, block), bf16)],
        own_grad,
        valid,
        stat,
        chunk,
        select,
        extra,
        received,
        anchors=(grad_wide,),
    )
    back = exchange(going.reshape(owners, ROWS, block), DP).reshape(slots, block)
    (spreading,) = call(tile_grads, [((parts,) + packed, bf16)], back, dispatch)

    size = (chips, share, units)
    swap = [(0, 1), (1, 0)]
    grad_embedding, two_sent = call(
        other_two,
        [((width, tiles), bf16), (size, bf16)],
        hidden,
        exchange(spreading, "mp"),
        scalars=(1 - core,),
    )
    two_got = lax.ppermute(two_sent, "core", swap)
    one_sent, one_own = call(
        both_one,
        [(size, bf16), (size, bf16)],
        w_two,
        slope,
        tile_other,
        tile_own,
        grad_embedding,
        scratch=[((units, tiles), bf16)],
    )
    one_got = lax.ppermute(one_sent, "core", swap)
    two_along = call(
        own_two,
        [((lines, share, units), bf16)] * side,
        hidden,
        grad_embedding,
        two_got,
        scalars=(core, column),
    )
    (one_across,) = call(
        own_one,
        [((lines, side, share, units), bf16)],
        one_own,
        one_got,
        anchors=(two_along[0],),
    )
    two_along = shift(two_along, "column")
    one_across = exchange(one_across, "line")
    (two_across,) = call(add_up, [((lines, share, units), bf16)], *two_along)
    one_along = call(add_lines, [((share, units), bf16)] * side, one_across, scalars=(column,))
    grad_one, grad_two = call(
        last_sums,
        [((share, units), f32)] * 2,
        exchange(two_across, "line"),
        *shift(one_along, "column"),
    )
    grad_two = grad_two.T

    terms = back.reshape(owners, ROWS, block)[:, capacity:].reshape(owners, -1).astype(f32)
    edge = heads * share
    from_values = terms[:, :edge].reshape(owners, heads, share)
    from_grads = terms[:, edge : edge + share]
    edge = edge + share
    from_up = terms[:, edge : edge + inner].reshape(owners, heads, HEAD)
    edge = edge + inner
    from_attended = terms[:, edge : edge + inner]
    grad_value = jnp.einsum("ohs,ohd->shd", from_values, from_up, precision=exact)
    grad_value = grad_value.reshape(share, inner)
    grad_out = contract(from_attended, from_grads, 0, 0, precision=exact)
    return (
        loss[0, 0],
        grad_one,
        grad_two,
        grad_wide[:, :inner],
        grad_wide[:, inner:],
        grad_value,
        grad_out,
    )


def solution(mesh):
    owners, parts = mesh.devices.shape
    side = math.isqrt(owners // CORES)
    split = Mesh(
        mesh.devices.reshape(owners // CORES // side, side, CORES, parts),
        ("line", "column", "core", "mp"),
    )
    return jax.shard_map(
        per_device,
        mesh=split,
        in_specs=(
            P(DP, None),
            P(DP, None),
            P(),
            P(DP, None),
            P(None, "mp"),
            P("mp", None),
            P(None, "mp"),
            P(None, "mp"),
            P(None, "mp"),
            P("mp", None),
        ),
        out_specs=(
            P(),
            P(DP, "mp"),
            P("mp", DP),
            P(DP, "mp"),
            P(DP, "mp"),
            P(DP, "mp"),
            P("mp", DP),
        ),
        check_vma=False,
    )
```

```python
import math

import jax
import jax.numpy as jnp
from jax import lax
from jax.experimental import pallas as pl
from jax.experimental.pallas import tpu as pltpu
from jax.sharding import Mesh, PartitionSpec as P

HEAD = 96
CORES = 2
ROWS = 16
EXTRA = 16

eps = 1e-05
contrast_divisor_factor = 0.07
score_scale = 10.0
loss_scale = 4096.0
exact = lax.Precision.HIGHEST
f32 = jnp.float32
bf16 = jnp.bfloat16
i32 = jnp.int32
DP = ("line", "column", "core")


def contract(left, right, left_dim, right_dim, **kw):
    return lax.dot_general(
        left, right, (((left_dim,), (right_dim,)), ((), ())), preferred_element_type=f32, **kw
    )


def exchange(values, axis):
    return lax.all_to_all(values, axis, 0, 0, tiled=True)


def pick(values, index, axis):
    return lax.dynamic_index_in_dim(values, index, axis, keepdims=False)


def call(body, outs, *args, scalars=(), scratch=(), anchors=(), far=(), limit=16):
    count = len(scalars)
    skip = len(anchors)
    vmem = pl.BlockSpec(memory_space=pltpu.VMEM)
    away = pl.BlockSpec(memory_space=pltpu.HBM)

    def kernel(*refs):
        body(*refs[skip:])

    return pl.pallas_call(
        kernel if skip else body,
        out_shape=[jax.ShapeDtypeStruct(out[0], out[1]) for out in outs],
        in_specs=[pl.BlockSpec(memory_space=pl.ANY)] * skip
        + [pl.BlockSpec(memory_space=pltpu.SMEM)] * count
        + [away if index in far else vmem for index in range(len(args))],
        out_specs=[vmem if len(out) == 2 else away for out in outs],
        scratch_shapes=[
            pltpu.VMEM(*part) if isinstance(part, tuple) else pltpu.SemaphoreType.DMA((part,))
            for part in scratch
        ],
        compiler_params=pltpu.CompilerParams(vmem_limit_bytes=limit * 1024 * 1024),
    )(*anchors, *[jnp.reshape(s, (1,)).astype(i32) for s in scalars], *args)


def fetch(sources, targets, semaphores):
    copies = [
        pltpu.make_async_copy(source, target, semaphores.at[index])
        for index, (source, target) in enumerate(zip(sources, targets))
    ]
    for copy in copies:
        copy.start()
    return copies


def turn(count, step):
    return [(index, (index + step) % count) for index in range(count)]


def gather_ring(piece, count):
    found = [piece]
    back = ahead = piece
    for _ in range(count // 2 - 1):
        back = lax.ppermute(back, "mp", turn(count, 1))
        ahead = lax.ppermute(ahead, "mp", turn(count, count - 1))
        found += [back, ahead]
    half = (piece.shape[0] // 2 + ROWS - 1) // ROWS * ROWS
    found.append(lax.ppermute(back[:half], "mp", turn(count, 1)))
    found.append(lax.ppermute(ahead[half:], "mp", turn(count, count - 1)))
    return found


def place(refs, here, count, store):
    half = count // 2
    store(here, refs[0][...])
    for step in range(1, half):
        for ref, sign in ((refs[2 * step - 1], -1), (refs[2 * step], 1)):
            store(lax.rem(here + sign * step + count, count), ref[...])
    store(
        lax.rem(here + half, count), jnp.concatenate([refs[-2][...], refs[-1][...]], 0)
    )


def pack(square):
    half = square.shape[0] // 2
    side = square[:, 128:]
    return jnp.concatenate(
        [square[:, :128], jnp.concatenate([side[:half], side[half:]], 1)], 0
    )


def unpack(packed):
    rows = packed.shape[0] // 3 * 2
    side = packed[rows:]
    return jnp.concatenate(
        [packed[:rows], jnp.concatenate([side[:, :64], side[:, 64:]], 0)], 1
    )


def tile_forward(
    far_x, far_one, far_two, norm_ref, hidden_ref, slope_ref, out_ref, x_ref, one_ref, two_ref, sems
):
    copies = fetch((far_x, far_one, far_two), (x_ref, one_ref, two_ref), sems)
    copies[0].wait()
    x = x_ref[...].astype(f32)
    centred = x - jnp.mean(x, -1, keepdims=True)
    normed = centred * lax.rsqrt(jnp.mean(centred * centred, -1, keepdims=True) + eps)
    normed = normed.astype(bf16)
    norm_ref[...] = normed
    copies[1].wait()
    pre = jnp.dot(normed, one_ref[...], preferred_element_type=f32)
    bell = 0.5 * (1.0 + lax.erf(pre * 0.7071067811865476))
    hidden = (pre * bell).astype(bf16)
    hidden_ref[...] = hidden
    slope_ref[...] = bell + pre * jnp.exp(-0.5 * pre * pre) * 0.3989422804014327
    copies[2].wait()
    partial = jnp.dot(hidden, two_ref[...], preferred_element_type=f32).astype(bf16)
    count = out_ref.shape[0]
    block = partial.shape[1] // count
    for j in range(count):
        out_ref[j] = pack(partial[:, j * block : (j + 1) * block])


def tile_dispatch(own_ref, report_ref, dispatch_ref, flags_ref, parts_ref, out_ref):
    total = parts_ref[0].astype(f32)
    for j in range(1, parts_ref.shape[0]):
        total = total + parts_ref[j].astype(f32)
    embedding = (own_ref[...].astype(f32) + unpack(total)).astype(bf16)
    rows = jnp.dot(dispatch_ref[...], embedding, preferred_element_type=f32)
    slot = lax.broadcasted_iota(i32, rows.shape, 0)
    rows = jnp.where(lax.rem(slot, ROWS) == ROWS - 1, report_ref[...].astype(f32), rows)
    out_ref[...] = jnp.concatenate([rows.astype(bf16), flags_ref[...]], 1)


def slot_rows(arrived_ref, select_ref, report_select_ref, chunk_ref, valid_ref):
    arrived = arrived_ref[...]
    chunk = contract(arrived, select_ref[...], 0, 0)
    block = chunk_ref.shape[0] - EXTRA
    chunk_ref[0:block, :] = chunk[:block].astype(bf16)
    valid_ref[...] = chunk[block : block + 1]
    reports = jnp.dot(report_select_ref[...], arrived, preferred_element_type=f32)
    reports = reports[:, :block].astype(bf16)
    chunk_ref[block : block + EXTRA, :] = jnp.concatenate(
        [reports[:EXTRA], reports[EXTRA:]], 1
    )


def slide_forward(
    here,
    valid_ref,
    far_query_weights,
    far_key_weights,
    far_value_weights,
    far_out_weights,
    *rest,
):
    pieces = rest[:9]
    (
        far_norm,
        far_heads,
        far_attention,
        stat_ref,
        scale_ref,
        mass_ref,
        attended_ref,
        pooled_ref,
        reports_ref,
        slide_ref,
        norm_ref,
        heads_ref,
        attention_ref,
        query_weights_ref,
        key_weights_ref,
        value_weights_ref,
        out_weights_ref,
        weight_sems,
        sems,
    ) = rest[9:]
    fetched = fetch(
        (far_query_weights, far_key_weights, far_value_weights, far_out_weights),
        (query_weights_ref, key_weights_ref, value_weights_ref, out_weights_ref),
        weight_sems,
    )
    count, owners, block = reports_ref.shape

    def store(index, piece):
        start = pl.multiple_of(index * block, 16)
        slide_ref[pl.ds(start, block), :] = piece[:block]
        reports = piece[block:]
        reports_ref[index] = jnp.concatenate([reports[:, :block], reports[:, block:]], 0)

    place(pieces, here[0], count, store)
    valid = valid_ref[...]
    valid_low = valid.astype(bf16)
    low = slide_ref[...]
    slide = low.astype(f32)
    mean = jnp.mean(slide, 0, keepdims=True)
    centred = slide - mean
    inverse = lax.rsqrt(jnp.mean(centred * centred, 0, keepdims=True) + eps)
    stat_ref[...] = jnp.concatenate([mean, inverse], 0)
    normed = (centred * inverse).astype(bf16)
    norm_ref[...] = normed
    copies = [pltpu.make_async_copy(norm_ref, far_norm, sems.at[0])]
    copies[0].start()
    for copy in fetched:
        copy.wait()
    all_query = jnp.dot(query_weights_ref[...], normed, preferred_element_type=f32)
    all_keys = jnp.dot(key_weights_ref[...], normed, preferred_element_type=f32)
    all_values = jnp.dot(value_weights_ref[...], normed, preferred_element_type=f32)
    heads = all_query.shape[0] // HEAD
    attended = []
    for h in range(heads):
        low_rows, high_rows = h * HEAD, (h + 1) * HEAD
        query = all_query[low_rows:high_rows]
        keys = all_keys[low_rows:high_rows]
        values = all_values[low_rows:high_rows]
        query_scale = lax.rsqrt(jnp.mean(query * query, 0, keepdims=True) + eps)
        key_scale = lax.rsqrt(jnp.mean(keys * keys, 0, keepdims=True) + eps)
        query_unit = query * query_scale
        key_unit = keys * key_scale
        heads_ref[h, 0] = query_unit
        heads_ref[h, 1] = key_unit
        heads_ref[h, 2] = values
        copies.append(pltpu.make_async_copy(heads_ref.at[h], far_heads.at[h], sems.at[1 + 2 * h]))
        copies[-1].start()
        scale_ref[h] = jnp.concatenate([query_scale, key_scale], 0)
        scores = contract(query_unit.astype(bf16), key_unit.astype(bf16), 0, 0)
        weights = jnp.exp(scores * (score_scale / HEAD)) * valid
        weights = weights * (1.0 / jnp.sum(weights, 1, keepdims=True))
        attention_ref[h] = weights.astype(bf16)
        copies.append(
            pltpu.make_async_copy(attention_ref.at[h], far_attention.at[h], sems.at[2 + 2 * h])
        )
        copies[-1].start()
        weights_low = weights.astype(bf16)
        mass_ref[h : h + 1, :] = jnp.dot(valid_low, weights_low, preferred_element_type=f32)
        attended.append(contract(values.astype(bf16), weights_low, 1, 1))
    attended = jnp.concatenate(attended, 0).astype(bf16)
    attended_sum = contract(valid_low, attended, 1, 1)
    attended_ref[...] = attended_sum
    high = attended_sum.astype(bf16)
    rest_low = (attended_sum - high.astype(f32)).astype(bf16)
    part = jnp.dot(high, out_weights_ref[...], preferred_element_type=f32)
    part = part + jnp.dot(rest_low, out_weights_ref[...], preferred_element_type=f32)
    slide_sum = contract(valid_low, low, 1, 1)
    pooled = (part + slide_sum * (1.0 / count)) / jnp.sum(valid)
    pooled_ref[...] = jnp.broadcast_to(pooled[None], pooled_ref.shape)
    for copy in copies:
        copy.wait()


def unit_vectors(parts_ref, reports_ref, report_ref):
    pooled = jnp.sum(parts_ref[...], 0)
    inverse = lax.rsqrt(jnp.sum(pooled * pooled, -1, keepdims=True) + eps)
    count, owners, block = reports_ref.shape
    squares = jnp.zeros((owners, 1), f32)
    for j in range(count):
        reports = reports_ref[j].astype(f32)
        report_ref[:, j * block : (j + 1) * block] = reports
        squares = squares + jnp.sum(reports * reports, -1, keepdims=True)
    report = report_ref[...] * lax.rsqrt(squares + eps)
    return pooled * inverse, inverse, report


def logits_row(parts_ref, reports_ref, row_ref, report_ref):
    unit, inverse, report = unit_vectors(parts_ref, reports_ref, report_ref)
    row = contract(unit, report, 1, 1, precision=exact) / contrast_divisor_factor
    pad = row_ref.shape[2] - row.shape[1]
    row = jnp.concatenate([row, jnp.zeros((1, pad), f32)], 1)
    row_ref[...] = jnp.broadcast_to(row[None], row_ref.shape)


def slide_backward(
    owner,
    logits_ref,
    pair_ref,
    parts_ref,
    reports_ref,
    valid_ref,
    scale_ref,
    mass_ref,
    far_out_weights,
    far_heads,
    far_attention,
    far_query_weights,
    far_key_weights,
    far_value_weights,
    far_norm,
    loss_ref,
    grad_ref,
    up_ref,
    grads_ref,
    out_ref,
    *rest,
):
    fetched, report_ref, sems = rest[:-2], rest[-2], rest[-1]
    (
        out_weights_ref,
        heads_ref,
        attention_ref,
        query_weights_ref,
        key_weights_ref,
        value_weights_ref,
        norm_ref,
    ) = fetched
    copies = fetch(
        (
            far_out_weights,
            far_heads,
            far_attention,
            far_query_weights,
            far_key_weights,
            far_value_weights,
            far_norm,
        ),
        fetched,
        sems,
    )
    unit, inverse, report = unit_vectors(parts_ref, reports_ref, report_ref)
    owners = report.shape[0]
    valid = valid_ref[...]
    logits = logits_ref[...]
    shape = logits.shape
    columns = lax.broadcasted_iota(i32, shape, 1)
    rows = lax.broadcasted_iota(i32, shape, 0)
    real = columns < owners
    expo = jnp.where(real, jnp.exp(logits), 0.0)
    row_total = jnp.sum(expo, 1, keepdims=True)
    column_total = jnp.where(real[:1], jnp.sum(expo, 0, keepdims=True), 1.0)
    target = jnp.where(pair_ref[...] == columns, 1.0, 0.0)
    loss = jnp.sum(
        0.5 * jnp.log(row_total) - jnp.sum(logits * target, 1, keepdims=True), 0, keepdims=True
    )
    loss = loss + 0.5 * jnp.sum(jnp.log(column_total), 1, keepdims=True)
    loss_ref[...] = loss * (1.0 / owners)
    grad_logits = (0.5 * expo / row_total + 0.5 * expo / column_total - target) * (
        loss_scale / owners
    )
    grad_row = jnp.sum(jnp.where(rows == owner[0], grad_logits, 0.0), 0, keepdims=True)
    grad_unit = (
        jnp.dot(grad_row[:, :owners], report, precision=exact, preferred_element_type=f32)
        / contrast_divisor_factor
    )
    grad_pooled = (grad_unit - unit * jnp.sum(unit * grad_unit, -1, keepdims=True)) * inverse
    grad = grad_pooled / jnp.sum(valid)
    grad_ref[...] = grad
    low = grad.astype(bf16)
    copies[0].wait()
    out_weights = out_weights_ref[...]
    up_ref[...] = contract(low, out_weights, 1, 1)
    up = jnp.sum(out_weights.astype(f32) * low.astype(f32), 1, keepdims=True)
    heads = heads_ref.shape[0]
    inner = heads * HEAD
    copies[1].wait()
    copies[2].wait()
    for h in range(heads):
        up_head = up[h * HEAD : (h + 1) * HEAD]
        values = heads_ref[h, 2]
        weights = attention_ref[h].astype(f32)
        pull = jnp.sum(up_head * values, 0, keepdims=True)
        pull_mean = jnp.sum(weights * pull, 1, keepdims=True)
        grad_scores = (weights * (pull - pull_mean) * (score_scale / HEAD)).astype(bf16)
        query_unit = heads_ref[h, 0]
        key_unit = heads_ref[h, 1]
        grad_query = contract(key_unit.astype(bf16), grad_scores, 1, 1) * valid
        grad_key = jnp.dot(query_unit.astype(bf16), grad_scores, preferred_element_type=f32)
        grad_query = scale_ref[h, 0:1] * (
            grad_query - query_unit * jnp.mean(query_unit * grad_query, 0, keepdims=True)
        )
        grad_key = scale_ref[h, 1:2] * (
            grad_key - key_unit * jnp.mean(key_unit * grad_key, 0, keepdims=True)
        )
        grad_value = up_head * mass_ref[h : h + 1]
        for part, values in enumerate((grad_query, grad_key, grad_value)):
            start = part * inner + h * HEAD
            grads_ref[start : start + HEAD, :] = values.astype(bf16)
    grad_query = grads_ref[0:inner, :]
    grad_key = grads_ref[inner : 2 * inner, :]
    grad_value = grads_ref[2 * inner : 3 * inner, :]
    for copy in copies[3:]:
        copy.wait()
    count = out_ref.shape[0]
    block = norm_ref.shape[0] // count
    first = jnp.zeros_like(valid)
    second = jnp.zeros_like(valid)
    for k in range(count):
        rows = slice(k * block, (k + 1) * block)
        part = jnp.dot(query_weights_ref[rows, :], grad_query, preferred_element_type=f32)
        part = part + jnp.dot(key_weights_ref[rows, :], grad_key, preferred_element_type=f32)
        part = part + jnp.dot(value_weights_ref[rows, :], grad_value, preferred_element_type=f32)
        out_ref[k, 0:block, :] = part.astype(bf16)
        first = first + jnp.sum(part, 0, keepdims=True)
        second = second + jnp.sum(part * norm_ref[rows, :].astype(f32), 0, keepdims=True)
    width = norm_ref.shape[0]
    stats = jnp.concatenate([first, second], 0) * (1.0 / width)
    high = stats.astype(bf16).astype(f32)
    stats = jnp.concatenate(
        [high, stats - high, jnp.zeros((EXTRA - 4, stats.shape[1]), f32)], 0
    ).astype(bf16)
    for k in range(count):
        out_ref[k, block : block + EXTRA, :] = stats


def wide_other(which, norm_ref, grads_ref, out_ref):
    chips, share, columns = out_ref.shape
    rows = [
        norm_ref[pl.ds(pl.multiple_of((CORES * chip + which[0]) * share, 16), share), :]
        for chip in range(chips)
    ]
    values = contract(jnp.concatenate(rows, 0), grads_ref[0:columns, :], 1, 1).astype(bf16)
    for chip in range(chips):
        out_ref[chip] = values[chip * share : (chip + 1) * share]


def wide_own(which, column, norm_ref, grads_ref, got_ref, *outs):
    side = len(outs)
    lines, share, columns = outs[0].shape
    chips = [
        line * side + lax.rem(column[0] + k, side) for k in range(side) for line in range(lines)
    ]
    rows = [
        norm_ref[pl.ds(pl.multiple_of((CORES * chip + which[0]) * share, 16), share), :]
        for chip in chips
    ]
    values = contract(jnp.concatenate(rows, 0), grads_ref[0:columns, :], 1, 1)
    for index, chip in enumerate(chips):
        part = values[index * share : (index + 1) * share] + got_ref[chip].astype(f32)
        outs[index // lines][index % lines] = part.astype(bf16)


def wide_line(line, *refs):
    side = len(refs) // 2
    for k in range(side):
        row = lax.rem(line[0] + k, side)
        total = refs[0][row].astype(f32)
        for ref in refs[1:side]:
            total = total + ref[row].astype(f32)
        refs[side + k][...] = total.astype(bf16)


def slot_grads(
    own_ref, valid_ref, stat_ref, chunk_ref, select_ref, extra_ref, parts_ref, out_ref
):
    total = parts_ref[0].astype(f32)
    for j in range(1, parts_ref.shape[0]):
        total = total + parts_ref[j].astype(f32)
    block = chunk_ref.shape[0] - EXTRA
    first = total[block : block + 1] + total[block + 2 : block + 3]
    second = total[block + 1 : block + 2] + total[block + 3 : block + 4]
    mean = stat_ref[0:1]
    inverse = stat_ref[1:2]
    normed = (chunk_ref[0:block, :].astype(f32) - mean) * inverse
    rows = own_ref[...] * valid_ref[...] + (total[:block] - first - normed * second) * inverse
    rows = contract(select_ref[...], rows.astype(bf16), 1, 1).astype(bf16)
    out_ref[...] = rows + extra_ref[...]


def tile_grads(back_ref, dispatch_ref, out_ref):
    piece = pack(contract(back_ref[...], dispatch_ref[...], 0, 0).astype(bf16))
    out_ref[...] = jnp.broadcast_to(piece[None], out_ref.shape)


def rows_of(which, ref, chips, share):
    rows = [
        ref[pl.ds(pl.multiple_of((CORES * chip + which) * share, 16), share), :]
        for chip in range(chips)
    ]
    return jnp.concatenate(rows, 0)


def other_two(other, hidden_ref, parts_ref, grad_ref, out_ref):
    count = parts_ref.shape[0]
    rows = grad_ref.shape[0] // count
    for j in range(count):
        grad_ref[j * rows : (j + 1) * rows, :] = unpack(parts_ref[j])
    chips, share = out_ref.shape[:2]
    rows = rows_of(other[0], grad_ref, chips, share)
    two = jnp.dot(rows, hidden_ref[...], preferred_element_type=f32).astype(bf16)
    for chip in range(chips):
        out_ref[chip] = two[chip * share : (chip + 1) * share]


def both_one(
    two_ref, slope_ref, other_norm_ref, own_norm_ref, grad_ref, out_ref, own_ref, hidden_grad_ref
):
    grad_hidden = jnp.dot(two_ref[...], grad_ref[...], preferred_element_type=f32)
    hidden_grad_ref[...] = (grad_hidden * slope_ref[...]).astype(bf16)
    chips, share = out_ref.shape[:2]
    for norm_ref, target_ref in ((other_norm_ref, out_ref), (own_norm_ref, own_ref)):
        one = contract(norm_ref[...], hidden_grad_ref[...], 1, 1).astype(bf16)
        for chip in range(chips):
            target_ref[chip] = one[chip * share : (chip + 1) * share]


def own_two(own, column, hidden_ref, grad_ref, got_ref, *outs):
    side = len(outs)
    lines, share = outs[0].shape[:2]
    for k in range(side):
        place = lax.rem(column[0] + k, side)
        chips = [line * side + place for line in range(lines)]
        rows = [
            grad_ref[pl.ds(pl.multiple_of((CORES * chip + own[0]) * share, 16), share), :]
            for chip in chips
        ]
        two = jnp.dot(jnp.concatenate(rows, 0), hidden_ref[...], preferred_element_type=f32)
        for line, chip in enumerate(chips):
            part = two[line * share : (line + 1) * share] + got_ref[chip].astype(f32)
            outs[k][line] = part.astype(bf16)


def own_one(own_ref, got_ref, out_ref):
    side = out_ref.shape[1]
    for chip in range(got_ref.shape[0]):
        part = own_ref[chip].astype(f32) + got_ref[chip].astype(f32)
        out_ref[chip // side, chip % side] = part.astype(bf16)


def add_up(*refs):
    total = refs[0][...].astype(f32)
    for ref in refs[1:-1]:
        total = total + ref[...].astype(f32)
    refs[-1][...] = total.astype(refs[-1].dtype)


def add_lines(column, lines_ref, *outs):
    side = len(outs)
    for k in range(side):
        place = lax.rem(column[0] + k, side)
        total = lines_ref[0, place].astype(f32)
        for line in range(1, lines_ref.shape[0]):
            total = total + lines_ref[line, place].astype(f32)
        outs[k][...] = total.astype(bf16)


def last_sums(lines_ref, *refs):
    one_ref, two_ref = refs[-2:]
    total = lines_ref[0].astype(f32)
    for line in range(1, lines_ref.shape[0]):
        total = total + lines_ref[line].astype(f32)
    two_ref[...] = total
    total = refs[0][...].astype(f32)
    for ref in refs[1:-2]:
        total = total + ref[...].astype(f32)
    one_ref[...] = total


def per_device(
    tile_features, tile_slide, slide_pair, reports, w_one, w_two, w_query, w_key, w_value, w_out
):
    lines = lax.axis_size("line")
    side = lax.axis_size("column")
    line = lax.axis_index("line")
    column = lax.axis_index("column")
    chips = lines * side
    owners = chips * CORES
    parts = lax.axis_size("mp")
    core = lax.axis_index("core")
    owner = lax.axis_index(DP)
    here = lax.axis_index("mp")
    tiles, width = tile_features.shape
    units = w_one.shape[1]
    capacity = 2 * tiles // owners
    length = owners * capacity
    slots = owners * ROWS
    block = width // parts
    share = width // owners
    inner = w_query.shape[1]
    heads = inner // HEAD
    packed = (block // 2 * 3, 128)

    def halves(values):
        rest = values.shape[1:]
        values = values.reshape((chips, CORES, share) + rest)
        own = pick(values, core, 1).reshape((chips * share,) + rest)
        other = pick(values, 1 - core, 1).reshape((chips * share,) + rest)
        return own, other

    tile_norm, hidden, slope, partial = call(
        tile_forward,
        [
            ((tiles, width), bf16),
            ((tiles, units), bf16),
            ((tiles, units), f32),
            ((parts,) + packed, bf16),
        ],
        tile_features,
        w_one,
        w_two,
        far=(0, 1, 2),
        scratch=[
            (tile_features.shape, bf16),
            (w_one.shape, bf16),
            (w_two.shape, bf16),
            3,
        ],
        limit=62,
    )
    partial = exchange(partial, "mp")

    slide_ids = tile_slide[:, 0]
    matches = (slide_ids[:, None] == jnp.arange(owners, dtype=i32)[None, :]).astype(i32)
    ordinal = jnp.sum(matches * (jnp.cumsum(matches, 0) - 1), 1)
    position = slide_ids * ROWS + ordinal
    dispatch = jnp.arange(slots, dtype=i32)[:, None] == position[None, :]
    flags = jnp.sum(dispatch.astype(f32), 1, keepdims=True).astype(bf16)
    flags = jnp.pad(flags, ((0, 0), (0, 256 - block - 1)))
    dispatch = dispatch.astype(bf16)
    slot = jnp.arange(slots, dtype=i32)
    row_of_slot = jnp.where(slot % ROWS < capacity, slot // ROWS * capacity + slot % ROWS, -1)
    select = (row_of_slot[:, None] == jnp.arange(length, dtype=i32)[None, :]).astype(bf16)
    last_slot = jnp.arange(owners, dtype=i32)[:, None] * ROWS + ROWS - 1
    report_select = (last_slot == slot[None, :]).astype(bf16)
    own_columns = pick(tile_features.reshape(tiles, parts, block), here, 1)
    own_report = pick(reports.reshape(1, parts, block), here, 1)
    tile_own, tile_other = halves(tile_norm.T)
    slope = slope.T

    (outgoing,) = call(
        tile_dispatch,
        [((slots, 256), bf16)],
        own_columns,
        own_report,
        dispatch,
        flags,
        partial,
        anchors=(select, report_select, tile_own, tile_other, slope),
    )
    arrived = exchange(outgoing.reshape(owners, ROWS, 256), DP).reshape(slots, 256)
    chunk, valid = call(
        slot_rows,
        [((block + EXTRA, length), bf16), ((1, length), f32)],
        arrived,
        select,
        report_select,
    )
    pieces = gather_ring(chunk, parts)

    (
        slide_norm,
        by_head,
        attention,
        stat,
        scales,
        mass,
        attended_sum,
        pooled,
        all_reports,
    ) = call(
        slide_forward,
        [
            ((width, length), bf16, "far"),
            ((heads, 3, HEAD, length), f32, "far"),
            ((heads, length, length), bf16, "far"),
            ((2, length), f32),
            ((heads, 2, length), f32),
            ((heads, length), f32),
            ((1, inner), f32),
            ((parts, 1, width), f32),
            ((parts, owners, block), bf16),
        ],
        valid,
        w_query.T,
        w_key.T,
        w_value.T,
        w_out,
        *pieces,
        scalars=(here,),
        far=(1, 2, 3, 4),
        scratch=[
            ((width, length), bf16),
            ((width, length), bf16),
            ((heads, 3, HEAD, length), f32),
            ((heads, length, length), bf16),
            ((inner, width), bf16),
            ((inner, width), bf16),
            ((inner, width), bf16),
            ((inner, width), bf16),
            4,
            1 + 2 * heads,
        ],
        limit=60,
    )
    pooled = exchange(pooled, "mp")
    (row,) = call(
        logits_row,
        [((owners, 1, 128), f32)],
        pooled,
        all_reports,
        scratch=[((owners, width), f32)],
    )
    logits = exchange(row, DP).reshape(owners, 128)
    loss, grad, up, grads, sending = call(
        slide_backward,
        [((1, 1), f32), ((1, width), f32), ((1, inner), f32), ((3 * inner, length), bf16)]
        + [((parts, block + EXTRA, length), bf16)],
        logits,
        slide_pair[:, None],
        pooled,
        all_reports,
        valid,
        scales,
        mass,
        w_out,
        by_head,
        attention,
        w_query,
        w_key,
        w_value,
        slide_norm,
        scalars=(owner,),
        far=tuple(range(7, 14)),
        scratch=[
            (w_out.shape, bf16),
            (by_head.shape, f32),
            (attention.shape, bf16),
            (w_query.shape, bf16),
            (w_key.shape, bf16),
            (w_value.shape, bf16),
            (slide_norm.shape, bf16),
            ((owners, width), f32),
            7,
        ],
        limit=60,
    )
    received = exchange(sending, "mp")

    (wide_sent,) = call(
        wide_other,
        [((chips, share, 2 * inner), bf16)],
        slide_norm,
        grads,
        scalars=(1 - core,),
    )
    wide_got = lax.ppermute(wide_sent, "core", [(0, 1), (1, 0)])
    along = call(
        wide_own,
        [((lines, share, 2 * inner), bf16)] * side,
        slide_norm,
        grads,
        wide_got,
        scalars=(core, column),
    )
    def shift(values, axis):
        return [values[0]] + [
            lax.ppermute(values[k], axis, turn(len(values), k)) for k in range(1, len(values))
        ]

    along = shift(along, "column")
    across = call(
        wide_line, [((share, 2 * inner), bf16)] * lines, *along, scalars=(line,)
    )
    across = shift(across, "line")
    grad_wide = sum(part.astype(f32) for part in across)
    value_rows = contract(mass.astype(bf16), slide_norm, 1, 1)
    extra = jnp.concatenate(
        [
            value_rows.reshape(heads, owners, share).transpose(1, 0, 2).reshape(owners, -1),
            grad.reshape(owners, share),
            jnp.broadcast_to(up, (owners, inner)),
            jnp.broadcast_to(attended_sum, (owners, inner)),
        ],
        1,
    ).astype(bf16)
    spare = ROWS - capacity
    extra = jnp.pad(extra, ((0, 0), (0, spare * block - extra.shape[1])))
    extra = extra.reshape(owners, spare, block)
    extra = jnp.pad(extra, ((0, 0), (capacity, 0), (0, 0))).reshape(slots, block)

    own_grad = lax.dynamic_slice_in_dim(grad, here * block, block, 1).reshape(block, 1)
    (going,) = call(
        slot_grads,
        [((slots, block), bf16)],
        own_grad,
        valid,
        stat,
        chunk,
        select,
        extra,
        received,
        anchors=(grad_wide,),
    )
    back = exchange(going.reshape(owners, ROWS, block), DP).reshape(slots, block)
    (spreading,) = call(tile_grads, [((parts,) + packed, bf16)], back, dispatch)

    size = (chips, share, units)
    swap = [(0, 1), (1, 0)]
    grad_embedding, two_sent = call(
        other_two,
        [((width, tiles), bf16), (size, bf16)],
        hidden,
        exchange(spreading, "mp"),
        scalars=(1 - core,),
    )
    two_got = lax.ppermute(two_sent, "core", swap)
    one_sent, one_own = call(
        both_one,
        [(size, bf16), (size, bf16)],
        w_two,
        slope,
        tile_other,
        tile_own,
        grad_embedding,
        scratch=[((units, tiles), bf16)],
    )
    one_got = lax.ppermute(one_sent, "core", swap)
    two_along = call(
        own_two,
        [((lines, share, units), bf16)] * side,
        hidden,
        grad_embedding,
        two_got,
        scalars=(core, column),
    )
    (one_across,) = call(
        own_one,
        [((lines, side, share, units), bf16)],
        one_own,
        one_got,
        anchors=(two_along[0],),
    )
    two_along = shift(two_along, "column")
    one_across = exchange(one_across, "line")
    (two_across,) = call(add_up, [((lines, share, units), bf16)], *two_along)
    one_along = call(add_lines, [((share, units), bf16)] * side, one_across, scalars=(column,))
    grad_one, grad_two = call(
        last_sums,
        [((share, units), f32)] * 2,
        exchange(two_across, "line"),
        *shift(one_along, "column"),
    )
    grad_two = grad_two.T

    terms = back.reshape(owners, ROWS, block)[:, capacity:].reshape(owners, -1).astype(f32)
    edge = heads * share
    from_values = terms[:, :edge].reshape(owners, heads, share)
    from_grads = terms[:, edge : edge + share]
    edge = edge + share
    from_up = terms[:, edge : edge + inner].reshape(owners, heads, HEAD)
    edge = edge + inner
    from_attended = terms[:, edge : edge + inner]
    grad_value = jnp.einsum("ohs,ohd->shd", from_values, from_up, precision=exact)
    grad_value = grad_value.reshape(share, inner)
    grad_out = contract(from_attended, from_grads, 0, 0, precision=exact)
    return (
        loss[0, 0],
        grad_one,
        grad_two,
        grad_wide[:, :inner],
        grad_wide[:, inner:],
        grad_value,
        grad_out,
    )


def solution(mesh):
    owners, parts = mesh.devices.shape
    side = math.isqrt(owners // CORES)
    split = Mesh(
        mesh.devices.reshape(owners // CORES // side, side, CORES, parts),
        ("line", "column", "core", "mp"),
    )
    return jax.shard_map(
        per_device,
        mesh=split,
        in_specs=(
            P(DP, None),
            P(DP, None),
            P(),
            P(DP, None),
            P(None, "mp"),
            P("mp", None),
            P(None, "mp"),
            P(None, "mp"),
            P(None, "mp"),
            P("mp", None),
        ),
        out_specs=(
            P(),
            P(DP, "mp"),
            P("mp", DP),
            P(DP, "mp"),
            P(DP, "mp"),
            P(DP, "mp"),
            P("mp", DP),
        ),
        check_vma=False,
    )
```
